32 devices in a mesh: section: 4 (over y, core), seq: 8 (over z, x).
Axes of the slice: x: 2, y: 2, z: 4, core: 2. Of those that a mesh axis runs over, the one named last changes fastest.
Arguments:
- activations: bfloat16 [4, 1088, 1024], P('section', 'seq'), may hold values from -60 to 60
- incoming: bfloat16 [4, 1088, 1024], P('section', 'seq'), may hold values from -6 to 6
- w_query: bfloat16 [4, 1024, 512], P('section'), may hold values from -0.1875 to 0.1875
- w_key: bfloat16 [4, 1024, 512], P('section'), may hold values from -0.1875 to 0.1875
- w_value: bfloat16 [4, 1024, 512], P('section'), may hold values from -0.1875 to 0.1875
- w_out: bfloat16 [4, 512, 2048], P('section'), may hold values from -0.25 to 0.25
- block_ids: int32 [1088], replicated, may hold values from 0 to 33, never falling along the last dimension, each value on 1 to 256 neighbouring positions
- flip_order: int32 [4, 136], P('section'), may hold values from 0 to 135, each once within a row
Outputs:
- carry_out: bfloat16 [4, 1088, 1024], P('section', 'seq')
- grad_query: float32 [4, 1024, 512], P('section', 'seq')
- grad_key: float32 [4, 1024, 512], P('section', 'seq')
- grad_value: float32 [4, 1024, 512], P('section', 'seq')
- grad_out: float32 [4, 512, 2048], P('section', 'seq')
The draws below stay inside these ranges and needn't reach their ends.
Inputs may be any that keep to these rules, and one draw needn't show every extreme that they name: `block_ids`: block ids never fall along the sequence; each block holds 1 to 256 tokens, one exactly 256. `flip_order`: each row is a permutation.
All inputs are finite; a program needn't handle non-finite values.
Results may differ from the reference program's by a relative error of at most 0.03.
Values may be sent and summed in bfloat16 or wider, within the bound.
No kernel may reach another device: no remote copies, remote signals or barrier semaphores. Data moves between devices by JAX's collectives and lax.ppermute only.
A program may use at most 128 MiB of HBM per device.

```python
import math
import jax
import jax.numpy as jnp
import numpy as np
from jax import lax

D = 1024
HEADS = 8
HEAD_DIM = 64
BLOCK_MOST = 256
TOK_DEV = 136
INNER = 512
TOKENS = 1088
SECTIONS = 4
BLOCKS = 34
N_SEQ = 8


def draw_activations(key, part):
    base_key, row_key, column_key = jax.random.split(key, 3)
    shape = (SECTIONS, TOKENS, D)
    base = jnp.clip(jax.random.normal(base_key, shape, jnp.float32), -6.0, 6.0)
    row_scale = jnp.exp(jax.random.uniform(row_key, (SECTIONS, TOKENS, 1), jnp.float32, math.log(0.3), math.log(3.0)))
    column_scale = jnp.exp(jax.random.uniform(column_key, (SECTIONS, 1, D), jnp.float32, math.log(0.3), math.log(3.0)))
    return (base * row_scale * column_scale).astype(jnp.bfloat16)


def steps_of(stream_key, extent, cuts, smallest, high):
    def one(position, blocks):
        draws = jax.random.uniform(jax.random.fold_in(jax.random.fold_in(stream_key, 6), position), (blocks,), jnp.float32, smallest / len(cuts), high / len(cuts))
        return jnp.repeat(jnp.exp(draws), extent[position] // blocks).reshape((-1,) + (1,) * (len(extent) - position - 1))

    level = one(*cuts[0])
    for cut in cuts[1:]:
        level = level * one(*cut)
    return level


def split_up(number_of, total, most, lean):
    weights = [(1 << 20) // math.isqrt(standing ** lean) + 1 for standing in range(2, number_of + 1)]
    spare, counts = total - most - (number_of - 1), [1] * (number_of - 1)
    while spare > 0:
        candidates = [i for i in range(number_of - 1) if counts[i] < most]
        whole, remaining = sum([weights[i] for i in candidates]), spare
        for i in candidates:
            more = min(most - counts[i], max(1, remaining * weights[i] // whole), spare)
            counts[i] = counts[i] + more
            spare = spare - more
    return np.array([most] + counts)


def ragged(key, count, total, bound, lean):
    if count == 2:
        one = jax.random.randint(key, (), max(1, total - bound), min(bound, total - 1) + 1)
        return jnp.stack([one, total - one])
    sizes = jnp.asarray(split_up(count, total, bound, lean), jnp.int32)
    pairs = (count - 1) // 2
    donor, taker = sizes[1:1 + 2 * pairs:2], sizes[2:2 + 2 * pairs:2]
    margin = jnp.minimum(donor - 1, bound - taker)
    shifted = jax.random.randint(jax.random.fold_in(key, 1), (pairs,), 0, 1 << 20) % (margin + 1)
    sizes = sizes.at[1:1 + 2 * pairs:2].set(donor - shifted).at[2:2 + 2 * pairs:2].set(taker + shifted)
    return sizes[jax.random.permutation(jax.random.fold_in(key, 2), count)]


def noise(key, shape, deviation, limit, cuts=(), dtype=jnp.bfloat16):
    drawn = deviation * jax.random.normal(key, shape, jnp.float32)
    if cuts:
        drawn = drawn * steps_of(key, shape, cuts, -0.22, 0.18)
    return jnp.clip(drawn, -limit, limit).astype(dtype)


def setup_inputs(seed: int = 0) -> dict:
    seeds = jax.random.split(jax.random.key(seed), 9)
    return {
        "activations": draw_activations(jax.random.fold_in(seeds[8], 71), 0),
        "incoming": noise(seeds[1], (SECTIONS, TOKENS, D), 1.0, 6.0, ((0, 4), (1, 8))),
        "w_query": noise(seeds[2], (SECTIONS, D, INNER), D ** -0.5, 0.1875, ((0, 4),)),
        "w_key": noise(seeds[3], (SECTIONS, D, INNER), D ** -0.5, 0.1875, ((0, 4),)),
        "w_value": noise(seeds[4], (SECTIONS, D, INNER), D ** -0.5, 0.1875, ((0, 4),)),
        "w_out": noise(seeds[5], (SECTIONS, INNER, 2 * D), INNER ** -0.5, 0.25, ((0, 4),)),
        "block_ids": jnp.searchsorted(jnp.cumsum(ragged(seeds[6], BLOCKS, TOKENS, BLOCK_MOST, 2)), jnp.arange(TOKENS), side="right").astype(jnp.int32),
        "flip_order": jax.vmap(lambda own: jax.random.permutation(own, TOK_DEV))(jax.random.split(seeds[7], SECTIONS)).reshape((SECTIONS, TOK_DEV)).astype(jnp.int32),
    }


EPSILON = 1e-06

def unit_heads(projected):
    parts = projected.reshape(projected.shape[0], HEADS, HEAD_DIM)
    factor = lax.rsqrt(lax.optimization_barrier(jnp.mean(parts * parts, axis=-1, keepdims=True)) + EPSILON)
    return (parts * factor, factor)

def unit_back(grad_heads, unit, factor):
    return factor * (grad_heads - unit * lax.optimization_barrier(jnp.mean(grad_heads * unit, axis=-1, keepdims=True)))

def head_major(matrix):
    return jnp.transpose(matrix.reshape(matrix.shape[0], HEADS, HEAD_DIM), (1, 0, 2))

def group_sum(left, right):
    left_groups = left.astype(jnp.float32).reshape(N_SEQ, TOK_DEV, left.shape[1])
    right_groups = right.astype(jnp.float32).reshape(N_SEQ, TOK_DEV, right.shape[1])
    terms = jnp.einsum('ntc,nte->nce', left_groups, right_groups)
    rounded = lax.optimization_barrier(terms.astype(jnp.bfloat16))
    return lax.optimization_barrier(jnp.sum(rounded.astype(jnp.float32), axis=0))

def layer_backward(field_low, cotangent, weight_query, weight_key, weight_value, weight_out, block_ids):
    field = field_low.astype(jnp.float32)
    upstream = cotangent.astype(jnp.float32)
    length = field.shape[0]
    scale = HEAD_DIM ** (-0.5)
    row_scale = lax.rsqrt(lax.optimization_barrier(jnp.mean(field * field, axis=-1, keepdims=True)) + EPSILON)
    unit_rows = field * row_scale
    normed = unit_rows.astype(jnp.bfloat16)
    query_raw = jnp.dot(normed, weight_query, preferred_element_type=jnp.float32)
    key_raw = jnp.dot(normed, weight_key, preferred_element_type=jnp.float32)
    values = jnp.dot(normed, weight_value, preferred_element_type=jnp.float32).astype(jnp.bfloat16)
    query_unit, query_scale = unit_heads(query_raw)
    key_unit, key_scale = unit_heads(key_raw)
    queries = query_unit.astype(jnp.bfloat16).reshape(length, INNER)
    keys = key_unit.astype(jnp.bfloat16).reshape(length, INNER)
    allowed = block_ids[None, :] <= block_ids[:, None]

    def probabilities(query_part, key_part):
        scores = jnp.dot(query_part, key_part.T, preferred_element_type=jnp.float32) * scale
        numerator = jnp.where(allowed, jnp.exp(scores), 0.0)
        return numerator / lax.optimization_barrier(jnp.sum(numerator, axis=-1, keepdims=True))

    def forward_head(operands):
        query_part, key_part, value_part = operands
        probs = probabilities(query_part, key_part)
        return jnp.dot(probs.astype(jnp.bfloat16), value_part, preferred_element_type=jnp.float32).astype(jnp.bfloat16)
    query_heads = head_major(queries)
    key_heads = head_major(keys)
    value_heads = head_major(values)
    heads_out = lax.map(forward_head, (query_heads, key_heads, value_heads))
    attended = jnp.transpose(heads_out, (1, 0, 2)).reshape(length, INNER)
    affine = jnp.dot(attended, weight_out, preferred_element_type=jnp.float32)
    shift_part = affine[:, :D]
    log_scale = affine[:, D:]
    factor = jnp.exp(-log_scale)
    latent = (field - shift_part) * factor
    grad_affine = jnp.concatenate([-upstream * factor, 1.0 - upstream * latent], axis=-1).astype(jnp.bfloat16)
    grad_out = group_sum(attended, grad_affine)
    grad_attn = jnp.dot(grad_affine, weight_out.T, preferred_element_type=jnp.float32).astype(jnp.bfloat16)
    grad_heads = head_major(grad_attn)

    def backward_head(operands):
        query_part, key_part, value_part, grad_part, out_part = operands
        probs = probabilities(query_part, key_part)
        grad_probs = jnp.dot(grad_part, value_part.T, preferred_element_type=jnp.float32)
        correction = lax.optimization_barrier(jnp.sum(grad_part.astype(jnp.float32) * out_part.astype(jnp.float32), axis=-1, keepdims=True))
        grad_scores = (probs * (grad_probs - correction)).astype(jnp.bfloat16)
        grad_qpart = jnp.dot(grad_scores, key_part, preferred_element_type=jnp.float32) * scale
        grad_kpart = jnp.dot(grad_scores.T, query_part, preferred_element_type=jnp.float32) * scale
        grad_vpart = jnp.dot(probs.astype(jnp.bfloat16).T, grad_part, preferred_element_type=jnp.float32)
        return (grad_qpart, grad_kpart, grad_vpart)
    grad_qheads, grad_kheads, grad_vheads = lax.map(backward_head, (query_heads, key_heads, value_heads, grad_heads, heads_out))
    grad_queries = unit_back(jnp.transpose(grad_qheads, (1, 0, 2)), query_unit, query_scale).reshape(length, INNER).astype(jnp.bfloat16)
    grad_keys = unit_back(jnp.transpose(grad_kheads, (1, 0, 2)), key_unit, key_scale).reshape(length, INNER).astype(jnp.bfloat16)
    grad_values = jnp.transpose(grad_vheads, (1, 0, 2)).reshape(length, INNER).astype(jnp.bfloat16)
    grad_query = group_sum(normed, grad_queries)
    grad_key = group_sum(normed, grad_keys)
    grad_value = group_sum(normed, grad_values)
    grad_normed = jnp.dot(grad_queries, weight_query.T, preferred_element_type=jnp.float32)
    grad_normed = grad_normed + jnp.dot(grad_keys, weight_key.T, preferred_element_type=jnp.float32)
    grad_normed = grad_normed + jnp.dot(grad_values, weight_value.T, preferred_element_type=jnp.float32)
    grad_input = upstream * factor + row_scale * (grad_normed - unit_rows * lax.optimization_barrier(jnp.mean(grad_normed * unit_rows, axis=-1, keepdims=True)))
    return (grad_input.astype(jnp.bfloat16), grad_query, grad_key, grad_value, grad_out)

def reference(activations, incoming, w_query, w_key, w_value, w_out, block_ids, flip_order):
    results = []
    for layer in range(SECTIONS):
        results.append(layer_backward(activations[layer], incoming[layer], w_query[layer], w_key[layer], w_value[layer], w_out[layer], block_ids))
    carries = []
    for layer in range(SECTIONS):
        if layer + 1 < SECTIONS:
            grouped = results[layer + 1][0].reshape(N_SEQ, TOK_DEV, D)[::-1]
            carries.append(grouped[:, flip_order[layer], :].reshape(TOKENS, D))
        else:
            carries.append(jnp.zeros((TOKENS, D), jnp.bfloat16))
    carry_out = jnp.stack(carries)
    grad_query = jnp.stack([item[1] for item in results])
    grad_key = jnp.stack([item[2] for item in results])
    grad_value = jnp.stack([item[3] for item in results])
    grad_out = jnp.stack([item[4] for item in results])
    return (carry_out, grad_query, grad_key, grad_value, grad_out)
```

```python
import jax
import jax.numpy as jnp
from jax import lax
from jax.sharding import PartitionSpec as P

HEADS = 8
HEAD_DIM = 64


EPSILON = 1e-06


def partner(block, axis, stride):
    count = lax.axis_size(axis)
    route = []
    for low in range(count):
        high = low | 1 << stride
        if high != low and high < count:
            route += [(low, high), (high, low)]
    return lax.ppermute(block, axis, route)


def shifted(block, axis, distance):
    devices = range(lax.axis_size(axis))
    route = [(i - distance, i) for i in devices if i - distance in devices]
    return lax.ppermute(block, axis, route)


def split_heads(matrix):
    return matrix.reshape(matrix.shape[0], HEADS, HEAD_DIM)


def head_major(matrix):
    return jnp.transpose(split_heads(matrix), (1, 0, 2))


def unit_heads(projected):
    parts = split_heads(projected)
    factor = lax.rsqrt(jnp.mean(parts * parts, axis=-1, keepdims=True) + EPSILON)
    return (parts * factor, factor)


def unit_back(grad_heads, unit, factor):
    return factor * (grad_heads - unit * jnp.mean(grad_heads * unit, axis=-1, keepdims=True))


def mirror(rows):
    for bit in range(lax.axis_size("seq").bit_length() - 1):
        rows = partner(rows, "seq", bit)
    return rows


def to_previous(rows):
    return shifted(rows, "section", -1)


def general_shards(activations, incoming, w_query, w_key, w_value, w_out, block_ids, flip_order):
    field = activations[0].astype(jnp.float32)
    upstream = incoming[0].astype(jnp.float32)
    weight_query = w_query[0]
    weight_key = w_key[0]
    weight_value = w_value[0]
    weight_out = w_out[0]
    flip_row = flip_order[0]
    rows = field.shape[0]
    width = field.shape[1]
    inner = weight_query.shape[1]
    scale = HEAD_DIM ** (-0.5)
    first = lax.axis_index("seq") * rows
    my_blocks = lax.dynamic_slice_in_dim(block_ids, first, rows)
    row_scale = lax.rsqrt(jnp.mean(field * field, axis=-1, keepdims=True) + EPSILON)
    unit_rows = field * row_scale
    normed = unit_rows.astype(jnp.bfloat16)
    query_raw = jnp.dot(normed, weight_query, preferred_element_type=jnp.float32)
    key_raw = jnp.dot(normed, weight_key, preferred_element_type=jnp.float32)
    values = jnp.dot(normed, weight_value, preferred_element_type=jnp.float32).astype(jnp.bfloat16)
    query_unit, query_scale = unit_heads(query_raw)
    key_unit, key_scale = unit_heads(key_raw)
    queries = query_unit.astype(jnp.bfloat16).reshape(rows, inner)
    keys = key_unit.astype(jnp.bfloat16).reshape(rows, inner)
    keys_all, values_all = (
        lax.all_gather(keys, "seq", axis=0, tiled=True),
        lax.all_gather(values, "seq", axis=0, tiled=True),
    )
    allowed = block_ids[None, :] <= my_blocks[:, None]
    query_heads = head_major(queries)
    key_heads_all = head_major(keys_all)
    value_heads_all = head_major(values_all)

    def probabilities(query_part, key_part):
        scores = jnp.dot(query_part, key_part.T, preferred_element_type=jnp.float32) * scale
        numerator = jnp.where(allowed, jnp.exp(scores), 0.0)
        denominator = jnp.sum(numerator, axis=-1, keepdims=True)
        return (numerator / denominator, denominator)

    def forward_head(operands):
        query_part, key_part, value_part = operands
        probs, denominator = probabilities(query_part, key_part)
        out_part = jnp.dot(
            probs.astype(jnp.bfloat16), value_part, preferred_element_type=jnp.float32
        ).astype(jnp.bfloat16)
        return (out_part, denominator[:, 0])

    heads_out, denominators = lax.map(forward_head, (query_heads, key_heads_all, value_heads_all))
    attended = jnp.transpose(heads_out, (1, 0, 2)).reshape(rows, inner)
    affine = jnp.dot(attended, weight_out, preferred_element_type=jnp.float32)
    shift_part = affine[:, :width]
    log_scale = affine[:, width:]
    factor = jnp.exp(-log_scale)
    latent = (field - shift_part) * factor
    grad_affine = jnp.concatenate([-upstream * factor, 1.0 - upstream * latent], axis=-1).astype(
        jnp.bfloat16
    )
    out_term = jnp.dot(attended.T, grad_affine, preferred_element_type=jnp.float32)
    grad_attn = jnp.dot(grad_affine, weight_out.T, preferred_element_type=jnp.float32).astype(
        jnp.bfloat16
    )
    correction = jnp.sum(
        split_heads(grad_attn.astype(jnp.float32)) * split_heads(attended.astype(jnp.float32)),
        axis=-1,
    )
    grad_heads = head_major(grad_attn)
    correction_heads = jnp.transpose(correction)[:, :, None]

    def backward_head(operands):
        query_part, key_part, value_part, grad_part, corr_part = operands
        probs, denominator = probabilities(query_part, key_part)
        grad_probs = jnp.dot(grad_part, value_part.T, preferred_element_type=jnp.float32)
        grad_scores = (probs * (grad_probs - corr_part)).astype(jnp.bfloat16)
        grad_qpart = jnp.dot(grad_scores, key_part, preferred_element_type=jnp.float32) * scale
        grad_kpart = jnp.dot(grad_scores.T, query_part, preferred_element_type=jnp.float32) * scale
        grad_vpart = jnp.dot(
            probs.astype(jnp.bfloat16).T, grad_part, preferred_element_type=jnp.float32
        )
        return (grad_qpart, grad_kpart, grad_vpart)

    grad_qheads, grad_kall, grad_vall = lax.map(
        backward_head, (query_heads, key_heads_all, value_heads_all, grad_heads, correction_heads)
    )
    key_terms = jnp.transpose(grad_kall, (1, 0, 2)).reshape(-1, inner)
    value_terms = jnp.transpose(grad_vall, (1, 0, 2)).reshape(-1, inner)
    grad_kunit, grad_vsum = (
        lax.psum_scatter(
            key_terms.astype(jnp.bfloat16), "seq", scatter_dimension=0, tiled=True
        ).astype(jnp.float32),
        lax.psum_scatter(
            value_terms.astype(jnp.bfloat16), "seq", scatter_dimension=0, tiled=True
        ).astype(jnp.float32),
    )
    grad_queries = (
        unit_back(jnp.transpose(grad_qheads, (1, 0, 2)), query_unit, query_scale)
        .reshape(rows, inner)
        .astype(jnp.bfloat16)
    )
    grad_keys = (
        unit_back(split_heads(grad_kunit), key_unit, key_scale)
        .reshape(rows, inner)
        .astype(jnp.bfloat16)
    )
    grad_values = grad_vsum.astype(jnp.bfloat16)
    query_term = jnp.dot(normed.T, grad_queries, preferred_element_type=jnp.float32)
    key_term = jnp.dot(normed.T, grad_keys, preferred_element_type=jnp.float32)
    value_term = jnp.dot(normed.T, grad_values, preferred_element_type=jnp.float32)
    sums = (
        lax.psum_scatter(
            query_term.astype(jnp.bfloat16), "seq", scatter_dimension=0, tiled=True
        ).astype(jnp.float32),
        lax.psum_scatter(
            key_term.astype(jnp.bfloat16), "seq", scatter_dimension=0, tiled=True
        ).astype(jnp.float32),
        lax.psum_scatter(
            value_term.astype(jnp.bfloat16), "seq", scatter_dimension=0, tiled=True
        ).astype(jnp.float32),
        lax.psum_scatter(
            out_term.astype(jnp.bfloat16), "seq", scatter_dimension=0, tiled=True
        ).astype(jnp.float32),
    )
    grad_normed = jnp.dot(grad_queries, weight_query.T, preferred_element_type=jnp.float32)
    grad_normed = grad_normed + jnp.dot(grad_keys, weight_key.T, preferred_element_type=jnp.float32)
    grad_normed = grad_normed + jnp.dot(
        grad_values, weight_value.T, preferred_element_type=jnp.float32
    )
    grad_input = upstream * factor + row_scale * (
        grad_normed - unit_rows * jnp.mean(grad_normed * unit_rows, axis=-1, keepdims=True)
    )
    grad_input = grad_input.astype(jnp.bfloat16)
    moved = mirror(to_previous(grad_input))
    carry = jnp.take(moved, flip_row, axis=0)
    return (carry[None], sums[0][None], sums[1][None], sums[2][None], sums[3][None])


def to_heads(matrix, parts):
    rows = matrix[0].shape[0]
    slabs = jnp.concatenate([head_major(part) for part in matrix], axis=-1)
    moved = lax.all_to_all(slabs, "seq", split_axis=0, concat_axis=0, tiled=True)
    return moved.reshape(parts * rows, -1)


def to_tokens(columns, parts):
    slabs = columns.reshape(parts, -1, columns.shape[-1])
    return lax.all_to_all(slabs, "seq", split_axis=0, concat_axis=0, tiled=True)


def side_by_side(slabs):
    return jnp.transpose(slabs, (1, 0, 2)).reshape(slabs.shape[1], -1)


def head_shards(
    activations, incoming, w_query, w_key, w_value, w_out, block_ids, flip_order
):
    parts = lax.axis_size("seq")
    sections = lax.axis_size("section")
    mine = lax.axis_index("seq")
    field = activations[0].astype(jnp.float32)
    upstream = incoming[0].astype(jnp.float32)
    weight_query, weight_key, weight_value, weight_out = w_query[0], w_key[0], w_value[0], w_out[0]
    rows, width = field.shape
    inner = weight_query.shape[1]
    scale = HEAD_DIM ** (-0.5)
    row_scale = lax.rsqrt(jnp.mean(field * field, axis=-1, keepdims=True) + EPSILON)
    unit_rows = field * row_scale
    normed = unit_rows.astype(jnp.bfloat16)
    query_raw = jnp.dot(normed, weight_query, preferred_element_type=jnp.float32)
    key_raw = jnp.dot(normed, weight_key, preferred_element_type=jnp.float32)
    values = jnp.dot(normed, weight_value, preferred_element_type=jnp.float32).astype(jnp.bfloat16)
    queries = unit_heads(query_raw)[0].astype(jnp.bfloat16).reshape(rows, inner)
    keys = unit_heads(key_raw)[0].astype(jnp.bfloat16).reshape(rows, inner)
    own = to_heads((queries, keys, values), parts)
    normed_all = lax.all_gather(normed, "seq", axis=0, tiled=True)
    query, key, value = jnp.split(own, 3, axis=-1)
    allowed = block_ids[None, :] <= block_ids[:, None]
    scores = jnp.dot(query, key.T, preferred_element_type=jnp.float32) * scale
    numerator = jnp.where(allowed, jnp.exp(scores), 0.0)
    probs = numerator / jnp.sum(numerator, axis=-1, keepdims=True)
    probs_low = probs.astype(jnp.bfloat16)
    head_out = jnp.dot(probs_low, value, preferred_element_type=jnp.float32).astype(jnp.bfloat16)
    attended = side_by_side(to_tokens(head_out, parts))
    affine = jnp.dot(attended, weight_out, preferred_element_type=jnp.float32)
    factor = jnp.exp(-affine[:, width:])
    latent = (field - affine[:, :width]) * factor
    grad_affine = jnp.concatenate([-upstream * factor, 1.0 - upstream * latent], axis=-1).astype(
        jnp.bfloat16
    )
    grad_attn = jnp.dot(grad_affine, weight_out.T, preferred_element_type=jnp.float32).astype(
        jnp.bfloat16
    )
    grad_own = to_heads((grad_attn,), parts)
    out_term = jnp.dot(attended.T, grad_affine, preferred_element_type=jnp.float32)
    grad_out = lax.psum_scatter(
        out_term.astype(jnp.bfloat16), "seq", scatter_dimension=0, tiled=True
    ).astype(jnp.float32)
    correction = jnp.sum(
        grad_own.astype(jnp.float32) * head_out.astype(jnp.float32), axis=-1, keepdims=True
    )
    grad_probs = jnp.dot(grad_own, value.T, preferred_element_type=jnp.float32)
    grad_scores = (probs * (grad_probs - correction)).astype(jnp.bfloat16)
    grad_q = jnp.dot(grad_scores, key, preferred_element_type=jnp.float32) * scale
    grad_k = jnp.dot(grad_scores.T, query, preferred_element_type=jnp.float32) * scale
    grad_v = jnp.dot(probs_low.T, grad_own, preferred_element_type=jnp.float32)

    def own_columns(weight):
        return lax.dynamic_slice_in_dim(weight, mine * HEAD_DIM, HEAD_DIM, axis=1)

    def own_back(grad, weight):
        raw = jnp.dot(normed_all, own_columns(weight), preferred_element_type=jnp.float32)
        back_scale = lax.rsqrt(jnp.mean(raw * raw, axis=-1, keepdims=True) + EPSILON)
        return unit_back(grad, raw * back_scale, back_scale)

    grads = jnp.concatenate(
        [own_back(grad_q, weight_query), own_back(grad_k, weight_key), grad_v], axis=-1
    ).astype(jnp.bfloat16)
    token_grads = to_tokens(grads, parts)
    grad_queries, grad_keys, grad_values = [
        side_by_side(part) for part in jnp.split(token_grads, 3, axis=-1)
    ]
    weight_terms = jnp.dot(normed_all.T, grads, preferred_element_type=jnp.float32)
    weight_terms = to_tokens(weight_terms.astype(jnp.bfloat16), parts)
    sums = [
        side_by_side(part).astype(jnp.float32) for part in jnp.split(weight_terms, 3, axis=-1)
    ]
    grad_normed = jnp.dot(grad_queries, weight_query.T, preferred_element_type=jnp.float32)
    grad_normed = grad_normed + jnp.dot(grad_keys, weight_key.T, preferred_element_type=jnp.float32)
    grad_normed = grad_normed + jnp.dot(
        grad_values, weight_value.T, preferred_element_type=jnp.float32
    )
    grad_input = upstream * factor + row_scale * (
        grad_normed - unit_rows * jnp.mean(grad_normed * unit_rows, axis=-1, keepdims=True)
    )
    grad_input = grad_input.astype(jnp.bfloat16)
    route = [
        (s * parts + d, (s - 1) * parts + parts - 1 - d)
        for s in range(1, sections)
        for d in range(parts)
    ]
    moved = lax.ppermute(grad_input, ("section", "seq"), route)
    carry = jnp.take(moved, flip_order[0], axis=0)
    return (carry[None], sums[0][None], sums[1][None], sums[2][None], grad_out[None])


def solution(mesh):
    shards = head_shards if mesh.shape["seq"] == HEADS else general_shards
    in_specs = (
        P("section", "seq", None),
        P("section", "seq", None),
        P("section", None, None),
        P("section", None, None),
        P("section", None, None),
        P("section", None, None),
        P(),
        P("section", None),
    )
    out_specs = (
        P("section", "seq", None),
        P("section", "seq", None),
        P("section", "seq", None),
        P("section", "seq", None),
        P("section", "seq", None),
    )
    return jax.shard_map(shards, mesh=mesh, in_specs=in_specs, out_specs=out_specs, check_vma=False)
```

```python
import jax
import jax.numpy as jnp
from jax import lax
from jax.experimental import pallas as pl
from jax.experimental.pallas import tpu as pltpu
from jax.sharding import PartitionSpec as P

HEADS = 8
HEAD_DIM = 64


EPSILON = 1e-06


def partner(block, axis, stride):
    count = lax.axis_size(axis)
    route = []
    for low in range(count):
        high = low | 1 << stride
        if high != low and high < count:
            route += [(low, high), (high, low)]
    return lax.ppermute(block, axis, route)


def shifted(block, axis, distance):
    devices = range(lax.axis_size(axis))
    route = [(i - distance, i) for i in devices if i - distance in devices]
    return lax.ppermute(block, axis, route)


def split_heads(matrix):
    return matrix.reshape(matrix.shape[0], HEADS, HEAD_DIM)


def head_major(matrix):
    return jnp.transpose(split_heads(matrix), (1, 0, 2))


def unit_heads(projected):
    parts = split_heads(projected)
    factor = lax.rsqrt(jnp.mean(parts * parts, axis=-1, keepdims=True) + EPSILON)
    return (parts * factor, factor)


def unit_back(grad_heads, unit, factor):
    return factor * (grad_heads - unit * jnp.mean(grad_heads * unit, axis=-1, keepdims=True))


def mirror(rows):
    for bit in range(lax.axis_size("seq").bit_length() - 1):
        rows = partner(rows, "seq", bit)
    return rows


def to_previous(rows):
    return shifted(rows, "section", -1)


def general_shards(activations, incoming, w_query, w_key, w_value, w_out, block_ids, flip_order):
    field = activations[0].astype(jnp.float32)
    upstream = incoming[0].astype(jnp.float32)
    weight_query = w_query[0]
    weight_key = w_key[0]
    weight_value = w_value[0]
    weight_out = w_out[0]
    flip_row = flip_order[0]
    rows = field.shape[0]
    width = field.shape[1]
    inner = weight_query.shape[1]
    scale = HEAD_DIM ** (-0.5)
    first = lax.axis_index("seq") * rows
    my_blocks = lax.dynamic_slice_in_dim(block_ids, first, rows)
    row_scale = lax.rsqrt(jnp.mean(field * field, axis=-1, keepdims=True) + EPSILON)
    unit_rows = field * row_scale
    normed = unit_rows.astype(jnp.bfloat16)
    query_raw = jnp.dot(normed, weight_query, preferred_element_type=jnp.float32)
    key_raw = jnp.dot(normed, weight_key, preferred_element_type=jnp.float32)
    values = jnp.dot(normed, weight_value, preferred_element_type=jnp.float32).astype(jnp.bfloat16)
    query_unit, query_scale = unit_heads(query_raw)
    key_unit, key_scale = unit_heads(key_raw)
    queries = query_unit.astype(jnp.bfloat16).reshape(rows, inner)
    keys = key_unit.astype(jnp.bfloat16).reshape(rows, inner)
    keys_all, values_all = (
        lax.all_gather(keys, "seq", axis=0, tiled=True),
        lax.all_gather(values, "seq", axis=0, tiled=True),
    )
    allowed = block_ids[None, :] <= my_blocks[:, None]
    query_heads = head_major(queries)
    key_heads_all = head_major(keys_all)
    value_heads_all = head_major(values_all)

    def probabilities(query_part, key_part):
        scores = jnp.dot(query_part, key_part.T, preferred_element_type=jnp.float32) * scale
        numerator = jnp.where(allowed, jnp.exp(scores), 0.0)
        denominator = jnp.sum(numerator, axis=-1, keepdims=True)
        return (numerator / denominator, denominator)

    def forward_head(operands):
        query_part, key_part, value_part = operands
        probs, denominator = probabilities(query_part, key_part)
        out_part = jnp.dot(
            probs.astype(jnp.bfloat16), value_part, preferred_element_type=jnp.float32
        ).astype(jnp.bfloat16)
        return (out_part, denominator[:, 0])

    heads_out, denominators = lax.map(forward_head, (query_heads, key_heads_all, value_heads_all))
    attended = jnp.transpose(heads_out, (1, 0, 2)).reshape(rows, inner)
    affine = jnp.dot(attended, weight_out, preferred_element_type=jnp.float32)
    shift_part = affine[:, :width]
    log_scale = affine[:, width:]
    factor = jnp.exp(-log_scale)
    latent = (field - shift_part) * factor
    grad_affine = jnp.concatenate([-upstream * factor, 1.0 - upstream * latent], axis=-1).astype(
        jnp.bfloat16
    )
    out_term = jnp.dot(attended.T, grad_affine, preferred_element_type=jnp.float32)
    grad_attn = jnp.dot(grad_affine, weight_out.T, preferred_element_type=jnp.float32).astype(
        jnp.bfloat16
    )
    correction = jnp.sum(
        split_heads(grad_attn.astype(jnp.float32)) * split_heads(attended.astype(jnp.float32)),
        axis=-1,
    )
    grad_heads = head_major(grad_attn)
    correction_heads = jnp.transpose(correction)[:, :, None]

    def backward_head(operands):
        query_part, key_part, value_part, grad_part, corr_part = operands
        probs, denominator = probabilities(query_part, key_part)
        grad_probs = jnp.dot(grad_part, value_part.T, preferred_element_type=jnp.float32)
        grad_scores = (probs * (grad_probs - corr_part)).astype(jnp.bfloat16)
        grad_qpart = jnp.dot(grad_scores, key_part, preferred_element_type=jnp.float32) * scale
        grad_kpart = jnp.dot(grad_scores.T, query_part, preferred_element_type=jnp.float32) * scale
        grad_vpart = jnp.dot(
            probs.astype(jnp.bfloat16).T, grad_part, preferred_element_type=jnp.float32
        )
        return (grad_qpart, grad_kpart, grad_vpart)

    grad_qheads, grad_kall, grad_vall = lax.map(
        backward_head, (query_heads, key_heads_all, value_heads_all, grad_heads, correction_heads)
    )
    key_terms = jnp.transpose(grad_kall, (1, 0, 2)).reshape(-1, inner)
    value_terms = jnp.transpose(grad_vall, (1, 0, 2)).reshape(-1, inner)
    grad_kunit, grad_vsum = (
        lax.psum_scatter(
            key_terms.astype(jnp.bfloat16), "seq", scatter_dimension=0, tiled=True
        ).astype(jnp.float32),
        lax.psum_scatter(
            value_terms.astype(jnp.bfloat16), "seq", scatter_dimension=0, tiled=True
        ).astype(jnp.float32),
    )
    grad_queries = (
        unit_back(jnp.transpose(grad_qheads, (1, 0, 2)), query_unit, query_scale)
        .reshape(rows, inner)
        .astype(jnp.bfloat16)
    )
    grad_keys = (
        unit_back(split_heads(grad_kunit), key_unit, key_scale)
        .reshape(rows, inner)
        .astype(jnp.bfloat16)
    )
    grad_values = grad_vsum.astype(jnp.bfloat16)
    query_term = jnp.dot(normed.T, grad_queries, preferred_element_type=jnp.float32)
    key_term = jnp.dot(normed.T, grad_keys, preferred_element_type=jnp.float32)
    value_term = jnp.dot(normed.T, grad_values, preferred_element_type=jnp.float32)
    sums = (
        lax.psum_scatter(
            query_term.astype(jnp.bfloat16), "seq", scatter_dimension=0, tiled=True
        ).astype(jnp.float32),
        lax.psum_scatter(
            key_term.astype(jnp.bfloat16), "seq", scatter_dimension=0, tiled=True
        ).astype(jnp.float32),
        lax.psum_scatter(
            value_term.astype(jnp.bfloat16), "seq", scatter_dimension=0, tiled=True
        ).astype(jnp.float32),
        lax.psum_scatter(
            out_term.astype(jnp.bfloat16), "seq", scatter_dimension=0, tiled=True
        ).astype(jnp.float32),
    )
    grad_normed = jnp.dot(grad_queries, weight_query.T, preferred_element_type=jnp.float32)
    grad_normed = grad_normed + jnp.dot(grad_keys, weight_key.T, preferred_element_type=jnp.float32)
    grad_normed = grad_normed + jnp.dot(
        grad_values, weight_value.T, preferred_element_type=jnp.float32
    )
    grad_input = upstream * factor + row_scale * (
        grad_normed - unit_rows * jnp.mean(grad_normed * unit_rows, axis=-1, keepdims=True)
    )
    grad_input = grad_input.astype(jnp.bfloat16)
    moved = mirror(to_previous(grad_input))
    carry = jnp.take(moved, flip_row, axis=0)
    return (carry[None], sums[0][None], sums[1][None], sums[2][None], sums[3][None])


PACKED = 80


def call(kernel, outs, operands, flops=0, specs=None, scratch=()):
    moved = sum(x.size * x.dtype.itemsize for x in operands) + sum(
        x.size * x.dtype.itemsize for x in outs
    )
    single = pl.BlockSpec(memory_space=pltpu.VMEM)
    return pl.pallas_call(
        kernel,
        out_shape=tuple(outs),
        in_specs=specs or [single] * len(operands),
        out_specs=tuple([single] * len(outs)),
        scratch_shapes=list(scratch),
        compiler_params=pltpu.CompilerParams(vmem_limit_bytes=40 * 2**20),
        cost_estimate=pl.CostEstimate(flops=flops, bytes_accessed=moved, transcendentals=0),
    )(*operands)


def shape(*dims, dtype=jnp.bfloat16):
    return jax.ShapeDtypeStruct(dims, dtype)


def dot(left, right, contract=((1,), (0,))):
    return lax.dot_general(left, right, (contract, ((), ())), preferred_element_type=jnp.float32)


def low_lanes(block):
    return lax.broadcasted_iota(jnp.int32, block.shape, len(block.shape) - 1) < HEAD_DIM


def swap(block):
    return pltpu.roll(block, HEAD_DIM, 1)


def half_sums(block):
    low = low_lanes(block)
    first = jnp.sum(jnp.where(low, block, 0.0), axis=-1, keepdims=True)
    second = jnp.sum(jnp.where(low, 0.0, block), axis=-1, keepdims=True)
    return jnp.where(low, first, second)


def pack(block):
    rows = block.shape[0]
    return jnp.concatenate([block[:PACKED], block[rows - PACKED :]], axis=1)


def unpack(slab, rows):
    right = swap(slab)[2 * PACKED - rows :, :HEAD_DIM]
    return jnp.concatenate([slab[:, :HEAD_DIM], right], axis=0)


def normalize(block):
    field = block.astype(jnp.float32)
    row_scale = lax.rsqrt(jnp.mean(field * field, axis=-1, keepdims=True) + EPSILON)
    return field * row_scale, row_scale


def project_kernel(act_ref, wq_ref, wk_ref, wv_ref, out_ref):
    normed = normalize(act_ref[...])[0].astype(jnp.bfloat16)
    rows = normed.shape[0]
    query, key = dot(normed, wq_ref[...]), dot(normed, wk_ref[...])
    value = dot(normed, wv_ref[...])
    for pair in range(HEADS // 2):
        lanes = slice(pair * 2 * HEAD_DIM, (pair + 1) * 2 * HEAD_DIM)
        q, k, v = query[:, lanes], key[:, lanes], value[:, lanes]
        q = q * lax.rsqrt(half_sums(q * q) / HEAD_DIM + EPSILON)
        k = k * lax.rsqrt(half_sums(k * k) / HEAD_DIM + EPSILON)
        first, last = v[:PACKED], v[rows - PACKED :]
        low, low_v = low_lanes(q), low_lanes(first)
        even = (jnp.where(low_v, first, swap(last)), jnp.where(low, q, swap(k)))
        odd = (jnp.where(low_v, swap(first), last), jnp.where(low, swap(q), k))
        for head, (upper, lower) in enumerate((even, odd)):
            out_ref[2 * pair + head, :PACKED, :] = upper.astype(jnp.bfloat16)
            out_ref[2 * pair + head, PACKED:, :] = lower.astype(jnp.bfloat16)


def tiles(tokens):
    size = 256
    return [
        (start, min(tokens, start + size), min(tokens, start + 2 * size))
        for start in range(0, tokens, size)
    ]


def attend_kernel(slab_ref, row_ids, column_ids, prob_ref, qk_ref, v_ref, out_t_ref, out_ref):
    parts, length, _ = slab_ref.shape
    rows = length - PACKED
    tokens = parts * rows
    slabs = [slab_ref[g].astype(jnp.float32) for g in range(parts)]
    qk = jnp.concatenate([slab[PACKED:] for slab in slabs], axis=0).astype(jnp.bfloat16)
    value = jnp.concatenate([unpack(slab[:PACKED], rows) for slab in slabs], axis=0)
    value = value.astype(jnp.bfloat16)
    qk_ref[...] = qk
    v_ref[...] = value
    query, key = qk[:, :HEAD_DIM] * HEAD_DIM ** (-0.5), qk[:, HEAD_DIM:]
    for start, stop, seen in tiles(tokens):
        scores = dot(key[:seen], query[start:stop], ((1,), (1,)))
        allowed = column_ids[:seen, :] <= row_ids[:, start:stop]
        numerator = jnp.where(allowed, jnp.exp(scores), 0.0)
        probs = numerator * (1.0 / jnp.sum(numerator, axis=0, keepdims=True))
        probs = probs.astype(jnp.bfloat16)
        prob_ref[:seen, start:stop] = probs
        out_t = dot(value[:seen], probs, ((0,), (0,)))
        out_t_ref[:, start:stop] = out_t.astype(jnp.bfloat16).astype(jnp.float32)
    out = jnp.transpose(out_t_ref[...])
    for g in range(parts):
        out_ref[g] = pack(out[g * rows : (g + 1) * rows]).astype(jnp.bfloat16)


def affine_kernel(slab_ref, act_ref, inc_ref, w_ref, att_ref, aff_ref, up_ref, out_ref):
    heads = slab_ref.shape[0]
    rows, width = act_ref.shape
    attended = jnp.concatenate(
        [unpack(slab_ref[h].astype(jnp.float32), rows) for h in range(heads)], axis=1
    ).astype(jnp.bfloat16)
    att_ref[...] = attended
    factor = jnp.exp(-dot(attended, w_ref[:, width:]))
    scaled = inc_ref[...].astype(jnp.float32) * factor
    up_ref[...] = scaled
    shift_part = dot(attended, w_ref[:, :width])
    aff_ref[:, :width] = (-scaled).astype(jnp.bfloat16)
    latent_part = scaled * (act_ref[...].astype(jnp.float32) - shift_part)
    aff_ref[:, width:] = (1.0 - latent_part).astype(jnp.bfloat16)
    grad = dot(aff_ref[...], w_ref[...], ((1,), (1,)))
    for h in range(heads):
        block = grad[:, h * HEAD_DIM : (h + 1) * HEAD_DIM]
        out_ref[h] = pack(block).astype(jnp.bfloat16)


def out_term_kernel(me_ref, slab_ref, aff_ref, *out_refs):
    heads = slab_ref.shape[0]
    rows, width = aff_ref.shape[0], aff_ref.shape[1] // 2
    columns = [
        unpack(slab_ref[me_ref[0] ^ m].astype(jnp.float32), rows) for m in range(heads)
    ]
    for half, order in enumerate(ORDERS):
        for out_ref, group in zip(out_refs[4 * half : 4 * half + 4], order):
            left = jnp.concatenate([columns[m] for m in group], axis=1).astype(jnp.bfloat16)
            right = aff_ref[:, half * width : (half + 1) * width]
            out_ref[...] = dot(left, right, ((0,), (0,))).astype(jnp.bfloat16)


ORDERS = (((1, 3, 5, 7), (2, 6), (4,), (0,)), ((2, 3, 6, 7), (1, 5), (4,), (0,)))


def gathered_kernel(me_ref, *refs):
    blocks, (wq_ref, wk_ref, normed_ref, back_ref) = refs[:HEADS], refs[HEADS:]
    me = me_ref[0]
    odd = lax.rem(me, 2) == 1
    pair = lax.div(me, 2)
    weights = [None, None]
    for i, ref in enumerate((wq_ref, wk_ref)):
        weights[i] = ref[:, pl.ds(pl.multiple_of(pair * 2 * HEAD_DIM, 2 * HEAD_DIM), 2 * HEAD_DIM)]
    for m, block in enumerate(blocks):
        normed = normalize(block[...])[0].astype(jnp.bfloat16)
        q, k = dot(normed, weights[0]), dot(normed, weights[1])
        low = low_lanes(q)
        raw = jnp.where(low, jnp.where(odd, swap(q), q), jnp.where(odd, k, swap(k)))
        scale = lax.rsqrt(half_sums(raw * raw) / HEAD_DIM + EPSILON)
        group = me ^ m
        normed_ref[group] = normed
        back_ref[group, :, : 2 * HEAD_DIM] = raw * scale
        back_ref[group, :, 2 * HEAD_DIM :] = scale


def backward_kernel(
    slab_ref, prob_ref, qk_ref, v_ref, out_t_ref, back_ref, out_ref, gk_ref, gv_ref, gq_ref
):
    parts, rows = back_ref.shape[:2]
    tokens = parts * rows
    grad_f = jnp.concatenate(
        [unpack(slab_ref[g].astype(jnp.float32), rows) for g in range(parts)], axis=0
    )
    grad = grad_f.astype(jnp.bfloat16)
    grad_t = jnp.transpose(grad_f)
    correction = jnp.sum(grad_t * out_t_ref[...], axis=0, keepdims=True)
    grad_t = grad_t.astype(jnp.bfloat16)
    qk, value = qk_ref[...], v_ref[...]
    query, key = qk[:, :HEAD_DIM], qk[:, HEAD_DIM:]
    gk_ref[...] = jnp.zeros_like(gk_ref)
    gv_ref[...] = jnp.zeros_like(gv_ref)
    for start, stop, seen in tiles(tokens):
        probs = prob_ref[:seen, start:stop]
        grad_probs = dot(value[:seen], grad_t[:, start:stop])
        scores = probs.astype(jnp.float32) * (grad_probs - correction[:, start:stop])
        scores = scores.astype(jnp.bfloat16)
        gv_ref[:seen, :] += dot(probs, grad[start:stop])
        gk_ref[:seen, :] += dot(scores, query[start:stop])
        gq_ref[:, start:stop] = dot(key[:seen], scores, ((0,), (0,)))
    grad_q = jnp.transpose(gq_ref[...])
    for g in range(parts):
        own = slice(g * rows, (g + 1) * rows)
        raw = jnp.concatenate([grad_q[own], gk_ref[own, :]], axis=1) * HEAD_DIM ** (-0.5)
        unit, scale = back_ref[g, :, : 2 * HEAD_DIM], back_ref[g, :, 2 * HEAD_DIM :]
        back = scale * (raw - unit * (half_sums(raw * unit) / HEAD_DIM))
        out_ref[g, :PACKED, :] = pack(gv_ref[own, :]).astype(jnp.bfloat16)
        out_ref[g, PACKED:, :] = back.astype(jnp.bfloat16)


def weights_kernel(slab_ref, normed_ref, out_ref):
    parts, rows, width = normed_ref.shape
    qk_sum = v_sum = 0.0
    for g in range(parts):
        slab = slab_ref[g].astype(jnp.float32)
        normed = normed_ref[g]
        qk, v = slab[PACKED:].astype(jnp.bfloat16), unpack(slab[:PACKED], rows)
        qk_sum = qk_sum + dot(qk, normed, ((0,), (0,)))
        v_sum = v_sum + dot(v.astype(jnp.bfloat16), normed, ((0,), (0,)))
    step = width // parts
    for g in range(parts):
        own = slice(g * step, (g + 1) * step)
        out_ref[g, : 2 * HEAD_DIM, :] = qk_sum[:, own].astype(jnp.bfloat16)
        out_ref[g, 2 * HEAD_DIM :, :] = v_sum[:, own].astype(jnp.bfloat16)


def turn_kernel(slab_ref, *out_refs):
    for i, out_ref in enumerate(out_refs):
        own = slice(i * HEAD_DIM, (i + 1) * HEAD_DIM)
        heads = [slab_ref[h, own, :].astype(jnp.float32) for h in range(slab_ref.shape[0])]
        out_ref[0] = jnp.transpose(jnp.concatenate(heads, axis=0))


def input_kernel(slab_ref, wq_ref, wk_ref, wv_ref, act_ref, up_ref, out_ref):
    rows = act_ref.shape[0]
    unit, row_scale = normalize(act_ref[...])
    queries, keys, values = [], [], []
    for pair in range(HEADS // 2):
        even = slab_ref[2 * pair].astype(jnp.float32)
        odd = slab_ref[2 * pair + 1].astype(jnp.float32)
        low = low_lanes(even[PACKED:])
        queries.append(jnp.where(low, even[PACKED:], swap(odd[PACKED:])))
        keys.append(jnp.where(low, swap(even[PACKED:]), odd[PACKED:]))
        values += [unpack(even[:PACKED], rows), unpack(odd[:PACKED], rows)]
    total = 0.0
    for parts, ref in ((queries, wq_ref), (keys, wk_ref), (values, wv_ref)):
        left = jnp.concatenate(parts, axis=1).astype(jnp.bfloat16)
        total = total + dot(left, ref[...], ((1,), (1,)))
    total = total - unit * jnp.mean(total * unit, axis=-1, keepdims=True)
    out_ref[...] = (up_ref[...] + row_scale * total).astype(jnp.bfloat16)


def reorder_kernel(order_ref, rows_ref, out_ref):
    rows = rows_ref.shape[0]
    chosen = lax.broadcasted_iota(jnp.int32, (rows, rows), 1) == order_ref[...]
    chosen = jnp.where(chosen, 1.0, 0.0).astype(jnp.bfloat16)
    out_ref[0] = dot(chosen, rows_ref[...]).astype(jnp.bfloat16)


def exchange(slabs):
    return lax.all_to_all(slabs, "seq", split_axis=0, concat_axis=0, tiled=True)


def spread(block):
    side, near, far = [partner(block, "seq", bit) for bit in range(3)]
    side_far = partner(far, "seq", 0)
    near_far = partner(far, "seq", 1)
    side_near = partner(near, "seq", 0)
    last = partner(side_far, "seq", 1)
    return block, side, near, side_near, far, side_far, near_far, last


def wide(matrix):
    return matrix.astype(jnp.float32)


def sum_to_owner(terms, bits):
    first, second, third, keep = terms
    size = keep.shape[0]
    got = wide(partner(first, "seq", bits[0]))
    at = {0: got[:size], 1: got[size : 2 * size], 2: got[2 * size : 3 * size], 3: got[3 * size :]}
    second = (wide(second) + jnp.concatenate([at[1], at[3]], axis=0)).astype(jnp.bfloat16)
    third, keep = wide(third) + at[2], wide(keep) + at[0]
    got = wide(partner(second, "seq", bits[1]))
    third, keep = (third + got[size:]).astype(jnp.bfloat16), keep + got[:size]
    return keep + wide(partner(third, "seq", bits[2]))


def head_shards(
    activations, incoming, w_query, w_key, w_value, w_out, block_ids, flip_order
):
    parts = lax.axis_size("seq")
    sections = lax.axis_size("section")
    me = lax.axis_index("seq").astype(jnp.int32).reshape(1)
    field, upstream = activations[0], incoming[0]
    wq, wk, wv, wo = w_query[0], w_key[0], w_value[0], w_out[0]
    rows, width = field.shape
    inner = wq.shape[1]
    tokens = parts * rows
    length = PACKED + rows
    smem = pl.BlockSpec(memory_space=pltpu.SMEM)
    vmem = pl.BlockSpec(memory_space=pltpu.VMEM)
    f32 = jnp.float32

    (slabs,) = call(
        project_kernel, [shape(HEADS, length, 128)], [field, wq, wk, wv], 6 * rows * width * inner
    )
    slabs = exchange(slabs)
    blocks = spread(field)
    probs, qk, value, out_t, packed = call(
        attend_kernel,
        [
            shape(tokens, tokens),
            shape(tokens, 128),
            shape(tokens, HEAD_DIM),
            shape(HEAD_DIM, tokens, dtype=f32),
            shape(parts, PACKED, 128),
        ],
        [slabs, block_ids[None, :], block_ids[:, None]],
        4 * tokens * tokens * 256,
    )
    packed = exchange(packed)
    attended, grad_affine, scaled, grad_slabs = call(
        affine_kernel,
        [
            shape(rows, inner),
            shape(rows, 2 * width),
            shape(rows, width, dtype=f32),
            shape(HEADS, PACKED, 128),
        ],
        [packed, field, upstream, wo],
        8 * rows * width * inner,
    )
    grad_slabs = exchange(grad_slabs)
    terms = call(
        out_term_kernel,
        [shape(len(group) * HEAD_DIM, width) for order in ORDERS for group in order],
        [me, packed, grad_affine],
        4 * rows * width * inner,
        specs=[smem, vmem, vmem],
    )
    normed, back = call(
        gathered_kernel,
        [shape(parts, rows, width), shape(parts, rows, 256, dtype=f32)],
        [me, *blocks, wq, wk],
        4 * tokens * width * 128,
        specs=[smem] + [vmem] * (HEADS + 2),
    )
    (grads,) = call(
        backward_kernel,
        [shape(parts, length, 128)],
        [grad_slabs, probs, qk, value, out_t, back],
        8 * tokens * tokens * 256,
        scratch=[
            pltpu.VMEM((tokens, HEAD_DIM), f32),
            pltpu.VMEM((tokens, HEAD_DIM), f32),
            pltpu.VMEM((HEAD_DIM, tokens), f32),
        ],
    )
    token_grads = exchange(grads)
    (weight_terms,) = call(
        weights_kernel,
        [shape(parts, 3 * HEAD_DIM, width // parts)],
        [grads, normed],
        2 * tokens * width * 256,
    )
    weight_terms = exchange(weight_terms)
    (grad_input,) = call(
        input_kernel,
        [shape(rows, width)],
        [token_grads, wq, wk, wv, field, scaled],
        6 * rows * width * inner,
    )
    route = [
        (s * parts + d, (s - 1) * parts + parts - 1 - d)
        for s in range(1, sections)
        for d in range(parts)
    ]
    moved = lax.ppermute(grad_input, ("section", "seq"), route)
    grad_out = jnp.concatenate(
        [sum_to_owner(terms[:4], (0, 1, 2)), sum_to_owner(terms[4:], (1, 0, 2))], axis=1
    )
    grad_q, grad_k, grad_v = call(
        turn_kernel, [shape(1, width // parts, inner, dtype=f32)] * 3, [weight_terms]
    )
    (carry,) = call(
        reorder_kernel, [shape(1, rows, width)], [flip_order[0][:, None], moved], 2 * rows * rows * width
    )
    return (carry, grad_q, grad_k, grad_v, grad_out[None])


def solution(mesh):
    shards = head_shards if mesh.shape["seq"] == HEADS else general_shards
    in_specs = (
        P("section", "seq", None),
        P("section", "seq", None),
        P("section", None, None),
        P("section", None, None),
        P("section", None, None),
        P("section", None, None),
        P(),
        P("section", None),
    )
    out_specs = (
        P("section", "seq", None),
        P("section", "seq", None),
        P("section", "seq", None),
        P("section", "seq", None),
        P("section", "seq", None),
    )
    return jax.shard_map(shards, mesh=mesh, in_specs=in_specs, out_specs=out_specs, check_vma=False)
```

```python
import jax
import jax.numpy as jnp
from jax import lax
from jax.experimental import pallas as pl
from jax.experimental.pallas import tpu as pltpu
from jax.sharding import PartitionSpec as P

HEADS = 8
HEAD_DIM = 64


EPSILON = 1e-06


def partner(block, axis, stride):
    count = lax.axis_size(axis)
    route = []
    for low in range(count):
        high = low | 1 << stride
        if high != low and high < count:
            route += [(low, high), (high, low)]
    return lax.ppermute(block, axis, route)


def shifted(block, axis, distance):
    devices = range(lax.axis_size(axis))
    route = [(i - distance, i) for i in devices if i - distance in devices]
    return lax.ppermute(block, axis, route)


def split_heads(matrix):
    return matrix.reshape(matrix.shape[0], HEADS, HEAD_DIM)


def head_major(matrix):
    return jnp.transpose(split_heads(matrix), (1, 0, 2))


def unit_heads(projected):
    parts = split_heads(projected)
    factor = lax.rsqrt(jnp.mean(parts * parts, axis=-1, keepdims=True) + EPSILON)
    return (parts * factor, factor)


def unit_back(grad_heads, unit, factor):
    return factor * (grad_heads - unit * jnp.mean(grad_heads * unit, axis=-1, keepdims=True))


def mirror(rows):
    for bit in range(lax.axis_size("seq").bit_length() - 1):
        rows = partner(rows, "seq", bit)
    return rows


def to_previous(rows):
    return shifted(rows, "section", -1)


def general_shards(activations, incoming, w_query, w_key, w_value, w_out, block_ids, flip_order):
    field = activations[0].astype(jnp.float32)
    upstream = incoming[0].astype(jnp.float32)
    weight_query = w_query[0]
    weight_key = w_key[0]
    weight_value = w_value[0]
    weight_out = w_out[0]
    flip_row = flip_order[0]
    rows = field.shape[0]
    width = field.shape[1]
    inner = weight_query.shape[1]
    scale = HEAD_DIM ** (-0.5)
    first = lax.axis_index("seq") * rows
    my_blocks = lax.dynamic_slice_in_dim(block_ids, first, rows)
    row_scale = lax.rsqrt(jnp.mean(field * field, axis=-1, keepdims=True) + EPSILON)
    unit_rows = field * row_scale
    normed = unit_rows.astype(jnp.bfloat16)
    query_raw = jnp.dot(normed, weight_query, preferred_element_type=jnp.float32)
    key_raw = jnp.dot(normed, weight_key, preferred_element_type=jnp.float32)
    values = jnp.dot(normed, weight_value, preferred_element_type=jnp.float32).astype(jnp.bfloat16)
    query_unit, query_scale = unit_heads(query_raw)
    key_unit, key_scale = unit_heads(key_raw)
    queries = query_unit.astype(jnp.bfloat16).reshape(rows, inner)
    keys = key_unit.astype(jnp.bfloat16).reshape(rows, inner)
    keys_all, values_all = (
        lax.all_gather(keys, "seq", axis=0, tiled=True),
        lax.all_gather(values, "seq", axis=0, tiled=True),
    )
    allowed = block_ids[None, :] <= my_blocks[:, None]
    query_heads = head_major(queries)
    key_heads_all = head_major(keys_all)
    value_heads_all = head_major(values_all)

    def probabilities(query_part, key_part):
        scores = jnp.dot(query_part, key_part.T, preferred_element_type=jnp.float32) * scale
        numerator = jnp.where(allowed, jnp.exp(scores), 0.0)
        denominator = jnp.sum(numerator, axis=-1, keepdims=True)
        return (numerator / denominator, denominator)

    def forward_head(operands):
        query_part, key_part, value_part = operands
        probs, denominator = probabilities(query_part, key_part)
        out_part = jnp.dot(
            probs.astype(jnp.bfloat16), value_part, preferred_element_type=jnp.float32
        ).astype(jnp.bfloat16)
        return (out_part, denominator[:, 0])

    heads_out, denominators = lax.map(forward_head, (query_heads, key_heads_all, value_heads_all))
    attended = jnp.transpose(heads_out, (1, 0, 2)).reshape(rows, inner)
    affine = jnp.dot(attended, weight_out, preferred_element_type=jnp.float32)
    shift_part = affine[:, :width]
    log_scale = affine[:, width:]
    factor = jnp.exp(-log_scale)
    latent = (field - shift_part) * factor
    grad_affine = jnp.concatenate([-upstream * factor, 1.0 - upstream * latent], axis=-1).astype(
        jnp.bfloat16
    )
    out_term = jnp.dot(attended.T, grad_affine, preferred_element_type=jnp.float32)
    grad_attn = jnp.dot(grad_affine, weight_out.T, preferred_element_type=jnp.float32).astype(
        jnp.bfloat16
    )
    correction = jnp.sum(
        split_heads(grad_attn.astype(jnp.float32)) * split_heads(attended.astype(jnp.float32)),
        axis=-1,
    )
    grad_heads = head_major(grad_attn)
    correction_heads = jnp.transpose(correction)[:, :, None]

    def backward_head(operands):
        query_part, key_part, value_part, grad_part, corr_part = operands
        probs, denominator = probabilities(query_part, key_part)
        grad_probs = jnp.dot(grad_part, value_part.T, preferred_element_type=jnp.float32)
        grad_scores = (probs * (grad_probs - corr_part)).astype(jnp.bfloat16)
        grad_qpart = jnp.dot(grad_scores, key_part, preferred_element_type=jnp.float32) * scale
        grad_kpart = jnp.dot(grad_scores.T, query_part, preferred_element_type=jnp.float32) * scale
        grad_vpart = jnp.dot(
            probs.astype(jnp.bfloat16).T, grad_part, preferred_element_type=jnp.float32
        )
        return (grad_qpart, grad_kpart, grad_vpart)

    grad_qheads, grad_kall, grad_vall = lax.map(
        backward_head, (query_heads, key_heads_all, value_heads_all, grad_heads, correction_heads)
    )
    key_terms = jnp.transpose(grad_kall, (1, 0, 2)).reshape(-1, inner)
    value_terms = jnp.transpose(grad_vall, (1, 0, 2)).reshape(-1, inner)
    grad_kunit, grad_vsum = (
        lax.psum_scatter(
            key_terms.astype(jnp.bfloat16), "seq", scatter_dimension=0, tiled=True
        ).astype(jnp.float32),
        lax.psum_scatter(
            value_terms.astype(jnp.bfloat16), "seq", scatter_dimension=0, tiled=True
        ).astype(jnp.float32),
    )
    grad_queries = (
        unit_back(jnp.transpose(grad_qheads, (1, 0, 2)), query_unit, query_scale)
        .reshape(rows, inner)
        .astype(jnp.bfloat16)
    )
    grad_keys = (
        unit_back(split_heads(grad_kunit), key_unit, key_scale)
        .reshape(rows, inner)
        .astype(jnp.bfloat16)
    )
    grad_values = grad_vsum.astype(jnp.bfloat16)
    query_term = jnp.dot(normed.T, grad_queries, preferred_element_type=jnp.float32)
    key_term = jnp.dot(normed.T, grad_keys, preferred_element_type=jnp.float32)
    value_term = jnp.dot(normed.T, grad_values, preferred_element_type=jnp.float32)
    sums = (
        lax.psum_scatter(
            query_term.astype(jnp.bfloat16), "seq", scatter_dimension=0, tiled=True
        ).astype(jnp.float32),
        lax.psum_scatter(
            key_term.astype(jnp.bfloat16), "seq", scatter_dimension=0, tiled=True
        ).astype(jnp.float32),
        lax.psum_scatter(
            value_term.astype(jnp.bfloat16), "seq", scatter_dimension=0, tiled=True
        ).astype(jnp.float32),
        lax.psum_scatter(
            out_term.astype(jnp.bfloat16), "seq", scatter_dimension=0, tiled=True
        ).astype(jnp.float32),
    )
    grad_normed = jnp.dot(grad_queries, weight_query.T, preferred_element_type=jnp.float32)
    grad_normed = grad_normed + jnp.dot(grad_keys, weight_key.T, preferred_element_type=jnp.float32)
    grad_normed = grad_normed + jnp.dot(
        grad_values, weight_value.T, preferred_element_type=jnp.float32
    )
    grad_input = upstream * factor + row_scale * (
        grad_normed - unit_rows * jnp.mean(grad_normed * unit_rows, axis=-1, keepdims=True)
    )
    grad_input = grad_input.astype(jnp.bfloat16)
    moved = mirror(to_previous(grad_input))
    carry = jnp.take(moved, flip_row, axis=0)
    return (carry[None], sums[0][None], sums[1][None], sums[2][None], sums[3][None])


PACKED = 80


def call(kernel, outs, operands, flops=0, specs=None, scratch=()):
    moved = sum(x.size * x.dtype.itemsize for x in operands) + sum(
        x.size * x.dtype.itemsize for x in outs
    )
    single = pl.BlockSpec(memory_space=pltpu.VMEM)
    return pl.pallas_call(
        kernel,
        out_shape=tuple(outs),
        in_specs=specs or [single] * len(operands),
        out_specs=tuple([single] * len(outs)),
        scratch_shapes=list(scratch),
        compiler_params=pltpu.CompilerParams(vmem_limit_bytes=14 * 2**20),
        cost_estimate=pl.CostEstimate(flops=flops, bytes_accessed=moved, transcendentals=0),
    )(*operands)


def shape(*dims, dtype=jnp.bfloat16):
    return jax.ShapeDtypeStruct(dims, dtype)


def dot(left, right, contract=((1,), (0,))):
    return lax.dot_general(left, right, (contract, ((), ())), preferred_element_type=jnp.float32)


def low_lanes(block):
    return lax.broadcasted_iota(jnp.int32, block.shape, len(block.shape) - 1) < HEAD_DIM


def swap(block):
    return pltpu.roll(block, HEAD_DIM, 1)


def half_sums(block):
    low = low_lanes(block)
    first = jnp.sum(jnp.where(low, block, 0.0), axis=-1, keepdims=True)
    second = jnp.sum(jnp.where(low, 0.0, block), axis=-1, keepdims=True)
    return jnp.where(low, first, second)


def pack(block):
    rows = block.shape[0]
    return jnp.concatenate([block[:PACKED], block[rows - PACKED :]], axis=1)


def unpack(slab, rows):
    right = swap(slab)[2 * PACKED - rows :, :HEAD_DIM]
    return jnp.concatenate([slab[:, :HEAD_DIM], right], axis=0)


def normalize(block):
    field = block.astype(jnp.float32)
    row_scale = lax.rsqrt(jnp.mean(field * field, axis=-1, keepdims=True) + EPSILON)
    return field * row_scale, row_scale


def project_kernel(me_ref, *refs):
    blocks, (wq_ref, wk_ref, wv_ref, normed_ref, back_ref, out_ref) = refs[:-6], refs[-6:]
    odd = lax.rem(me_ref[0], 2) == 1
    pair = pl.multiple_of(lax.div(me_ref[0], 2) * 2 * HEAD_DIM, 2 * HEAD_DIM)
    weights = [ref[:, pl.ds(pair, 2 * HEAD_DIM)] for ref in (wq_ref, wk_ref, wv_ref)]
    for m, block in enumerate(blocks):
        normed = normalize(block[...])[0].astype(jnp.bfloat16)
        q, k, v = [dot(normed, weight) for weight in weights]
        low = low_lanes(q)
        raw = jnp.where(low, jnp.where(odd, swap(q), q), jnp.where(odd, k, swap(k)))
        scale = lax.rsqrt(half_sums(raw * raw) / HEAD_DIM + EPSILON)
        unit = raw * scale
        normed_ref[m] = normed
        back_ref[m, :, : 2 * HEAD_DIM] = unit
        back_ref[m, :, 2 * HEAD_DIM :] = scale
        out_ref[m, :, : 2 * HEAD_DIM] = unit.astype(jnp.bfloat16)
        out_ref[m, :, 2 * HEAD_DIM :] = jnp.where(odd, swap(v), v).astype(jnp.bfloat16)


def tiles(tokens):
    size = 256
    return [(start, min(tokens, start + size)) for start in range(0, tokens, size)]


def attend_kernel(
    me_ref, first_ref, last_ref, row_ids, column_ids, prob_ref, qk_ref, v_ref, out_t_ref, out_ref
):
    rows = first_ref.shape[1]
    parts = 2 * first_ref.shape[0]
    tokens = parts * rows
    slabs = [ref[m] for ref in (first_ref, last_ref) for m in range(parts // 2)]
    whole = jnp.concatenate([slab.astype(jnp.float32) for slab in slabs], axis=0)
    qk = whole[:, : 2 * HEAD_DIM].astype(jnp.bfloat16)
    value = whole[:, 2 * HEAD_DIM : 3 * HEAD_DIM].astype(jnp.bfloat16)
    qk_ref[...] = qk
    v_ref[...] = value
    query, key = qk[:, :HEAD_DIM] * HEAD_DIM ** (-0.5), qk[:, HEAD_DIM:]
    for start, stop in tiles(tokens):
        scores = dot(key, query[start:stop], ((1,), (1,)))
        allowed = column_ids[...] <= row_ids[:, start:stop]
        numerator = jnp.where(allowed, jnp.exp(scores), 0.0)
        probs = numerator * (1.0 / jnp.sum(numerator, axis=0, keepdims=True))
        probs = probs.astype(jnp.bfloat16)
        prob_ref[:, start:stop] = probs
        out_t = dot(value, probs, ((0,), (0,)))
        out_t_ref[:, start:stop] = out_t.astype(jnp.bfloat16).astype(jnp.float32)
    out = jnp.transpose(out_t_ref[...])
    for m in range(parts):
        out_ref[me_ref[0] ^ DISTANCES[m]] = pack(out[m * rows : (m + 1) * rows]).astype(jnp.bfloat16)


def affine_kernel(slab_ref, act_ref, inc_ref, w_ref, att_ref, aff_ref, up_ref, out_ref):
    heads = slab_ref.shape[0]
    rows, width = act_ref.shape
    attended = jnp.concatenate(
        [unpack(slab_ref[h].astype(jnp.float32), rows) for h in range(heads)], axis=1
    ).astype(jnp.bfloat16)
    att_ref[...] = attended
    factor = jnp.exp(-dot(attended, w_ref[:, width:]))
    scaled = inc_ref[...].astype(jnp.float32) * factor
    up_ref[...] = scaled
    shift_part = dot(attended, w_ref[:, :width])
    aff_ref[:, :width] = (-scaled).astype(jnp.bfloat16)
    latent_part = scaled * (act_ref[...].astype(jnp.float32) - shift_part)
    aff_ref[:, width:] = (1.0 - latent_part).astype(jnp.bfloat16)
    grad = dot(aff_ref[...], w_ref[...], ((1,), (1,)))
    for h in range(heads):
        block = grad[:, h * HEAD_DIM : (h + 1) * HEAD_DIM]
        out_ref[h] = pack(block).astype(jnp.bfloat16)


ORDER = ((1, 5, 3, 7), (2, 6), (4,), (0,))


def out_term_kernel(me_ref, slab_ref, aff_ref, *out_refs):
    heads, rows = slab_ref.shape[0], aff_ref.shape[0]
    columns = [
        unpack(slab_ref[me_ref[0] ^ m].astype(jnp.float32), rows) for m in range(heads)
    ]
    for out_ref, group in zip(out_refs, ORDER):
        left = jnp.concatenate([columns[m] for m in group], axis=1).astype(jnp.bfloat16)
        out_ref[...] = dot(left, aff_ref[...], ((0,), (0,))).astype(jnp.bfloat16)


def backward_kernel(
    me_ref, slab_ref, prob_ref, qk_ref, v_ref, out_t_ref, first_ref, last_ref, out_ref, gk_ref, gv_ref, gq_ref
):
    parts, rows = slab_ref.shape[0], first_ref.shape[1]
    tokens = parts * rows
    me = me_ref[0]
    grad_f = jnp.concatenate(
        [unpack(slab_ref[me ^ DISTANCES[m]].astype(jnp.float32), rows) for m in range(parts)], axis=0
    )
    grad = grad_f.astype(jnp.bfloat16)
    grad_t = jnp.transpose(grad_f)
    correction = jnp.sum(grad_t * out_t_ref[...], axis=0, keepdims=True)
    grad_t = grad_t.astype(jnp.bfloat16)
    qk, value = qk_ref[...], v_ref[...]
    query, key = qk[:, :HEAD_DIM], qk[:, HEAD_DIM:]
    gk_ref[...] = jnp.zeros_like(gk_ref)
    gv_ref[...] = jnp.zeros_like(gv_ref)
    for start, stop in tiles(tokens):
        probs = prob_ref[:, start:stop]
        grad_probs = dot(value, grad_t[:, start:stop])
        scores = probs.astype(jnp.float32) * (grad_probs - correction[:, start:stop])
        scores = scores.astype(jnp.bfloat16)
        gv_ref[...] += dot(probs, grad[start:stop])
        gk_ref[...] += dot(scores, query[start:stop])
        gq_ref[:, start:stop] = dot(key, scores, ((0,), (0,)))
    grad_q = jnp.transpose(gq_ref[...])
    for m in range(parts):
        own = slice(m * rows, (m + 1) * rows)
        back_ref, at = (first_ref, m) if m < parts // 2 else (last_ref, m - parts // 2)
        raw = jnp.concatenate([grad_q[own], gk_ref[own, :]], axis=1) * HEAD_DIM ** (-0.5)
        unit, scale = back_ref[at, :, : 2 * HEAD_DIM], back_ref[at, :, 2 * HEAD_DIM :]
        back = scale * (raw - unit * (half_sums(raw * unit) / HEAD_DIM))
        out_ref[me ^ DISTANCES[m], :PACKED, :] = pack(gv_ref[own, :]).astype(jnp.bfloat16)
        out_ref[me ^ DISTANCES[m], PACKED:, :] = back.astype(jnp.bfloat16)


def weights_kernel(me_ref, slab_ref, first_ref, last_ref, out_ref):
    half, rows, width = first_ref.shape
    parts = 2 * half
    qk_sum = v_sum = 0.0
    for m in range(parts):
        slab = slab_ref[me_ref[0] ^ DISTANCES[m]].astype(jnp.float32)
        normed = first_ref[m] if m < half else last_ref[m - half]
        qk, v = slab[PACKED:].astype(jnp.bfloat16), unpack(slab[:PACKED], rows)
        qk_sum = qk_sum + dot(qk, normed, ((0,), (0,)))
        v_sum = v_sum + dot(v.astype(jnp.bfloat16), normed, ((0,), (0,)))
    step = width // parts
    for g in range(parts):
        own = slice(g * step, (g + 1) * step)
        out_ref[g, : 2 * HEAD_DIM, :] = qk_sum[:, own].astype(jnp.bfloat16)
        out_ref[g, 2 * HEAD_DIM :, :] = v_sum[:, own].astype(jnp.bfloat16)


def turn_kernel(slab_ref, *out_refs):
    for i, out_ref in enumerate(out_refs):
        own = slice(i * HEAD_DIM, (i + 1) * HEAD_DIM)
        heads = [slab_ref[h, own, :].astype(jnp.float32) for h in range(slab_ref.shape[0])]
        out_ref[0] = jnp.transpose(jnp.concatenate(heads, axis=0))


def input_kernel(slab_ref, wq_ref, wk_ref, wv_ref, act_ref, up_ref, out_ref):
    rows = act_ref.shape[0]
    unit, row_scale = normalize(act_ref[...])
    queries, keys, values = [], [], []
    for pair in range(HEADS // 2):
        even = slab_ref[2 * pair].astype(jnp.float32)
        odd = slab_ref[2 * pair + 1].astype(jnp.float32)
        low = low_lanes(even[PACKED:])
        queries.append(jnp.where(low, even[PACKED:], swap(odd[PACKED:])))
        keys.append(jnp.where(low, swap(even[PACKED:]), odd[PACKED:]))
        values += [unpack(even[:PACKED], rows), unpack(odd[:PACKED], rows)]
    total = 0.0
    for parts, ref in ((queries, wq_ref), (keys, wk_ref), (values, wv_ref)):
        left = jnp.concatenate(parts, axis=1).astype(jnp.bfloat16)
        total = total + dot(left, ref[...], ((1,), (1,)))
    total = total - unit * jnp.mean(total * unit, axis=-1, keepdims=True)
    out_ref[...] = (up_ref[...] + row_scale * total).astype(jnp.bfloat16)


def reorder_kernel(order_ref, rows_ref, out_ref):
    rows = rows_ref.shape[0]
    chosen = lax.broadcasted_iota(jnp.int32, (rows, rows), 1) == order_ref[...]
    chosen = jnp.where(chosen, 1.0, 0.0).astype(jnp.bfloat16)
    out_ref[0] = dot(chosen, rows_ref[...]).astype(jnp.bfloat16)


def exchange(slabs):
    return lax.all_to_all(slabs, "seq", split_axis=0, concat_axis=0, tiled=True)


def spread(block):
    side, near, far = [partner(block, "seq", bit) for bit in range(3)]
    side_far = partner(far, "seq", 0)
    near_far = partner(far, "seq", 1)
    side_near = partner(near, "seq", 0)
    last = partner(side_far, "seq", 1)
    return block, side, near, far, side_near, side_far, near_far, last


DISTANCES = (0, 1, 2, 4, 3, 5, 6, 7)


def wide(matrix):
    return matrix.astype(jnp.float32)


def low(matrix):
    return matrix.astype(jnp.bfloat16)


def sum_to_owner(first, second, third, keep):
    size = keep.shape[0]
    got = partner(first, "seq", 0)
    more = partner(low(wide(second) + wide(got[2 * size :])), "seq", 1)
    third = wide(third) + wide(got[size : 2 * size]) + wide(more[size:])
    keep = wide(keep) + wide(got[:size]) + wide(more[:size])
    return keep + wide(partner(low(third), "seq", 2))


def head_shards(
    activations, incoming, w_query, w_key, w_value, w_out, block_ids, flip_order
):
    parts = lax.axis_size("seq")
    sections = lax.axis_size("section")
    me = lax.axis_index("seq").astype(jnp.int32).reshape(1)
    field, upstream = activations[0], incoming[0]
    wq, wk, wv, wo = w_query[0], w_key[0], w_value[0], w_out[0]
    rows, width = field.shape
    inner = wq.shape[1]
    tokens = parts * rows
    length = PACKED + rows
    smem = pl.BlockSpec(memory_space=pltpu.SMEM)
    vmem = pl.BlockSpec(memory_space=pltpu.VMEM)
    f32 = jnp.float32

    blocks = spread(field)
    order = me[0] ^ jnp.array(DISTANCES, jnp.int32)
    ids = jnp.take(block_ids.reshape(parts, rows), order, axis=0).reshape(tokens)
    half = parts // 2
    pieces = [
        call(
            project_kernel,
            [
                shape(half, rows, width),
                shape(half, rows, 256, dtype=f32),
                shape(half, rows, 256),
            ],
            [me, *group, wq, wk, wv],
            2 * half * rows * width * 512,
            specs=[smem] + [vmem] * (half + 3),
        )
        for group in (blocks[:half], blocks[half:])
    ]
    normed, back, projected = zip(*pieces)
    probs, qk, value, out_t, packed = call(
        attend_kernel,
        [
            shape(tokens, tokens),
            shape(tokens, 128),
            shape(tokens, HEAD_DIM),
            shape(HEAD_DIM, tokens, dtype=f32),
            shape(parts, PACKED, 128),
        ],
        [me, *projected, ids[None, :], ids[:, None]],
        4 * tokens * tokens * 256,
        specs=[smem] + [vmem] * 4,
    )
    packed = exchange(packed)
    attended, grad_affine, scaled, grad_slabs = call(
        affine_kernel,
        [
            shape(rows, inner),
            shape(rows, 2 * width),
            shape(rows, width, dtype=f32),
            shape(HEADS, PACKED, 128),
        ],
        [packed, field, upstream, wo],
        8 * rows * width * inner,
    )
    grad_slabs = exchange(grad_slabs)
    terms = call(
        out_term_kernel,
        [shape(len(group) * HEAD_DIM, 2 * width) for group in ORDER],
        [me, packed, grad_affine],
        4 * rows * width * inner,
        specs=[smem, vmem, vmem],
    )
    (grads,) = call(
        backward_kernel,
        [shape(parts, length, 128)],
        [me, grad_slabs, probs, qk, value, out_t, *back],
        8 * tokens * tokens * 256,
        specs=[smem] + [vmem] * 7,
        scratch=[
            pltpu.VMEM((tokens, HEAD_DIM), f32),
            pltpu.VMEM((tokens, HEAD_DIM), f32),
            pltpu.VMEM((HEAD_DIM, tokens), f32),
        ],
    )
    token_grads = exchange(grads)
    (weight_terms,) = call(
        weights_kernel,
        [shape(parts, 3 * HEAD_DIM, width // parts)],
        [me, grads, *normed],
        2 * tokens * width * 256,
        specs=[smem] + [vmem] * 3,
    )
    weight_terms = exchange(weight_terms)
    (grad_input,) = call(
        input_kernel,
        [shape(rows, width)],
        [token_grads, wq, wk, wv, field, scaled],
        6 * rows * width * inner,
    )
    route = [
        (s * parts + d, (s - 1) * parts + parts - 1 - d)
        for s in range(1, sections)
        for d in range(parts)
    ]
    moved = lax.ppermute(grad_input, ("section", "seq"), route)
    grad_out = sum_to_owner(*terms)
    grad_q, grad_k, grad_v = call(
        turn_kernel, [shape(1, width // parts, inner, dtype=f32)] * 3, [weight_terms]
    )
    (carry,) = call(
        reorder_kernel, [shape(1, rows, width)], [flip_order[0][:, None], moved], 2 * rows * rows * width
    )
    return (carry, grad_q, grad_k, grad_v, grad_out[None])


def solution(mesh):
    shards = head_shards if mesh.shape["seq"] == HEADS else general_shards
    in_specs = (
        P("section", "seq", None),
        P("section", "seq", None),
        P("section", None, None),
        P("section", None, None),
        P("section", None, None),
        P("section", None, None),
        P(),
        P("section", None),
    )
    out_specs = (
        P("section", "seq", None),
        P("section", "seq", None),
        P("section", "seq", None),
        P("section", "seq", None),
        P("section", "seq", None),
    )
    return jax.shard_map(shards, mesh=mesh, in_specs=in_specs, out_specs=out_specs, check_vma=False)
```

```python
import jax
import jax.numpy as jnp
from jax import lax
from jax.experimental import pallas as pl
from jax.experimental.pallas import tpu as pltpu
from jax.sharding import PartitionSpec as P

HEADS = 8
HEAD_DIM = 64


EPSILON = 1e-06


def partner(block, axis, stride):
    count = lax.axis_size(axis)
    route = []
    for low in range(count):
        high = low | 1 << stride
        if high != low and high < count:
            route += [(low, high), (high, low)]
    return lax.ppermute(block, axis, route)


def shifted(block, axis, distance):
    devices = range(lax.axis_size(axis))
    route = [(i - distance, i) for i in devices if i - distance in devices]
    return lax.ppermute(block, axis, route)


def split_heads(matrix):
    return matrix.reshape(matrix.shape[0], HEADS, HEAD_DIM)


def head_major(matrix):
    return jnp.transpose(split_heads(matrix), (1, 0, 2))


def unit_heads(projected):
    parts = split_heads(projected)
    factor = lax.rsqrt(jnp.mean(parts * parts, axis=-1, keepdims=True) + EPSILON)
    return (parts * factor, factor)


def unit_back(grad_heads, unit, factor):
    return factor * (grad_heads - unit * jnp.mean(grad_heads * unit, axis=-1, keepdims=True))


def mirror(rows):
    for bit in range(lax.axis_size("seq").bit_length() - 1):
        rows = partner(rows, "seq", bit)
    return rows


def to_previous(rows):
    return shifted(rows, "section", -1)


def general_shards(activations, incoming, w_query, w_key, w_value, w_out, block_ids, flip_order):
    field = activations[0].astype(jnp.float32)
    upstream = incoming[0].astype(jnp.float32)
    weight_query = w_query[0]
    weight_key = w_key[0]
    weight_value = w_value[0]
    weight_out = w_out[0]
    flip_row = flip_order[0]
    rows = field.shape[0]
    width = field.shape[1]
    inner = weight_query.shape[1]
    scale = HEAD_DIM ** (-0.5)
    first = lax.axis_index("seq") * rows
    my_blocks = lax.dynamic_slice_in_dim(block_ids, first, rows)
    row_scale = lax.rsqrt(jnp.mean(field * field, axis=-1, keepdims=True) + EPSILON)
    unit_rows = field * row_scale
    normed = unit_rows.astype(jnp.bfloat16)
    query_raw = jnp.dot(normed, weight_query, preferred_element_type=jnp.float32)
    key_raw = jnp.dot(normed, weight_key, preferred_element_type=jnp.float32)
    values = jnp.dot(normed, weight_value, preferred_element_type=jnp.float32).astype(jnp.bfloat16)
    query_unit, query_scale = unit_heads(query_raw)
    key_unit, key_scale = unit_heads(key_raw)
    queries = query_unit.astype(jnp.bfloat16).reshape(rows, inner)
    keys = key_unit.astype(jnp.bfloat16).reshape(rows, inner)
    keys_all, values_all = (
        lax.all_gather(keys, "seq", axis=0, tiled=True),
        lax.all_gather(values, "seq", axis=0, tiled=True),
    )
    allowed = block_ids[None, :] <= my_blocks[:, None]
    query_heads = head_major(queries)
    key_heads_all = head_major(keys_all)
    value_heads_all = head_major(values_all)

    def probabilities(query_part, key_part):
        scores = jnp.dot(query_part, key_part.T, preferred_element_type=jnp.float32) * scale
        numerator = jnp.where(allowed, jnp.exp(scores), 0.0)
        denominator = jnp.sum(numerator, axis=-1, keepdims=True)
        return (numerator / denominator, denominator)

    def forward_head(operands):
        query_part, key_part, value_part = operands
        probs, denominator = probabilities(query_part, key_part)
        out_part = jnp.dot(
            probs.astype(jnp.bfloat16), value_part, preferred_element_type=jnp.float32
        ).astype(jnp.bfloat16)
        return (out_part, denominator[:, 0])

    heads_out, denominators = lax.map(forward_head, (query_heads, key_heads_all, value_heads_all))
    attended = jnp.transpose(heads_out, (1, 0, 2)).reshape(rows, inner)
    affine = jnp.dot(attended, weight_out, preferred_element_type=jnp.float32)
    shift_part = affine[:, :width]
    log_scale = affine[:, width:]
    factor = jnp.exp(-log_scale)
    latent = (field - shift_part) * factor
    grad_affine = jnp.concatenate([-upstream * factor, 1.0 - upstream * latent], axis=-1).astype(
        jnp.bfloat16
    )
    out_term = jnp.dot(attended.T, grad_affine, preferred_element_type=jnp.float32)
    grad_attn = jnp.dot(grad_affine, weight_out.T, preferred_element_type=jnp.float32).astype(
        jnp.bfloat16
    )
    correction = jnp.sum(
        split_heads(grad_attn.astype(jnp.float32)) * split_heads(attended.astype(jnp.float32)),
        axis=-1,
    )
    grad_heads = head_major(grad_attn)
    correction_heads = jnp.transpose(correction)[:, :, None]

    def backward_head(operands):
        query_part, key_part, value_part, grad_part, corr_part = operands
        probs, denominator = probabilities(query_part, key_part)
        grad_probs = jnp.dot(grad_part, value_part.T, preferred_element_type=jnp.float32)
        grad_scores = (probs * (grad_probs - corr_part)).astype(jnp.bfloat16)
        grad_qpart = jnp.dot(grad_scores, key_part, preferred_element_type=jnp.float32) * scale
        grad_kpart = jnp.dot(grad_scores.T, query_part, preferred_element_type=jnp.float32) * scale
        grad_vpart = jnp.dot(
            probs.astype(jnp.bfloat16).T, grad_part, preferred_element_type=jnp.float32
        )
        return (grad_qpart, grad_kpart, grad_vpart)

    grad_qheads, grad_kall, grad_vall = lax.map(
        backward_head, (query_heads, key_heads_all, value_heads_all, grad_heads, correction_heads)
    )
    key_terms = jnp.transpose(grad_kall, (1, 0, 2)).reshape(-1, inner)
    value_terms = jnp.transpose(grad_vall, (1, 0, 2)).reshape(-1, inner)
    grad_kunit, grad_vsum = (
        lax.psum_scatter(
            key_terms.astype(jnp.bfloat16), "seq", scatter_dimension=0, tiled=True
        ).astype(jnp.float32),
        lax.psum_scatter(
            value_terms.astype(jnp.bfloat16), "seq", scatter_dimension=0, tiled=True
        ).astype(jnp.float32),
    )
    grad_queries = (
        unit_back(jnp.transpose(grad_qheads, (1, 0, 2)), query_unit, query_scale)
        .reshape(rows, inner)
        .astype(jnp.bfloat16)
    )
    grad_keys = (
        unit_back(split_heads(grad_kunit), key_unit, key_scale)
        .reshape(rows, inner)
        .astype(jnp.bfloat16)
    )
    grad_values = grad_vsum.astype(jnp.bfloat16)
    query_term = jnp.dot(normed.T, grad_queries, preferred_element_type=jnp.float32)
    key_term = jnp.dot(normed.T, grad_keys, preferred_element_type=jnp.float32)
    value_term = jnp.dot(normed.T, grad_values, preferred_element_type=jnp.float32)
    sums = (
        lax.psum_scatter(
            query_term.astype(jnp.bfloat16), "seq", scatter_dimension=0, tiled=True
        ).astype(jnp.float32),
        lax.psum_scatter(
            key_term.astype(jnp.bfloat16), "seq", scatter_dimension=0, tiled=True
        ).astype(jnp.float32),
        lax.psum_scatter(
            value_term.astype(jnp.bfloat16), "seq", scatter_dimension=0, tiled=True
        ).astype(jnp.float32),
        lax.psum_scatter(
            out_term.astype(jnp.bfloat16), "seq", scatter_dimension=0, tiled=True
        ).astype(jnp.float32),
    )
    grad_normed = jnp.dot(grad_queries, weight_query.T, preferred_element_type=jnp.float32)
    grad_normed = grad_normed + jnp.dot(grad_keys, weight_key.T, preferred_element_type=jnp.float32)
    grad_normed = grad_normed + jnp.dot(
        grad_values, weight_value.T, preferred_element_type=jnp.float32
    )
    grad_input = upstream * factor + row_scale * (
        grad_normed - unit_rows * jnp.mean(grad_normed * unit_rows, axis=-1, keepdims=True)
    )
    grad_input = grad_input.astype(jnp.bfloat16)
    moved = mirror(to_previous(grad_input))
    carry = jnp.take(moved, flip_row, axis=0)
    return (carry[None], sums[0][None], sums[1][None], sums[2][None], sums[3][None])


PACKED = 80


class Fetched:
    def __init__(self, source, ref, semaphore):
        self.ref, self.shape, self.waiting = ref, ref.shape, True
        self.copy = pltpu.make_async_copy(source, ref, semaphore)
        self.copy.start()

    def __getitem__(self, index):
        if self.waiting:
            self.copy.wait()
            self.waiting = False
        return self.ref[index]


class Staged:
    def __init__(self, target, ref, semaphores):
        self.target, self.ref, self.semaphores = target, ref, semaphores
        self.shape, self.copies = ref.shape, []

    def __getitem__(self, index):
        return self.ref[index]

    def __setitem__(self, index, value):
        self.ref[index] = value

    def leave(self, index):
        semaphore = self.semaphores.at[len(self.copies)]
        copy = pltpu.make_async_copy(self.ref.at[index], self.target.at[index], semaphore)
        copy.start()
        self.copies.append(copy)


def call(kernel, ins, outs, flops=0, scratch=()):
    in_places, operands = zip(*ins)
    out_places, results = zip(*outs)
    spaces = {"s": pltpu.SMEM, "v": pltpu.VMEM, "h": pltpu.HBM, "r": pltpu.HBM}
    staged = [x for place, x in zip(in_places + out_places, operands + results) if place == "h"]
    count = in_places.count("h")

    def body(*refs):
        refs = list(refs)
        n_in, n_out = len(operands), len(results)
        arrays, rest = refs[: n_in + n_out], refs[n_in + n_out :]
        buffers, (in_sems, out_sems), rest = (
            rest[: len(staged)],
            rest[len(staged) : len(staged) + 2],
            rest[len(staged) + 2 :],
        )
        late, slot = [], 0
        for i, place in enumerate(in_places + out_places):
            if place != "h":
                continue
            if i < n_in:
                arrays[i] = Fetched(arrays[i], buffers[slot], in_sems.at[slot])
            else:
                arrays[i] = Staged(arrays[i], buffers[slot], out_sems.at[slot - count])
            late.append(arrays[i])
            slot += 1
        kernel(*arrays, *rest)
        for item in late[count:]:
            if not item.copies:
                item.leave(slice(None))
        for item in late[count:]:
            for copy in item.copies:
                copy.wait()

    moved = sum(x.size * x.dtype.itemsize for x in operands + results)
    return pl.pallas_call(
        body,
        out_shape=results,
        in_specs=[pl.BlockSpec(memory_space=spaces[place]) for place in in_places],
        out_specs=tuple(pl.BlockSpec(memory_space=spaces[place]) for place in out_places),
        scratch_shapes=[pltpu.VMEM(x.shape, x.dtype) for x in staged]
        + [
            pltpu.SemaphoreType.DMA((max(1, count),)),
            pltpu.SemaphoreType.DMA((max(1, len(staged) - count), HEADS)),
        ]
        + list(scratch),
        compiler_params=pltpu.CompilerParams(vmem_limit_bytes=58 * 2**20),
        cost_estimate=pl.CostEstimate(flops=flops, bytes_accessed=moved, transcendentals=0),
    )(*operands)


def dot(left, right, contract=((1,), (0,))):
    return lax.dot_general(left, right, (contract, ((), ())), preferred_element_type=jnp.float32)


def low_lanes(block):
    return lax.broadcasted_iota(jnp.int32, block.shape, len(block.shape) - 1) < HEAD_DIM


def swap(block):
    return pltpu.roll(block, HEAD_DIM, 1)


def half_sums(block):
    low = low_lanes(block)
    first = jnp.sum(jnp.where(low, block, 0.0), axis=-1, keepdims=True)
    second = jnp.sum(jnp.where(low, 0.0, block), axis=-1, keepdims=True)
    return jnp.where(low, first, second)


def pack(block):
    rows = block.shape[0]
    return jnp.concatenate([block[:PACKED], block[rows - PACKED :]], axis=1)


def unpack(slab, rows):
    right = swap(slab)[2 * PACKED - rows :, :HEAD_DIM]
    return jnp.concatenate([slab[:, :HEAD_DIM], right], axis=0)


def normalize(block):
    field = block.astype(jnp.float32)
    row_scale = lax.rsqrt(jnp.mean(field * field, axis=-1, keepdims=True) + EPSILON)
    return field * row_scale, row_scale


def project_kernel(me_ref, *refs):
    count = len(refs) - 10
    blocks, weight_refs = refs[:count], refs[count : count + 3]
    normed_ref, back_ref, out_ref, *held, semaphores = refs[count + 3 :]
    odd = lax.rem(me_ref[0], 2) == 1
    pair = pl.multiple_of(lax.div(me_ref[0], 2) * 2 * HEAD_DIM, 2 * HEAD_DIM)
    copies = [
        pltpu.make_async_copy(ref.at[:, pl.ds(pair, 2 * HEAD_DIM)], kept, semaphores.at[i])
        for i, (ref, kept) in enumerate(zip(weight_refs, held))
    ]
    for copy in copies:
        copy.start()
    for copy in copies:
        copy.wait()
    weights = [kept[...] for kept in held]
    for m, block in enumerate(blocks):
        normed = normalize(block[...])[0].astype(jnp.bfloat16)
        normed_ref[m] = normed
        normed_ref.leave(m)
        q, k, v = [dot(normed, weight) for weight in weights]
        low = low_lanes(q)
        raw = jnp.where(low, jnp.where(odd, swap(q), q), jnp.where(odd, k, swap(k)))
        scale = lax.rsqrt(half_sums(raw * raw) / HEAD_DIM + EPSILON)
        unit = raw * scale
        back_ref[m, :, : 2 * HEAD_DIM] = unit
        back_ref[m, :, 2 * HEAD_DIM :] = scale
        back_ref.leave(m)
        out_ref[m, :, : 2 * HEAD_DIM] = unit.astype(jnp.bfloat16)
        out_ref[m, :, 2 * HEAD_DIM :] = jnp.where(odd, swap(v), v).astype(jnp.bfloat16)


TILE = 256


def tiles(tokens):
    starts = range(0, tokens, TILE)
    return [(i, start, min(tokens, start + TILE)) for i, start in enumerate(starts)]


def attend_kernel(
    me_ref, first_ref, last_ref, row_ids, column_ids, prob_ref, qk_ref, v_ref, out_t_ref, out_ref
):
    rows = first_ref.shape[1]
    parts = first_ref.shape[0] + last_ref.shape[0]
    tokens = parts * rows
    slabs = [ref[m] for ref in (first_ref, last_ref) for m in range(ref.shape[0])]
    whole = jnp.concatenate([slab.astype(jnp.float32) for slab in slabs], axis=0)
    qk = whole[:, : 2 * HEAD_DIM].astype(jnp.bfloat16)
    value = whole[:, 2 * HEAD_DIM : 3 * HEAD_DIM].astype(jnp.bfloat16)
    qk_ref[...] = qk
    v_ref[...] = value
    qk_ref.leave(slice(None))
    v_ref.leave(slice(None))
    query, key = qk[:, :HEAD_DIM] * HEAD_DIM ** (-0.5), qk[:, HEAD_DIM:]
    for i, start, stop in tiles(tokens):
        scores = dot(key, query[start:stop], ((1,), (1,)))
        allowed = column_ids[...] <= row_ids[:, start:stop]
        numerator = jnp.where(allowed, jnp.exp(scores), 0.0)
        probs = numerator * (1.0 / jnp.sum(numerator, axis=0, keepdims=True))
        probs = probs.astype(jnp.bfloat16)
        prob_ref[i, :, : stop - start] = probs
        prob_ref.leave(i)
        out_t = dot(value, probs, ((0,), (0,)))
        out_t_ref[:, start:stop] = out_t.astype(jnp.bfloat16).astype(jnp.float32)
    out = jnp.transpose(out_t_ref[...])
    for m in range(parts):
        group = me_ref[0] ^ DISTANCES[m]
        out_ref[group] = pack(out[m * rows : (m + 1) * rows]).astype(jnp.bfloat16)


def affine_kernel(slab_ref, act_ref, inc_ref, w_ref, aff_ref, up_ref, out_ref):
    heads = slab_ref.shape[0]
    rows, width = act_ref.shape
    attended = jnp.concatenate(
        [unpack(slab_ref[h].astype(jnp.float32), rows) for h in range(heads)], axis=1
    ).astype(jnp.bfloat16)
    factor = jnp.exp(-dot(attended, w_ref[:, width:]))
    scaled = inc_ref[...].astype(jnp.float32) * factor
    up_ref[...] = scaled
    up_ref.leave(slice(None))
    shift_part = dot(attended, w_ref[:, :width])
    latent_part = scaled * (act_ref[...].astype(jnp.float32) - shift_part)
    grad_affine = jnp.concatenate([-scaled, 1.0 - latent_part], axis=1).astype(jnp.bfloat16)
    aff_ref[...] = grad_affine
    grad = dot(grad_affine, w_ref[...], ((1,), (1,)))
    for h in range(heads):
        block = grad[:, h * HEAD_DIM : (h + 1) * HEAD_DIM]
        out_ref[h] = pack(block).astype(jnp.bfloat16)


ORDERS = (((1, 5, 3, 7), (2, 6), (4,), (0,)), ((2, 6, 3, 7), (1, 5), (4,), (0,)))


def out_term_kernel(me_ref, slab_ref, aff_ref, *out_refs):
    heads, rows = slab_ref.shape[0], aff_ref.shape[0]
    width = aff_ref.shape[1] // 2
    columns = [
        unpack(slab_ref[me_ref[0] ^ m].astype(jnp.float32), rows) for m in range(heads)
    ]
    for half, order in enumerate(ORDERS):
        right = aff_ref[:, half * width : (half + 1) * width]
        for out_ref, group in zip(out_refs[4 * half : 4 * half + 4], order):
            left = jnp.concatenate([columns[m] for m in group], axis=1).astype(jnp.bfloat16)
            out_ref[...] = dot(left, right, ((0,), (0,))).astype(jnp.bfloat16)
            out_ref.leave(slice(None))


def backward_kernel(
    me_ref, slab_ref, prob_ref, qk_ref, v_ref, out_t_ref, first_ref, last_ref, out_ref, *sums
):
    parts, (early, rows) = slab_ref.shape[0], first_ref.shape[:2]
    tokens = parts * rows
    me = me_ref[0]
    gk_ref, gv_ref, gq_ref = sums
    grad_f = jnp.concatenate(
        [unpack(slab_ref[me ^ DISTANCES[m]].astype(jnp.float32), rows) for m in range(parts)], axis=0
    )
    grad = grad_f.astype(jnp.bfloat16)
    grad_t = jnp.transpose(grad_f)
    correction = jnp.sum(grad_t * out_t_ref[...], axis=0, keepdims=True)
    grad_t = grad_t.astype(jnp.bfloat16)
    qk, value = qk_ref[...], v_ref[...]
    query, key = qk[:, :HEAD_DIM], qk[:, HEAD_DIM:]
    gk_ref[...] = jnp.zeros_like(gk_ref)
    gv_ref[...] = jnp.zeros_like(gv_ref)
    for i, start, stop in tiles(tokens):
        probs = prob_ref[i, :, : stop - start]
        grad_probs = dot(value, grad_t[:, start:stop])
        scores = probs.astype(jnp.float32) * (grad_probs - correction[:, start:stop])
        scores = scores.astype(jnp.bfloat16)
        gv_ref[...] += dot(probs, grad[start:stop])
        gk_ref[...] += dot(scores, query[start:stop])
        gq_ref[:, start:stop] = dot(key, scores, ((0,), (0,)))
    grad_q = jnp.transpose(gq_ref[...])
    for m in range(parts):
        own = slice(m * rows, (m + 1) * rows)
        back_ref, at = (first_ref, m) if m < early else (last_ref, m - early)
        raw = jnp.concatenate([grad_q[own], gk_ref[own, :]], axis=1) * HEAD_DIM ** (-0.5)
        unit, scale = back_ref[at, :, : 2 * HEAD_DIM], back_ref[at, :, 2 * HEAD_DIM :]
        back = scale * (raw - unit * (half_sums(raw * unit) / HEAD_DIM))
        out_ref[me ^ DISTANCES[m], :PACKED, :] = pack(gv_ref[own, :]).astype(jnp.bfloat16)
        out_ref[me ^ DISTANCES[m], PACKED:, :] = back.astype(jnp.bfloat16)
        out_ref.leave(me ^ DISTANCES[m])


def weights_kernel(me_ref, slab_ref, first_ref, last_ref, out_ref):
    early, rows, width = first_ref.shape
    parts = early + last_ref.shape[0]
    qk_sum = v_sum = 0.0
    for m in range(parts):
        slab = slab_ref[me_ref[0] ^ DISTANCES[m]].astype(jnp.float32)
        normed = first_ref[m] if m < early else last_ref[m - early]
        qk, v = slab[PACKED:].astype(jnp.bfloat16), unpack(slab[:PACKED], rows)
        qk_sum = qk_sum + dot(qk, normed, ((0,), (0,)))
        v_sum = v_sum + dot(v.astype(jnp.bfloat16), normed, ((0,), (0,)))
    step = width // parts
    for g in range(parts):
        own = slice(g * step, (g + 1) * step)
        out_ref[g, : 2 * HEAD_DIM, :] = qk_sum[:, own].astype(jnp.bfloat16)
        out_ref[g, 2 * HEAD_DIM :, :] = v_sum[:, own].astype(jnp.bfloat16)


def turn_kernel(slab_ref, *out_refs):
    for i, out_ref in enumerate(out_refs):
        own = slice(i * HEAD_DIM, (i + 1) * HEAD_DIM)
        heads = [slab_ref[h, own, :].astype(jnp.float32) for h in range(slab_ref.shape[0])]
        out_ref[0] = jnp.transpose(jnp.concatenate(heads, axis=0))


def input_kernel(slab_ref, wq_ref, wk_ref, wv_ref, act_ref, up_ref, out_ref):
    rows = act_ref.shape[0]
    unit, row_scale = normalize(act_ref[...])
    queries, keys, values = [], [], []
    for pair in range(HEADS // 2):
        even = slab_ref[2 * pair].astype(jnp.float32)
        odd = slab_ref[2 * pair + 1].astype(jnp.float32)
        low = low_lanes(even[PACKED:])
        queries.append(jnp.where(low, even[PACKED:], swap(odd[PACKED:])))
        keys.append(jnp.where(low, swap(even[PACKED:]), odd[PACKED:]))
        values += [unpack(even[:PACKED], rows), unpack(odd[:PACKED], rows)]
    total = 0.0
    for parts, ref in ((queries, wq_ref), (keys, wk_ref), (values, wv_ref)):
        left = jnp.concatenate(parts, axis=1).astype(jnp.bfloat16)
        total = total + dot(left, ref[...], ((1,), (1,)))
    total = total - unit * jnp.mean(total * unit, axis=-1, keepdims=True)
    out_ref[...] = (up_ref[...] + row_scale * total).astype(jnp.bfloat16)


def reorder_kernel(order_ref, rows_ref, out_ref):
    rows = rows_ref.shape[0]
    chosen = lax.broadcasted_iota(jnp.int32, (rows, rows), 1) == order_ref[...]
    chosen = jnp.where(chosen, 1.0, 0.0).astype(jnp.bfloat16)
    out_ref[0] = dot(chosen, rows_ref[...]).astype(jnp.bfloat16)


def exchange(slabs):
    return lax.all_to_all(slabs, "seq", split_axis=0, concat_axis=0, tiled=True)


def spread(block):
    side, near, far = [partner(block, "seq", bit) for bit in range(3)]
    side_far = partner(far, "seq", 0)
    near_far = partner(far, "seq", 1)
    side_near = partner(near, "seq", 0)
    last = partner(side_far, "seq", 1)
    return block, side, near, far, side_near, side_far, near_far, last


DISTANCES = (0, 1, 2, 4, 3, 5, 6, 7)


def wide(matrix):
    return matrix.astype(jnp.float32)


def low(matrix):
    return matrix.astype(jnp.bfloat16)


def sum_to_owner(first, second, third, keep, bits):
    size = keep.shape[0]
    got = partner(first, "seq", bits[0])
    more = partner(low(wide(second) + wide(got[2 * size :])), "seq", bits[1])
    third = wide(third) + wide(got[size : 2 * size]) + wide(more[size:])
    keep = wide(keep) + wide(got[:size]) + wide(more[:size])
    return keep + wide(partner(low(third), "seq", bits[2]))


EARLY = 6


def head_shards(
    activations, incoming, w_query, w_key, w_value, w_out, block_ids, flip_order
):
    parts = lax.axis_size("seq")
    sections = lax.axis_size("section")
    me = lax.axis_index("seq").astype(jnp.int32).reshape(1)
    field, upstream = activations[0], incoming[0]
    wq, wk, wv, wo = w_query[0], w_key[0], w_value[0], w_out[0]
    rows, width = field.shape
    inner = wq.shape[1]
    tokens = parts * rows
    length = PACKED + rows
    f32 = jnp.float32

    def out(place, *dims, dtype=jnp.bfloat16):
        return place, jax.ShapeDtypeStruct(dims, dtype)

    blocks = spread(field)
    order = me[0] ^ jnp.array(DISTANCES, jnp.int32)
    ids = jnp.take(block_ids.reshape(parts, rows), order, axis=0).reshape(tokens)
    pieces = [
        call(
            project_kernel,
            [("s", me), *[("h", block) for block in group], ("r", wq), ("r", wk), ("r", wv)],
            [
                out("h", len(group), rows, width),
                out("h", len(group), rows, 256, dtype=f32),
                out("h", len(group), rows, 256),
            ],
            2 * len(group) * rows * width * 512,
            [pltpu.VMEM((width, 2 * HEAD_DIM), jnp.bfloat16)] * 3
            + [pltpu.SemaphoreType.DMA((3,))],
        )
        for group in (blocks[:EARLY], blocks[EARLY:])
    ]
    normed, back, projected = zip(*pieces)
    probs, qk, value, out_t, packed = call(
        attend_kernel,
        [("s", me), *[("h", piece) for piece in projected], ("v", ids[None, :]), ("v", ids[:, None])],
        [
            out("h", len(tiles(tokens)), tokens, TILE),
            out("h", tokens, 128),
            out("h", tokens, HEAD_DIM),
            out("h", HEAD_DIM, tokens, dtype=f32),
            out("h", parts, PACKED, 128),
        ],
        4 * tokens * tokens * 256,
    )
    packed = exchange(packed)
    grad_affine, scaled, grad_slabs = call(
        affine_kernel,
        [("h", packed), ("h", field), ("h", upstream), ("h", wo)],
        [
            out("h", rows, 2 * width),
            out("h", rows, width, dtype=f32),
            out("h", HEADS, PACKED, 128),
        ],
        8 * rows * width * inner,
    )
    grad_slabs = exchange(grad_slabs)
    terms = call(
        out_term_kernel,
        [("s", me), ("h", packed), ("h", grad_affine)],
        [out("h", len(group) * HEAD_DIM, width) for order in ORDERS for group in order],
        4 * rows * width * inner,
    )
    grad_slabs, terms = lax.optimization_barrier((grad_slabs, terms))
    (grads,) = call(
        backward_kernel,
        [("s", me), ("h", grad_slabs), ("h", probs), ("h", qk), ("h", value), ("h", out_t)]
        + [("h", piece) for piece in back],
        [out("h", parts, length, 128)],
        8 * tokens * tokens * 256,
        [
            pltpu.VMEM((tokens, HEAD_DIM), f32),
            pltpu.VMEM((tokens, HEAD_DIM), f32),
            pltpu.VMEM((HEAD_DIM, tokens), f32),
        ],
    )
    token_grads = exchange(grads)
    (weight_terms,) = call(
        weights_kernel,
        [("s", me), ("h", grads)] + [("h", piece) for piece in normed],
        [out("h", parts, 3 * HEAD_DIM, width // parts)],
        2 * tokens * width * 256,
    )
    weight_terms = exchange(weight_terms)
    (grad_input,) = call(
        input_kernel,
        [("h", token_grads), ("h", wq), ("h", wk), ("h", wv), ("h", field), ("h", scaled)],
        [out("h", rows, width)],
        6 * rows * width * inner,
    )
    route = [
        (s * parts + d, (s - 1) * parts + parts - 1 - d)
        for s in range(1, sections)
        for d in range(parts)
    ]
    moved = lax.ppermute(grad_input, ("section", "seq"), route)
    grad_out = jnp.concatenate(
        [sum_to_owner(*terms[:4], (0, 1, 2)), sum_to_owner(*terms[4:], (1, 0, 2))], axis=1
    )
    grad_q, grad_k, grad_v = call(
        turn_kernel, [("h", weight_terms)], [out("h", 1, width // parts, inner, dtype=f32)] * 3
    )
    (carry,) = call(
        reorder_kernel,
        [("v", flip_order[0][:, None]), ("h", moved)],
        [out("h", 1, rows, width)],
        2 * rows * rows * width,
    )
    return (carry, grad_q, grad_k, grad_v, grad_out[None])


def solution(mesh):
    shards = head_shards if mesh.shape["seq"] == HEADS else general_shards
    in_specs = (
        P("section", "seq", None),
        P("section", "seq", None),
        P("section", None, None),
        P("section", None, None),
        P("section", None, None),
        P("section", None, None),
        P(),
        P("section", None),
    )
    out_specs = (
        P("section", "seq", None),
        P("section", "seq", None),
        P("section", "seq", None),
        P("section", "seq", None),
        P("section", "seq", None),
    )
    return jax.shard_map(shards, mesh=mesh, in_specs=in_specs, out_specs=out_specs, check_vma=False)
```

```python
import jax
import jax.numpy as jnp
from jax import lax
from jax.experimental import pallas as pl
from jax.experimental.pallas import tpu as pltpu
from jax.sharding import PartitionSpec as P

HEADS = 8
HEAD_DIM = 64


EPSILON = 1e-06


def partner(block, axis, stride):
    count = lax.axis_size(axis)
    route = []
    for low in range(count):
        high = low | 1 << stride
        if high != low and high < count:
            route += [(low, high), (high, low)]
    return lax.ppermute(block, axis, route)


def shifted(block, axis, distance):
    devices = range(lax.axis_size(axis))
    route = [(i - distance, i) for i in devices if i - distance in devices]
    return lax.ppermute(block, axis, route)


def split_heads(matrix):
    return matrix.reshape(matrix.shape[0], HEADS, HEAD_DIM)


def head_major(matrix):
    return jnp.transpose(split_heads(matrix), (1, 0, 2))


def unit_heads(projected):
    parts = split_heads(projected)
    factor = lax.rsqrt(jnp.mean(parts * parts, axis=-1, keepdims=True) + EPSILON)
    return (parts * factor, factor)


def unit_back(grad_heads, unit, factor):
    return factor * (grad_heads - unit * jnp.mean(grad_heads * unit, axis=-1, keepdims=True))


def mirror(rows):
    for bit in range(lax.axis_size("seq").bit_length() - 1):
        rows = partner(rows, "seq", bit)
    return rows


def to_previous(rows):
    return shifted(rows, "section", -1)


def general_shards(activations, incoming, w_query, w_key, w_value, w_out, block_ids, flip_order):
    field = activations[0].astype(jnp.float32)
    upstream = incoming[0].astype(jnp.float32)
    weight_query = w_query[0]
    weight_key = w_key[0]
    weight_value = w_value[0]
    weight_out = w_out[0]
    flip_row = flip_order[0]
    rows = field.shape[0]
    width = field.shape[1]
    inner = weight_query.shape[1]
    scale = HEAD_DIM ** (-0.5)
    first = lax.axis_index("seq") * rows
    my_blocks = lax.dynamic_slice_in_dim(block_ids, first, rows)
    row_scale = lax.rsqrt(jnp.mean(field * field, axis=-1, keepdims=True) + EPSILON)
    unit_rows = field * row_scale
    normed = unit_rows.astype(jnp.bfloat16)
    query_raw = jnp.dot(normed, weight_query, preferred_element_type=jnp.float32)
    key_raw = jnp.dot(normed, weight_key, preferred_element_type=jnp.float32)
    values = jnp.dot(normed, weight_value, preferred_element_type=jnp.float32).astype(jnp.bfloat16)
    query_unit, query_scale = unit_heads(query_raw)
    key_unit, key_scale = unit_heads(key_raw)
    queries = query_unit.astype(jnp.bfloat16).reshape(rows, inner)
    keys = key_unit.astype(jnp.bfloat16).reshape(rows, inner)
    keys_all, values_all = (
        lax.all_gather(keys, "seq", axis=0, tiled=True),
        lax.all_gather(values, "seq", axis=0, tiled=True),
    )
    allowed = block_ids[None, :] <= my_blocks[:, None]
    query_heads = head_major(queries)
    key_heads_all = head_major(keys_all)
    value_heads_all = head_major(values_all)

    def probabilities(query_part, key_part):
        scores = jnp.dot(query_part, key_part.T, preferred_element_type=jnp.float32) * scale
        numerator = jnp.where(allowed, jnp.exp(scores), 0.0)
        denominator = jnp.sum(numerator, axis=-1, keepdims=True)
        return (numerator / denominator, denominator)

    def forward_head(operands):
        query_part, key_part, value_part = operands
        probs, denominator = probabilities(query_part, key_part)
        out_part = jnp.dot(
            probs.astype(jnp.bfloat16), value_part, preferred_element_type=jnp.float32
        ).astype(jnp.bfloat16)
        return (out_part, denominator[:, 0])

    heads_out, denominators = lax.map(forward_head, (query_heads, key_heads_all, value_heads_all))
    attended = jnp.transpose(heads_out, (1, 0, 2)).reshape(rows, inner)
    affine = jnp.dot(attended, weight_out, preferred_element_type=jnp.float32)
    shift_part = affine[:, :width]
    log_scale = affine[:, width:]
    factor = jnp.exp(-log_scale)
    latent = (field - shift_part) * factor
    grad_affine = jnp.concatenate([-upstream * factor, 1.0 - upstream * latent], axis=-1).astype(
        jnp.bfloat16
    )
    out_term = jnp.dot(attended.T, grad_affine, preferred_element_type=jnp.float32)
    grad_attn = jnp.dot(grad_affine, weight_out.T, preferred_element_type=jnp.float32).astype(
        jnp.bfloat16
    )
    correction = jnp.sum(
        split_heads(grad_attn.astype(jnp.float32)) * split_heads(attended.astype(jnp.float32)),
        axis=-1,
    )
    grad_heads = head_major(grad_attn)
    correction_heads = jnp.transpose(correction)[:, :, None]

    def backward_head(operands):
        query_part, key_part, value_part, grad_part, corr_part = operands
        probs, denominator = probabilities(query_part, key_part)
        grad_probs = jnp.dot(grad_part, value_part.T, preferred_element_type=jnp.float32)
        grad_scores = (probs * (grad_probs - corr_part)).astype(jnp.bfloat16)
        grad_qpart = jnp.dot(grad_scores, key_part, preferred_element_type=jnp.float32) * scale
        grad_kpart = jnp.dot(grad_scores.T, query_part, preferred_element_type=jnp.float32) * scale
        grad_vpart = jnp.dot(
            probs.astype(jnp.bfloat16).T, grad_part, preferred_element_type=jnp.float32
        )
        return (grad_qpart, grad_kpart, grad_vpart)

    grad_qheads, grad_kall, grad_vall = lax.map(
        backward_head, (query_heads, key_heads_all, value_heads_all, grad_heads, correction_heads)
    )
    key_terms = jnp.transpose(grad_kall, (1, 0, 2)).reshape(-1, inner)
    value_terms = jnp.transpose(grad_vall, (1, 0, 2)).reshape(-1, inner)
    grad_kunit, grad_vsum = (
        lax.psum_scatter(
            key_terms.astype(jnp.bfloat16), "seq", scatter_dimension=0, tiled=True
        ).astype(jnp.float32),
        lax.psum_scatter(
            value_terms.astype(jnp.bfloat16), "seq", scatter_dimension=0, tiled=True
        ).astype(jnp.float32),
    )
    grad_queries = (
        unit_back(jnp.transpose(grad_qheads, (1, 0, 2)), query_unit, query_scale)
        .reshape(rows, inner)
        .astype(jnp.bfloat16)
    )
    grad_keys = (
        unit_back(split_heads(grad_kunit), key_unit, key_scale)
        .reshape(rows, inner)
        .astype(jnp.bfloat16)
    )
    grad_values = grad_vsum.astype(jnp.bfloat16)
    query_term = jnp.dot(normed.T, grad_queries, preferred_element_type=jnp.float32)
    key_term = jnp.dot(normed.T, grad_keys, preferred_element_type=jnp.float32)
    value_term = jnp.dot(normed.T, grad_values, preferred_element_type=jnp.float32)
    sums = (
        lax.psum_scatter(
            query_term.astype(jnp.bfloat16), "seq", scatter_dimension=0, tiled=True
        ).astype(jnp.float32),
        lax.psum_scatter(
            key_term.astype(jnp.bfloat16), "seq", scatter_dimension=0, tiled=True
        ).astype(jnp.float32),
        lax.psum_scatter(
            value_term.astype(jnp.bfloat16), "seq", scatter_dimension=0, tiled=True
        ).astype(jnp.float32),
        lax.psum_scatter(
            out_term.astype(jnp.bfloat16), "seq", scatter_dimension=0, tiled=True
        ).astype(jnp.float32),
    )
    grad_normed = jnp.dot(grad_queries, weight_query.T, preferred_element_type=jnp.float32)
    grad_normed = grad_normed + jnp.dot(grad_keys, weight_key.T, preferred_element_type=jnp.float32)
    grad_normed = grad_normed + jnp.dot(
        grad_values, weight_value.T, preferred_element_type=jnp.float32
    )
    grad_input = upstream * factor + row_scale * (
        grad_normed - unit_rows * jnp.mean(grad_normed * unit_rows, axis=-1, keepdims=True)
    )
    grad_input = grad_input.astype(jnp.bfloat16)
    moved = mirror(to_previous(grad_input))
    carry = jnp.take(moved, flip_row, axis=0)
    return (carry[None], sums[0][None], sums[1][None], sums[2][None], sums[3][None])


PACKED = 80


def call(kernel, ins, outs, scratch=()):
    spaces = {"s": pltpu.SMEM, "v": pltpu.VMEM, "a": pl.ANY}
    places, operands = zip(*ins)
    return pl.pallas_call(
        kernel,
        out_shape=tuple(outs),
        in_specs=[pl.BlockSpec(memory_space=spaces[place]) for place in places],
        out_specs=(pl.BlockSpec(memory_space=pltpu.VMEM),) * len(outs),
        scratch_shapes=list(scratch),
        compiler_params=pltpu.CompilerParams(vmem_limit_bytes=14 * 2**20),
        cost_estimate=pl.CostEstimate(flops=1024, bytes_accessed=1024, transcendentals=0),
    )(*operands)


def dot(left, right, contract=((1,), (0,))):
    return lax.dot_general(left, right, (contract, ((), ())), preferred_element_type=jnp.float32)


def low_lanes(block):
    return lax.broadcasted_iota(jnp.int32, block.shape, len(block.shape) - 1) < HEAD_DIM


def swap(block):
    return pltpu.roll(block, HEAD_DIM, 1)


def half_sums(block):
    low = low_lanes(block)
    first = jnp.sum(jnp.where(low, block, 0.0), axis=-1, keepdims=True)
    second = jnp.sum(jnp.where(low, 0.0, block), axis=-1, keepdims=True)
    return jnp.where(low, first, second)


def pack(block):
    rows = block.shape[0]
    return jnp.concatenate([block[:PACKED], block[rows - PACKED :]], axis=1)


def unpack(slab, rows):
    right = swap(slab)[2 * PACKED - rows :, :HEAD_DIM]
    return jnp.concatenate([slab[:, :HEAD_DIM], right], axis=0)


def normalize(block):
    field = block.astype(jnp.float32)
    row_scale = lax.rsqrt(jnp.mean(field * field, axis=-1, keepdims=True) + EPSILON)
    return field * row_scale, row_scale


def project(block, weight):
    normed = normalize(block)[0].astype(jnp.bfloat16)
    product = dot(normed, weight)
    raw, value = product[:, : 2 * HEAD_DIM], product[:, 2 * HEAD_DIM :]
    scale = lax.rsqrt(half_sums(raw * raw) / HEAD_DIM + EPSILON)
    return normed, raw * scale, scale, value


def project_kernel(*refs):
    blocks, (weight_ref, normed_ref, unit_ref, scale_ref, value_ref) = refs[:-5], refs[-5:]
    for m, block in enumerate(blocks):
        made = project(block[...], weight_ref[...])
        for ref, part in zip((normed_ref, unit_ref, scale_ref, value_ref), made):
            ref[m] = part.astype(ref.dtype)


TILE = 256


def tiles(tokens):
    starts = range(0, tokens, TILE)
    return [(start, min(tokens, start + TILE)) for start in starts]


def attend_kernel(
    me_ref, unit_ref, value_ref, near_ref, last_ref, weight_ref, row_ids, column_ids, *out_refs
):
    normed_ref, late_unit, late_scale, prob_ref, qk_ref, v_ref, out_t_ref, out_ref = out_refs
    early, rows = unit_ref.shape[:2]
    units = [unit_ref[m] for m in range(early)]
    values = [value_ref[m] for m in range(early)]
    for m, ref in enumerate((near_ref, last_ref)):
        normed, unit, scale, value = project(ref[...], weight_ref[...])
        normed_ref[m], late_unit[m], late_scale[m] = normed, unit, scale
        units.append(unit)
        values.append(value)
    parts = len(units)
    tokens = parts * rows
    qk = jnp.concatenate(units, axis=0).astype(jnp.bfloat16)
    value = jnp.concatenate(values, axis=0).astype(jnp.bfloat16)
    qk_ref[...] = qk
    v_ref[...] = value
    query, key = qk[:, :HEAD_DIM] * HEAD_DIM ** (-0.5), qk[:, HEAD_DIM:]
    for start, stop in tiles(tokens):
        scores = dot(key, query[start:stop], ((1,), (1,)))
        allowed = column_ids[...] <= row_ids[:, start:stop]
        numerator = jnp.where(allowed, jnp.exp(scores), 0.0)
        probs = numerator * (1.0 / jnp.sum(numerator, axis=0, keepdims=True))
        probs = probs.astype(jnp.bfloat16)
        prob_ref[:, start:stop] = probs
        out_t = dot(value, probs, ((0,), (0,)))
        out_t_ref[:, start:stop] = out_t.astype(jnp.bfloat16).astype(jnp.float32)
    out = jnp.transpose(out_t_ref[...])
    for m in range(parts):
        group = me_ref[0] ^ DISTANCES[m]
        out_ref[group] = pack(out[m * rows : (m + 1) * rows]).astype(jnp.bfloat16)


def affine_kernel(slab_ref, act_ref, inc_ref, w_ref, aff_ref, up_ref, out_ref):
    heads = slab_ref.shape[0]
    rows, width = act_ref.shape
    attended = jnp.concatenate(
        [unpack(slab_ref[h].astype(jnp.float32), rows) for h in range(heads)], axis=1
    ).astype(jnp.bfloat16)
    factor = jnp.exp(-dot(attended, w_ref[:, width:]))
    scaled = inc_ref[...].astype(jnp.float32) * factor
    up_ref[...] = scaled
    shift_part = dot(attended, w_ref[:, :width])
    latent_part = scaled * (act_ref[...].astype(jnp.float32) - shift_part)
    grad_affine = jnp.concatenate([-scaled, 1.0 - latent_part], axis=1).astype(jnp.bfloat16)
    aff_ref[...] = grad_affine
    grad = dot(grad_affine, w_ref[...], ((1,), (1,)))
    for h in range(heads):
        block = grad[:, h * HEAD_DIM : (h + 1) * HEAD_DIM]
        out_ref[h] = pack(block).astype(jnp.bfloat16)


ORDERS = (((1, 5, 3, 7), (2, 6), (4,), (0,)), ((2, 6, 3, 7), (1, 5), (4,), (0,)))


def out_term_kernel(me_ref, slab_ref, aff_ref, *out_refs):
    heads, rows = slab_ref.shape[0], aff_ref.shape[0]
    width = aff_ref.shape[1] // 2
    columns = [
        unpack(slab_ref[me_ref[0] ^ m].astype(jnp.float32), rows) for m in range(heads)
    ]
    for half, order in enumerate(ORDERS):
        right = aff_ref[:, half * width : (half + 1) * width]
        for out_ref, group in zip(out_refs[4 * half : 4 * half + 4], order):
            left = jnp.concatenate([columns[m] for m in group], axis=1).astype(jnp.bfloat16)
            out_ref[...] = dot(left, right, ((0,), (0,))).astype(jnp.bfloat16)


def backward_kernel(me_ref, slab_ref, prob_ref, qk_ref, v_ref, out_t_ref, *refs):
    early, late, (out_ref, gk_ref, gv_ref, gq_ref) = refs[:3], refs[3:6], refs[6:]
    parts, rows = slab_ref.shape[0], early[0].shape[1]
    tokens = parts * rows
    me = me_ref[0]
    first = early[0].shape[0]
    grad_f = jnp.concatenate(
        [unpack(slab_ref[me ^ DISTANCES[m]].astype(jnp.float32), rows) for m in range(parts)], axis=0
    )
    grad = grad_f.astype(jnp.bfloat16)
    grad_t = jnp.transpose(grad_f)
    correction = jnp.sum(grad_t * out_t_ref[...], axis=0, keepdims=True)
    grad_t = grad_t.astype(jnp.bfloat16)
    qk, value = qk_ref[...], v_ref[...]
    query, key = qk[:, :HEAD_DIM], qk[:, HEAD_DIM:]
    gk_ref[...] = jnp.zeros_like(gk_ref)
    gv_ref[...] = jnp.zeros_like(gv_ref)
    for start, stop in tiles(tokens):
        probs = prob_ref[:, start:stop]
        grad_probs = dot(value, grad_t[:, start:stop])
        scores = probs.astype(jnp.float32) * (grad_probs - correction[:, start:stop])
        scores = scores.astype(jnp.bfloat16)
        gv_ref[...] += dot(probs, grad[start:stop])
        gk_ref[...] += dot(scores, query[start:stop])
        gq_ref[:, start:stop] = dot(key, scores, ((0,), (0,)))
    grad_q = jnp.transpose(gq_ref[...])
    qk_sum = v_sum = 0.0
    for m in range(parts):
        own = slice(m * rows, (m + 1) * rows)
        normed, unit, scale = [
            early[i][m] if m < first else late[i][m - first] for i in range(3)
        ]
        raw = jnp.concatenate([grad_q[own], gk_ref[own, :]], axis=1) * HEAD_DIM ** (-0.5)
        back = scale * (raw - unit * (half_sums(raw * unit) / HEAD_DIM))
        back, grad_v = back.astype(jnp.bfloat16), gv_ref[own, :]
        out_ref[me ^ DISTANCES[m], :PACKED, :] = pack(grad_v).astype(jnp.bfloat16)
        out_ref[me ^ DISTANCES[m], PACKED : PACKED + rows, :] = back
        qk_sum = qk_sum + dot(back, normed, ((0,), (0,)))
        v_sum = v_sum + dot(grad_v.astype(jnp.bfloat16), normed, ((0,), (0,)))
    step = qk_sum.shape[1] // parts
    middle = PACKED + rows + 2 * HEAD_DIM
    for g in range(parts):
        own = slice(g * step, (g + 1) * step)
        out_ref[g, PACKED + rows : middle, :] = qk_sum[:, own].astype(jnp.bfloat16)
        out_ref[g, middle:, :] = v_sum[:, own].astype(jnp.bfloat16)


def turn_kernel(slab_ref, *out_refs):
    start = slab_ref.shape[1] - 3 * HEAD_DIM
    for i, out_ref in enumerate(out_refs):
        own = slice(start + i * HEAD_DIM, start + (i + 1) * HEAD_DIM)
        heads = [slab_ref[h, own, :].astype(jnp.float32) for h in range(slab_ref.shape[0])]
        out_ref[0] = jnp.transpose(jnp.concatenate(heads, axis=0))


def second_sum_kernel(*refs):
    for second, got, out in zip(refs[0:2], refs[2:4], refs[5:7]):
        start = got.shape[0] - second.shape[0]
        out[...] = low(wide(second[...]) + wide(got[start:, :]))


def third_sum_kernel(*refs):
    for i in range(2):
        third, keep, got, more = [ref[...] for ref in refs[i:8:2]]
        size = third.shape[0]
        leaving, staying = refs[9 + i], refs[11 + i]
        leaving[...] = low(wide(third) + wide(got[size : 2 * size]) + wide(more[size:]))
        staying[...] = wide(keep) + wide(got[:size]) + wide(more[:size])


def last_sum_kernel(keep_a, keep_b, got_a, got_b, out_ref):
    for i, (keep, got) in enumerate(((keep_a, got_a), (keep_b, got_b))):
        width = keep.shape[1]
        out_ref[0, :, i * width : (i + 1) * width] = keep[...] + wide(got[...])


def input_kernel(slab_ref, wq_ref, wk_ref, wv_ref, act_ref, up_ref, out_ref):
    rows = act_ref.shape[0]
    unit, row_scale = normalize(act_ref[...])
    queries, keys, values = [], [], []
    for pair in range(HEADS // 2):
        even, odd = [
            slab_ref[2 * pair + i, : PACKED + rows, :].astype(jnp.float32) for i in range(2)
        ]
        low = low_lanes(even[PACKED:])
        queries.append(jnp.where(low, even[PACKED:], swap(odd[PACKED:])))
        keys.append(jnp.where(low, swap(even[PACKED:]), odd[PACKED:]))
        values += [unpack(even[:PACKED], rows), unpack(odd[:PACKED], rows)]
    total = 0.0
    for parts, ref in ((queries, wq_ref), (keys, wk_ref), (values, wv_ref)):
        left = jnp.concatenate(parts, axis=1).astype(jnp.bfloat16)
        total = total + dot(left, ref[...], ((1,), (1,)))
    total = total - unit * jnp.mean(total * unit, axis=-1, keepdims=True)
    out_ref[...] = (up_ref[...] + row_scale * total).astype(jnp.bfloat16)


def reorder_kernel(order_ref, rows_ref, out_ref):
    rows = rows_ref.shape[0]
    chosen = lax.broadcasted_iota(jnp.int32, (rows, rows), 1) == order_ref[...]
    chosen = jnp.where(chosen, 1.0, 0.0).astype(jnp.bfloat16)
    out_ref[0] = dot(chosen, rows_ref[...]).astype(jnp.bfloat16)


def exchange(slabs):
    return lax.all_to_all(slabs, "seq", split_axis=0, concat_axis=0, tiled=True)


def spread(block):
    side, near, far = [partner(block, "seq", bit) for bit in range(3)]
    side_far = partner(far, "seq", 0)
    near_far = partner(far, "seq", 1)
    side_near = partner(near, "seq", 0)
    last = partner(side_far, "seq", 1)
    return block, side, near, far, side_near, side_far, near_far, last


DISTANCES = (0, 1, 2, 4, 3, 5, 6, 7)


def wide(matrix):
    return matrix.astype(jnp.float32)


def low(matrix):
    return matrix.astype(jnp.bfloat16)


EARLY = 6


def head_shards(
    activations, incoming, w_query, w_key, w_value, w_out, block_ids, flip_order
):
    parts = lax.axis_size("seq")
    sections = lax.axis_size("section")
    me = lax.axis_index("seq").astype(jnp.int32).reshape(1)
    field, upstream = activations[0], incoming[0]
    wq, wk, wv, wo = w_query[0], w_key[0], w_value[0], w_out[0]
    rows, width = field.shape
    inner = wq.shape[1]
    tokens = parts * rows
    f32 = jnp.float32

    def out(*dims, dtype=jnp.bfloat16):
        return jax.ShapeDtypeStruct(dims, dtype)

    blocks = spread(field)
    order = me[0] ^ jnp.array(DISTANCES, jnp.int32)
    ids = jnp.take(block_ids.reshape(parts, rows), order, axis=0).reshape(tokens)
    weight = jnp.concatenate(
        [lax.dynamic_slice_in_dim(w, me[0] * HEAD_DIM, HEAD_DIM, axis=1) for w in (wq, wk, wv)],
        axis=1,
    )
    pair = 2 * HEAD_DIM
    normed, unit, unit_scale, projected = call(
        project_kernel,
        [("v", block) for block in blocks[:EARLY]] + [("v", weight)],
        [
            out(EARLY, rows, width),
            out(EARLY, rows, pair, dtype=f32),
            out(EARLY, rows, pair, dtype=f32),
            out(EARLY, rows, HEAD_DIM, dtype=f32),
        ],
    )
    late = parts - EARLY
    *late_parts, probs, qk, value, out_t, packed = call(
        attend_kernel,
        [("s", me), ("v", unit), ("v", projected), *[("v", block) for block in blocks[EARLY:]]]
        + [("v", weight), ("v", ids[None, :]), ("v", ids[:, None])],
        [
            out(late, rows, width),
            out(late, rows, pair, dtype=f32),
            out(late, rows, pair, dtype=f32),
            out(tokens, tokens),
            out(tokens, pair),
            out(tokens, HEAD_DIM),
            out(HEAD_DIM, tokens, dtype=f32),
            out(parts, PACKED, 128),
        ],
    )
    packed = exchange(packed)
    grad_affine, scaled, grad_slabs = call(
        affine_kernel,
        [("v", packed), ("v", field), ("v", upstream), ("v", wo)],
        [out(rows, 2 * width), out(rows, width, dtype=f32), out(HEADS, PACKED, 128)],
    )
    grad_slabs = exchange(grad_slabs)
    terms = call(
        out_term_kernel,
        [("s", me), ("v", packed), ("v", grad_affine)],
        [out(len(group) * HEAD_DIM, width) for order in ORDERS for group in order],
    )
    grad_slabs, terms = lax.optimization_barrier((grad_slabs, terms))
    first, second, third, keep = zip(terms[:4], terms[4:])
    got = [partner(part, "seq", bit) for bit, part in enumerate(first)]
    (grads,) = call(
        backward_kernel,
        [("s", me), ("v", grad_slabs), ("v", probs), ("v", qk), ("v", value), ("v", out_t)]
        + [("v", x) for x in (normed, unit, unit_scale, *late_parts)],
        [out(parts, PACKED + rows + 3 * HEAD_DIM, 128)],
        [
            pltpu.VMEM((tokens, HEAD_DIM), f32),
            pltpu.VMEM((tokens, HEAD_DIM), f32),
            pltpu.VMEM((HEAD_DIM, tokens), f32),
        ],
    )
    slabs = exchange(grads)
    leaving = call(
        second_sum_kernel,
        [("v", x) for x in (*second, *got)] + [("a", grads)],
        [out(*second[0].shape)] * 2,
    )
    more = [partner(part, "seq", 1 - bit) for bit, part in enumerate(leaving)]
    *leaving, keep_a, keep_b = call(
        third_sum_kernel,
        [("v", x) for x in (*third, *keep, *got, *more)] + [("a", slabs)],
        [out(*third[0].shape)] * 2 + [out(*keep[0].shape, dtype=f32)] * 2,
    )
    rest = [partner(part, "seq", 2) for part in leaving]
    (grad_input,) = call(
        input_kernel,
        [("v", x) for x in (slabs, wq, wk, wv, field, scaled)],
        [out(rows, width)],
    )
    route = [
        (s * parts + d, (s - 1) * parts + parts - 1 - d)
        for s in range(1, sections)
        for d in range(parts)
    ]
    moved = lax.ppermute(grad_input, ("section", "seq"), route)
    grad_q, grad_k, grad_v = call(
        turn_kernel, [("v", slabs)], [out(1, width // parts, inner, dtype=f32)] * 3
    )
    (grad_out,) = call(
        last_sum_kernel,
        [("v", x) for x in (keep_a, keep_b, *rest)],
        [out(1, keep_a.shape[0], 2 * width, dtype=f32)],
    )
    (carry,) = call(
        reorder_kernel, [("v", flip_order[0][:, None]), ("v", moved)], [out(1, rows, width)]
    )
    return (carry, grad_q, grad_k, grad_v, grad_out)


def solution(mesh):
    shards = head_shards if mesh.shape["seq"] == HEADS else general_shards
    in_specs = (
        P("section", "seq", None),
        P("section", "seq", None),
        P("section", None, None),
        P("section", None, None),
        P("section", None, None),
        P("section", None, None),
        P(),
        P("section", None),
    )
    out_specs = (
        P("section", "seq", None),
        P("section", "seq", None),
        P("section", "seq", None),
        P("section", "seq", None),
        P("section", "seq", None),
    )
    return jax.shard_map(shards, mesh=mesh, in_specs=in_specs, out_specs=out_specs, check_vma=False)
```

```python
import jax
import jax.numpy as jnp
from jax import lax
from jax.experimental import pallas as pl
from jax.experimental.pallas import tpu as pltpu
from jax.sharding import PartitionSpec as P

HEADS = 8
HEAD_DIM = 64


EPSILON = 1e-06


def partner(block, axis, stride):
    count = lax.axis_size(axis)
    route = []
    for low in range(count):
        high = low | 1 << stride
        if high != low and high < count:
            route += [(low, high), (high, low)]
    return lax.ppermute(block, axis, route)


def shifted(block, axis, distance):
    devices = range(lax.axis_size(axis))
    route = [(i - distance, i) for i in devices if i - distance in devices]
    return lax.ppermute(block, axis, route)


def split_heads(matrix):
    return matrix.reshape(matrix.shape[0], HEADS, HEAD_DIM)


def head_major(matrix):
    return jnp.transpose(split_heads(matrix), (1, 0, 2))


def unit_heads(projected):
    parts = split_heads(projected)
    factor = lax.rsqrt(jnp.mean(parts * parts, axis=-1, keepdims=True) + EPSILON)
    return (parts * factor, factor)


def unit_back(grad_heads, unit, factor):
    return factor * (grad_heads - unit * jnp.mean(grad_heads * unit, axis=-1, keepdims=True))


def mirror(rows):
    for bit in range(lax.axis_size("seq").bit_length() - 1):
        rows = partner(rows, "seq", bit)
    return rows


def to_previous(rows):
    return shifted(rows, "section", -1)


def general_shards(activations, incoming, w_query, w_key, w_value, w_out, block_ids, flip_order):
    field = activations[0].astype(jnp.float32)
    upstream = incoming[0].astype(jnp.float32)
    weight_query = w_query[0]
    weight_key = w_key[0]
    weight_value = w_value[0]
    weight_out = w_out[0]
    flip_row = flip_order[0]
    rows = field.shape[0]
    width = field.shape[1]
    inner = weight_query.shape[1]
    scale = HEAD_DIM ** (-0.5)
    first = lax.axis_index("seq") * rows
    my_blocks = lax.dynamic_slice_in_dim(block_ids, first, rows)
    row_scale = lax.rsqrt(jnp.mean(field * field, axis=-1, keepdims=True) + EPSILON)
    unit_rows = field * row_scale
    normed = unit_rows.astype(jnp.bfloat16)
    query_raw = jnp.dot(normed, weight_query, preferred_element_type=jnp.float32)
    key_raw = jnp.dot(normed, weight_key, preferred_element_type=jnp.float32)
    values = jnp.dot(normed, weight_value, preferred_element_type=jnp.float32).astype(jnp.bfloat16)
    query_unit, query_scale = unit_heads(query_raw)
    key_unit, key_scale = unit_heads(key_raw)
    queries = query_unit.astype(jnp.bfloat16).reshape(rows, inner)
    keys = key_unit.astype(jnp.bfloat16).reshape(rows, inner)
    keys_all, values_all = (
        lax.all_gather(keys, "seq", axis=0, tiled=True),
        lax.all_gather(values, "seq", axis=0, tiled=True),
    )
    allowed = block_ids[None, :] <= my_blocks[:, None]
    query_heads = head_major(queries)
    key_heads_all = head_major(keys_all)
    value_heads_all = head_major(values_all)

    def probabilities(query_part, key_part):
        scores = jnp.dot(query_part, key_part.T, preferred_element_type=jnp.float32) * scale
        numerator = jnp.where(allowed, jnp.exp(scores), 0.0)
        denominator = jnp.sum(numerator, axis=-1, keepdims=True)
        return (numerator / denominator, denominator)

    def forward_head(operands):
        query_part, key_part, value_part = operands
        probs, denominator = probabilities(query_part, key_part)
        out_part = jnp.dot(
            probs.astype(jnp.bfloat16), value_part, preferred_element_type=jnp.float32
        ).astype(jnp.bfloat16)
        return (out_part, denominator[:, 0])

    heads_out, denominators = lax.map(forward_head, (query_heads, key_heads_all, value_heads_all))
    attended = jnp.transpose(heads_out, (1, 0, 2)).reshape(rows, inner)
    affine = jnp.dot(attended, weight_out, preferred_element_type=jnp.float32)
    shift_part = affine[:, :width]
    log_scale = affine[:, width:]
    factor = jnp.exp(-log_scale)
    latent = (field - shift_part) * factor
    grad_affine = jnp.concatenate([-upstream * factor, 1.0 - upstream * latent], axis=-1).astype(
        jnp.bfloat16
    )
    out_term = jnp.dot(attended.T, grad_affine, preferred_element_type=jnp.float32)
    grad_attn = jnp.dot(grad_affine, weight_out.T, preferred_element_type=jnp.float32).astype(
        jnp.bfloat16
    )
    correction = jnp.sum(
        split_heads(grad_attn.astype(jnp.float32)) * split_heads(attended.astype(jnp.float32)),
        axis=-1,
    )
    grad_heads = head_major(grad_attn)
    correction_heads = jnp.transpose(correction)[:, :, None]

    def backward_head(operands):
        query_part, key_part, value_part, grad_part, corr_part = operands
        probs, denominator = probabilities(query_part, key_part)
        grad_probs = jnp.dot(grad_part, value_part.T, preferred_element_type=jnp.float32)
        grad_scores = (probs * (grad_probs - corr_part)).astype(jnp.bfloat16)
        grad_qpart = jnp.dot(grad_scores, key_part, preferred_element_type=jnp.float32) * scale
        grad_kpart = jnp.dot(grad_scores.T, query_part, preferred_element_type=jnp.float32) * scale
        grad_vpart = jnp.dot(
            probs.astype(jnp.bfloat16).T, grad_part, preferred_element_type=jnp.float32
        )
        return (grad_qpart, grad_kpart, grad_vpart)

    grad_qheads, grad_kall, grad_vall = lax.map(
        backward_head, (query_heads, key_heads_all, value_heads_all, grad_heads, correction_heads)
    )
    key_terms = jnp.transpose(grad_kall, (1, 0, 2)).reshape(-1, inner)
    value_terms = jnp.transpose(grad_vall, (1, 0, 2)).reshape(-1, inner)
    grad_kunit, grad_vsum = (
        lax.psum_scatter(
            key_terms.astype(jnp.bfloat16), "seq", scatter_dimension=0, tiled=True
        ).astype(jnp.float32),
        lax.psum_scatter(
            value_terms.astype(jnp.bfloat16), "seq", scatter_dimension=0, tiled=True
        ).astype(jnp.float32),
    )
    grad_queries = (
        unit_back(jnp.transpose(grad_qheads, (1, 0, 2)), query_unit, query_scale)
        .reshape(rows, inner)
        .astype(jnp.bfloat16)
    )
    grad_keys = (
        unit_back(split_heads(grad_kunit), key_unit, key_scale)
        .reshape(rows, inner)
        .astype(jnp.bfloat16)
    )
    grad_values = grad_vsum.astype(jnp.bfloat16)
    query_term = jnp.dot(normed.T, grad_queries, preferred_element_type=jnp.float32)
    key_term = jnp.dot(normed.T, grad_keys, preferred_element_type=jnp.float32)
    value_term = jnp.dot(normed.T, grad_values, preferred_element_type=jnp.float32)
    sums = (
        lax.psum_scatter(
            query_term.astype(jnp.bfloat16), "seq", scatter_dimension=0, tiled=True
        ).astype(jnp.float32),
        lax.psum_scatter(
            key_term.astype(jnp.bfloat16), "seq", scatter_dimension=0, tiled=True
        ).astype(jnp.float32),
        lax.psum_scatter(
            value_term.astype(jnp.bfloat16), "seq", scatter_dimension=0, tiled=True
        ).astype(jnp.float32),
        lax.psum_scatter(
            out_term.astype(jnp.bfloat16), "seq", scatter_dimension=0, tiled=True
        ).astype(jnp.float32),
    )
    grad_normed = jnp.dot(grad_queries, weight_query.T, preferred_element_type=jnp.float32)
    grad_normed = grad_normed + jnp.dot(grad_keys, weight_key.T, preferred_element_type=jnp.float32)
    grad_normed = grad_normed + jnp.dot(
        grad_values, weight_value.T, preferred_element_type=jnp.float32
    )
    grad_input = upstream * factor + row_scale * (
        grad_normed - unit_rows * jnp.mean(grad_normed * unit_rows, axis=-1, keepdims=True)
    )
    grad_input = grad_input.astype(jnp.bfloat16)
    moved = mirror(to_previous(grad_input))
    carry = jnp.take(moved, flip_row, axis=0)
    return (carry[None], sums[0][None], sums[1][None], sums[2][None], sums[3][None])


PACKED = 80


def call(kernel, microseconds, ins, outs, scratch=()):
    spaces = {"s": pltpu.SMEM, "v": pltpu.VMEM, "a": pl.ANY}
    places, operands = zip(*ins)
    return pl.pallas_call(
        kernel,
        out_shape=tuple(outs),
        in_specs=[pl.BlockSpec(memory_space=spaces[place]) for place in places],
        out_specs=(pl.BlockSpec(memory_space=pltpu.VMEM),) * len(outs),
        scratch_shapes=list(scratch),
        compiler_params=pltpu.CompilerParams(vmem_limit_bytes=14 * 2**20),
        cost_estimate=pl.CostEstimate(
            flops=int(microseconds * 1e9), bytes_accessed=1024, transcendentals=0
        ),
    )(*operands)


def dot(left, right, contract=((1,), (0,))):
    return lax.dot_general(left, right, (contract, ((), ())), preferred_element_type=jnp.float32)


def low_lanes(block):
    return lax.broadcasted_iota(jnp.int32, block.shape, len(block.shape) - 1) < HEAD_DIM


def swap(block):
    return pltpu.roll(block, HEAD_DIM, 1)


def half_sums(block):
    low = low_lanes(block)
    first = jnp.sum(jnp.where(low, block, 0.0), axis=-1, keepdims=True)
    second = jnp.sum(jnp.where(low, 0.0, block), axis=-1, keepdims=True)
    return jnp.where(low, first, second)


def pack(block):
    rows = block.shape[0]
    return jnp.concatenate([block[:PACKED], block[rows - PACKED :]], axis=1)


def unpack(slab, rows):
    right = swap(slab)[2 * PACKED - rows :, :HEAD_DIM]
    return jnp.concatenate([slab[:, :HEAD_DIM], right], axis=0)


def normalize(block):
    field = block.astype(jnp.float32)
    row_scale = lax.rsqrt(jnp.mean(field * field, axis=-1, keepdims=True) + EPSILON)
    return field * row_scale, row_scale


def project(block, weight):
    normed = normalize(block)[0].astype(jnp.bfloat16)
    product = dot(normed, weight)
    raw, value = product[:, : 2 * HEAD_DIM], product[:, 2 * HEAD_DIM :]
    scale = lax.rsqrt(half_sums(raw * raw) / HEAD_DIM + EPSILON)
    return normed, raw * scale, scale, value


def select_kernel(me_ref, wq_ref, wk_ref, wv_ref, out_ref, *scratch):
    held, semaphores = scratch[:3], scratch[3]
    odd = lax.rem(me_ref[0], 2) == 1
    pair = pl.multiple_of(lax.div(me_ref[0], 2) * 2 * HEAD_DIM, 2 * HEAD_DIM)
    copies = [
        pltpu.make_async_copy(ref.at[:, pl.ds(pair, 2 * HEAD_DIM)], kept, semaphores.at[i])
        for i, (ref, kept) in enumerate(zip((wq_ref, wk_ref, wv_ref), held))
    ]
    for copy in copies:
        copy.start()
    for copy in copies:
        copy.wait()
    q, k, v = [wide(kept[...]) for kept in held]
    lower = low_lanes(q)
    qk = jnp.where(lower, jnp.where(odd, swap(q), q), jnp.where(odd, k, swap(k)))
    out_ref[:, : 2 * HEAD_DIM] = low(qk)
    out_ref[:, 2 * HEAD_DIM :] = low(jnp.where(odd, swap(v), v)[:, :HEAD_DIM])


def project_kernel(*refs):
    blocks, (weight_ref, normed_ref, unit_ref, scale_ref, value_ref) = refs[:-5], refs[-5:]
    for m, block in enumerate(blocks):
        made = project(block[...], weight_ref[...])
        for ref, part in zip((normed_ref, unit_ref, scale_ref, value_ref), made):
            ref[m] = part.astype(ref.dtype)


TILE = 256


def tiles(tokens):
    starts = range(0, tokens, TILE)
    return [(start, min(tokens, start + TILE)) for start in starts]


def attend_kernel(
    unit_ref, value_ref, near_ref, last_ref, weight_ref, row_ids, column_ids, *out_refs
):
    normed_ref, late_unit, late_scale, prob_ref, qk_ref, v_ref, out_t_ref = out_refs[:7]
    early, rows = unit_ref.shape[:2]
    units = [unit_ref[m] for m in range(early)]
    values = [value_ref[m] for m in range(early)]
    for m, ref in enumerate((near_ref, last_ref)):
        normed, unit, scale, value = project(ref[...], weight_ref[...])
        normed_ref[m], late_unit[m], late_scale[m] = normed, unit, scale
        units.append(unit)
        values.append(value)
    parts = len(units)
    tokens = parts * rows
    qk = jnp.concatenate(units, axis=0).astype(jnp.bfloat16)
    value = jnp.concatenate(values, axis=0).astype(jnp.bfloat16)
    qk_ref[...] = qk
    v_ref[...] = value
    query, key = qk[:, :HEAD_DIM] * HEAD_DIM ** (-0.5), qk[:, HEAD_DIM:]
    for start, stop in tiles(tokens):
        scores = dot(key, query[start:stop], ((1,), (1,)))
        allowed = column_ids[...] <= row_ids[:, start:stop]
        numerator = jnp.where(allowed, jnp.exp(scores), 0.0)
        probs = numerator * (1.0 / jnp.sum(numerator, axis=0, keepdims=True))
        probs = probs.astype(jnp.bfloat16)
        prob_ref[:, start:stop] = probs
        out_t = dot(value, probs, ((0,), (0,)))
        out_t_ref[:, start:stop] = out_t.astype(jnp.bfloat16).astype(jnp.float32)
    out = jnp.transpose(out_t_ref[...])
    for m, out_ref in enumerate(out_refs[7:]):
        out_ref[...] = low(pack(out[m * rows : (m + 1) * rows]))


def affine_kernel(me_ref, *refs):
    slabs, (act_ref, inc_ref, w_ref, aff_ref, up_ref) = refs[:HEADS], refs[HEADS : HEADS + 5]
    out_refs, held_ref = refs[HEADS + 5 : -1], refs[-1]
    rows, width = act_ref.shape
    for m, slab in enumerate(slabs):
        held_ref[me_ref[0] ^ DISTANCES[m]] = slab[...]
    attended = jnp.concatenate([unpack(wide(held_ref[h]), rows) for h in range(HEADS)], axis=1)
    attended = low(attended)
    factor = jnp.exp(-dot(attended, w_ref[:, width:]))
    scaled = inc_ref[...].astype(jnp.float32) * factor
    up_ref[...] = scaled
    shift_part = dot(attended, w_ref[:, :width])
    latent_part = scaled * (act_ref[...].astype(jnp.float32) - shift_part)
    grad_affine = jnp.concatenate([-scaled, 1.0 - latent_part], axis=1).astype(jnp.bfloat16)
    aff_ref[...] = grad_affine
    grad = dot(grad_affine, w_ref[...], ((1,), (1,)))
    for h in range(HEADS):
        held_ref[h] = low(pack(grad[:, h * HEAD_DIM : (h + 1) * HEAD_DIM]))
    for m, out_ref in enumerate(out_refs):
        out_ref[...] = held_ref[me_ref[0] ^ DISTANCES[m]]


ORDERS = (((1, 5, 3, 7), (2, 6), (4,), (0,)), ((2, 6, 3, 7), (1, 5), (4,), (0,)))


def out_term_kernel(*refs):
    slabs, aff_ref, out_refs = refs[:HEADS], refs[HEADS], refs[HEADS + 1 :]
    rows, width = aff_ref.shape[0], aff_ref.shape[1] // 2
    columns = {m: unpack(wide(slab[...]), rows) for m, slab in zip(DISTANCES, slabs)}
    for half, order in enumerate(ORDERS):
        right = aff_ref[:, half * width : (half + 1) * width]
        for out_ref, group in zip(out_refs[4 * half : 4 * half + 4], order):
            left = jnp.concatenate([columns[m] for m in group], axis=1).astype(jnp.bfloat16)
            out_ref[...] = dot(left, right, ((0,), (0,))).astype(jnp.bfloat16)


def backward_kernel(me_ref, *refs):
    slabs, (prob_ref, qk_ref, v_ref, out_t_ref) = refs[:HEADS], refs[HEADS : HEADS + 4]
    early, late = refs[HEADS + 4 : HEADS + 7], refs[HEADS + 7 : HEADS + 10]
    out_refs, (gk_ref, gv_ref, gq_ref, held_ref) = refs[HEADS + 10 : -4], refs[-4:]
    first, rows = early[0].shape[:2]
    grad_f = jnp.concatenate([unpack(wide(slab[...]), rows) for slab in slabs], axis=0)
    grad = grad_f.astype(jnp.bfloat16)
    tokens = grad_f.shape[0]
    grad_t = jnp.transpose(grad_f)
    correction = jnp.sum(grad_t * out_t_ref[...], axis=0, keepdims=True)
    grad_t = grad_t.astype(jnp.bfloat16)
    qk, value = qk_ref[...], v_ref[...]
    query, key = qk[:, :HEAD_DIM], qk[:, HEAD_DIM:]
    gk_ref[...] = jnp.zeros_like(gk_ref)
    gv_ref[...] = jnp.zeros_like(gv_ref)
    for start, stop in tiles(tokens):
        probs = prob_ref[:, start:stop]
        grad_probs = dot(value, grad_t[:, start:stop])
        scores = probs.astype(jnp.float32) * (grad_probs - correction[:, start:stop])
        scores = scores.astype(jnp.bfloat16)
        gv_ref[...] += dot(probs, grad[start:stop])
        gk_ref[...] += dot(scores, query[start:stop])
        gq_ref[:, start:stop] = dot(key, scores, ((0,), (0,)))
    grad_q = jnp.transpose(gq_ref[...])
    qk_sum = v_sum = 0.0
    for m, out_ref in enumerate(out_refs):
        own = slice(m * rows, (m + 1) * rows)
        normed, unit, scale = [
            early[i][m] if m < first else late[i][m - first] for i in range(3)
        ]
        raw = jnp.concatenate([grad_q[own], gk_ref[own, :]], axis=1) * HEAD_DIM ** (-0.5)
        back = scale * (raw - unit * (half_sums(raw * unit) / HEAD_DIM))
        back, grad_v = back.astype(jnp.bfloat16), gv_ref[own, :]
        out_ref[:PACKED, :] = low(pack(grad_v))
        out_ref[PACKED : PACKED + rows, :] = back
        qk_sum = qk_sum + dot(back, normed, ((0,), (0,)))
        v_sum = v_sum + dot(grad_v.astype(jnp.bfloat16), normed, ((0,), (0,)))
    step = qk_sum.shape[1] // HEADS
    for g in range(HEADS):
        own = slice(g * step, (g + 1) * step)
        held_ref[g] = low(jnp.concatenate([qk_sum[:, own], v_sum[:, own]], axis=0))
    for m, out_ref in enumerate(out_refs):
        out_ref[PACKED + rows :, :] = held_ref[me_ref[0] ^ DISTANCES[m]]


def turn_kernel(me_ref, *refs):
    slabs, out_refs, held_ref = refs[:HEADS], refs[HEADS:-1], refs[-1]
    start = slabs[0].shape[0] - 3 * HEAD_DIM
    for m, slab in enumerate(slabs):
        held_ref[me_ref[0] ^ DISTANCES[m]] = slab[start:, :]
    for i, out_ref in enumerate(out_refs):
        own = slice(i * HEAD_DIM, (i + 1) * HEAD_DIM)
        heads = [wide(held_ref[h, own, :]) for h in range(HEADS)]
        out_ref[0] = jnp.transpose(jnp.concatenate(heads, axis=0))


def second_sum_kernel(*refs):
    for second, got, out in zip(refs[0:2], refs[2:4], refs[5:7]):
        start = got.shape[0] - second.shape[0]
        out[...] = low(wide(second[...]) + wide(got[start:, :]))


def third_sum_kernel(*refs):
    for i in range(2):
        third, keep, got, more = [ref[...] for ref in refs[i:8:2]]
        size = third.shape[0]
        leaving, staying = refs[8 + i], refs[10 + i]
        leaving[...] = low(wide(third) + wide(got[size : 2 * size]) + wide(more[size:]))
        staying[...] = wide(keep) + wide(got[:size]) + wide(more[:size])


def last_sum_kernel(keep_a, keep_b, got_a, got_b, out_ref):
    for i, (keep, got) in enumerate(((keep_a, got_a), (keep_b, got_b))):
        width = keep.shape[1]
        out_ref[0, :, i * width : (i + 1) * width] = keep[...] + wide(got[...])


def input_kernel(me_ref, *refs):
    slabs, (wq_ref, wk_ref, wv_ref, act_ref, up_ref, out_ref) = refs[:HEADS], refs[HEADS:-1]
    held_ref = refs[-1]
    rows = act_ref.shape[0]
    for m, slab in enumerate(slabs):
        held_ref[me_ref[0] ^ DISTANCES[m]] = slab[: PACKED + rows, :]
    unit, row_scale = normalize(act_ref[...])
    queries, keys, values = [], [], []
    for pair in range(HEADS // 2):
        even, odd = [wide(held_ref[2 * pair + i]) for i in range(2)]
        lower = low_lanes(even[PACKED:])
        queries.append(jnp.where(lower, even[PACKED:], swap(odd[PACKED:])))
        keys.append(jnp.where(lower, swap(even[PACKED:]), odd[PACKED:]))
        values += [unpack(even[:PACKED], rows), unpack(odd[:PACKED], rows)]
    total = 0.0
    for parts, ref in ((queries, wq_ref), (keys, wk_ref), (values, wv_ref)):
        left = jnp.concatenate(parts, axis=1).astype(jnp.bfloat16)
        total = total + dot(left, ref[...], ((1,), (1,)))
    total = total - unit * jnp.mean(total * unit, axis=-1, keepdims=True)
    out_ref[...] = (up_ref[...] + row_scale * total).astype(jnp.bfloat16)


def reorder_kernel(order_ref, rows_ref, out_ref):
    rows = rows_ref.shape[0]
    chosen = lax.broadcasted_iota(jnp.int32, (rows, rows), 1) == order_ref[...]
    chosen = jnp.where(chosen, 1.0, 0.0).astype(jnp.bfloat16)
    out_ref[0] = dot(chosen, rows_ref[...]).astype(jnp.bfloat16)


def hop(block, distance):
    route = [(i, i ^ distance) for i in range(lax.axis_size("seq"))]
    return lax.ppermute(block, "seq", route)


def exchange(slabs):
    return [hop(slab, m) if m else slab for m, slab in zip(DISTANCES, slabs)]


def spread(block):
    side, near, far = [partner(block, "seq", bit) for bit in range(3)]
    side_far = partner(far, "seq", 0)
    near_far = partner(far, "seq", 1)
    side_near = partner(near, "seq", 0)
    last = partner(side_far, "seq", 1)
    return block, side, near, far, side_near, side_far, near_far, last


DISTANCES = (0, 1, 2, 4, 3, 5, 6, 7)


def wide(matrix):
    return matrix.astype(jnp.float32)


def low(matrix):
    return matrix.astype(jnp.bfloat16)


EARLY = 6


def head_shards(
    activations, incoming, w_query, w_key, w_value, w_out, block_ids, flip_order
):
    parts = lax.axis_size("seq")
    sections = lax.axis_size("section")
    me = lax.axis_index("seq").astype(jnp.int32).reshape(1)
    field, upstream = activations[0], incoming[0]
    wq, wk, wv, wo = w_query[0], w_key[0], w_value[0], w_out[0]
    rows, width = field.shape
    inner = wq.shape[1]
    tokens = parts * rows
    f32 = jnp.float32

    def out(*dims, dtype=jnp.bfloat16):
        return jax.ShapeDtypeStruct(dims, dtype)

    blocks = spread(field)
    order = me[0] ^ jnp.array(DISTANCES, jnp.int32)
    ids = jnp.take(block_ids.reshape(parts, rows), order, axis=0).reshape(tokens)
    (weight,) = call(
        select_kernel,
        1.5,
        [("s", me), ("a", wq), ("a", wk), ("a", wv)],
        [out(width, 3 * HEAD_DIM)],
        [pltpu.VMEM((width, 2 * HEAD_DIM), jnp.bfloat16)] * 3 + [pltpu.SemaphoreType.DMA((3,))],
    )
    pair = 2 * HEAD_DIM
    normed, unit, unit_scale, projected = call(
        project_kernel,
        2,
        [("v", block) for block in blocks[:EARLY]] + [("v", weight)],
        [
            out(EARLY, rows, width),
            out(EARLY, rows, pair, dtype=f32),
            out(EARLY, rows, pair, dtype=f32),
            out(EARLY, rows, HEAD_DIM, dtype=f32),
        ],
    )
    late = parts - EARLY
    made = call(
        attend_kernel,
        5,
        [("v", unit), ("v", projected), *[("v", block) for block in blocks[EARLY:]]]
        + [("v", weight), ("v", ids[None, :]), ("v", ids[:, None])],
        [
            out(late, rows, width),
            out(late, rows, pair, dtype=f32),
            out(late, rows, pair, dtype=f32),
            out(tokens, tokens),
            out(tokens, pair),
            out(tokens, HEAD_DIM),
            out(HEAD_DIM, tokens, dtype=f32),
        ]
        + [out(PACKED, 128)] * parts,
    )
    late_parts, (probs, qk, value, out_t), packed = made[:3], made[3:7], made[7:]
    packed = exchange(packed)
    grad_affine, scaled, *grad_slabs = call(
        affine_kernel,
        2,
        [("s", me)] + [("v", x) for x in (*packed, field, upstream, wo)],
        [out(rows, 2 * width), out(rows, width, dtype=f32)] + [out(PACKED, 128)] * HEADS,
        [pltpu.VMEM((HEADS, PACKED, 128), jnp.bfloat16)],
    )
    grad_slabs = exchange(grad_slabs)
    terms = call(
        out_term_kernel,
        2,
        [("v", x) for x in (*packed, grad_affine)],
        [out(len(group) * HEAD_DIM, width) for order in ORDERS for group in order],
    )
    grad_slabs, terms = lax.optimization_barrier((grad_slabs, terms))
    first, second, third, keep = zip(terms[:4], terms[4:])
    got = [partner(part, "seq", bit) for bit, part in enumerate(first)]
    grads = call(
        backward_kernel,
        6,
        [("s", me)]
        + [("v", x) for x in (*grad_slabs, probs, qk, value, out_t)]
        + [("v", x) for x in (normed, unit, unit_scale, *late_parts)],
        [out(PACKED + rows + 3 * HEAD_DIM, 128)] * parts,
        [
            pltpu.VMEM((tokens, HEAD_DIM), f32),
            pltpu.VMEM((tokens, HEAD_DIM), f32),
            pltpu.VMEM((HEAD_DIM, tokens), f32),
            pltpu.VMEM((HEADS, 3 * HEAD_DIM, 128), jnp.bfloat16),
        ],
    )
    slabs = exchange(grads)
    leaving = call(
        second_sum_kernel,
        1,
        [("v", x) for x in (*second, *got)] + [("a", grads[0])],
        [out(*second[0].shape)] * 2,
    )
    more = [partner(part, "seq", 1 - bit) for bit, part in enumerate(leaving)]
    *leaving, keep_a, keep_b = call(
        third_sum_kernel,
        2,
        [("v", x) for x in (*third, *keep, *got, *more)],
        [out(*third[0].shape)] * 2 + [out(*keep[0].shape, dtype=f32)] * 2,
    )
    rest = [partner(part, "seq", 2) for part in leaving]
    (grad_input,) = call(
        input_kernel,
        1.5,
        [("s", me)] + [("v", x) for x in (*slabs, wq, wk, wv, field, scaled)],
        [out(rows, width)],
        [pltpu.VMEM((HEADS, PACKED + rows, 128), jnp.bfloat16)],
    )
    route = [
        (s * parts + d, (s - 1) * parts + parts - 1 - d)
        for s in range(1, sections)
        for d in range(parts)
    ]
    moved = lax.ppermute(grad_input, ("section", "seq"), route)
    grad_q, grad_k, grad_v = call(
        turn_kernel,
        1,
        [("s", me)] + [("v", x) for x in slabs],
        [out(1, width // parts, inner, dtype=f32)] * 3,
        [pltpu.VMEM((HEADS, 3 * HEAD_DIM, 128), jnp.bfloat16)],
    )
    (grad_out,) = call(
        last_sum_kernel,
        1,
        [("v", x) for x in (keep_a, keep_b, *rest)],
        [out(1, keep_a.shape[0], 2 * width, dtype=f32)],
    )
    (carry,) = call(
        reorder_kernel, 1, [("v", flip_order[0][:, None]), ("v", moved)], [out(1, rows, width)]
    )
    return (carry, grad_q, grad_k, grad_v, grad_out)


def solution(mesh):
    shards = head_shards if mesh.shape["seq"] == HEADS else general_shards
    in_specs = (
        P("section", "seq", None),
        P("section", "seq", None),
        P("section", None, None),
        P("section", None, None),
        P("section", None, None),
        P("section", None, None),
        P(),
        P("section", None),
    )
    out_specs = (
        P("section", "seq", None),
        P("section", "seq", None),
        P("section", "seq", None),
        P("section", "seq", None),
        P("section", "seq", None),
    )
    return jax.shard_map(shards, mesh=mesh, in_specs=in_specs, out_specs=out_specs, check_vma=False)
```

```python
import jax
import jax.numpy as jnp
from jax import lax
from jax.experimental import pallas as pl
from jax.experimental.pallas import tpu as pltpu
from jax.sharding import PartitionSpec as P

HEADS = 8
HEAD_DIM = 64


EPSILON = 1e-06


def partner(block, axis, stride):
    count = lax.axis_size(axis)
    route = []
    for low in range(count):
        high = low | 1 << stride
        if high != low and high < count:
            route += [(low, high), (high, low)]
    return lax.ppermute(block, axis, route)


def shifted(block, axis, distance):
    devices = range(lax.axis_size(axis))
    route = [(i - distance, i) for i in devices if i - distance in devices]
    return lax.ppermute(block, axis, route)


def split_heads(matrix):
    return matrix.reshape(matrix.shape[0], HEADS, HEAD_DIM)


def head_major(matrix):
    return jnp.transpose(split_heads(matrix), (1, 0, 2))


def unit_heads(projected):
    parts = split_heads(projected)
    factor = lax.rsqrt(jnp.mean(parts * parts, axis=-1, keepdims=True) + EPSILON)
    return (parts * factor, factor)


def unit_back(grad_heads, unit, factor):
    return factor * (grad_heads - unit * jnp.mean(grad_heads * unit, axis=-1, keepdims=True))


def mirror(rows):
    for bit in range(lax.axis_size("seq").bit_length() - 1):
        rows = partner(rows, "seq", bit)
    return rows


def to_previous(rows):
    return shifted(rows, "section", -1)


def general_shards(activations, incoming, w_query, w_key, w_value, w_out, block_ids, flip_order):
    field = activations[0].astype(jnp.float32)
    upstream = incoming[0].astype(jnp.float32)
    weight_query = w_query[0]
    weight_key = w_key[0]
    weight_value = w_value[0]
    weight_out = w_out[0]
    flip_row = flip_order[0]
    rows = field.shape[0]
    width = field.shape[1]
    inner = weight_query.shape[1]
    scale = HEAD_DIM ** (-0.5)
    first = lax.axis_index("seq") * rows
    my_blocks = lax.dynamic_slice_in_dim(block_ids, first, rows)
    row_scale = lax.rsqrt(jnp.mean(field * field, axis=-1, keepdims=True) + EPSILON)
    unit_rows = field * row_scale
    normed = unit_rows.astype(jnp.bfloat16)
    query_raw = jnp.dot(normed, weight_query, preferred_element_type=jnp.float32)
    key_raw = jnp.dot(normed, weight_key, preferred_element_type=jnp.float32)
    values = jnp.dot(normed, weight_value, preferred_element_type=jnp.float32).astype(jnp.bfloat16)
    query_unit, query_scale = unit_heads(query_raw)
    key_unit, key_scale = unit_heads(key_raw)
    queries = query_unit.astype(jnp.bfloat16).reshape(rows, inner)
    keys = key_unit.astype(jnp.bfloat16).reshape(rows, inner)
    keys_all, values_all = (
        lax.all_gather(keys, "seq", axis=0, tiled=True),
        lax.all_gather(values, "seq", axis=0, tiled=True),
    )
    allowed = block_ids[None, :] <= my_blocks[:, None]
    query_heads = head_major(queries)
    key_heads_all = head_major(keys_all)
    value_heads_all = head_major(values_all)

    def probabilities(query_part, key_part):
        scores = jnp.dot(query_part, key_part.T, preferred_element_type=jnp.float32) * scale
        numerator = jnp.where(allowed, jnp.exp(scores), 0.0)
        denominator = jnp.sum(numerator, axis=-1, keepdims=True)
        return (numerator / denominator, denominator)

    def forward_head(operands):
        query_part, key_part, value_part = operands
        probs, denominator = probabilities(query_part, key_part)
        out_part = jnp.dot(
            probs.astype(jnp.bfloat16), value_part, preferred_element_type=jnp.float32
        ).astype(jnp.bfloat16)
        return (out_part, denominator[:, 0])

    heads_out, denominators = lax.map(forward_head, (query_heads, key_heads_all, value_heads_all))
    attended = jnp.transpose(heads_out, (1, 0, 2)).reshape(rows, inner)
    affine = jnp.dot(attended, weight_out, preferred_element_type=jnp.float32)
    shift_part = affine[:, :width]
    log_scale = affine[:, width:]
    factor = jnp.exp(-log_scale)
    latent = (field - shift_part) * factor
    grad_affine = jnp.concatenate([-upstream * factor, 1.0 - upstream * latent], axis=-1).astype(
        jnp.bfloat16
    )
    out_term = jnp.dot(attended.T, grad_affine, preferred_element_type=jnp.float32)
    grad_attn = jnp.dot(grad_affine, weight_out.T, preferred_element_type=jnp.float32).astype(
        jnp.bfloat16
    )
    correction = jnp.sum(
        split_heads(grad_attn.astype(jnp.float32)) * split_heads(attended.astype(jnp.float32)),
        axis=-1,
    )
    grad_heads = head_major(grad_attn)
    correction_heads = jnp.transpose(correction)[:, :, None]

    def backward_head(operands):
        query_part, key_part, value_part, grad_part, corr_part = operands
        probs, denominator = probabilities(query_part, key_part)
        grad_probs = jnp.dot(grad_part, value_part.T, preferred_element_type=jnp.float32)
        grad_scores = (probs * (grad_probs - corr_part)).astype(jnp.bfloat16)
        grad_qpart = jnp.dot(grad_scores, key_part, preferred_element_type=jnp.float32) * scale
        grad_kpart = jnp.dot(grad_scores.T, query_part, preferred_element_type=jnp.float32) * scale
        grad_vpart = jnp.dot(
            probs.astype(jnp.bfloat16).T, grad_part, preferred_element_type=jnp.float32
        )
        return (grad_qpart, grad_kpart, grad_vpart)

    grad_qheads, grad_kall, grad_vall = lax.map(
        backward_head, (query_heads, key_heads_all, value_heads_all, grad_heads, correction_heads)
    )
    key_terms = jnp.transpose(grad_kall, (1, 0, 2)).reshape(-1, inner)
    value_terms = jnp.transpose(grad_vall, (1, 0, 2)).reshape(-1, inner)
    grad_kunit, grad_vsum = (
        lax.psum_scatter(
            key_terms.astype(jnp.bfloat16), "seq", scatter_dimension=0, tiled=True
        ).astype(jnp.float32),
        lax.psum_scatter(
            value_terms.astype(jnp.bfloat16), "seq", scatter_dimension=0, tiled=True
        ).astype(jnp.float32),
    )
    grad_queries = (
        unit_back(jnp.transpose(grad_qheads, (1, 0, 2)), query_unit, query_scale)
        .reshape(rows, inner)
        .astype(jnp.bfloat16)
    )
    grad_keys = (
        unit_back(split_heads(grad_kunit), key_unit, key_scale)
        .reshape(rows, inner)
        .astype(jnp.bfloat16)
    )
    grad_values = grad_vsum.astype(jnp.bfloat16)
    query_term = jnp.dot(normed.T, grad_queries, preferred_element_type=jnp.float32)
    key_term = jnp.dot(normed.T, grad_keys, preferred_element_type=jnp.float32)
    value_term = jnp.dot(normed.T, grad_values, preferred_element_type=jnp.float32)
    sums = (
        lax.psum_scatter(
            query_term.astype(jnp.bfloat16), "seq", scatter_dimension=0, tiled=True
        ).astype(jnp.float32),
        lax.psum_scatter(
            key_term.astype(jnp.bfloat16), "seq", scatter_dimension=0, tiled=True
        ).astype(jnp.float32),
        lax.psum_scatter(
            value_term.astype(jnp.bfloat16), "seq", scatter_dimension=0, tiled=True
        ).astype(jnp.float32),
        lax.psum_scatter(
            out_term.astype(jnp.bfloat16), "seq", scatter_dimension=0, tiled=True
        ).astype(jnp.float32),
    )
    grad_normed = jnp.dot(grad_queries, weight_query.T, preferred_element_type=jnp.float32)
    grad_normed = grad_normed + jnp.dot(grad_keys, weight_key.T, preferred_element_type=jnp.float32)
    grad_normed = grad_normed + jnp.dot(
        grad_values, weight_value.T, preferred_element_type=jnp.float32
    )
    grad_input = upstream * factor + row_scale * (
        grad_normed - unit_rows * jnp.mean(grad_normed * unit_rows, axis=-1, keepdims=True)
    )
    grad_input = grad_input.astype(jnp.bfloat16)
    moved = mirror(to_previous(grad_input))
    carry = jnp.take(moved, flip_row, axis=0)
    return (carry[None], sums[0][None], sums[1][None], sums[2][None], sums[3][None])


PACKED = 80


def call(kernel, microseconds, ins, outs, scratch=()):
    spaces = {"s": pltpu.SMEM, "v": pltpu.VMEM, "a": pl.ANY}
    places, operands = zip(*ins)
    return pl.pallas_call(
        kernel,
        out_shape=tuple(outs),
        in_specs=[pl.BlockSpec(memory_space=spaces[place]) for place in places],
        out_specs=(pl.BlockSpec(memory_space=pltpu.VMEM),) * len(outs),
        scratch_shapes=list(scratch),
        compiler_params=pltpu.CompilerParams(vmem_limit_bytes=14 * 2**20),
        cost_estimate=pl.CostEstimate(
            flops=int(microseconds * 1e9), bytes_accessed=1024, transcendentals=0
        ),
    )(*operands)


def dot(left, right, contract=((1,), (0,))):
    return lax.dot_general(left, right, (contract, ((), ())), preferred_element_type=jnp.float32)


def low_lanes(block):
    return lax.broadcasted_iota(jnp.int32, block.shape, len(block.shape) - 1) < HEAD_DIM


def swap(block):
    return pltpu.roll(block, HEAD_DIM, 1)


def half_sums(block):
    low = low_lanes(block)
    first = jnp.sum(jnp.where(low, block, 0.0), axis=-1, keepdims=True)
    second = jnp.sum(jnp.where(low, 0.0, block), axis=-1, keepdims=True)
    return jnp.where(low, first, second)


def pack(block):
    rows = block.shape[0]
    return jnp.concatenate([block[:PACKED], block[rows - PACKED :]], axis=1)


def unpack(slab, rows):
    right = swap(slab)[2 * PACKED - rows :, :HEAD_DIM]
    return jnp.concatenate([slab[:, :HEAD_DIM], right], axis=0)


def normalize(block):
    field = block.astype(jnp.float32)
    row_scale = lax.rsqrt(jnp.mean(field * field, axis=-1, keepdims=True) + EPSILON)
    return field * row_scale, row_scale


def project(block, weight):
    normed = normalize(block)[0].astype(jnp.bfloat16)
    product = dot(normed, weight)
    raw, value = product[:, : 2 * HEAD_DIM], product[:, 2 * HEAD_DIM :]
    scale = lax.rsqrt(half_sums(raw * raw) / HEAD_DIM + EPSILON)
    return normed, raw * scale, scale, value


def select_kernel(me_ref, wq_ref, wk_ref, wv_ref, out_ref, *scratch):
    held, semaphores = scratch[:3], scratch[3]
    odd = lax.rem(me_ref[0], 2) == 1
    pair = pl.multiple_of(lax.div(me_ref[0], 2) * 2 * HEAD_DIM, 2 * HEAD_DIM)
    copies = [
        pltpu.make_async_copy(ref.at[:, pl.ds(pair, 2 * HEAD_DIM)], kept, semaphores.at[i])
        for i, (ref, kept) in enumerate(zip((wq_ref, wk_ref, wv_ref), held))
    ]
    for copy in copies:
        copy.start()
    for copy in copies:
        copy.wait()
    q, k, v = [wide(kept[...]) for kept in held]
    lower = low_lanes(q)
    qk = jnp.where(lower, jnp.where(odd, swap(q), q), jnp.where(odd, k, swap(k)))
    out_ref[:, : 2 * HEAD_DIM] = low(qk)
    out_ref[:, 2 * HEAD_DIM :] = low(jnp.where(odd, swap(v), v)[:, :HEAD_DIM])


def project_kernel(*refs):
    blocks, (weight_ref, normed_ref, unit_ref, scale_ref, value_ref) = refs[:-5], refs[-5:]
    for m, block in enumerate(blocks):
        made = project(block[...], weight_ref[...])
        for ref, part in zip((normed_ref, unit_ref, scale_ref, value_ref), made):
            ref[m] = part.astype(ref.dtype)


TILE = 256


def tiles(tokens):
    starts = range(0, tokens, TILE)
    return [(start, min(tokens, start + TILE)) for start in starts]


def attend_kernel(
    unit_ref, value_ref, near_ref, last_ref, weight_ref, row_ids, column_ids, *out_refs
):
    normed_ref, late_unit, late_scale, prob_ref, qk_ref, v_ref, out_t_ref = out_refs[:7]
    early, rows = unit_ref.shape[:2]
    units = [unit_ref[m] for m in range(early)]
    values = [value_ref[m] for m in range(early)]
    for m, ref in enumerate((near_ref, last_ref)):
        normed, unit, scale, value = project(ref[...], weight_ref[...])
        normed_ref[m], late_unit[m], late_scale[m] = normed, unit, scale
        units.append(unit)
        values.append(value)
    parts = len(units)
    tokens = parts * rows
    qk = jnp.concatenate(units, axis=0).astype(jnp.bfloat16)
    value = jnp.concatenate(values, axis=0).astype(jnp.bfloat16)
    qk_ref[...] = qk
    v_ref[...] = value
    query, key = qk[:, :HEAD_DIM] * HEAD_DIM ** (-0.5), qk[:, HEAD_DIM:]
    for start, stop in tiles(tokens):
        scores = dot(key, query[start:stop], ((1,), (1,)))
        allowed = column_ids[...] <= row_ids[:, start:stop]
        numerator = jnp.where(allowed, jnp.exp(scores), 0.0)
        probs = numerator * (1.0 / jnp.sum(numerator, axis=0, keepdims=True))
        probs = probs.astype(jnp.bfloat16)
        prob_ref[:, start:stop] = probs
        out_t = dot(value, probs, ((0,), (0,)))
        out_t_ref[:, start:stop] = out_t.astype(jnp.bfloat16).astype(jnp.float32)
    out = jnp.transpose(out_t_ref[...])
    for m, out_ref in enumerate(out_refs[7:]):
        out_ref[...] = low(pack(out[m * rows : (m + 1) * rows]))


def affine_kernel(me_ref, *refs):
    slabs, (act_ref, inc_ref, w_ref, aff_ref, up_ref) = refs[:HEADS], refs[HEADS : HEADS + 5]
    out_refs, held_ref = refs[HEADS + 5 : -1], refs[-1]
    rows, width = act_ref.shape
    for m, slab in enumerate(slabs):
        held_ref[me_ref[0] ^ DISTANCES[m]] = slab[...]
    attended = jnp.concatenate([unpack(wide(held_ref[h]), rows) for h in range(HEADS)], axis=1)
    attended = low(attended)
    factor = jnp.exp(-dot(attended, w_ref[:, width:]))
    scaled = inc_ref[...].astype(jnp.float32) * factor
    up_ref[...] = scaled
    shift_part = dot(attended, w_ref[:, :width])
    latent_part = scaled * (act_ref[...].astype(jnp.float32) - shift_part)
    grad_affine = jnp.concatenate([-scaled, 1.0 - latent_part], axis=1).astype(jnp.bfloat16)
    aff_ref[...] = grad_affine
    grad = dot(grad_affine, w_ref[...], ((1,), (1,)))
    for h in range(HEADS):
        held_ref[h] = low(pack(grad[:, h * HEAD_DIM : (h + 1) * HEAD_DIM]))
    for m, out_ref in enumerate(out_refs):
        out_ref[...] = held_ref[me_ref[0] ^ DISTANCES[m]]


ORDERS = (((1, 5, 3, 7), (2, 6), (4,), (0,)), ((2, 6, 3, 7), (1, 5), (4,), (0,)))


def out_term_kernel(*refs):
    slabs, aff_ref, out_refs = refs[:HEADS], refs[HEADS], refs[HEADS + 1 :]
    rows, width = aff_ref.shape[0], aff_ref.shape[1] // 2
    columns = {m: unpack(wide(slab[...]), rows) for m, slab in zip(DISTANCES, slabs)}
    for half, order in enumerate(ORDERS):
        right = aff_ref[:, half * width : (half + 1) * width]
        for out_ref, group in zip(out_refs[4 * half : 4 * half + 4], order):
            left = jnp.concatenate([columns[m] for m in group], axis=1).astype(jnp.bfloat16)
            out_ref[...] = dot(left, right, ((0,), (0,))).astype(jnp.bfloat16)


def backward_kernel(me_ref, *refs):
    slabs, (prob_ref, qk_ref, v_ref, out_t_ref) = refs[:HEADS], refs[HEADS : HEADS + 4]
    early, late = refs[HEADS + 4 : HEADS + 7], refs[HEADS + 7 : HEADS + 10]
    out_refs, (gk_ref, gv_ref, gq_ref, held_ref) = refs[HEADS + 10 : -4], refs[-4:]
    first, rows = early[0].shape[:2]
    grad_f = jnp.concatenate([unpack(wide(slab[...]), rows) for slab in slabs], axis=0)
    grad = grad_f.astype(jnp.bfloat16)
    tokens = grad_f.shape[0]
    grad_t = jnp.transpose(grad_f)
    correction = jnp.sum(grad_t * out_t_ref[...], axis=0, keepdims=True)
    grad_t = grad_t.astype(jnp.bfloat16)
    qk, value = qk_ref[...], v_ref[...]
    query, key = qk[:, :HEAD_DIM], qk[:, HEAD_DIM:]
    gk_ref[...] = jnp.zeros_like(gk_ref)
    gv_ref[...] = jnp.zeros_like(gv_ref)
    for start, stop in tiles(tokens):
        probs = prob_ref[:, start:stop]
        grad_probs = dot(value, grad_t[:, start:stop])
        scores = probs.astype(jnp.float32) * (grad_probs - correction[:, start:stop])
        scores = scores.astype(jnp.bfloat16)
        gv_ref[...] += dot(probs, grad[start:stop])
        gk_ref[...] += dot(scores, query[start:stop])
        gq_ref[:, start:stop] = dot(key, scores, ((0,), (0,)))
    grad_q = jnp.transpose(gq_ref[...])
    qk_sum = v_sum = 0.0
    for m, out_ref in enumerate(out_refs):
        own = slice(m * rows, (m + 1) * rows)
        normed, unit, scale = [
            early[i][m] if m < first else late[i][m - first] for i in range(3)
        ]
        raw = jnp.concatenate([grad_q[own], gk_ref[own, :]], axis=1) * HEAD_DIM ** (-0.5)
        back = scale * (raw - unit * (half_sums(raw * unit) / HEAD_DIM))
        back, grad_v = back.astype(jnp.bfloat16), gv_ref[own, :]
        out_ref[:PACKED, :] = low(pack(grad_v))
        out_ref[PACKED : PACKED + rows, :] = back
        qk_sum = qk_sum + dot(back, normed, ((0,), (0,)))
        v_sum = v_sum + dot(grad_v.astype(jnp.bfloat16), normed, ((0,), (0,)))
    step = qk_sum.shape[1] // HEADS
    for g in range(HEADS):
        own = slice(g * step, (g + 1) * step)
        held_ref[g] = low(jnp.concatenate([qk_sum[:, own], v_sum[:, own]], axis=0))
    for m, out_ref in enumerate(out_refs):
        out_ref[PACKED + rows :, :] = held_ref[me_ref[0] ^ DISTANCES[m]]


def turn_kernel(me_ref, *refs):
    slabs, out_refs, held_ref = refs[:HEADS], refs[HEADS:-1], refs[-1]
    start = slabs[0].shape[0] - 3 * HEAD_DIM
    for m, slab in enumerate(slabs):
        held_ref[me_ref[0] ^ DISTANCES[m]] = slab[start:, :]
    for i, out_ref in enumerate(out_refs):
        own = slice(i * HEAD_DIM, (i + 1) * HEAD_DIM)
        heads = [wide(held_ref[h, own, :]) for h in range(HEADS)]
        out_ref[0] = jnp.transpose(jnp.concatenate(heads, axis=0))


def second_sum_kernel(*refs):
    for second, got, out in zip(refs[0:2], refs[2:4], refs[5:7]):
        start = got.shape[0] - second.shape[0]
        out[...] = low(wide(second[...]) + wide(got[start:, :]))


def third_sum_kernel(*refs):
    for i in range(2):
        third, keep, got, more = [ref[...] for ref in refs[i:8:2]]
        size = third.shape[0]
        leaving, staying = refs[8 + i], refs[10 + i]
        leaving[...] = low(wide(third) + wide(got[size : 2 * size]) + wide(more[size:]))
        staying[...] = wide(keep) + wide(got[:size]) + wide(more[:size])


def last_sum_kernel(keep_a, keep_b, got_a, got_b, out_ref):
    for i, (keep, got) in enumerate(((keep_a, got_a), (keep_b, got_b))):
        width = keep.shape[1]
        out_ref[0, :, i * width : (i + 1) * width] = keep[...] + wide(got[...])


def input_kernel(me_ref, *refs):
    slabs, (wq_ref, wk_ref, wv_ref, act_ref, up_ref, _, out_ref) = refs[:HEADS], refs[HEADS:-1]
    held_ref = refs[-1]
    rows = act_ref.shape[0]
    for m, slab in enumerate(slabs):
        held_ref[me_ref[0] ^ DISTANCES[m]] = slab[: PACKED + rows, :]
    unit, row_scale = normalize(act_ref[...])
    queries, keys, values = [], [], []
    for pair in range(HEADS // 2):
        even, odd = [wide(held_ref[2 * pair + i]) for i in range(2)]
        lower = low_lanes(even[PACKED:])
        queries.append(jnp.where(lower, even[PACKED:], swap(odd[PACKED:])))
        keys.append(jnp.where(lower, swap(even[PACKED:]), odd[PACKED:]))
        values += [unpack(even[:PACKED], rows), unpack(odd[:PACKED], rows)]
    total = 0.0
    for parts, ref in ((queries, wq_ref), (keys, wk_ref), (values, wv_ref)):
        left = jnp.concatenate(parts, axis=1).astype(jnp.bfloat16)
        total = total + dot(left, ref[...], ((1,), (1,)))
    total = total - unit * jnp.mean(total * unit, axis=-1, keepdims=True)
    out_ref[...] = (up_ref[...] + row_scale * total).astype(jnp.bfloat16)


def reorder_kernel(order_ref, rows_ref, out_ref):
    rows = rows_ref.shape[0]
    chosen = lax.broadcasted_iota(jnp.int32, (rows, rows), 0) == order_ref[...]
    chosen = low(jnp.where(chosen, 1.0, 0.0))
    out_ref[0] = low(dot(chosen, rows_ref[...], ((0,), (0,))))


def hop(block, distance):
    route = [(i, i ^ distance) for i in range(lax.axis_size("seq"))]
    return lax.ppermute(block, "seq", route)


def exchange(slabs):
    return [hop(slab, m) if m else slab for m, slab in zip(DISTANCES, slabs)]


def spread(block):
    side, near, far = [partner(block, "seq", bit) for bit in range(3)]
    side_far = partner(far, "seq", 0)
    near_far = partner(far, "seq", 1)
    side_near = partner(near, "seq", 0)
    last = partner(side_far, "seq", 1)
    return block, side, near, far, side_near, side_far, near_far, last


DISTANCES = (0, 1, 2, 4, 3, 5, 6, 7)


def wide(matrix):
    return matrix.astype(jnp.float32)


def low(matrix):
    return matrix.astype(jnp.bfloat16)


EARLY = 6


def head_shards(
    activations, incoming, w_query, w_key, w_value, w_out, block_ids, flip_order
):
    parts = lax.axis_size("seq")
    sections = lax.axis_size("section")
    me = lax.axis_index("seq").astype(jnp.int32).reshape(1)
    field, upstream = activations[0], incoming[0]
    wq, wk, wv, wo = w_query[0], w_key[0], w_value[0], w_out[0]
    rows, width = field.shape
    inner = wq.shape[1]
    tokens = parts * rows
    f32 = jnp.float32

    def out(*dims, dtype=jnp.bfloat16):
        return jax.ShapeDtypeStruct(dims, dtype)

    blocks = spread(field)
    order = me[0] ^ jnp.array(DISTANCES, jnp.int32)
    ids = jnp.take(block_ids.reshape(parts, rows), order, axis=0).reshape(tokens)
    (weight,) = call(
        select_kernel,
        1.5,
        [("s", me), ("a", wq), ("a", wk), ("a", wv)],
        [out(width, 3 * HEAD_DIM)],
        [pltpu.VMEM((width, 2 * HEAD_DIM), jnp.bfloat16)] * 3 + [pltpu.SemaphoreType.DMA((3,))],
    )
    pair = 2 * HEAD_DIM
    normed, unit, unit_scale, projected = call(
        project_kernel,
        2,
        [("v", block) for block in blocks[:EARLY]] + [("v", weight)],
        [
            out(EARLY, rows, width),
            out(EARLY, rows, pair, dtype=f32),
            out(EARLY, rows, pair, dtype=f32),
            out(EARLY, rows, HEAD_DIM, dtype=f32),
        ],
    )
    late = parts - EARLY
    made = call(
        attend_kernel,
        5,
        [("v", unit), ("v", projected), *[("v", block) for block in blocks[EARLY:]]]
        + [("v", weight), ("v", ids[None, :]), ("v", ids[:, None])],
        [
            out(late, rows, width),
            out(late, rows, pair, dtype=f32),
            out(late, rows, pair, dtype=f32),
            out(tokens, tokens),
            out(tokens, pair),
            out(tokens, HEAD_DIM),
            out(HEAD_DIM, tokens, dtype=f32),
        ]
        + [out(PACKED, 128)] * parts,
    )
    late_parts, (probs, qk, value, out_t), packed = made[:3], made[3:7], made[7:]
    packed = exchange(packed)
    grad_affine, scaled, *grad_slabs = call(
        affine_kernel,
        2,
        [("s", me)] + [("v", x) for x in (*packed, field, upstream, wo)],
        [out(rows, 2 * width), out(rows, width, dtype=f32)] + [out(PACKED, 128)] * HEADS,
        [pltpu.VMEM((HEADS, PACKED, 128), jnp.bfloat16)],
    )
    grad_slabs = exchange(grad_slabs)
    terms = call(
        out_term_kernel,
        2,
        [("v", x) for x in (*packed, grad_affine)],
        [out(len(group) * HEAD_DIM, width) for order in ORDERS for group in order],
    )
    grad_slabs, terms = lax.optimization_barrier((grad_slabs, terms))
    first, second, third, keep = zip(terms[:4], terms[4:])
    got = [partner(part, "seq", bit) for bit, part in enumerate(first)]
    grads = call(
        backward_kernel,
        6,
        [("s", me)]
        + [("v", x) for x in (*grad_slabs, probs, qk, value, out_t)]
        + [("v", x) for x in (normed, unit, unit_scale, *late_parts)],
        [out(PACKED + rows + 3 * HEAD_DIM, 128)] * parts,
        [
            pltpu.VMEM((tokens, HEAD_DIM), f32),
            pltpu.VMEM((tokens, HEAD_DIM), f32),
            pltpu.VMEM((HEAD_DIM, tokens), f32),
            pltpu.VMEM((HEADS, 3 * HEAD_DIM, 128), jnp.bfloat16),
        ],
    )
    slabs = exchange(grads)
    leaving = call(
        second_sum_kernel,
        1,
        [("v", x) for x in (*second, *got)] + [("a", grads[0])],
        [out(*second[0].shape)] * 2,
    )
    more = [partner(part, "seq", 1 - bit) for bit, part in enumerate(leaving)]
    *leaving, keep_a, keep_b = call(
        third_sum_kernel,
        2,
        [("v", x) for x in (*third, *keep, *got, *more)],
        [out(*third[0].shape)] * 2 + [out(*keep[0].shape, dtype=f32)] * 2,
    )
    rest = [partner(part, "seq", 2) for part in leaving]
    (grad_input,) = call(
        input_kernel,
        1.5,
        [("s", me)] + [("v", x) for x in (*slabs, wq, wk, wv, field, scaled)] + [("a", leaving[0])],
        [out(rows, width)],
        [pltpu.VMEM((HEADS, PACKED + rows, 128), jnp.bfloat16)],
    )
    route = [
        (s * parts + d, (s - 1) * parts + parts - 1 - d)
        for s in range(1, sections)
        for d in range(parts)
    ]
    moved = lax.ppermute(grad_input, ("section", "seq"), route)
    grad_q, grad_k, grad_v = call(
        turn_kernel,
        1,
        [("s", me)] + [("v", x) for x in slabs],
        [out(1, width // parts, inner, dtype=f32)] * 3,
        [pltpu.VMEM((HEADS, 3 * HEAD_DIM, 128), jnp.bfloat16)],
    )
    (grad_out,) = call(
        last_sum_kernel,
        1,
        [("v", x) for x in (keep_a, keep_b, *rest)],
        [out(1, keep_a.shape[0], 2 * width, dtype=f32)],
    )
    (carry,) = call(
        reorder_kernel, 1, [("v", flip_order), ("v", moved)], [out(1, rows, width)]
    )
    return (carry, grad_q, grad_k, grad_v, grad_out)


def solution(mesh):
    shards = head_shards if mesh.shape["seq"] == HEADS else general_shards
    in_specs = (
        P("section", "seq", None),
        P("section", "seq", None),
        P("section", None, None),
        P("section", None, None),
        P("section", None, None),
        P("section", None, None),
        P(),
        P("section", None),
    )
    out_specs = (
        P("section", "seq", None),
        P("section", "seq", None),
        P("section", "seq", None),
        P("section", "seq", None),
        P("section", "seq", None),
    )
    return jax.shard_map(shards, mesh=mesh, in_specs=in_specs, out_specs=out_specs, check_vma=False)
```

```python
import jax
import jax.numpy as jnp
from jax import lax
from jax.experimental import pallas as pl
from jax.experimental.pallas import tpu as pltpu
from jax.sharding import PartitionSpec as P

HEADS = 8
HEAD_DIM = 64


EPSILON = 1e-06


def partner(block, axis, stride):
    count = lax.axis_size(axis)
    route = []
    for low in range(count):
        high = low | 1 << stride
        if high != low and high < count:
            route += [(low, high), (high, low)]
    return lax.ppermute(block, axis, route)


def shifted(block, axis, distance):
    devices = range(lax.axis_size(axis))
    route = [(i - distance, i) for i in devices if i - distance in devices]
    return lax.ppermute(block, axis, route)


def split_heads(matrix):
    return matrix.reshape(matrix.shape[0], HEADS, HEAD_DIM)


def head_major(matrix):
    return jnp.transpose(split_heads(matrix), (1, 0, 2))


def unit_heads(projected):
    parts = split_heads(projected)
    factor = lax.rsqrt(jnp.mean(parts * parts, axis=-1, keepdims=True) + EPSILON)
    return (parts * factor, factor)


def unit_back(grad_heads, unit, factor):
    return factor * (grad_heads - unit * jnp.mean(grad_heads * unit, axis=-1, keepdims=True))


def mirror(rows):
    for bit in range(lax.axis_size("seq").bit_length() - 1):
        rows = partner(rows, "seq", bit)
    return rows


def to_previous(rows):
    return shifted(rows, "section", -1)


def general_shards(activations, incoming, w_query, w_key, w_value, w_out, block_ids, flip_order):
    field = activations[0].astype(jnp.float32)
    upstream = incoming[0].astype(jnp.float32)
    weight_query = w_query[0]
    weight_key = w_key[0]
    weight_value = w_value[0]
    weight_out = w_out[0]
    flip_row = flip_order[0]
    rows = field.shape[0]
    width = field.shape[1]
    inner = weight_query.shape[1]
    scale = HEAD_DIM ** (-0.5)
    first = lax.axis_index("seq") * rows
    my_blocks = lax.dynamic_slice_in_dim(block_ids, first, rows)
    row_scale = lax.rsqrt(jnp.mean(field * field, axis=-1, keepdims=True) + EPSILON)
    unit_rows = field * row_scale
    normed = unit_rows.astype(jnp.bfloat16)
    query_raw = jnp.dot(normed, weight_query, preferred_element_type=jnp.float32)
    key_raw = jnp.dot(normed, weight_key, preferred_element_type=jnp.float32)
    values = jnp.dot(normed, weight_value, preferred_element_type=jnp.float32).astype(jnp.bfloat16)
    query_unit, query_scale = unit_heads(query_raw)
    key_unit, key_scale = unit_heads(key_raw)
    queries = query_unit.astype(jnp.bfloat16).reshape(rows, inner)
    keys = key_unit.astype(jnp.bfloat16).reshape(rows, inner)
    keys_all, values_all = (
        lax.all_gather(keys, "seq", axis=0, tiled=True),
        lax.all_gather(values, "seq", axis=0, tiled=True),
    )
    allowed = block_ids[None, :] <= my_blocks[:, None]
    query_heads = head_major(queries)
    key_heads_all = head_major(keys_all)
    value_heads_all = head_major(values_all)

    def probabilities(query_part, key_part):
        scores = jnp.dot(query_part, key_part.T, preferred_element_type=jnp.float32) * scale
        numerator = jnp.where(allowed, jnp.exp(scores), 0.0)
        denominator = jnp.sum(numerator, axis=-1, keepdims=True)
        return (numerator / denominator, denominator)

    def forward_head(operands):
        query_part, key_part, value_part = operands
        probs, denominator = probabilities(query_part, key_part)
        out_part = jnp.dot(
            probs.astype(jnp.bfloat16), value_part, preferred_element_type=jnp.float32
        ).astype(jnp.bfloat16)
        return (out_part, denominator[:, 0])

    heads_out, denominators = lax.map(forward_head, (query_heads, key_heads_all, value_heads_all))
    attended = jnp.transpose(heads_out, (1, 0, 2)).reshape(rows, inner)
    affine = jnp.dot(attended, weight_out, preferred_element_type=jnp.float32)
    shift_part = affine[:, :width]
    log_scale = affine[:, width:]
    factor = jnp.exp(-log_scale)
    latent = (field - shift_part) * factor
    grad_affine = jnp.concatenate([-upstream * factor, 1.0 - upstream * latent], axis=-1).astype(
        jnp.bfloat16
    )
    out_term = jnp.dot(attended.T, grad_affine, preferred_element_type=jnp.float32)
    grad_attn = jnp.dot(grad_affine, weight_out.T, preferred_element_type=jnp.float32).astype(
        jnp.bfloat16
    )
    correction = jnp.sum(
        split_heads(grad_attn.astype(jnp.float32)) * split_heads(attended.astype(jnp.float32)),
        axis=-1,
    )
    grad_heads = head_major(grad_attn)
    correction_heads = jnp.transpose(correction)[:, :, None]

    def backward_head(operands):
        query_part, key_part, value_part, grad_part, corr_part = operands
        probs, denominator = probabilities(query_part, key_part)
        grad_probs = jnp.dot(grad_part, value_part.T, preferred_element_type=jnp.float32)
        grad_scores = (probs * (grad_probs - corr_part)).astype(jnp.bfloat16)
        grad_qpart = jnp.dot(grad_scores, key_part, preferred_element_type=jnp.float32) * scale
        grad_kpart = jnp.dot(grad_scores.T, query_part, preferred_element_type=jnp.float32) * scale
        grad_vpart = jnp.dot(
            probs.astype(jnp.bfloat16).T, grad_part, preferred_element_type=jnp.float32
        )
        return (grad_qpart, grad_kpart, grad_vpart)

    grad_qheads, grad_kall, grad_vall = lax.map(
        backward_head, (query_heads, key_heads_all, value_heads_all, grad_heads, correction_heads)
    )
    key_terms = jnp.transpose(grad_kall, (1, 0, 2)).reshape(-1, inner)
    value_terms = jnp.transpose(grad_vall, (1, 0, 2)).reshape(-1, inner)
    grad_kunit, grad_vsum = (
        lax.psum_scatter(
            key_terms.astype(jnp.bfloat16), "seq", scatter_dimension=0, tiled=True
        ).astype(jnp.float32),
        lax.psum_scatter(
            value_terms.astype(jnp.bfloat16), "seq", scatter_dimension=0, tiled=True
        ).astype(jnp.float32),
    )
    grad_queries = (
        unit_back(jnp.transpose(grad_qheads, (1, 0, 2)), query_unit, query_scale)
        .reshape(rows, inner)
        .astype(jnp.bfloat16)
    )
    grad_keys = (
        unit_back(split_heads(grad_kunit), key_unit, key_scale)
        .reshape(rows, inner)
        .astype(jnp.bfloat16)
    )
    grad_values = grad_vsum.astype(jnp.bfloat16)
    query_term = jnp.dot(normed.T, grad_queries, preferred_element_type=jnp.float32)
    key_term = jnp.dot(normed.T, grad_keys, preferred_element_type=jnp.float32)
    value_term = jnp.dot(normed.T, grad_values, preferred_element_type=jnp.float32)
    sums = (
        lax.psum_scatter(
            query_term.astype(jnp.bfloat16), "seq", scatter_dimension=0, tiled=True
        ).astype(jnp.float32),
        lax.psum_scatter(
            key_term.astype(jnp.bfloat16), "seq", scatter_dimension=0, tiled=True
        ).astype(jnp.float32),
        lax.psum_scatter(
            value_term.astype(jnp.bfloat16), "seq", scatter_dimension=0, tiled=True
        ).astype(jnp.float32),
        lax.psum_scatter(
            out_term.astype(jnp.bfloat16), "seq", scatter_dimension=0, tiled=True
        ).astype(jnp.float32),
    )
    grad_normed = jnp.dot(grad_queries, weight_query.T, preferred_element_type=jnp.float32)
    grad_normed = grad_normed + jnp.dot(grad_keys, weight_key.T, preferred_element_type=jnp.float32)
    grad_normed = grad_normed + jnp.dot(
        grad_values, weight_value.T, preferred_element_type=jnp.float32
    )
    grad_input = upstream * factor + row_scale * (
        grad_normed - unit_rows * jnp.mean(grad_normed * unit_rows, axis=-1, keepdims=True)
    )
    grad_input = grad_input.astype(jnp.bfloat16)
    moved = mirror(to_previous(grad_input))
    carry = jnp.take(moved, flip_row, axis=0)
    return (carry[None], sums[0][None], sums[1][None], sums[2][None], sums[3][None])


PACKED = 80


def call(kernel, microseconds, ins, outs, scratch=()):
    spaces = {"s": pltpu.SMEM, "v": pltpu.VMEM, "a": pl.ANY}
    places, operands = zip(*ins)
    return pl.pallas_call(
        kernel,
        out_shape=tuple(outs),
        in_specs=[pl.BlockSpec(memory_space=spaces[place]) for place in places],
        out_specs=(pl.BlockSpec(memory_space=pltpu.VMEM),) * len(outs),
        scratch_shapes=list(scratch),
        compiler_params=pltpu.CompilerParams(vmem_limit_bytes=14 * 2**20),
        cost_estimate=pl.CostEstimate(
            flops=int(microseconds * 1e9), bytes_accessed=1024, transcendentals=0
        ),
    )(*operands)


def dot(left, right, contract=((1,), (0,))):
    return lax.dot_general(left, right, (contract, ((), ())), preferred_element_type=jnp.float32)


def low_lanes(block):
    return lax.broadcasted_iota(jnp.int32, block.shape, len(block.shape) - 1) < HEAD_DIM


def swap(block):
    return pltpu.roll(block, HEAD_DIM, 1)


def half_sums(block):
    low = low_lanes(block)
    first = jnp.sum(jnp.where(low, block, 0.0), axis=-1, keepdims=True)
    second = jnp.sum(jnp.where(low, 0.0, block), axis=-1, keepdims=True)
    return jnp.where(low, first, second)


def pack(block):
    rows = block.shape[0]
    return jnp.concatenate([block[:PACKED], block[rows - PACKED :]], axis=1)


def unpack(slab, rows):
    right = swap(slab)[2 * PACKED - rows :, :HEAD_DIM]
    return jnp.concatenate([slab[:, :HEAD_DIM], right], axis=0)


def normalize(block):
    field = block.astype(jnp.float32)
    row_scale = lax.rsqrt(jnp.mean(field * field, axis=-1, keepdims=True) + EPSILON)
    return field * row_scale, row_scale


def project(block, weight):
    normed = normalize(block)[0].astype(jnp.bfloat16)
    product = dot(normed, weight)
    raw, value = product[:, : 2 * HEAD_DIM], product[:, 2 * HEAD_DIM :]
    scale = lax.rsqrt(half_sums(raw * raw) / HEAD_DIM + EPSILON)
    return normed, raw * scale, scale, value


def select_kernel(me_ref, wq_ref, wk_ref, wv_ref, out_ref, *scratch):
    held, semaphores = scratch[:3], scratch[3]
    odd = lax.rem(me_ref[0], 2) == 1
    pair = pl.multiple_of(lax.div(me_ref[0], 2) * 2 * HEAD_DIM, 2 * HEAD_DIM)
    copies = [
        pltpu.make_async_copy(ref.at[:, pl.ds(pair, 2 * HEAD_DIM)], kept, semaphores.at[i])
        for i, (ref, kept) in enumerate(zip((wq_ref, wk_ref, wv_ref), held))
    ]
    for copy in copies:
        copy.start()
    for copy in copies:
        copy.wait()
    q, k, v = [wide(kept[...]) for kept in held]
    lower = low_lanes(q)
    qk = jnp.where(lower, jnp.where(odd, swap(q), q), jnp.where(odd, k, swap(k)))
    out_ref[:, : 2 * HEAD_DIM] = low(qk)
    out_ref[:, 2 * HEAD_DIM :] = low(jnp.where(odd, swap(v), v)[:, :HEAD_DIM])


def project_kernel(*refs):
    blocks, (weight_ref, normed_ref, unit_ref, scale_ref, value_ref) = refs[:-5], refs[-5:]
    for m, block in enumerate(blocks):
        made = project(block[...], weight_ref[...])
        for ref, part in zip((normed_ref, unit_ref, scale_ref, value_ref), made):
            ref[m] = part.astype(ref.dtype)


TILE = 256


def tiles(tokens):
    starts = range(0, tokens, TILE)
    return [(start, min(tokens, start + TILE)) for start in starts]


def attend_kernel(
    unit_ref, value_ref, near_ref, last_ref, weight_ref, row_ids, column_ids, *out_refs
):
    normed_ref, late_unit, late_scale, prob_ref, qk_ref, v_ref, out_t_ref = out_refs[:7]
    early, rows = unit_ref.shape[:2]
    units = [unit_ref[m] for m in range(early)]
    values = [value_ref[m] for m in range(early)]
    for m, ref in enumerate((near_ref, last_ref)):
        normed, unit, scale, value = project(ref[...], weight_ref[...])
        normed_ref[m], late_unit[m], late_scale[m] = normed, unit, scale
        units.append(unit)
        values.append(value)
    parts = len(units)
    tokens = parts * rows
    qk = jnp.concatenate(units, axis=0).astype(jnp.bfloat16)
    value = jnp.concatenate(values, axis=0).astype(jnp.bfloat16)
    qk_ref[...] = qk
    v_ref[...] = value
    query, key = qk[:, :HEAD_DIM] * HEAD_DIM ** (-0.5), qk[:, HEAD_DIM:]
    for start, stop in tiles(tokens):
        scores = dot(key, query[start:stop], ((1,), (1,)))
        allowed = column_ids[...] <= row_ids[:, start:stop]
        numerator = jnp.where(allowed, jnp.exp(scores), 0.0)
        probs = numerator * (1.0 / jnp.sum(numerator, axis=0, keepdims=True))
        probs = probs.astype(jnp.bfloat16)
        prob_ref[:, start:stop] = probs
        out_t = dot(value, probs, ((0,), (0,)))
        out_t_ref[:, start:stop] = out_t.astype(jnp.bfloat16).astype(jnp.float32)
    out = jnp.transpose(out_t_ref[...])
    for m, out_ref in enumerate(out_refs[7:]):
        out_ref[...] = low(pack(out[m * rows : (m + 1) * rows]))


def affine_kernel(me_ref, *refs):
    slabs, (act_ref, inc_ref, w_ref, aff_ref, up_ref) = refs[:HEADS], refs[HEADS : HEADS + 5]
    out_refs, held_ref = refs[HEADS + 5 : -1], refs[-1]
    rows, width = act_ref.shape
    for m, slab in enumerate(slabs):
        held_ref[me_ref[0] ^ DISTANCES[m]] = slab[...]
    attended = jnp.concatenate([unpack(wide(held_ref[h]), rows) for h in range(HEADS)], axis=1)
    attended = low(attended)
    factor = jnp.exp(-dot(attended, w_ref[:, width:]))
    scaled = inc_ref[...].astype(jnp.float32) * factor
    up_ref[...] = low(scaled)
    shift_part = dot(attended, w_ref[:, :width])
    latent_part = scaled * (act_ref[...].astype(jnp.float32) - shift_part)
    grad_affine = jnp.concatenate([-scaled, 1.0 - latent_part], axis=1).astype(jnp.bfloat16)
    aff_ref[...] = grad_affine
    grad = dot(grad_affine, w_ref[...], ((1,), (1,)))
    for h in range(HEADS):
        held_ref[h] = low(pack(grad[:, h * HEAD_DIM : (h + 1) * HEAD_DIM]))
    for m, out_ref in enumerate(out_refs):
        out_ref[...] = held_ref[me_ref[0] ^ DISTANCES[m]]


ORDERS = (((1, 5, 3, 7), (2, 6), (4,), (0,)), ((2, 6, 3, 7), (1, 5), (4,), (0,)))


def out_term_kernel(*refs):
    slabs, aff_ref, out_refs = refs[:HEADS], refs[HEADS], refs[HEADS + 1 :]
    rows, width = aff_ref.shape[0], aff_ref.shape[1] // 2
    columns = {m: unpack(wide(slab[...]), rows) for m, slab in zip(DISTANCES, slabs)}
    for half, order in enumerate(ORDERS):
        right = aff_ref[:, half * width : (half + 1) * width]
        for out_ref, group in zip(out_refs[4 * half : 4 * half + 4], order):
            left = jnp.concatenate([columns[m] for m in group], axis=1).astype(jnp.bfloat16)
            out_ref[...] = dot(left, right, ((0,), (0,))).astype(jnp.bfloat16)


def backward_kernel(me_ref, *refs):
    slabs, (prob_ref, qk_ref, v_ref, out_t_ref) = refs[:HEADS], refs[HEADS : HEADS + 4]
    early, late = refs[HEADS + 4 : HEADS + 7], refs[HEADS + 7 : HEADS + 10]
    out_refs, (gk_ref, gv_ref, gq_ref, held_ref) = refs[HEADS + 10 : -4], refs[-4:]
    first, rows = early[0].shape[:2]
    grad_f = jnp.concatenate([unpack(wide(slab[...]), rows) for slab in slabs], axis=0)
    grad = grad_f.astype(jnp.bfloat16)
    tokens = grad_f.shape[0]
    grad_t = jnp.transpose(grad_f)
    correction = jnp.sum(grad_t * out_t_ref[...], axis=0, keepdims=True)
    grad_t = grad_t.astype(jnp.bfloat16)
    qk, value = qk_ref[...], v_ref[...]
    query, key = qk[:, :HEAD_DIM], qk[:, HEAD_DIM:]
    gk_ref[...] = jnp.zeros_like(gk_ref)
    gv_ref[...] = jnp.zeros_like(gv_ref)
    for start, stop in tiles(tokens):
        probs = prob_ref[:, start:stop]
        grad_probs = dot(value, grad_t[:, start:stop])
        scores = probs.astype(jnp.float32) * (grad_probs - correction[:, start:stop])
        scores = scores.astype(jnp.bfloat16)
        gv_ref[...] += dot(probs, grad[start:stop])
        gk_ref[...] += dot(scores, query[start:stop])
        gq_ref[:, start:stop] = dot(key, scores, ((0,), (0,)))
    grad_q = jnp.transpose(gq_ref[...])
    qk_sum = v_sum = 0.0
    for m in range(HEADS):
        own = slice(m * rows, (m + 1) * rows)
        normed, unit, scale = [
            early[i][m] if m < first else late[i][m - first] for i in range(3)
        ]
        raw = jnp.concatenate([grad_q[own], gk_ref[own, :]], axis=1) * HEAD_DIM ** (-0.5)
        back = scale * (raw - unit * (half_sums(raw * unit) / HEAD_DIM))
        back, grad_v = back.astype(jnp.bfloat16), gv_ref[own, :]
        mirrored = out_refs[DISTANCES.index(DISTANCES[m] ^ HEADS - 1)]
        mirrored[:PACKED, :] = low(pack(grad_v))
        mirrored[PACKED : PACKED + rows, :] = back
        qk_sum = qk_sum + dot(back, normed, ((0,), (0,)))
        v_sum = v_sum + dot(grad_v.astype(jnp.bfloat16), normed, ((0,), (0,)))
    step = qk_sum.shape[1] // HEADS
    for g in range(HEADS):
        own = slice(g * step, (g + 1) * step)
        held_ref[g] = low(jnp.concatenate([qk_sum[:, own], v_sum[:, own]], axis=0))
    for m, out_ref in enumerate(out_refs):
        out_ref[PACKED + rows :, :] = held_ref[me_ref[0] ^ DISTANCES[m]]


def turn_kernel(me_ref, *refs):
    slabs, out_refs, held_ref = refs[:HEADS], refs[HEADS:-1], refs[-1]
    start = slabs[0].shape[0] - 3 * HEAD_DIM
    for m, slab in enumerate(slabs):
        held_ref[me_ref[0] ^ DISTANCES[m]] = slab[start:, :]
    for i, out_ref in enumerate(out_refs):
        own = slice(i * HEAD_DIM, (i + 1) * HEAD_DIM)
        heads = [wide(held_ref[h, own, :]) for h in range(HEADS)]
        out_ref[0] = jnp.transpose(jnp.concatenate(heads, axis=0))


def second_sum_kernel(*refs):
    for second, got, out in zip(refs[0:2], refs[2:4], refs[-2:]):
        start = got.shape[0] - second.shape[0]
        out[...] = low(wide(second[...]) + wide(got[start:, :]))


def third_sum_kernel(*refs):
    for i in range(2):
        third, keep, got, more = [ref[...] for ref in refs[i:8:2]]
        size = third.shape[0]
        leaving, staying = refs[9 + i], refs[11 + i]
        leaving[...] = low(wide(third) + wide(got[size : 2 * size]) + wide(more[size:]))
        staying[...] = wide(keep) + wide(got[:size]) + wide(more[:size])


def last_sum_kernel(keep_a, keep_b, got_a, got_b, out_ref):
    for i, (keep, got) in enumerate(((keep_a, got_a), (keep_b, got_b))):
        width = keep.shape[1]
        out_ref[0, :, i * width : (i + 1) * width] = keep[...] + wide(got[...])


def input_kernel(me_ref, *refs):
    slabs, (wq_ref, wk_ref, wv_ref, act_ref, up_ref, _, out_ref) = refs[:HEADS], refs[HEADS:-1]
    held_ref = refs[-1]
    rows = act_ref.shape[0]
    for m, slab in enumerate(slabs):
        held_ref[me_ref[0] ^ DISTANCES[m]] = slab[: PACKED + rows, :]
    unit, row_scale = normalize(act_ref[...])
    queries, keys, values = [], [], []
    for pair in range(HEADS // 2):
        even, odd = [wide(held_ref[2 * pair + i]) for i in range(2)]
        lower = low_lanes(even[PACKED:])
        queries.append(jnp.where(lower, even[PACKED:], swap(odd[PACKED:])))
        keys.append(jnp.where(lower, swap(even[PACKED:]), odd[PACKED:]))
        values += [unpack(even[:PACKED], rows), unpack(odd[:PACKED], rows)]
    total = 0.0
    for parts, ref in ((queries, wq_ref), (keys, wk_ref), (values, wv_ref)):
        left = jnp.concatenate(parts, axis=1).astype(jnp.bfloat16)
        total = total + dot(left, ref[...], ((1,), (1,)))
    total = total - unit * jnp.mean(total * unit, axis=-1, keepdims=True)
    out_ref[...] = (wide(up_ref[...]) + row_scale * total).astype(jnp.bfloat16)


def reorder_kernel(order_ref, rows_ref, out_ref):
    rows = rows_ref.shape[0]
    chosen = lax.broadcasted_iota(jnp.int32, (rows, rows), 0) == order_ref[...]
    chosen = low(jnp.where(chosen, 1.0, 0.0))
    out_ref[0] = low(dot(chosen, rows_ref[...], ((0,), (0,))))


def hop(block, distance):
    route = [(i, i ^ distance) for i in range(lax.axis_size("seq"))]
    return lax.ppermute(block, "seq", route)


def exchange(slabs):
    return [hop(slab, m) if m else slab for m, slab in zip(DISTANCES, slabs)]


def spread(block):
    side, near, far = [partner(block, "seq", bit) for bit in range(3)]
    side_far = partner(far, "seq", 0)
    near_far = partner(far, "seq", 1)
    side_near = partner(near, "seq", 0)
    last = partner(side_far, "seq", 1)
    return block, side, near, far, side_near, side_far, near_far, last


DISTANCES = (0, 1, 2, 4, 3, 5, 6, 7)


def wide(matrix):
    return matrix.astype(jnp.float32)


def low(matrix):
    return matrix.astype(jnp.bfloat16)


EARLY = 6


def head_shards(
    activations, incoming, w_query, w_key, w_value, w_out, block_ids, flip_order
):
    parts = lax.axis_size("seq")
    me = lax.axis_index("seq").astype(jnp.int32).reshape(1)
    field, upstream = activations[0], incoming[0]
    wq, wk, wv, wo = w_query[0], w_key[0], w_value[0], w_out[0]
    rows, width = field.shape
    inner = wq.shape[1]
    tokens = parts * rows
    f32 = jnp.float32

    def out(*dims, dtype=jnp.bfloat16):
        return jax.ShapeDtypeStruct(dims, dtype)

    blocks = spread(field)
    order = me[0] ^ jnp.array(DISTANCES, jnp.int32)
    ids = jnp.take(block_ids.reshape(parts, rows), order, axis=0).reshape(tokens)
    (weight,) = call(
        select_kernel,
        1.5,
        [("s", me), ("a", wq), ("a", wk), ("a", wv)],
        [out(width, 3 * HEAD_DIM)],
        [pltpu.VMEM((width, 2 * HEAD_DIM), jnp.bfloat16)] * 3 + [pltpu.SemaphoreType.DMA((3,))],
    )
    pair = 2 * HEAD_DIM
    normed, unit, unit_scale, projected = call(
        project_kernel,
        2,
        [("v", block) for block in blocks[:EARLY]] + [("v", weight)],
        [
            out(EARLY, rows, width),
            out(EARLY, rows, pair, dtype=f32),
            out(EARLY, rows, pair, dtype=f32),
            out(EARLY, rows, HEAD_DIM, dtype=f32),
        ],
    )
    late = parts - EARLY
    made = call(
        attend_kernel,
        5,
        [("v", unit), ("v", projected), *[("v", block) for block in blocks[EARLY:]]]
        + [("v", weight), ("v", ids[None, :]), ("v", ids[:, None])],
        [
            out(late, rows, width),
            out(late, rows, pair, dtype=f32),
            out(late, rows, pair, dtype=f32),
            out(tokens, tokens),
            out(tokens, pair),
            out(tokens, HEAD_DIM),
            out(HEAD_DIM, tokens, dtype=f32),
        ]
        + [out(PACKED, 128)] * parts,
    )
    late_parts, (probs, qk, value, out_t), packed = made[:3], made[3:7], made[7:]
    packed = exchange(packed)
    grad_affine, scaled, *grad_slabs = call(
        affine_kernel,
        2,
        [("s", me)] + [("v", x) for x in (*packed, field, upstream, wo)],
        [out(rows, 2 * width), out(rows, width)] + [out(PACKED, 128)] * HEADS,
        [pltpu.VMEM((HEADS, PACKED, 128), jnp.bfloat16)],
    )
    grad_slabs = exchange(grad_slabs)
    terms = call(
        out_term_kernel,
        2,
        [("v", x) for x in (*packed, grad_affine)],
        [out(len(group) * HEAD_DIM, width) for order in ORDERS for group in order],
    )
    grad_slabs, terms, scaled = lax.optimization_barrier((grad_slabs, terms, scaled))
    scaled = hop(scaled, parts - 1)
    first, second, third, keep = zip(terms[:4], terms[4:])
    got = [partner(part, "seq", bit) for bit, part in enumerate(first)]
    grads = call(
        backward_kernel,
        6,
        [("s", me)]
        + [("v", x) for x in (*grad_slabs, probs, qk, value, out_t)]
        + [("v", x) for x in (normed, unit, unit_scale, *late_parts)],
        [out(PACKED + rows + 3 * HEAD_DIM, 128)] * parts,
        [
            pltpu.VMEM((tokens, HEAD_DIM), f32),
            pltpu.VMEM((tokens, HEAD_DIM), f32),
            pltpu.VMEM((HEAD_DIM, tokens), f32),
            pltpu.VMEM((HEADS, 3 * HEAD_DIM, 128), jnp.bfloat16),
        ],
    )
    slabs = exchange(grads)
    leaving = call(
        second_sum_kernel,
        1,
        [("v", x) for x in (*second, *got)] + [("a", x) for x in (*slabs[1:3], scaled)],
        [out(*second[0].shape)] * 2,
    )
    more = [partner(part, "seq", 1 - bit) for bit, part in enumerate(leaving)]
    *leaving, keep_a, keep_b = call(
        third_sum_kernel,
        2,
        [("v", x) for x in (*third, *keep, *got, *more)] + [("a", slabs[5])],
        [out(*third[0].shape)] * 2 + [out(*keep[0].shape, dtype=f32)] * 2,
    )
    rest = [partner(part, "seq", 2) for part in leaving]
    (grad_input,) = call(
        input_kernel,
        1.5,
        [("s", me)] + [("v", x) for x in (*slabs, wq, wk, wv, blocks[-1], scaled)] + [("a", leaving[0])],
        [out(rows, width)],
        [pltpu.VMEM((HEADS, PACKED + rows, 128), jnp.bfloat16)],
    )
    moved = to_previous(grad_input)
    grad_q, grad_k, grad_v = call(
        turn_kernel,
        1,
        [("s", me)] + [("v", x) for x in slabs],
        [out(1, width // parts, inner, dtype=f32)] * 3,
        [pltpu.VMEM((HEADS, 3 * HEAD_DIM, 128), jnp.bfloat16)],
    )
    (grad_out,) = call(
        last_sum_kernel,
        1,
        [("v", x) for x in (keep_a, keep_b, *rest)],
        [out(1, keep_a.shape[0], 2 * width, dtype=f32)],
    )
    (carry,) = call(
        reorder_kernel, 1, [("v", flip_order), ("v", moved)], [out(1, rows, width)]
    )
    return (carry, grad_q, grad_k, grad_v, grad_out)


def solution(mesh):
    shards = head_shards if mesh.shape["seq"] == HEADS else general_shards
    in_specs = (
        P("section", "seq", None),
        P("section", "seq", None),
        P("section", None, None),
        P("section", None, None),
        P("section", None, None),
        P("section", None, None),
        P(),
        P("section", None),
    )
    out_specs = (
        P("section", "seq", None),
        P("section", "seq", None),
        P("section", "seq", None),
        P("section", "seq", None),
        P("section", "seq", None),
    )
    return jax.shard_map(shards, mesh=mesh, in_specs=in_specs, out_specs=out_specs, check_vma=False)
```

```python
import jax
import jax.numpy as jnp
from jax import lax
from jax.experimental import pallas as pl
from jax.experimental.pallas import tpu as pltpu
from jax.sharding import PartitionSpec as P

HEADS = 8
HEAD_DIM = 64


EPSILON = 1e-06


def partner(block, axis, stride):
    count = lax.axis_size(axis)
    route = []
    for low in range(count):
        high = low | 1 << stride
        if high != low and high < count:
            route += [(low, high), (high, low)]
    return lax.ppermute(block, axis, route)


def shifted(block, axis, distance):
    devices = range(lax.axis_size(axis))
    route = [(i - distance, i) for i in devices if i - distance in devices]
    return lax.ppermute(block, axis, route)


def split_heads(matrix):
    return matrix.reshape(matrix.shape[0], HEADS, HEAD_DIM)


def head_major(matrix):
    return jnp.transpose(split_heads(matrix), (1, 0, 2))


def unit_heads(projected):
    parts = split_heads(projected)
    factor = lax.rsqrt(jnp.mean(parts * parts, axis=-1, keepdims=True) + EPSILON)
    return (parts * factor, factor)


def unit_back(grad_heads, unit, factor):
    return factor * (grad_heads - unit * jnp.mean(grad_heads * unit, axis=-1, keepdims=True))


def mirror(rows):
    for bit in range(lax.axis_size("seq").bit_length() - 1):
        rows = partner(rows, "seq", bit)
    return rows


def to_previous(rows):
    return shifted(rows, "section", -1)


def general_shards(activations, incoming, w_query, w_key, w_value, w_out, block_ids, flip_order):
    field = activations[0].astype(jnp.float32)
    upstream = incoming[0].astype(jnp.float32)
    weight_query = w_query[0]
    weight_key = w_key[0]
    weight_value = w_value[0]
    weight_out = w_out[0]
    flip_row = flip_order[0]
    rows = field.shape[0]
    width = field.shape[1]
    inner = weight_query.shape[1]
    scale = HEAD_DIM ** (-0.5)
    first = lax.axis_index("seq") * rows
    my_blocks = lax.dynamic_slice_in_dim(block_ids, first, rows)
    row_scale = lax.rsqrt(jnp.mean(field * field, axis=-1, keepdims=True) + EPSILON)
    unit_rows = field * row_scale
    normed = unit_rows.astype(jnp.bfloat16)
    query_raw = jnp.dot(normed, weight_query, preferred_element_type=jnp.float32)
    key_raw = jnp.dot(normed, weight_key, preferred_element_type=jnp.float32)
    values = jnp.dot(normed, weight_value, preferred_element_type=jnp.float32).astype(jnp.bfloat16)
    query_unit, query_scale = unit_heads(query_raw)
    key_unit, key_scale = unit_heads(key_raw)
    queries = query_unit.astype(jnp.bfloat16).reshape(rows, inner)
    keys = key_unit.astype(jnp.bfloat16).reshape(rows, inner)
    keys_all, values_all = (
        lax.all_gather(keys, "seq", axis=0, tiled=True),
        lax.all_gather(values, "seq", axis=0, tiled=True),
    )
    allowed = block_ids[None, :] <= my_blocks[:, None]
    query_heads = head_major(queries)
    key_heads_all = head_major(keys_all)
    value_heads_all = head_major(values_all)

    def probabilities(query_part, key_part):
        scores = jnp.dot(query_part, key_part.T, preferred_element_type=jnp.float32) * scale
        numerator = jnp.where(allowed, jnp.exp(scores), 0.0)
        denominator = jnp.sum(numerator, axis=-1, keepdims=True)
        return (numerator / denominator, denominator)

    def forward_head(operands):
        query_part, key_part, value_part = operands
        probs, denominator = probabilities(query_part, key_part)
        out_part = jnp.dot(
            probs.astype(jnp.bfloat16), value_part, preferred_element_type=jnp.float32
        ).astype(jnp.bfloat16)
        return (out_part, denominator[:, 0])

    heads_out, denominators = lax.map(forward_head, (query_heads, key_heads_all, value_heads_all))
    attended = jnp.transpose(heads_out, (1, 0, 2)).reshape(rows, inner)
    affine = jnp.dot(attended, weight_out, preferred_element_type=jnp.float32)
    shift_part = affine[:, :width]
    log_scale = affine[:, width:]
    factor = jnp.exp(-log_scale)
    latent = (field - shift_part) * factor
    grad_affine = jnp.concatenate([-upstream * factor, 1.0 - upstream * latent], axis=-1).astype(
        jnp.bfloat16
    )
    out_term = jnp.dot(attended.T, grad_affine, preferred_element_type=jnp.float32)
    grad_attn = jnp.dot(grad_affine, weight_out.T, preferred_element_type=jnp.float32).astype(
        jnp.bfloat16
    )
    correction = jnp.sum(
        split_heads(grad_attn.astype(jnp.float32)) * split_heads(attended.astype(jnp.float32)),
        axis=-1,
    )
    grad_heads = head_major(grad_attn)
    correction_heads = jnp.transpose(correction)[:, :, None]

    def backward_head(operands):
        query_part, key_part, value_part, grad_part, corr_part = operands
        probs, denominator = probabilities(query_part, key_part)
        grad_probs = jnp.dot(grad_part, value_part.T, preferred_element_type=jnp.float32)
        grad_scores = (probs * (grad_probs - corr_part)).astype(jnp.bfloat16)
        grad_qpart = jnp.dot(grad_scores, key_part, preferred_element_type=jnp.float32) * scale
        grad_kpart = jnp.dot(grad_scores.T, query_part, preferred_element_type=jnp.float32) * scale
        grad_vpart = jnp.dot(
            probs.astype(jnp.bfloat16).T, grad_part, preferred_element_type=jnp.float32
        )
        return (grad_qpart, grad_kpart, grad_vpart)

    grad_qheads, grad_kall, grad_vall = lax.map(
        backward_head, (query_heads, key_heads_all, value_heads_all, grad_heads, correction_heads)
    )
    key_terms = jnp.transpose(grad_kall, (1, 0, 2)).reshape(-1, inner)
    value_terms = jnp.transpose(grad_vall, (1, 0, 2)).reshape(-1, inner)
    grad_kunit, grad_vsum = (
        lax.psum_scatter(
            key_terms.astype(jnp.bfloat16), "seq", scatter_dimension=0, tiled=True
        ).astype(jnp.float32),
        lax.psum_scatter(
            value_terms.astype(jnp.bfloat16), "seq", scatter_dimension=0, tiled=True
        ).astype(jnp.float32),
    )
    grad_queries = (
        unit_back(jnp.transpose(grad_qheads, (1, 0, 2)), query_unit, query_scale)
        .reshape(rows, inner)
        .astype(jnp.bfloat16)
    )
    grad_keys = (
        unit_back(split_heads(grad_kunit), key_unit, key_scale)
        .reshape(rows, inner)
        .astype(jnp.bfloat16)
    )
    grad_values = grad_vsum.astype(jnp.bfloat16)
    query_term = jnp.dot(normed.T, grad_queries, preferred_element_type=jnp.float32)
    key_term = jnp.dot(normed.T, grad_keys, preferred_element_type=jnp.float32)
    value_term = jnp.dot(normed.T, grad_values, preferred_element_type=jnp.float32)
    sums = (
        lax.psum_scatter(
            query_term.astype(jnp.bfloat16), "seq", scatter_dimension=0, tiled=True
        ).astype(jnp.float32),
        lax.psum_scatter(
            key_term.astype(jnp.bfloat16), "seq", scatter_dimension=0, tiled=True
        ).astype(jnp.float32),
        lax.psum_scatter(
            value_term.astype(jnp.bfloat16), "seq", scatter_dimension=0, tiled=True
        ).astype(jnp.float32),
        lax.psum_scatter(
            out_term.astype(jnp.bfloat16), "seq", scatter_dimension=0, tiled=True
        ).astype(jnp.float32),
    )
    grad_normed = jnp.dot(grad_queries, weight_query.T, preferred_element_type=jnp.float32)
    grad_normed = grad_normed + jnp.dot(grad_keys, weight_key.T, preferred_element_type=jnp.float32)
    grad_normed = grad_normed + jnp.dot(
        grad_values, weight_value.T, preferred_element_type=jnp.float32
    )
    grad_input = upstream * factor + row_scale * (
        grad_normed - unit_rows * jnp.mean(grad_normed * unit_rows, axis=-1, keepdims=True)
    )
    grad_input = grad_input.astype(jnp.bfloat16)
    moved = mirror(to_previous(grad_input))
    carry = jnp.take(moved, flip_row, axis=0)
    return (carry[None], sums[0][None], sums[1][None], sums[2][None], sums[3][None])


PACKED = 80


def call(kernel, microseconds, ins, outs, scratch=()):
    spaces = {"s": pltpu.SMEM, "v": pltpu.VMEM, "a": pl.ANY}
    places, operands = zip(*ins)
    return pl.pallas_call(
        kernel,
        out_shape=tuple(outs),
        in_specs=[pl.BlockSpec(memory_space=spaces[place]) for place in places],
        out_specs=(pl.BlockSpec(memory_space=pltpu.VMEM),) * len(outs),
        scratch_shapes=list(scratch),
        compiler_params=pltpu.CompilerParams(vmem_limit_bytes=14 * 2**20),
        cost_estimate=pl.CostEstimate(
            flops=int(microseconds * 1e9), bytes_accessed=1024, transcendentals=0
        ),
    )(*operands)


def dot(left, right, contract=((1,), (0,))):
    return lax.dot_general(left, right, (contract, ((), ())), preferred_element_type=jnp.float32)


def low_lanes(block):
    return lax.broadcasted_iota(jnp.int32, block.shape, len(block.shape) - 1) < HEAD_DIM


def swap(block):
    return pltpu.roll(block, HEAD_DIM, 1)


def half_sums(block):
    low = low_lanes(block)
    first = jnp.sum(jnp.where(low, block, 0.0), axis=-1, keepdims=True)
    second = jnp.sum(jnp.where(low, 0.0, block), axis=-1, keepdims=True)
    return jnp.where(low, first, second)


def pack(block):
    rows = block.shape[0]
    return jnp.concatenate([block[:PACKED], block[rows - PACKED :]], axis=1)


def unpack(slab, rows):
    right = swap(slab)[2 * PACKED - rows :, :HEAD_DIM]
    return jnp.concatenate([slab[:, :HEAD_DIM], right], axis=0)


def normalize(block):
    field = block.astype(jnp.float32)
    row_scale = lax.rsqrt(jnp.mean(field * field, axis=-1, keepdims=True) + EPSILON)
    return field * row_scale, row_scale


def project(block, weight):
    normed = normalize(block)[0].astype(jnp.bfloat16)
    product = dot(normed, weight)
    raw, value = product[:, : 2 * HEAD_DIM], product[:, 2 * HEAD_DIM :]
    scale = lax.rsqrt(half_sums(raw * raw) / HEAD_DIM + EPSILON)
    return normed, raw * scale, scale, value


def select_kernel(me_ref, wq_ref, wk_ref, wv_ref, out_ref, *scratch):
    held, semaphores = scratch[:3], scratch[3]
    odd = lax.rem(me_ref[0], 2) == 1
    pair = pl.multiple_of(lax.div(me_ref[0], 2) * 2 * HEAD_DIM, 2 * HEAD_DIM)
    copies = [
        pltpu.make_async_copy(ref.at[:, pl.ds(pair, 2 * HEAD_DIM)], kept, semaphores.at[i])
        for i, (ref, kept) in enumerate(zip((wq_ref, wk_ref, wv_ref), held))
    ]
    for copy in copies:
        copy.start()
    for copy in copies:
        copy.wait()
    q, k, v = [wide(kept[...]) for kept in held]
    lower = low_lanes(q)
    qk = jnp.where(lower, jnp.where(odd, swap(q), q), jnp.where(odd, k, swap(k)))
    out_ref[:, : 2 * HEAD_DIM] = low(qk)
    out_ref[:, 2 * HEAD_DIM :] = low(jnp.where(odd, swap(v), v)[:, :HEAD_DIM])


def project_kernel(*refs):
    blocks, (weight_ref, normed_ref, unit_ref, scale_ref, value_ref) = refs[:-5], refs[-5:]
    for m, block in enumerate(blocks):
        made = project(block[...], weight_ref[...])
        for ref, part in zip((normed_ref, unit_ref, scale_ref, value_ref), made):
            ref[m] = part.astype(ref.dtype)


TILE = 256


def tiles(tokens):
    starts = range(0, tokens, TILE)
    return [(start, min(tokens, start + TILE)) for start in starts]


def attend_kernel(
    me_ref, unit_ref, value_ref, near_ref, last_ref, weight_ref, row_ids, column_ids, *out_refs
):
    normed_ref, late_unit, late_scale, prob_ref, qk_ref, v_ref, out_t_ref = out_refs[:7]
    early, rows = unit_ref.shape[:2]
    units = [unit_ref[m] for m in range(early)]
    values = [value_ref[m] for m in range(early)]
    for m, ref in enumerate((near_ref, last_ref)):
        normed, unit, scale, value = project(ref[...], weight_ref[...])
        normed_ref[m], late_unit[m], late_scale[m] = normed, unit, scale
        units.append(unit)
        values.append(value)
    parts = len(units)
    tokens = parts * rows
    qk = jnp.concatenate(units, axis=0).astype(jnp.bfloat16)
    value = jnp.concatenate(values, axis=0).astype(jnp.bfloat16)
    qk_ref[...] = qk
    v_ref[...] = value
    query, key = qk[:, :HEAD_DIM] * HEAD_DIM ** (-0.5), qk[:, HEAD_DIM:]
    for start, stop in tiles(tokens):
        scores = dot(key, query[start:stop], ((1,), (1,)))
        allowed = column_ids[...] <= row_ids[:, start:stop]
        numerator = jnp.where(allowed, jnp.exp(scores), 0.0)
        probs = numerator * (1.0 / jnp.sum(numerator, axis=0, keepdims=True))
        probs = probs.astype(jnp.bfloat16)
        prob_ref[:, start:stop] = probs
        out_t = dot(value, probs, ((0,), (0,)))
        out_t_ref[:, start:stop] = out_t.astype(jnp.bfloat16).astype(jnp.float32)
    out = jnp.transpose(out_t_ref[...])
    for m, distance in enumerate(DISTANCES):
        out_refs[7][me_ref[0] ^ distance] = low(pack(out[m * rows : (m + 1) * rows]))


def affine_kernel(me_ref, slab_ref, act_ref, inc_ref, w_ref, up_ref, out_ref, *term_refs):
    rows, width = act_ref.shape
    columns = [unpack(wide(slab_ref[h]), rows) for h in range(HEADS)]
    attended = low(jnp.concatenate(columns, axis=1))
    factor = jnp.exp(-dot(attended, w_ref[:, width:]))
    scaled = inc_ref[...].astype(jnp.float32) * factor
    up_ref[...] = low(scaled)
    shift_part = dot(attended, w_ref[:, :width])
    latent_part = scaled * (act_ref[...].astype(jnp.float32) - shift_part)
    grad_affine = jnp.concatenate([-scaled, 1.0 - latent_part], axis=1).astype(jnp.bfloat16)
    grad = dot(grad_affine, w_ref[...], ((1,), (1,)))
    for h in range(HEADS):
        out_ref[h] = low(pack(grad[:, h * HEAD_DIM : (h + 1) * HEAD_DIM]))
    columns = [unpack(wide(slab_ref[me_ref[0] ^ m]), rows) for m in range(HEADS)]
    for half, order in enumerate(ORDERS):
        right = grad_affine[:, half * width : (half + 1) * width]
        for term_ref, group in zip(term_refs[4 * half : 4 * half + 4], order):
            left = low(jnp.concatenate([columns[m] for m in group], axis=1))
            term_ref[...] = low(dot(left, right, ((0,), (0,))))


ORDERS = (((1, 5, 3, 7), (2, 6), (4,), (0,)), ((2, 6, 3, 7), (1, 5), (4,), (0,)))


def backward_kernel(me_ref, slab_ref, prob_ref, qk_ref, v_ref, out_t_ref, *refs):
    early, late, out_refs = refs[:3], refs[3:6], refs[6:-4]
    gk_ref, gv_ref, gq_ref, held_ref = refs[-4:]
    first, rows = early[0].shape[:2]
    slabs = [wide(slab_ref[me_ref[0] ^ distance]) for distance in DISTANCES]
    grad_f = jnp.concatenate([unpack(slab, rows) for slab in slabs], axis=0)
    grad = grad_f.astype(jnp.bfloat16)
    tokens = grad_f.shape[0]
    grad_t = jnp.transpose(grad_f)
    correction = jnp.sum(grad_t * out_t_ref[...], axis=0, keepdims=True)
    grad_t = grad_t.astype(jnp.bfloat16)
    qk, value = qk_ref[...], v_ref[...]
    query, key = qk[:, :HEAD_DIM], qk[:, HEAD_DIM:]
    gk_ref[...] = jnp.zeros_like(gk_ref)
    gv_ref[...] = jnp.zeros_like(gv_ref)
    for start, stop in tiles(tokens):
        probs = prob_ref[:, start:stop]
        grad_probs = dot(value, grad_t[:, start:stop])
        scores = probs.astype(jnp.float32) * (grad_probs - correction[:, start:stop])
        scores = scores.astype(jnp.bfloat16)
        gv_ref[...] += dot(probs, grad[start:stop])
        gk_ref[...] += dot(scores, query[start:stop])
        gq_ref[:, start:stop] = dot(key, scores, ((0,), (0,)))
    grad_q = jnp.transpose(gq_ref[...])
    qk_sum = v_sum = 0.0
    for m in range(HEADS):
        own = slice(m * rows, (m + 1) * rows)
        normed, unit, scale = [
            early[i][m] if m < first else late[i][m - first] for i in range(3)
        ]
        raw = jnp.concatenate([grad_q[own], gk_ref[own, :]], axis=1) * HEAD_DIM ** (-0.5)
        back = scale * (raw - unit * (half_sums(raw * unit) / HEAD_DIM))
        back, grad_v = back.astype(jnp.bfloat16), gv_ref[own, :]
        mirrored = out_refs[DISTANCES.index(DISTANCES[m] ^ HEADS - 1)]
        mirrored[:PACKED, :] = low(pack(grad_v))
        mirrored[PACKED : PACKED + rows, :] = back
        qk_sum = qk_sum + dot(back, normed, ((0,), (0,)))
        v_sum = v_sum + dot(grad_v.astype(jnp.bfloat16), normed, ((0,), (0,)))
    step = qk_sum.shape[1] // HEADS
    for g in range(HEADS):
        own = slice(g * step, (g + 1) * step)
        held_ref[g] = low(jnp.concatenate([qk_sum[:, own], v_sum[:, own]], axis=0))
    for m, out_ref in enumerate(out_refs):
        out_ref[PACKED + rows :, :] = held_ref[me_ref[0] ^ DISTANCES[m]]


def turn_kernel(me_ref, *refs):
    slabs, out_refs, held_ref = refs[:HEADS], refs[HEADS:-1], refs[-1]
    start = slabs[0].shape[0] - 3 * HEAD_DIM
    for m, slab in enumerate(slabs):
        held_ref[me_ref[0] ^ DISTANCES[m]] = slab[start:, :]
    for i, out_ref in enumerate(out_refs):
        own = slice(i * HEAD_DIM, (i + 1) * HEAD_DIM)
        heads = [wide(held_ref[h, own, :]) for h in range(HEADS)]
        out_ref[0] = jnp.transpose(jnp.concatenate(heads, axis=0))


def second_sum_kernel(*refs):
    for second, got, out in zip(refs[0:2], refs[2:4], refs[-2:]):
        start = got.shape[0] - second.shape[0]
        out[...] = low(wide(second[...]) + wide(got[start:, :]))


def third_sum_kernel(*refs):
    for i in range(2):
        third, keep, got, more = [ref[...] for ref in refs[i:8:2]]
        size = third.shape[0]
        leaving, staying = refs[9 + i], refs[11 + i]
        leaving[...] = low(wide(third) + wide(got[size : 2 * size]) + wide(more[size:]))
        staying[...] = wide(keep) + wide(got[:size]) + wide(more[:size])


def last_sum_kernel(keep_a, keep_b, got_a, got_b, out_ref):
    for i, (keep, got) in enumerate(((keep_a, got_a), (keep_b, got_b))):
        width = keep.shape[1]
        out_ref[0, :, i * width : (i + 1) * width] = keep[...] + wide(got[...])


def input_kernel(me_ref, *refs):
    slabs, (wq_ref, wk_ref, wv_ref, act_ref, up_ref, _, out_ref) = refs[:HEADS], refs[HEADS:-1]
    held_ref = refs[-1]
    rows = act_ref.shape[0]
    for m, slab in enumerate(slabs):
        held_ref[me_ref[0] ^ DISTANCES[m]] = slab[: PACKED + rows, :]
    unit, row_scale = normalize(act_ref[...])
    queries, keys, values = [], [], []
    for pair in range(HEADS // 2):
        even, odd = [wide(held_ref[2 * pair + i]) for i in range(2)]
        lower = low_lanes(even[PACKED:])
        queries.append(jnp.where(lower, even[PACKED:], swap(odd[PACKED:])))
        keys.append(jnp.where(lower, swap(even[PACKED:]), odd[PACKED:]))
        values += [unpack(even[:PACKED], rows), unpack(odd[:PACKED], rows)]
    total = 0.0
    for parts, ref in ((queries, wq_ref), (keys, wk_ref), (values, wv_ref)):
        left = jnp.concatenate(parts, axis=1).astype(jnp.bfloat16)
        total = total + dot(left, ref[...], ((1,), (1,)))
    total = total - unit * jnp.mean(total * unit, axis=-1, keepdims=True)
    out_ref[...] = (wide(up_ref[...]) + row_scale * total).astype(jnp.bfloat16)


def reorder_kernel(order_ref, rows_ref, out_ref):
    rows = rows_ref.shape[0]
    chosen = lax.broadcasted_iota(jnp.int32, (rows, rows), 0) == order_ref[...]
    chosen = low(jnp.where(chosen, 1.0, 0.0))
    out_ref[0] = low(dot(chosen, rows_ref[...], ((0,), (0,))))


def hop(block, distance):
    route = [(i, i ^ distance) for i in range(lax.axis_size("seq"))]
    return lax.ppermute(block, "seq", route)


def exchange(slabs):
    return [hop(slab, m) if m else slab for m, slab in zip(DISTANCES, slabs)]


def switch(slabs):
    return lax.all_to_all(slabs, "seq", split_axis=0, concat_axis=0, tiled=True)


def spread(block):
    side, near, far = [partner(block, "seq", bit) for bit in range(3)]
    side_far = partner(far, "seq", 0)
    near_far = partner(far, "seq", 1)
    side_near = partner(near, "seq", 0)
    last = partner(side_far, "seq", 1)
    return block, side, near, far, side_near, side_far, near_far, last


DISTANCES = (0, 1, 2, 4, 3, 5, 6, 7)


def wide(matrix):
    return matrix.astype(jnp.float32)


def low(matrix):
    return matrix.astype(jnp.bfloat16)


EARLY = 6


def head_shards(
    activations, incoming, w_query, w_key, w_value, w_out, block_ids, flip_order
):
    parts = lax.axis_size("seq")
    me = lax.axis_index("seq").astype(jnp.int32).reshape(1)
    field, upstream = activations[0], incoming[0]
    wq, wk, wv, wo = w_query[0], w_key[0], w_value[0], w_out[0]
    rows, width = field.shape
    inner = wq.shape[1]
    tokens = parts * rows
    f32 = jnp.float32

    def out(*dims, dtype=jnp.bfloat16):
        return jax.ShapeDtypeStruct(dims, dtype)

    blocks = spread(field)
    order = me[0] ^ jnp.array(DISTANCES, jnp.int32)
    ids = jnp.take(block_ids.reshape(parts, rows), order, axis=0).reshape(tokens)
    (weight,) = call(
        select_kernel,
        1.5,
        [("s", me), ("a", wq), ("a", wk), ("a", wv)],
        [out(width, 3 * HEAD_DIM)],
        [pltpu.VMEM((width, 2 * HEAD_DIM), jnp.bfloat16)] * 3 + [pltpu.SemaphoreType.DMA((3,))],
    )
    pair = 2 * HEAD_DIM
    normed, unit, unit_scale, projected = call(
        project_kernel,
        2,
        [("v", block) for block in blocks[:EARLY]] + [("v", weight)],
        [
            out(EARLY, rows, width),
            out(EARLY, rows, pair, dtype=f32),
            out(EARLY, rows, pair, dtype=f32),
            out(EARLY, rows, HEAD_DIM, dtype=f32),
        ],
    )
    late = parts - EARLY
    made = call(
        attend_kernel,
        5,
        [("s", me), ("v", unit), ("v", projected), *[("v", block) for block in blocks[EARLY:]]]
        + [("v", weight), ("v", ids[None, :]), ("v", ids[:, None])],
        [
            out(late, rows, width),
            out(late, rows, pair, dtype=f32),
            out(late, rows, pair, dtype=f32),
            out(tokens, tokens),
            out(tokens, pair),
            out(tokens, HEAD_DIM),
            out(HEAD_DIM, tokens, dtype=f32),
        ]
        + [out(parts, PACKED, 128)],
    )
    late_parts, (probs, qk, value, out_t), packed = made[:3], made[3:7], switch(made[7])
    scaled, grad_slabs, *terms = call(
        affine_kernel,
        3,
        [("s", me)] + [("v", x) for x in (packed, field, upstream, wo)],
        [out(rows, width), out(HEADS, PACKED, 128)]
        + [out(len(group) * HEAD_DIM, width) for order in ORDERS for group in order],
    )
    grad_slabs = switch(grad_slabs)
    grad_slabs, terms, scaled = lax.optimization_barrier((grad_slabs, terms, scaled))
    scaled = hop(scaled, parts - 1)
    first, second, third, keep = zip(terms[:4], terms[4:])
    got = [partner(part, "seq", bit) for bit, part in enumerate(first)]
    grads = call(
        backward_kernel,
        6,
        [("s", me)]
        + [("v", x) for x in (grad_slabs, probs, qk, value, out_t)]
        + [("v", x) for x in (normed, unit, unit_scale, *late_parts)],
        [out(PACKED + rows + 3 * HEAD_DIM, 128)] * parts,
        [
            pltpu.VMEM((tokens, HEAD_DIM), f32),
            pltpu.VMEM((tokens, HEAD_DIM), f32),
            pltpu.VMEM((HEAD_DIM, tokens), f32),
            pltpu.VMEM((HEADS, 3 * HEAD_DIM, 128), jnp.bfloat16),
        ],
    )
    slabs = exchange(grads)
    leaving = call(
        second_sum_kernel,
        1,
        [("v", x) for x in (*second, *got)] + [("a", x) for x in (*slabs[1:3], scaled)],
        [out(*second[0].shape)] * 2,
    )
    more = [partner(part, "seq", 1 - bit) for bit, part in enumerate(leaving)]
    *leaving, keep_a, keep_b = call(
        third_sum_kernel,
        2,
        [("v", x) for x in (*third, *keep, *got, *more)] + [("a", slabs[5])],
        [out(*third[0].shape)] * 2 + [out(*keep[0].shape, dtype=f32)] * 2,
    )
    rest = [partner(part, "seq", 2) for part in leaving]
    (grad_input,) = call(
        input_kernel,
        1.5,
        [("s", me)] + [("v", x) for x in (*slabs, wq, wk, wv, blocks[-1], scaled)] + [("a", leaving[0])],
        [out(rows, width)],
        [pltpu.VMEM((HEADS, PACKED + rows, 128), jnp.bfloat16)],
    )
    (grad_out,) = call(
        last_sum_kernel,
        1,
        [("v", x) for x in (keep_a, keep_b, *rest)],
        [out(1, keep_a.shape[0], 2 * width, dtype=f32)],
    )
    grad_input, grad_out = lax.optimization_barrier((grad_input, grad_out))
    moved = to_previous(grad_input)
    grad_q, grad_k, grad_v = call(
        turn_kernel,
        1,
        [("s", me)] + [("v", x) for x in slabs],
        [out(1, width // parts, inner, dtype=f32)] * 3,
        [pltpu.VMEM((HEADS, 3 * HEAD_DIM, 128), jnp.bfloat16)],
    )
    (carry,) = call(
        reorder_kernel, 1, [("v", flip_order), ("v", moved)], [out(1, rows, width)]
    )
    return (carry, grad_q, grad_k, grad_v, grad_out)


def solution(mesh):
    shards = head_shards if mesh.shape["seq"] == HEADS else general_shards
    in_specs = (
        P("section", "seq", None),
        P("section", "seq", None),
        P("section", None, None),
        P("section", None, None),
        P("section", None, None),
        P("section", None, None),
        P(),
        P("section", None),
    )
    out_specs = (
        P("section", "seq", None),
        P("section", "seq", None),
        P("section", "seq", None),
        P("section", "seq", None),
        P("section", "seq", None),
    )
    return jax.shard_map(shards, mesh=mesh, in_specs=in_specs, out_specs=out_specs, check_vma=False)
```

```python
import jax
import jax.numpy as jnp
from jax import lax
from jax.experimental import pallas as pl
from jax.experimental.pallas import tpu as pltpu
from jax.sharding import PartitionSpec as P

HEADS = 8
HEAD_DIM = 64


EPSILON = 1e-06


def partner(block, axis, stride):
    count = lax.axis_size(axis)
    route = []
    for low in range(count):
        high = low | 1 << stride
        if high != low and high < count:
            route += [(low, high), (high, low)]
    return lax.ppermute(block, axis, route)


def shifted(block, axis, distance):
    devices = range(lax.axis_size(axis))
    route = [(i - distance, i) for i in devices if i - distance in devices]
    return lax.ppermute(block, axis, route)


def split_heads(matrix):
    return matrix.reshape(matrix.shape[0], HEADS, HEAD_DIM)


def head_major(matrix):
    return jnp.transpose(split_heads(matrix), (1, 0, 2))


def unit_heads(projected):
    parts = split_heads(projected)
    factor = lax.rsqrt(jnp.mean(parts * parts, axis=-1, keepdims=True) + EPSILON)
    return (parts * factor, factor)


def unit_back(grad_heads, unit, factor):
    return factor * (grad_heads - unit * jnp.mean(grad_heads * unit, axis=-1, keepdims=True))


def mirror(rows):
    for bit in range(lax.axis_size("seq").bit_length() - 1):
        rows = partner(rows, "seq", bit)
    return rows


def to_previous(rows):
    return shifted(rows, "section", -1)


def general_shards(activations, incoming, w_query, w_key, w_value, w_out, block_ids, flip_order):
    field = activations[0].astype(jnp.float32)
    upstream = incoming[0].astype(jnp.float32)
    weight_query = w_query[0]
    weight_key = w_key[0]
    weight_value = w_value[0]
    weight_out = w_out[0]
    flip_row = flip_order[0]
    rows = field.shape[0]
    width = field.shape[1]
    inner = weight_query.shape[1]
    scale = HEAD_DIM ** (-0.5)
    first = lax.axis_index("seq") * rows
    my_blocks = lax.dynamic_slice_in_dim(block_ids, first, rows)
    row_scale = lax.rsqrt(jnp.mean(field * field, axis=-1, keepdims=True) + EPSILON)
    unit_rows = field * row_scale
    normed = unit_rows.astype(jnp.bfloat16)
    query_raw = jnp.dot(normed, weight_query, preferred_element_type=jnp.float32)
    key_raw = jnp.dot(normed, weight_key, preferred_element_type=jnp.float32)
    values = jnp.dot(normed, weight_value, preferred_element_type=jnp.float32).astype(jnp.bfloat16)
    query_unit, query_scale = unit_heads(query_raw)
    key_unit, key_scale = unit_heads(key_raw)
    queries = query_unit.astype(jnp.bfloat16).reshape(rows, inner)
    keys = key_unit.astype(jnp.bfloat16).reshape(rows, inner)
    keys_all, values_all = (
        lax.all_gather(keys, "seq", axis=0, tiled=True),
        lax.all_gather(values, "seq", axis=0, tiled=True),
    )
    allowed = block_ids[None, :] <= my_blocks[:, None]
    query_heads = head_major(queries)
    key_heads_all = head_major(keys_all)
    value_heads_all = head_major(values_all)

    def probabilities(query_part, key_part):
        scores = jnp.dot(query_part, key_part.T, preferred_element_type=jnp.float32) * scale
        numerator = jnp.where(allowed, jnp.exp(scores), 0.0)
        denominator = jnp.sum(numerator, axis=-1, keepdims=True)
        return (numerator / denominator, denominator)

    def forward_head(operands):
        query_part, key_part, value_part = operands
        probs, denominator = probabilities(query_part, key_part)
        out_part = jnp.dot(
            probs.astype(jnp.bfloat16), value_part, preferred_element_type=jnp.float32
        ).astype(jnp.bfloat16)
        return (out_part, denominator[:, 0])

    heads_out, denominators = lax.map(forward_head, (query_heads, key_heads_all, value_heads_all))
    attended = jnp.transpose(heads_out, (1, 0, 2)).reshape(rows, inner)
    affine = jnp.dot(attended, weight_out, preferred_element_type=jnp.float32)
    shift_part = affine[:, :width]
    log_scale = affine[:, width:]
    factor = jnp.exp(-log_scale)
    latent = (field - shift_part) * factor
    grad_affine = jnp.concatenate([-upstream * factor, 1.0 - upstream * latent], axis=-1).astype(
        jnp.bfloat16
    )
    out_term = jnp.dot(attended.T, grad_affine, preferred_element_type=jnp.float32)
    grad_attn = jnp.dot(grad_affine, weight_out.T, preferred_element_type=jnp.float32).astype(
        jnp.bfloat16
    )
    correction = jnp.sum(
        split_heads(grad_attn.astype(jnp.float32)) * split_heads(attended.astype(jnp.float32)),
        axis=-1,
    )
    grad_heads = head_major(grad_attn)
    correction_heads = jnp.transpose(correction)[:, :, None]

    def backward_head(operands):
        query_part, key_part, value_part, grad_part, corr_part = operands
        probs, denominator = probabilities(query_part, key_part)
        grad_probs = jnp.dot(grad_part, value_part.T, preferred_element_type=jnp.float32)
        grad_scores = (probs * (grad_probs - corr_part)).astype(jnp.bfloat16)
        grad_qpart = jnp.dot(grad_scores, key_part, preferred_element_type=jnp.float32) * scale
        grad_kpart = jnp.dot(grad_scores.T, query_part, preferred_element_type=jnp.float32) * scale
        grad_vpart = jnp.dot(
            probs.astype(jnp.bfloat16).T, grad_part, preferred_element_type=jnp.float32
        )
        return (grad_qpart, grad_kpart, grad_vpart)

    grad_qheads, grad_kall, grad_vall = lax.map(
        backward_head, (query_heads, key_heads_all, value_heads_all, grad_heads, correction_heads)
    )
    key_terms = jnp.transpose(grad_kall, (1, 0, 2)).reshape(-1, inner)
    value_terms = jnp.transpose(grad_vall, (1, 0, 2)).reshape(-1, inner)
    grad_kunit, grad_vsum = (
        lax.psum_scatter(
            key_terms.astype(jnp.bfloat16), "seq", scatter_dimension=0, tiled=True
        ).astype(jnp.float32),
        lax.psum_scatter(
            value_terms.astype(jnp.bfloat16), "seq", scatter_dimension=0, tiled=True
        ).astype(jnp.float32),
    )
    grad_queries = (
        unit_back(jnp.transpose(grad_qheads, (1, 0, 2)), query_unit, query_scale)
        .reshape(rows, inner)
        .astype(jnp.bfloat16)
    )
    grad_keys = (
        unit_back(split_heads(grad_kunit), key_unit, key_scale)
        .reshape(rows, inner)
        .astype(jnp.bfloat16)
    )
    grad_values = grad_vsum.astype(jnp.bfloat16)
    query_term = jnp.dot(normed.T, grad_queries, preferred_element_type=jnp.float32)
    key_term = jnp.dot(normed.T, grad_keys, preferred_element_type=jnp.float32)
    value_term = jnp.dot(normed.T, grad_values, preferred_element_type=jnp.float32)
    sums = (
        lax.psum_scatter(
            query_term.astype(jnp.bfloat16), "seq", scatter_dimension=0, tiled=True
        ).astype(jnp.float32),
        lax.psum_scatter(
            key_term.astype(jnp.bfloat16), "seq", scatter_dimension=0, tiled=True
        ).astype(jnp.float32),
        lax.psum_scatter(
            value_term.astype(jnp.bfloat16), "seq", scatter_dimension=0, tiled=True
        ).astype(jnp.float32),
        lax.psum_scatter(
            out_term.astype(jnp.bfloat16), "seq", scatter_dimension=0, tiled=True
        ).astype(jnp.float32),
    )
    grad_normed = jnp.dot(grad_queries, weight_query.T, preferred_element_type=jnp.float32)
    grad_normed = grad_normed + jnp.dot(grad_keys, weight_key.T, preferred_element_type=jnp.float32)
    grad_normed = grad_normed + jnp.dot(
        grad_values, weight_value.T, preferred_element_type=jnp.float32
    )
    grad_input = upstream * factor + row_scale * (
        grad_normed - unit_rows * jnp.mean(grad_normed * unit_rows, axis=-1, keepdims=True)
    )
    grad_input = grad_input.astype(jnp.bfloat16)
    moved = mirror(to_previous(grad_input))
    carry = jnp.take(moved, flip_row, axis=0)
    return (carry[None], sums[0][None], sums[1][None], sums[2][None], sums[3][None])


PACKED = 80


def call(kernel, microseconds, ins, outs, scratch=()):
    spaces = {"s": pltpu.SMEM, "v": pltpu.VMEM, "a": pl.ANY}
    places, operands = zip(*ins)
    return pl.pallas_call(
        kernel,
        out_shape=tuple(outs),
        in_specs=[pl.BlockSpec(memory_space=spaces[place]) for place in places],
        out_specs=(pl.BlockSpec(memory_space=pltpu.VMEM),) * len(outs),
        scratch_shapes=list(scratch),
        compiler_params=pltpu.CompilerParams(vmem_limit_bytes=14 * 2**20),
        cost_estimate=pl.CostEstimate(
            flops=int(microseconds * 1e9), bytes_accessed=1024, transcendentals=0
        ),
    )(*operands)


def dot(left, right, contract=((1,), (0,))):
    return lax.dot_general(left, right, (contract, ((), ())), preferred_element_type=jnp.float32)


def low_lanes(block):
    return lax.broadcasted_iota(jnp.int32, block.shape, len(block.shape) - 1) < HEAD_DIM


def swap(block):
    return pltpu.roll(block, HEAD_DIM, 1)


def half_sums(block):
    low = low_lanes(block)
    first = jnp.sum(jnp.where(low, block, 0.0), axis=-1, keepdims=True)
    second = jnp.sum(jnp.where(low, 0.0, block), axis=-1, keepdims=True)
    return jnp.where(low, first, second)


def pack(block):
    rows = block.shape[0]
    return jnp.concatenate([block[:PACKED], block[rows - PACKED :]], axis=1)


def unpack(slab, rows):
    right = swap(slab)[2 * PACKED - rows :, :HEAD_DIM]
    return jnp.concatenate([slab[:, :HEAD_DIM], right], axis=0)


def normalize(block):
    field = block.astype(jnp.float32)
    row_scale = lax.rsqrt(jnp.mean(field * field, axis=-1, keepdims=True) + EPSILON)
    return field * row_scale, row_scale


def project(block, weight):
    normed = normalize(block)[0].astype(jnp.bfloat16)
    product = dot(normed, weight)
    raw, value = product[:, : 2 * HEAD_DIM], product[:, 2 * HEAD_DIM :]
    scale = lax.rsqrt(half_sums(raw * raw) / HEAD_DIM + EPSILON)
    return normed, raw * scale, scale, value


def select_kernel(me_ref, wq_ref, wk_ref, wv_ref, out_ref, *scratch):
    held, semaphores = scratch[:3], scratch[3]
    odd = lax.rem(me_ref[0], 2) == 1
    pair = pl.multiple_of(lax.div(me_ref[0], 2) * 2 * HEAD_DIM, 2 * HEAD_DIM)
    copies = [
        pltpu.make_async_copy(ref.at[:, pl.ds(pair, 2 * HEAD_DIM)], kept, semaphores.at[i])
        for i, (ref, kept) in enumerate(zip((wq_ref, wk_ref, wv_ref), held))
    ]
    for copy in copies:
        copy.start()
    for copy in copies:
        copy.wait()
    q, k, v = [wide(kept[...]) for kept in held]
    lower = low_lanes(q)
    qk = jnp.where(lower, jnp.where(odd, swap(q), q), jnp.where(odd, k, swap(k)))
    out_ref[:, : 2 * HEAD_DIM] = low(qk)
    out_ref[:, 2 * HEAD_DIM :] = low(jnp.where(odd, swap(v), v)[:, :HEAD_DIM])


def joined(refs, width):
    pieces, blocks = [], []
    for ref in refs:
        pieces.append(ref[...])
        if sum(piece.shape[1] for piece in pieces) == width:
            blocks.append(jnp.concatenate(pieces, axis=1) if len(pieces) > 1 else pieces[0])
            pieces = []
    return blocks


def project_kernel(*refs):
    blocks, (weight_ref, normed_ref, unit_ref, scale_ref, value_ref) = refs[:-5], refs[-5:]
    for m, block in enumerate(joined(blocks, normed_ref.shape[2])):
        made = project(block, weight_ref[...])
        for ref, part in zip((normed_ref, unit_ref, scale_ref, value_ref), made):
            ref[m] = part.astype(ref.dtype)


TILE = 256


def tiles(tokens):
    starts = range(0, tokens, TILE)
    return [(start, min(tokens, start + TILE)) for start in starts]


def attend_kernel(
    me_ref, unit_ref, value_ref, weight_ref, row_ids, column_ids, *refs
):
    pieces, out_refs = refs[:-8], refs[-8:]
    normed_ref, late_unit, late_scale, prob_ref, qk_ref, v_ref, out_t_ref = out_refs[:7]
    early, rows = unit_ref.shape[:2]
    units = [unit_ref[m] for m in range(early)]
    values = [value_ref[m] for m in range(early)]
    for m, block in enumerate(joined(pieces, normed_ref.shape[2])):
        normed, unit, scale, value = project(block, weight_ref[...])
        normed_ref[m], late_unit[m], late_scale[m] = normed, unit, scale
        units.append(unit)
        values.append(value)
    parts = early + normed_ref.shape[0]
    tokens = parts * rows
    qk = jnp.concatenate(units, axis=0).astype(jnp.bfloat16)
    value = jnp.concatenate(values, axis=0).astype(jnp.bfloat16)
    qk_ref[...] = qk
    v_ref[...] = value
    query, key = qk[:, :HEAD_DIM] * HEAD_DIM ** (-0.5), qk[:, HEAD_DIM:]
    for start, stop in tiles(tokens):
        scores = dot(key, query[start:stop], ((1,), (1,)))
        allowed = column_ids[...] <= row_ids[:, start:stop]
        numerator = jnp.where(allowed, jnp.exp(scores), 0.0)
        probs = numerator * (1.0 / jnp.sum(numerator, axis=0, keepdims=True))
        probs = probs.astype(jnp.bfloat16)
        prob_ref[:, start:stop] = probs
        out_t = dot(value, probs, ((0,), (0,)))
        out_t_ref[:, start:stop] = out_t.astype(jnp.bfloat16).astype(jnp.float32)
    out = jnp.transpose(out_t_ref[...])
    for m, distance in enumerate(DISTANCES):
        out_refs[7][me_ref[0] ^ distance] = low(pack(out[m * rows : (m + 1) * rows]))


def affine_kernel(me_ref, slab_ref, act_ref, inc_ref, w_ref, up_ref, out_ref, *term_refs):
    rows, width = act_ref.shape
    columns = [unpack(wide(slab_ref[h]), rows) for h in range(HEADS)]
    attended = low(jnp.concatenate(columns, axis=1))
    factor = jnp.exp(-dot(attended, w_ref[:, width:]))
    scaled = inc_ref[...].astype(jnp.float32) * factor
    up_ref[...] = low(scaled)
    shift_part = dot(attended, w_ref[:, :width])
    latent_part = scaled * (act_ref[...].astype(jnp.float32) - shift_part)
    grad_affine = jnp.concatenate([-scaled, 1.0 - latent_part], axis=1).astype(jnp.bfloat16)
    grad = dot(grad_affine, w_ref[...], ((1,), (1,)))
    for h in range(HEADS):
        out_ref[h] = low(pack(grad[:, h * HEAD_DIM : (h + 1) * HEAD_DIM]))
    columns = [unpack(wide(slab_ref[me_ref[0] ^ m]), rows) for m in range(HEADS)]
    for half, order in enumerate(ORDERS):
        right = grad_affine[:, half * width : (half + 1) * width]
        for term_ref, group in zip(term_refs[4 * half : 4 * half + 4], order):
            left = low(jnp.concatenate([columns[m] for m in group], axis=1))
            term_ref[...] = low(dot(left, right, ((0,), (0,))))


ORDERS = (((1, 5, 3, 7), (2, 6), (4,), (0,)), ((2, 6, 3, 7), (1, 5), (4,), (0,)))


def backward_kernel(me_ref, slab_ref, prob_ref, qk_ref, v_ref, out_t_ref, *refs):
    early, late, out_refs = refs[:3], refs[3:6], refs[6:-4]
    gk_ref, gv_ref, gq_ref, held_ref = refs[-4:]
    first, rows = early[0].shape[:2]
    slabs = [wide(slab_ref[me_ref[0] ^ distance]) for distance in DISTANCES]
    grad_f = jnp.concatenate([unpack(slab, rows) for slab in slabs], axis=0)
    grad = grad_f.astype(jnp.bfloat16)
    tokens = grad_f.shape[0]
    grad_t = jnp.transpose(grad_f)
    correction = jnp.sum(grad_t * out_t_ref[...], axis=0, keepdims=True)
    grad_t = grad_t.astype(jnp.bfloat16)
    qk, value = qk_ref[...], v_ref[...]
    query, key = qk[:, :HEAD_DIM], qk[:, HEAD_DIM:]
    gk_ref[...] = jnp.zeros_like(gk_ref)
    gv_ref[...] = jnp.zeros_like(gv_ref)
    for start, stop in tiles(tokens):
        probs = prob_ref[:, start:stop]
        grad_probs = dot(value, grad_t[:, start:stop])
        scores = probs.astype(jnp.float32) * (grad_probs - correction[:, start:stop])
        scores = scores.astype(jnp.bfloat16)
        gv_ref[...] += dot(probs, grad[start:stop])
        gk_ref[...] += dot(scores, query[start:stop])
        gq_ref[:, start:stop] = dot(key, scores, ((0,), (0,)))
    grad_q = jnp.transpose(gq_ref[...])
    qk_sum = v_sum = 0.0
    for m in range(HEADS):
        own = slice(m * rows, (m + 1) * rows)
        normed, unit, scale = [
            early[i][m] if m < first else late[i][m - first] for i in range(3)
        ]
        raw = jnp.concatenate([grad_q[own], gk_ref[own, :]], axis=1) * HEAD_DIM ** (-0.5)
        back = scale * (raw - unit * (half_sums(raw * unit) / HEAD_DIM))
        back, grad_v = back.astype(jnp.bfloat16), gv_ref[own, :]
        mirrored = out_refs[DISTANCES.index(DISTANCES[m] ^ HEADS - 1)]
        mirrored[:PACKED, :] = low(pack(grad_v))
        mirrored[PACKED : PACKED + rows, :] = back
        qk_sum = qk_sum + dot(back, normed, ((0,), (0,)))
        v_sum = v_sum + dot(grad_v.astype(jnp.bfloat16), normed, ((0,), (0,)))
    step = qk_sum.shape[1] // HEADS
    for g in range(HEADS):
        own = slice(g * step, (g + 1) * step)
        held_ref[g] = low(jnp.concatenate([qk_sum[:, own], v_sum[:, own]], axis=0))
    for m, out_ref in enumerate(out_refs):
        out_ref[PACKED + rows :, :] = held_ref[me_ref[0] ^ DISTANCES[m]]


def turn_kernel(me_ref, *refs):
    slabs, out_refs, held_ref = refs[:HEADS], refs[HEADS:-1], refs[-1]
    start = slabs[0].shape[0] - 3 * HEAD_DIM
    for m, slab in enumerate(slabs):
        held_ref[me_ref[0] ^ DISTANCES[m]] = slab[start:, :]
    for i, out_ref in enumerate(out_refs):
        own = slice(i * HEAD_DIM, (i + 1) * HEAD_DIM)
        heads = [wide(held_ref[h, own, :]) for h in range(HEADS)]
        out_ref[0] = jnp.transpose(jnp.concatenate(heads, axis=0))


def second_sum_kernel(*refs):
    for second, got, out in zip(refs[0:2], refs[2:4], refs[-2:]):
        start = got.shape[0] - second.shape[0]
        out[...] = low(wide(second[...]) + wide(got[start:, :]))


def third_sum_kernel(*refs):
    for i in range(2):
        third, keep, got, more = [ref[...] for ref in refs[i:8:2]]
        size = third.shape[0]
        leaving, staying = refs[9 + i], refs[11 + i]
        leaving[...] = low(wide(third) + wide(got[size : 2 * size]) + wide(more[size:]))
        staying[...] = wide(keep) + wide(got[:size]) + wide(more[:size])


def last_sum_kernel(keep_a, keep_b, got_a, got_b, out_ref):
    for i, (keep, got) in enumerate(((keep_a, got_a), (keep_b, got_b))):
        width = keep.shape[1]
        out_ref[0, :, i * width : (i + 1) * width] = keep[...] + wide(got[...])


def input_kernel(me_ref, *refs):
    slabs, (wq_ref, wk_ref, wv_ref, *acts, up_ref, _, out_ref) = refs[:HEADS], refs[HEADS:-1]
    held_ref = refs[-1]
    rows = up_ref.shape[0]
    for m, slab in enumerate(slabs):
        held_ref[me_ref[0] ^ DISTANCES[m]] = slab[: PACKED + rows, :]
    unit, row_scale = normalize(joined(acts, up_ref.shape[1])[0])
    queries, keys, values = [], [], []
    for pair in range(HEADS // 2):
        even, odd = [wide(held_ref[2 * pair + i]) for i in range(2)]
        lower = low_lanes(even[PACKED:])
        queries.append(jnp.where(lower, even[PACKED:], swap(odd[PACKED:])))
        keys.append(jnp.where(lower, swap(even[PACKED:]), odd[PACKED:]))
        values += [unpack(even[:PACKED], rows), unpack(odd[:PACKED], rows)]
    total = 0.0
    for parts, ref in ((queries, wq_ref), (keys, wk_ref), (values, wv_ref)):
        left = jnp.concatenate(parts, axis=1).astype(jnp.bfloat16)
        total = total + dot(left, ref[...], ((1,), (1,)))
    total = total - unit * jnp.mean(total * unit, axis=-1, keepdims=True)
    out_ref[...] = (wide(up_ref[...]) + row_scale * total).astype(jnp.bfloat16)


def reorder_kernel(order_ref, rows_ref, out_ref):
    rows = rows_ref.shape[0]
    chosen = lax.broadcasted_iota(jnp.int32, (rows, rows), 0) == order_ref[...]
    chosen = low(jnp.where(chosen, 1.0, 0.0))
    out_ref[0] = low(dot(chosen, rows_ref[...], ((0,), (0,))))


def hop(block, distance):
    route = [(i, i ^ distance) for i in range(lax.axis_size("seq"))]
    return lax.ppermute(block, "seq", route)


def exchange(slabs):
    return [hop(slab, m) if m else slab for m, slab in zip(DISTANCES, slabs)]


def switch(slabs):
    return lax.all_to_all(slabs, "seq", split_axis=0, concat_axis=0, tiled=True)


def spread(block):
    middle = block.shape[1] // 2
    pieces = [block[:, :middle], block[:, middle:]]
    far = [hop(piece, 4) for piece in pieces]
    near, side = hop(block, 2), hop(block, 1)
    side_far = [hop(piece, 1) for piece in far]
    near_far = [hop(piece, 2) for piece in far]
    side_near = hop(near, 1)
    last = [hop(side_far[0], 2), hop(near_far[1], 1)]
    early = [block, side, near, *far, side_near, *side_far]
    return early, near_far, last


DISTANCES = (0, 1, 2, 4, 3, 5, 6, 7)


def wide(matrix):
    return matrix.astype(jnp.float32)


def low(matrix):
    return matrix.astype(jnp.bfloat16)


EARLY = 6


def head_shards(
    activations, incoming, w_query, w_key, w_value, w_out, block_ids, flip_order
):
    parts = lax.axis_size("seq")
    me = lax.axis_index("seq").astype(jnp.int32).reshape(1)
    field, upstream = activations[0], incoming[0]
    wq, wk, wv, wo = w_query[0], w_key[0], w_value[0], w_out[0]
    rows, width = field.shape
    inner = wq.shape[1]
    tokens = parts * rows
    f32 = jnp.float32

    def out(*dims, dtype=jnp.bfloat16):
        return jax.ShapeDtypeStruct(dims, dtype)

    first_blocks, near_far, mirrored = spread(field)
    order = me[0] ^ jnp.array(DISTANCES, jnp.int32)
    ids = jnp.take(block_ids.reshape(parts, rows), order, axis=0).reshape(tokens)
    (weight,) = call(
        select_kernel,
        1.5,
        [("s", me), ("a", wq), ("a", wk), ("a", wv)],
        [out(width, 3 * HEAD_DIM)],
        [pltpu.VMEM((width, 2 * HEAD_DIM), jnp.bfloat16)] * 3 + [pltpu.SemaphoreType.DMA((3,))],
    )
    pair = 2 * HEAD_DIM
    normed, unit, unit_scale, projected = call(
        project_kernel,
        2,
        [("v", block) for block in first_blocks] + [("v", weight)],
        [
            out(EARLY, rows, width),
            out(EARLY, rows, pair, dtype=f32),
            out(EARLY, rows, pair, dtype=f32),
            out(EARLY, rows, HEAD_DIM, dtype=f32),
        ],
    )
    late = parts - EARLY
    made = call(
        attend_kernel,
        5,
        [("s", me), ("v", unit), ("v", projected), ("v", weight)]
        + [("v", ids[None, :]), ("v", ids[:, None])]
        + [("v", block) for block in (*near_far, *mirrored)],
        [
            out(late, rows, width),
            out(late, rows, pair, dtype=f32),
            out(late, rows, pair, dtype=f32),
            out(tokens, tokens),
            out(tokens, pair),
            out(tokens, HEAD_DIM),
            out(HEAD_DIM, tokens, dtype=f32),
        ]
        + [out(parts, PACKED, 128)],
    )
    late_parts, (probs, qk, value, out_t), packed = made[:3], made[3:7], switch(made[7])
    scaled, grad_slabs, *terms = call(
        affine_kernel,
        3,
        [("s", me)] + [("v", x) for x in (packed, field, upstream, wo)],
        [out(rows, width), out(HEADS, PACKED, 128)]
        + [out(len(group) * HEAD_DIM, width) for order in ORDERS for group in order],
    )
    grad_slabs = switch(grad_slabs)
    grad_slabs, terms, scaled = lax.optimization_barrier((grad_slabs, terms, scaled))
    scaled = hop(scaled, parts - 1)
    first, second, third, keep = zip(terms[:4], terms[4:])
    got = [partner(part, "seq", bit) for bit, part in enumerate(first)]
    grads = call(
        backward_kernel,
        6,
        [("s", me)]
        + [("v", x) for x in (grad_slabs, probs, qk, value, out_t)]
        + [("v", x) for x in (normed, unit, unit_scale, *late_parts)],
        [out(PACKED + rows + 3 * HEAD_DIM, 128)] * parts,
        [
            pltpu.VMEM((tokens, HEAD_DIM), f32),
            pltpu.VMEM((tokens, HEAD_DIM), f32),
            pltpu.VMEM((HEAD_DIM, tokens), f32),
            pltpu.VMEM((HEADS, 3 * HEAD_DIM, 128), jnp.bfloat16),
        ],
    )
    slabs = exchange(grads)
    leaving = call(
        second_sum_kernel,
        1,
        [("v", x) for x in (*second, *got)] + [("a", x) for x in (*slabs[1:3], scaled)],
        [out(*second[0].shape)] * 2,
    )
    more = [partner(part, "seq", 1 - bit) for bit, part in enumerate(leaving)]
    *leaving, keep_a, keep_b = call(
        third_sum_kernel,
        2,
        [("v", x) for x in (*third, *keep, *got, *more)] + [("a", slabs[5])],
        [out(*third[0].shape)] * 2 + [out(*keep[0].shape, dtype=f32)] * 2,
    )
    rest = [partner(part, "seq", 2) for part in leaving]
    (grad_input,) = call(
        input_kernel,
        1.5,
        [("s", me)] + [("v", x) for x in (*slabs, wq, wk, wv, *mirrored, scaled)] + [("a", leaving[0])],
        [out(rows, width)],
        [pltpu.VMEM((HEADS, PACKED + rows, 128), jnp.bfloat16)],
    )
    grad_input, rest[0] = lax.optimization_barrier((grad_input, rest[0]))
    moved = to_previous(grad_input)
    (grad_out,) = call(
        last_sum_kernel,
        1,
        [("v", x) for x in (keep_a, keep_b, *rest)],
        [out(1, keep_a.shape[0], 2 * width, dtype=f32)],
    )
    grad_q, grad_k, grad_v = call(
        turn_kernel,
        1,
        [("s", me)] + [("v", x) for x in slabs],
        [out(1, width // parts, inner, dtype=f32)] * 3,
        [pltpu.VMEM((HEADS, 3 * HEAD_DIM, 128), jnp.bfloat16)],
    )
    (carry,) = call(
        reorder_kernel, 1, [("v", flip_order), ("v", moved)], [out(1, rows, width)]
    )
    return (carry, grad_q, grad_k, grad_v, grad_out)


def solution(mesh):
    shards = head_shards if mesh.shape["seq"] == HEADS else general_shards
    in_specs = (
        P("section", "seq", None),
        P("section", "seq", None),
        P("section", None, None),
        P("section", None, None),
        P("section", None, None),
        P("section", None, None),
        P(),
        P("section", None),
    )
    out_specs = (
        P("section", "seq", None),
        P("section", "seq", None),
        P("section", "seq", None),
        P("section", "seq", None),
        P("section", "seq", None),
    )
    return jax.shard_map(shards, mesh=mesh, in_specs=in_specs, out_specs=out_specs, check_vma=False)
```

```python
import jax
import jax.numpy as jnp
from jax import lax
from jax.experimental import pallas as pl
from jax.experimental.pallas import tpu as pltpu
from jax.sharding import PartitionSpec as P

HEADS = 8
HEAD_DIM = 64


EPSILON = 1e-06


def partner(block, axis, stride):
    count = lax.axis_size(axis)
    route = []
    for low in range(count):
        high = low | 1 << stride
        if high != low and high < count:
            route += [(low, high), (high, low)]
    return lax.ppermute(block, axis, route)


def shifted(block, axis, distance):
    devices = range(lax.axis_size(axis))
    route = [(i - distance, i) for i in devices if i - distance in devices]
    return lax.ppermute(block, axis, route)


def split_heads(matrix):
    return matrix.reshape(matrix.shape[0], HEADS, HEAD_DIM)


def head_major(matrix):
    return jnp.transpose(split_heads(matrix), (1, 0, 2))


def unit_heads(projected):
    parts = split_heads(projected)
    factor = lax.rsqrt(jnp.mean(parts * parts, axis=-1, keepdims=True) + EPSILON)
    return (parts * factor, factor)


def unit_back(grad_heads, unit, factor):
    return factor * (grad_heads - unit * jnp.mean(grad_heads * unit, axis=-1, keepdims=True))


def mirror(rows):
    for bit in range(lax.axis_size("seq").bit_length() - 1):
        rows = partner(rows, "seq", bit)
    return rows


def to_previous(rows):
    return shifted(rows, "section", -1)


def general_shards(activations, incoming, w_query, w_key, w_value, w_out, block_ids, flip_order):
    field = activations[0].astype(jnp.float32)
    upstream = incoming[0].astype(jnp.float32)
    weight_query = w_query[0]
    weight_key = w_key[0]
    weight_value = w_value[0]
    weight_out = w_out[0]
    flip_row = flip_order[0]
    rows = field.shape[0]
    width = field.shape[1]
    inner = weight_query.shape[1]
    scale = HEAD_DIM ** (-0.5)
    first = lax.axis_index("seq") * rows
    my_blocks = lax.dynamic_slice_in_dim(block_ids, first, rows)
    row_scale = lax.rsqrt(jnp.mean(field * field, axis=-1, keepdims=True) + EPSILON)
    unit_rows = field * row_scale
    normed = unit_rows.astype(jnp.bfloat16)
    query_raw = jnp.dot(normed, weight_query, preferred_element_type=jnp.float32)
    key_raw = jnp.dot(normed, weight_key, preferred_element_type=jnp.float32)
    values = jnp.dot(normed, weight_value, preferred_element_type=jnp.float32).astype(jnp.bfloat16)
    query_unit, query_scale = unit_heads(query_raw)
    key_unit, key_scale = unit_heads(key_raw)
    queries = query_unit.astype(jnp.bfloat16).reshape(rows, inner)
    keys = key_unit.astype(jnp.bfloat16).reshape(rows, inner)
    keys_all, values_all = (
        lax.all_gather(keys, "seq", axis=0, tiled=True),
        lax.all_gather(values, "seq", axis=0, tiled=True),
    )
    allowed = block_ids[None, :] <= my_blocks[:, None]
    query_heads = head_major(queries)
    key_heads_all = head_major(keys_all)
    value_heads_all = head_major(values_all)

    def probabilities(query_part, key_part):
        scores = jnp.dot(query_part, key_part.T, preferred_element_type=jnp.float32) * scale
        numerator = jnp.where(allowed, jnp.exp(scores), 0.0)
        denominator = jnp.sum(numerator, axis=-1, keepdims=True)
        return (numerator / denominator, denominator)

    def forward_head(operands):
        query_part, key_part, value_part = operands
        probs, denominator = probabilities(query_part, key_part)
        out_part = jnp.dot(
            probs.astype(jnp.bfloat16), value_part, preferred_element_type=jnp.float32
        ).astype(jnp.bfloat16)
        return (out_part, denominator[:, 0])

    heads_out, denominators = lax.map(forward_head, (query_heads, key_heads_all, value_heads_all))
    attended = jnp.transpose(heads_out, (1, 0, 2)).reshape(rows, inner)
    affine = jnp.dot(attended, weight_out, preferred_element_type=jnp.float32)
    shift_part = affine[:, :width]
    log_scale = affine[:, width:]
    factor = jnp.exp(-log_scale)
    latent = (field - shift_part) * factor
    grad_affine = jnp.concatenate([-upstream * factor, 1.0 - upstream * latent], axis=-1).astype(
        jnp.bfloat16
    )
    out_term = jnp.dot(attended.T, grad_affine, preferred_element_type=jnp.float32)
    grad_attn = jnp.dot(grad_affine, weight_out.T, preferred_element_type=jnp.float32).astype(
        jnp.bfloat16
    )
    correction = jnp.sum(
        split_heads(grad_attn.astype(jnp.float32)) * split_heads(attended.astype(jnp.float32)),
        axis=-1,
    )
    grad_heads = head_major(grad_attn)
    correction_heads = jnp.transpose(correction)[:, :, None]

    def backward_head(operands):
        query_part, key_part, value_part, grad_part, corr_part = operands
        probs, denominator = probabilities(query_part, key_part)
        grad_probs = jnp.dot(grad_part, value_part.T, preferred_element_type=jnp.float32)
        grad_scores = (probs * (grad_probs - corr_part)).astype(jnp.bfloat16)
        grad_qpart = jnp.dot(grad_scores, key_part, preferred_element_type=jnp.float32) * scale
        grad_kpart = jnp.dot(grad_scores.T, query_part, preferred_element_type=jnp.float32) * scale
        grad_vpart = jnp.dot(
            probs.astype(jnp.bfloat16).T, grad_part, preferred_element_type=jnp.float32
        )
        return (grad_qpart, grad_kpart, grad_vpart)

    grad_qheads, grad_kall, grad_vall = lax.map(
        backward_head, (query_heads, key_heads_all, value_heads_all, grad_heads, correction_heads)
    )
    key_terms = jnp.transpose(grad_kall, (1, 0, 2)).reshape(-1, inner)
    value_terms = jnp.transpose(grad_vall, (1, 0, 2)).reshape(-1, inner)
    grad_kunit, grad_vsum = (
        lax.psum_scatter(
            key_terms.astype(jnp.bfloat16), "seq", scatter_dimension=0, tiled=True
        ).astype(jnp.float32),
        lax.psum_scatter(
            value_terms.astype(jnp.bfloat16), "seq", scatter_dimension=0, tiled=True
        ).astype(jnp.float32),
    )
    grad_queries = (
        unit_back(jnp.transpose(grad_qheads, (1, 0, 2)), query_unit, query_scale)
        .reshape(rows, inner)
        .astype(jnp.bfloat16)
    )
    grad_keys = (
        unit_back(split_heads(grad_kunit), key_unit, key_scale)
        .reshape(rows, inner)
        .astype(jnp.bfloat16)
    )
    grad_values = grad_vsum.astype(jnp.bfloat16)
    query_term = jnp.dot(normed.T, grad_queries, preferred_element_type=jnp.float32)
    key_term = jnp.dot(normed.T, grad_keys, preferred_element_type=jnp.float32)
    value_term = jnp.dot(normed.T, grad_values, preferred_element_type=jnp.float32)
    sums = (
        lax.psum_scatter(
            query_term.astype(jnp.bfloat16), "seq", scatter_dimension=0, tiled=True
        ).astype(jnp.float32),
        lax.psum_scatter(
            key_term.astype(jnp.bfloat16), "seq", scatter_dimension=0, tiled=True
        ).astype(jnp.float32),
        lax.psum_scatter(
            value_term.astype(jnp.bfloat16), "seq", scatter_dimension=0, tiled=True
        ).astype(jnp.float32),
        lax.psum_scatter(
            out_term.astype(jnp.bfloat16), "seq", scatter_dimension=0, tiled=True
        ).astype(jnp.float32),
    )
    grad_normed = jnp.dot(grad_queries, weight_query.T, preferred_element_type=jnp.float32)
    grad_normed = grad_normed + jnp.dot(grad_keys, weight_key.T, preferred_element_type=jnp.float32)
    grad_normed = grad_normed + jnp.dot(
        grad_values, weight_value.T, preferred_element_type=jnp.float32
    )
    grad_input = upstream * factor + row_scale * (
        grad_normed - unit_rows * jnp.mean(grad_normed * unit_rows, axis=-1, keepdims=True)
    )
    grad_input = grad_input.astype(jnp.bfloat16)
    moved = mirror(to_previous(grad_input))
    carry = jnp.take(moved, flip_row, axis=0)
    return (carry[None], sums[0][None], sums[1][None], sums[2][None], sums[3][None])


PACKED = 80


def call(kernel, microseconds, ins, outs, scratch=()):
    spaces = {"s": pltpu.SMEM, "v": pltpu.VMEM, "a": pl.ANY}
    places, operands = zip(*ins)
    return pl.pallas_call(
        kernel,
        out_shape=tuple(outs),
        in_specs=[pl.BlockSpec(memory_space=spaces[place]) for place in places],
        out_specs=(pl.BlockSpec(memory_space=pltpu.VMEM),) * len(outs),
        scratch_shapes=list(scratch),
        compiler_params=pltpu.CompilerParams(vmem_limit_bytes=14 * 2**20),
        cost_estimate=pl.CostEstimate(
            flops=int(microseconds * 1e9), bytes_accessed=1024, transcendentals=0
        ),
    )(*operands)


def dot(left, right, contract=((1,), (0,))):
    return lax.dot_general(left, right, (contract, ((), ())), preferred_element_type=jnp.float32)


def low_lanes(block):
    return lax.broadcasted_iota(jnp.int32, block.shape, len(block.shape) - 1) < HEAD_DIM


def swap(block):
    return pltpu.roll(block, HEAD_DIM, 1)


def half_sums(block):
    low = low_lanes(block)
    first = jnp.sum(jnp.where(low, block, 0.0), axis=-1, keepdims=True)
    second = jnp.sum(jnp.where(low, 0.0, block), axis=-1, keepdims=True)
    return jnp.where(low, first, second)


def pack(block):
    rows = block.shape[0]
    return jnp.concatenate([block[:PACKED], block[rows - PACKED :]], axis=1)


def unpack(slab, rows):
    right = swap(slab)[2 * PACKED - rows :, :HEAD_DIM]
    return jnp.concatenate([slab[:, :HEAD_DIM], right], axis=0)


def normalize(block):
    field = block.astype(jnp.float32)
    row_scale = lax.rsqrt(jnp.mean(field * field, axis=-1, keepdims=True) + EPSILON)
    return field * row_scale, row_scale


def project(block, weight):
    normed = normalize(block)[0].astype(jnp.bfloat16)
    product = dot(normed, weight)
    raw, value = product[:, : 2 * HEAD_DIM], product[:, 2 * HEAD_DIM :]
    scale = lax.rsqrt(half_sums(raw * raw) / HEAD_DIM + EPSILON)
    return normed, raw * scale, scale, value


def select_kernel(me_ref, wq_ref, wk_ref, wv_ref, out_ref, *scratch):
    held, semaphores = scratch[:3], scratch[3]
    odd = lax.rem(me_ref[0], 2) == 1
    pair = pl.multiple_of(lax.div(me_ref[0], 2) * 2 * HEAD_DIM, 2 * HEAD_DIM)
    copies = [
        pltpu.make_async_copy(ref.at[:, pl.ds(pair, 2 * HEAD_DIM)], kept, semaphores.at[i])
        for i, (ref, kept) in enumerate(zip((wq_ref, wk_ref, wv_ref), held))
    ]
    for copy in copies:
        copy.start()
    for copy in copies:
        copy.wait()
    q, k, v = [wide(kept[...]) for kept in held]
    lower = low_lanes(q)
    qk = jnp.where(lower, jnp.where(odd, swap(q), q), jnp.where(odd, k, swap(k)))
    out_ref[:, : 2 * HEAD_DIM] = low(qk)
    out_ref[:, 2 * HEAD_DIM :] = low(jnp.where(odd, swap(v), v)[:, :HEAD_DIM])


def joined(refs, width):
    pieces, blocks = [], []
    for ref in refs:
        pieces.append(ref[...])
        if sum(piece.shape[1] for piece in pieces) == width:
            blocks.append(jnp.concatenate(pieces, axis=1) if len(pieces) > 1 else pieces[0])
            pieces = []
    return blocks


def project_kernel(*refs):
    blocks, (weight_ref, normed_ref, unit_ref, scale_ref, value_ref) = refs[:-5], refs[-5:]
    for m, block in enumerate(joined(blocks, normed_ref.shape[2])):
        made = project(block, weight_ref[...])
        for ref, part in zip((normed_ref, unit_ref, scale_ref, value_ref), made):
            ref[m] = part.astype(ref.dtype)


TILE = 256


def tiles(tokens):
    starts = range(0, tokens, TILE)
    return [(start, min(tokens, start + TILE)) for start in starts]


def attend_kernel(
    me_ref, unit_ref, value_ref, weight_ref, row_ids, column_ids, *refs
):
    pieces, out_refs = refs[:-8], refs[-8:]
    normed_ref, late_unit, late_scale, prob_ref, qk_ref, v_ref, out_t_ref = out_refs[:7]
    early, rows = unit_ref.shape[:2]
    units = [unit_ref[m] for m in range(early)]
    values = [value_ref[m] for m in range(early)]
    for m, block in enumerate(joined(pieces, normed_ref.shape[2])):
        normed, unit, scale, value = project(block, weight_ref[...])
        normed_ref[m], late_unit[m], late_scale[m] = normed, unit, scale
        units.append(unit)
        values.append(value)
    parts = early + normed_ref.shape[0]
    tokens = parts * rows
    qk = jnp.concatenate(units, axis=0).astype(jnp.bfloat16)
    value = jnp.concatenate(values, axis=0).astype(jnp.bfloat16)
    qk_ref[...] = qk
    v_ref[...] = value
    query, key = qk[:, :HEAD_DIM] * HEAD_DIM ** (-0.5), qk[:, HEAD_DIM:]
    for start, stop in tiles(tokens):
        scores = dot(key, query[start:stop], ((1,), (1,)))
        allowed = column_ids[...] <= row_ids[:, start:stop]
        numerator = jnp.where(allowed, jnp.exp(scores), 0.0)
        probs = numerator * (1.0 / jnp.sum(numerator, axis=0, keepdims=True))
        probs = probs.astype(jnp.bfloat16)
        prob_ref[:, start:stop] = probs
        out_t = dot(value, probs, ((0,), (0,)))
        out_t_ref[:, start:stop] = out_t.astype(jnp.bfloat16).astype(jnp.float32)
    out = jnp.transpose(out_t_ref[...])
    for m, distance in enumerate(DISTANCES):
        out_refs[7][me_ref[0] ^ distance] = low(pack(out[m * rows : (m + 1) * rows]))


def affine_kernel(me_ref, slab_ref, act_ref, inc_ref, w_ref, up_ref, out_ref, *term_refs):
    rows, width = act_ref.shape
    columns = [unpack(wide(slab_ref[h]), rows) for h in range(HEADS)]
    attended = low(jnp.concatenate(columns, axis=1))
    factor = jnp.exp(-dot(attended, w_ref[:, width:]))
    scaled = inc_ref[...].astype(jnp.float32) * factor
    up_ref[...] = low(scaled)
    shift_part = dot(attended, w_ref[:, :width])
    latent_part = scaled * (act_ref[...].astype(jnp.float32) - shift_part)
    grad_affine = jnp.concatenate([-scaled, 1.0 - latent_part], axis=1).astype(jnp.bfloat16)
    grad = dot(grad_affine, w_ref[...], ((1,), (1,)))
    for h in range(HEADS):
        out_ref[h] = low(pack(grad[:, h * HEAD_DIM : (h + 1) * HEAD_DIM]))
    columns = [unpack(wide(slab_ref[me_ref[0] ^ m]), rows) for m in range(HEADS)]
    for half, order in enumerate(ORDERS):
        right = grad_affine[:, half * width : (half + 1) * width]
        for term_ref, group in zip(term_refs[4 * half : 4 * half + 4], order):
            left = low(jnp.concatenate([columns[m] for m in group], axis=1))
            term_ref[...] = low(dot(left, right, ((0,), (0,))))


ORDERS = (((1, 5, 3, 7), (2, 6), (4,), (0,)), ((2, 6, 3, 7), (1, 5), (4,), (0,)))


def backward_kernel(me_ref, slab_ref, prob_ref, qk_ref, v_ref, out_t_ref, *refs):
    early, late, out_refs = refs[:3], refs[3:6], refs[6:-4]
    gk_ref, gv_ref, gq_ref, held_ref = refs[-4:]
    first, rows = early[0].shape[:2]
    slabs = [wide(slab_ref[me_ref[0] ^ distance]) for distance in DISTANCES]
    grad_f = jnp.concatenate([unpack(slab, rows) for slab in slabs], axis=0)
    grad = grad_f.astype(jnp.bfloat16)
    tokens = grad_f.shape[0]
    grad_t = jnp.transpose(grad_f)
    correction = jnp.sum(grad_t * out_t_ref[...], axis=0, keepdims=True)
    grad_t = grad_t.astype(jnp.bfloat16)
    qk, value = qk_ref[...], v_ref[...]
    query, key = qk[:, :HEAD_DIM], qk[:, HEAD_DIM:]
    gk_ref[...] = jnp.zeros_like(gk_ref)
    gv_ref[...] = jnp.zeros_like(gv_ref)
    for start, stop in tiles(tokens):
        probs = prob_ref[:, start:stop]
        grad_probs = dot(value, grad_t[:, start:stop])
        scores = probs.astype(jnp.float32) * (grad_probs - correction[:, start:stop])
        scores = scores.astype(jnp.bfloat16)
        gv_ref[...] += dot(probs, grad[start:stop])
        gk_ref[...] += dot(scores, query[start:stop])
        gq_ref[:, start:stop] = dot(key, scores, ((0,), (0,)))
    grad_q = jnp.transpose(gq_ref[...])
    qk_sum = v_sum = 0.0
    for m in range(HEADS):
        own = slice(m * rows, (m + 1) * rows)
        normed, unit, scale = [
            early[i][m] if m < first else late[i][m - first] for i in range(3)
        ]
        raw = jnp.concatenate([grad_q[own], gk_ref[own, :]], axis=1) * HEAD_DIM ** (-0.5)
        back = scale * (raw - unit * (half_sums(raw * unit) / HEAD_DIM))
        back, grad_v = back.astype(jnp.bfloat16), gv_ref[own, :]
        mirrored = out_refs[DISTANCES.index(DISTANCES[m] ^ HEADS - 1)]
        mirrored[:PACKED, :] = low(pack(grad_v))
        mirrored[PACKED : PACKED + rows, :] = back
        qk_sum = qk_sum + dot(back, normed, ((0,), (0,)))
        v_sum = v_sum + dot(grad_v.astype(jnp.bfloat16), normed, ((0,), (0,)))
    step = qk_sum.shape[1] // HEADS
    for g in range(HEADS):
        own = slice(g * step, (g + 1) * step)
        held_ref[g] = low(jnp.concatenate([qk_sum[:, own], v_sum[:, own]], axis=0))
    for m, out_ref in enumerate(out_refs):
        out_ref[PACKED + rows :, :] = held_ref[me_ref[0] ^ DISTANCES[m]]


def turn_kernel(me_ref, *refs):
    slabs, out_refs, held_ref = refs[:HEADS], refs[HEADS + 2 : -1], refs[-1]
    start = slabs[0].shape[0] - 3 * HEAD_DIM
    for m, slab in enumerate(slabs):
        held_ref[me_ref[0] ^ DISTANCES[m]] = slab[start:, :]
    for i, out_ref in enumerate(out_refs):
        own = slice(i * HEAD_DIM, (i + 1) * HEAD_DIM)
        heads = [wide(held_ref[h, own, :]) for h in range(HEADS)]
        out_ref[0] = jnp.transpose(jnp.concatenate(heads, axis=0))


def second_sum_kernel(*refs):
    for second, got, out in zip(refs[0:2], refs[2:4], refs[-2:]):
        start = got.shape[0] - second.shape[0]
        out[...] = low(wide(second[...]) + wide(got[start:, :]))


def third_sum_kernel(*refs):
    for i in range(2):
        third, keep, got, more = [ref[...] for ref in refs[i:8:2]]
        size = third.shape[0]
        leaving, staying = refs[9 + i], refs[11 + i]
        leaving[...] = low(wide(third) + wide(got[size : 2 * size]) + wide(more[size:]))
        staying[...] = wide(keep) + wide(got[:size]) + wide(more[:size])


def last_sum_kernel(keep_a, keep_b, got_a, got_b, out_ref):
    for i, (keep, got) in enumerate(((keep_a, got_a), (keep_b, got_b))):
        width = keep.shape[1]
        out_ref[0, :, i * width : (i + 1) * width] = keep[...] + wide(got[...])


def input_kernel(me_ref, *refs):
    slabs, (wq_ref, wk_ref, wv_ref, *acts, up_ref, _, out_ref) = refs[:HEADS], refs[HEADS:-1]
    held_ref = refs[-1]
    rows = up_ref.shape[0]
    for m, slab in enumerate(slabs):
        held_ref[me_ref[0] ^ DISTANCES[m]] = slab[: PACKED + rows, :]
    unit, row_scale = normalize(joined(acts, up_ref.shape[1])[0])
    queries, keys, values = [], [], []
    for pair in range(HEADS // 2):
        even, odd = [wide(held_ref[2 * pair + i]) for i in range(2)]
        lower = low_lanes(even[PACKED:])
        queries.append(jnp.where(lower, even[PACKED:], swap(odd[PACKED:])))
        keys.append(jnp.where(lower, swap(even[PACKED:]), odd[PACKED:]))
        values += [unpack(even[:PACKED], rows), unpack(odd[:PACKED], rows)]
    total = 0.0
    for parts, ref in ((queries, wq_ref), (keys, wk_ref), (values, wv_ref)):
        left = jnp.concatenate(parts, axis=1).astype(jnp.bfloat16)
        total = total + dot(left, ref[...], ((1,), (1,)))
    total = total - unit * jnp.mean(total * unit, axis=-1, keepdims=True)
    out_ref[...] = (wide(up_ref[...]) + row_scale * total).astype(jnp.bfloat16)


def reorder_kernel(order_ref, rows_ref, out_ref):
    rows = rows_ref.shape[0]
    chosen = lax.broadcasted_iota(jnp.int32, (rows, rows), 0) == order_ref[...]
    chosen = low(jnp.where(chosen, 1.0, 0.0))
    out_ref[0] = low(dot(chosen, rows_ref[...], ((0,), (0,))))


def hop(block, distance):
    route = [(i, i ^ distance) for i in range(lax.axis_size("seq"))]
    return lax.ppermute(block, "seq", route)


def exchange(slabs):
    return [hop(slab, m) if m else slab for m, slab in zip(DISTANCES, slabs)]


def switch(slabs):
    return lax.all_to_all(slabs, "seq", split_axis=0, concat_axis=0, tiled=True)


def spread(block, weight):
    middle = block.shape[1] // 2
    pieces = [block[:, :middle], block[:, middle:]]
    far = [hop(piece, 4) for piece in pieces]
    near, side = hop(block, 2), hop(block, 1)
    near, weight = lax.optimization_barrier((near, weight))
    side_far = [hop(piece, 1) for piece in far]
    near_far = [hop(piece, 2) for piece in far]
    side_near = hop(near, 1)
    last = [hop(side_far[0], 2), hop(near_far[1], 1)]
    early = [block, side, near, *far, side_near, *side_far]
    return early, near_far, last, weight


DISTANCES = (0, 1, 2, 4, 3, 5, 6, 7)


def wide(matrix):
    return matrix.astype(jnp.float32)


def low(matrix):
    return matrix.astype(jnp.bfloat16)


EARLY = 6


def head_shards(
    activations, incoming, w_query, w_key, w_value, w_out, block_ids, flip_order
):
    parts = lax.axis_size("seq")
    me = lax.axis_index("seq").astype(jnp.int32).reshape(1)
    field, upstream = activations[0], incoming[0]
    wq, wk, wv, wo = w_query[0], w_key[0], w_value[0], w_out[0]
    rows, width = field.shape
    inner = wq.shape[1]
    tokens = parts * rows
    f32 = jnp.float32

    def out(*dims, dtype=jnp.bfloat16):
        return jax.ShapeDtypeStruct(dims, dtype)

    order = me[0] ^ jnp.array(DISTANCES, jnp.int32)
    ids = jnp.take(block_ids.reshape(parts, rows), order, axis=0).reshape(tokens)
    (weight,) = call(
        select_kernel,
        1.5,
        [("s", me), ("a", wq), ("a", wk), ("a", wv)],
        [out(width, 3 * HEAD_DIM)],
        [pltpu.VMEM((width, 2 * HEAD_DIM), jnp.bfloat16)] * 3 + [pltpu.SemaphoreType.DMA((3,))],
    )
    first_blocks, near_far, mirrored, weight = spread(field, weight)
    pair = 2 * HEAD_DIM
    normed, unit, unit_scale, projected = call(
        project_kernel,
        2,
        [("v", block) for block in first_blocks] + [("v", weight)],
        [
            out(EARLY, rows, width),
            out(EARLY, rows, pair, dtype=f32),
            out(EARLY, rows, pair, dtype=f32),
            out(EARLY, rows, HEAD_DIM, dtype=f32),
        ],
    )
    late = parts - EARLY
    made = call(
        attend_kernel,
        5,
        [("s", me), ("v", unit), ("v", projected), ("v", weight)]
        + [("v", ids[None, :]), ("v", ids[:, None])]
        + [("v", block) for block in (*near_far, *mirrored)],
        [
            out(late, rows, width),
            out(late, rows, pair, dtype=f32),
            out(late, rows, pair, dtype=f32),
            out(tokens, tokens),
            out(tokens, pair),
            out(tokens, HEAD_DIM),
            out(HEAD_DIM, tokens, dtype=f32),
        ]
        + [out(parts, PACKED, 128)],
    )
    late_parts, (probs, qk, value, out_t), packed = made[:3], made[3:7], switch(made[7])
    scaled, grad_slabs, *terms = call(
        affine_kernel,
        3,
        [("s", me)] + [("v", x) for x in (packed, field, upstream, wo)],
        [out(rows, width), out(HEADS, PACKED, 128)]
        + [out(len(group) * HEAD_DIM, width) for order in ORDERS for group in order],
    )
    grad_slabs = switch(grad_slabs)
    grad_slabs, terms, scaled = lax.optimization_barrier((grad_slabs, terms, scaled))
    scaled = hop(scaled, parts - 1)
    first, second, third, keep = zip(terms[:4], terms[4:])
    got = [partner(part, "seq", bit) for bit, part in enumerate(first)]
    grads = call(
        backward_kernel,
        6,
        [("s", me)]
        + [("v", x) for x in (grad_slabs, probs, qk, value, out_t)]
        + [("v", x) for x in (normed, unit, unit_scale, *late_parts)],
        [out(PACKED + rows + 3 * HEAD_DIM, 128)] * parts,
        [
            pltpu.VMEM((tokens, HEAD_DIM), f32),
            pltpu.VMEM((tokens, HEAD_DIM), f32),
            pltpu.VMEM((HEAD_DIM, tokens), f32),
            pltpu.VMEM((HEADS, 3 * HEAD_DIM, 128), jnp.bfloat16),
        ],
    )
    slabs = exchange(grads)
    leaving = call(
        second_sum_kernel,
        1,
        [("v", x) for x in (*second, *got)] + [("a", x) for x in (*slabs[1:3], scaled)],
        [out(*second[0].shape)] * 2,
    )
    more = [partner(part, "seq", 1 - bit) for bit, part in enumerate(leaving)]
    *leaving, keep_a, keep_b = call(
        third_sum_kernel,
        2,
        [("v", x) for x in (*third, *keep, *got, *more)] + [("a", slabs[5])],
        [out(*third[0].shape)] * 2 + [out(*keep[0].shape, dtype=f32)] * 2,
    )
    rest = [partner(part, "seq", 2) for part in leaving]
    (grad_input,) = call(
        input_kernel,
        1.5,
        [("s", me)] + [("v", x) for x in (*slabs, wq, wk, wv, *mirrored, scaled)] + [("a", leaving[0])],
        [out(rows, width)],
        [pltpu.VMEM((HEADS, PACKED + rows, 128), jnp.bfloat16)],
    )
    moved = to_previous(grad_input)
    (grad_out,) = call(
        last_sum_kernel,
        2,
        [("v", x) for x in (keep_a, keep_b, *rest)],
        [out(1, keep_a.shape[0], 2 * width, dtype=f32)],
    )
    grad_q, grad_k, grad_v = call(
        turn_kernel,
        3,
        [("s", me)] + [("v", x) for x in slabs] + [("a", x) for x in rest],
        [out(1, width // parts, inner, dtype=f32)] * 3,
        [pltpu.VMEM((HEADS, 3 * HEAD_DIM, 128), jnp.bfloat16)],
    )
    (carry,) = call(
        reorder_kernel, 1, [("v", flip_order), ("v", moved)], [out(1, rows, width)]
    )
    return (carry, grad_q, grad_k, grad_v, grad_out)


def solution(mesh):
    shards = head_shards if mesh.shape["seq"] == HEADS else general_shards
    in_specs = (
        P("section", "seq", None),
        P("section", "seq", None),
        P("section", None, None),
        P("section", None, None),
        P("section", None, None),
        P("section", None, None),
        P(),
        P("section", None),
    )
    out_specs = (
        P("section", "seq", None),
        P("section", "seq", None),
        P("section", "seq", None),
        P("section", "seq", None),
        P("section", "seq", None),
    )
    return jax.shard_map(shards, mesh=mesh, in_specs=in_specs, out_specs=out_specs, check_vma=False)
```

```python
import jax
import jax.numpy as jnp
from jax import lax
from jax.experimental import pallas as pl
from jax.experimental.pallas import tpu as pltpu
from jax.sharding import PartitionSpec as P

HEADS = 8
HEAD_DIM = 64


EPSILON = 1e-06


def partner(block, axis, stride):
    count = lax.axis_size(axis)
    route = []
    for low in range(count):
        high = low | 1 << stride
        if high != low and high < count:
            route += [(low, high), (high, low)]
    return lax.ppermute(block, axis, route)


def shifted(block, axis, distance):
    devices = range(lax.axis_size(axis))
    route = [(i - distance, i) for i in devices if i - distance in devices]
    return lax.ppermute(block, axis, route)


def split_heads(matrix):
    return matrix.reshape(matrix.shape[0], HEADS, HEAD_DIM)


def head_major(matrix):
    return jnp.transpose(split_heads(matrix), (1, 0, 2))


def unit_heads(projected):
    parts = split_heads(projected)
    factor = lax.rsqrt(jnp.mean(parts * parts, axis=-1, keepdims=True) + EPSILON)
    return (parts * factor, factor)


def unit_back(grad_heads, unit, factor):
    return factor * (grad_heads - unit * jnp.mean(grad_heads * unit, axis=-1, keepdims=True))


def mirror(rows):
    for bit in range(lax.axis_size("seq").bit_length() - 1):
        rows = partner(rows, "seq", bit)
    return rows


def to_previous(rows):
    return shifted(rows, "section", -1)


def general_shards(activations, incoming, w_query, w_key, w_value, w_out, block_ids, flip_order):
    field = activations[0].astype(jnp.float32)
    upstream = incoming[0].astype(jnp.float32)
    weight_query = w_query[0]
    weight_key = w_key[0]
    weight_value = w_value[0]
    weight_out = w_out[0]
    flip_row = flip_order[0]
    rows = field.shape[0]
    width = field.shape[1]
    inner = weight_query.shape[1]
    scale = HEAD_DIM ** (-0.5)
    first = lax.axis_index("seq") * rows
    my_blocks = lax.dynamic_slice_in_dim(block_ids, first, rows)
    row_scale = lax.rsqrt(jnp.mean(field * field, axis=-1, keepdims=True) + EPSILON)
    unit_rows = field * row_scale
    normed = unit_rows.astype(jnp.bfloat16)
    query_raw = jnp.dot(normed, weight_query, preferred_element_type=jnp.float32)
    key_raw = jnp.dot(normed, weight_key, preferred_element_type=jnp.float32)
    values = jnp.dot(normed, weight_value, preferred_element_type=jnp.float32).astype(jnp.bfloat16)
    query_unit, query_scale = unit_heads(query_raw)
    key_unit, key_scale = unit_heads(key_raw)
    queries = query_unit.astype(jnp.bfloat16).reshape(rows, inner)
    keys = key_unit.astype(jnp.bfloat16).reshape(rows, inner)
    keys_all, values_all = (
        lax.all_gather(keys, "seq", axis=0, tiled=True),
        lax.all_gather(values, "seq", axis=0, tiled=True),
    )
    allowed = block_ids[None, :] <= my_blocks[:, None]
    query_heads = head_major(queries)
    key_heads_all = head_major(keys_all)
    value_heads_all = head_major(values_all)

    def probabilities(query_part, key_part):
        scores = jnp.dot(query_part, key_part.T, preferred_element_type=jnp.float32) * scale
        numerator = jnp.where(allowed, jnp.exp(scores), 0.0)
        denominator = jnp.sum(numerator, axis=-1, keepdims=True)
        return (numerator / denominator, denominator)

    def forward_head(operands):
        query_part, key_part, value_part = operands
        probs, denominator = probabilities(query_part, key_part)
        out_part = jnp.dot(
            probs.astype(jnp.bfloat16), value_part, preferred_element_type=jnp.float32
        ).astype(jnp.bfloat16)
        return (out_part, denominator[:, 0])

    heads_out, denominators = lax.map(forward_head, (query_heads, key_heads_all, value_heads_all))
    attended = jnp.transpose(heads_out, (1, 0, 2)).reshape(rows, inner)
    affine = jnp.dot(attended, weight_out, preferred_element_type=jnp.float32)
    shift_part = affine[:, :width]
    log_scale = affine[:, width:]
    factor = jnp.exp(-log_scale)
    latent = (field - shift_part) * factor
    grad_affine = jnp.concatenate([-upstream * factor, 1.0 - upstream * latent], axis=-1).astype(
        jnp.bfloat16
    )
    out_term = jnp.dot(attended.T, grad_affine, preferred_element_type=jnp.float32)
    grad_attn = jnp.dot(grad_affine, weight_out.T, preferred_element_type=jnp.float32).astype(
        jnp.bfloat16
    )
    correction = jnp.sum(
        split_heads(grad_attn.astype(jnp.float32)) * split_heads(attended.astype(jnp.float32)),
        axis=-1,
    )
    grad_heads = head_major(grad_attn)
    correction_heads = jnp.transpose(correction)[:, :, None]

    def backward_head(operands):
        query_part, key_part, value_part, grad_part, corr_part = operands
        probs, denominator = probabilities(query_part, key_part)
        grad_probs = jnp.dot(grad_part, value_part.T, preferred_element_type=jnp.float32)
        grad_scores = (probs * (grad_probs - corr_part)).astype(jnp.bfloat16)
        grad_qpart = jnp.dot(grad_scores, key_part, preferred_element_type=jnp.float32) * scale
        grad_kpart = jnp.dot(grad_scores.T, query_part, preferred_element_type=jnp.float32) * scale
        grad_vpart = jnp.dot(
            probs.astype(jnp.bfloat16).T, grad_part, preferred_element_type=jnp.float32
        )
        return (grad_qpart, grad_kpart, grad_vpart)

    grad_qheads, grad_kall, grad_vall = lax.map(
        backward_head, (query_heads, key_heads_all, value_heads_all, grad_heads, correction_heads)
    )
    key_terms = jnp.transpose(grad_kall, (1, 0, 2)).reshape(-1, inner)
    value_terms = jnp.transpose(grad_vall, (1, 0, 2)).reshape(-1, inner)
    grad_kunit, grad_vsum = (
        lax.psum_scatter(
            key_terms.astype(jnp.bfloat16), "seq", scatter_dimension=0, tiled=True
        ).astype(jnp.float32),
        lax.psum_scatter(
            value_terms.astype(jnp.bfloat16), "seq", scatter_dimension=0, tiled=True
        ).astype(jnp.float32),
    )
    grad_queries = (
        unit_back(jnp.transpose(grad_qheads, (1, 0, 2)), query_unit, query_scale)
        .reshape(rows, inner)
        .astype(jnp.bfloat16)
    )
    grad_keys = (
        unit_back(split_heads(grad_kunit), key_unit, key_scale)
        .reshape(rows, inner)
        .astype(jnp.bfloat16)
    )
    grad_values = grad_vsum.astype(jnp.bfloat16)
    query_term = jnp.dot(normed.T, grad_queries, preferred_element_type=jnp.float32)
    key_term = jnp.dot(normed.T, grad_keys, preferred_element_type=jnp.float32)
    value_term = jnp.dot(normed.T, grad_values, preferred_element_type=jnp.float32)
    sums = (
        lax.psum_scatter(
            query_term.astype(jnp.bfloat16), "seq", scatter_dimension=0, tiled=True
        ).astype(jnp.float32),
        lax.psum_scatter(
            key_term.astype(jnp.bfloat16), "seq", scatter_dimension=0, tiled=True
        ).astype(jnp.float32),
        lax.psum_scatter(
            value_term.astype(jnp.bfloat16), "seq", scatter_dimension=0, tiled=True
        ).astype(jnp.float32),
        lax.psum_scatter(
            out_term.astype(jnp.bfloat16), "seq", scatter_dimension=0, tiled=True
        ).astype(jnp.float32),
    )
    grad_normed = jnp.dot(grad_queries, weight_query.T, preferred_element_type=jnp.float32)
    grad_normed = grad_normed + jnp.dot(grad_keys, weight_key.T, preferred_element_type=jnp.float32)
    grad_normed = grad_normed + jnp.dot(
        grad_values, weight_value.T, preferred_element_type=jnp.float32
    )
    grad_input = upstream * factor + row_scale * (
        grad_normed - unit_rows * jnp.mean(grad_normed * unit_rows, axis=-1, keepdims=True)
    )
    grad_input = grad_input.astype(jnp.bfloat16)
    moved = mirror(to_previous(grad_input))
    carry = jnp.take(moved, flip_row, axis=0)
    return (carry[None], sums[0][None], sums[1][None], sums[2][None], sums[3][None])


PACKED = 80


def call(kernel, microseconds, ins, outs, scratch=()):
    spaces = {"s": pltpu.SMEM, "v": pltpu.VMEM, "a": pl.ANY}
    places, operands = zip(*ins)
    return pl.pallas_call(
        kernel,
        out_shape=tuple(outs),
        in_specs=[pl.BlockSpec(memory_space=spaces[place]) for place in places],
        out_specs=(pl.BlockSpec(memory_space=pltpu.VMEM),) * len(outs),
        scratch_shapes=list(scratch),
        compiler_params=pltpu.CompilerParams(vmem_limit_bytes=14 * 2**20),
        cost_estimate=pl.CostEstimate(
            flops=int(microseconds * 1e9), bytes_accessed=1024, transcendentals=0
        ),
    )(*operands)


def dot(left, right, contract=((1,), (0,))):
    return lax.dot_general(left, right, (contract, ((), ())), preferred_element_type=jnp.float32)


def low_lanes(block):
    return lax.broadcasted_iota(jnp.int32, block.shape, len(block.shape) - 1) < HEAD_DIM


def swap(block):
    return pltpu.roll(block, HEAD_DIM, 1)


def half_sums(block):
    low = low_lanes(block)
    first = jnp.sum(jnp.where(low, block, 0.0), axis=-1, keepdims=True)
    second = jnp.sum(jnp.where(low, 0.0, block), axis=-1, keepdims=True)
    return jnp.where(low, first, second)


def pack(block):
    rows = block.shape[0]
    return jnp.concatenate([block[:PACKED], block[rows - PACKED :]], axis=1)


def unpack(slab, rows):
    right = swap(slab)[2 * PACKED - rows :, :HEAD_DIM]
    return jnp.concatenate([slab[:, :HEAD_DIM], right], axis=0)


def normalize(block):
    field = block.astype(jnp.float32)
    row_scale = lax.rsqrt(jnp.mean(field * field, axis=-1, keepdims=True) + EPSILON)
    return field * row_scale, row_scale


def project(block, weight):
    normed = normalize(block)[0].astype(jnp.bfloat16)
    product = dot(normed, weight)
    raw, value = product[:, : 2 * HEAD_DIM], product[:, 2 * HEAD_DIM :]
    scale = lax.rsqrt(half_sums(raw * raw) / HEAD_DIM + EPSILON)
    return normed, raw * scale, scale, value


def select_kernel(me_ref, wq_ref, wk_ref, wv_ref, out_ref, *scratch):
    held, semaphores = scratch[:3], scratch[3]
    odd = lax.rem(me_ref[0], 2) == 1
    pair = pl.multiple_of(lax.div(me_ref[0], 2) * 2 * HEAD_DIM, 2 * HEAD_DIM)
    copies = [
        pltpu.make_async_copy(ref.at[:, pl.ds(pair, 2 * HEAD_DIM)], kept, semaphores.at[i])
        for i, (ref, kept) in enumerate(zip((wq_ref, wk_ref, wv_ref), held))
    ]
    for copy in copies:
        copy.start()
    for copy in copies:
        copy.wait()
    q, k, v = [wide(kept[...]) for kept in held]
    lower = low_lanes(q)
    qk = jnp.where(lower, jnp.where(odd, swap(q), q), jnp.where(odd, k, swap(k)))
    out_ref[:, : 2 * HEAD_DIM] = low(qk)
    out_ref[:, 2 * HEAD_DIM :] = low(jnp.where(odd, swap(v), v)[:, :HEAD_DIM])


def joined(refs, width):
    pieces, blocks = [], []
    for ref in refs:
        pieces.append(ref[...])
        if sum(piece.shape[1] for piece in pieces) == width:
            blocks.append(jnp.concatenate(pieces, axis=1) if len(pieces) > 1 else pieces[0])
            pieces = []
    return blocks


def project_kernel(*refs):
    blocks, (weight_ref, normed_ref, unit_ref, scale_ref, value_ref) = refs[:-5], refs[-5:]
    for m, block in enumerate(joined(blocks, normed_ref.shape[2])):
        made = project(block, weight_ref[...])
        for ref, part in zip((normed_ref, unit_ref, scale_ref, value_ref), made):
            ref[m] = part.astype(ref.dtype)


TILE = 256


def tiles(tokens):
    starts = range(0, tokens, TILE)
    return [(start, min(tokens, start + TILE)) for start in starts]


def attend_kernel(
    me_ref, unit_ref, value_ref, weight_ref, row_ids, column_ids, *refs
):
    pieces, out_refs = refs[:-8], refs[-8:]
    normed_ref, late_unit, late_scale, prob_ref, qk_ref, v_ref, out_t_ref = out_refs[:7]
    early, rows = unit_ref.shape[:2]
    units = [unit_ref[m] for m in range(early)]
    values = [value_ref[m] for m in range(early)]
    for m, block in enumerate(joined(pieces, normed_ref.shape[2])):
        normed, unit, scale, value = project(block, weight_ref[...])
        normed_ref[m], late_unit[m], late_scale[m] = normed, unit, scale
        units.append(unit)
        values.append(value)
    parts = early + normed_ref.shape[0]
    tokens = parts * rows
    qk = jnp.concatenate(units, axis=0).astype(jnp.bfloat16)
    value = jnp.concatenate(values, axis=0).astype(jnp.bfloat16)
    qk_ref[...] = qk
    v_ref[...] = value
    query, key = qk[:, :HEAD_DIM] * HEAD_DIM ** (-0.5), qk[:, HEAD_DIM:]
    for start, stop in tiles(tokens):
        scores = dot(key, query[start:stop], ((1,), (1,)))
        allowed = column_ids[...] <= row_ids[:, start:stop]
        numerator = jnp.where(allowed, jnp.exp(scores), 0.0)
        probs = numerator * (1.0 / jnp.sum(numerator, axis=0, keepdims=True))
        probs = probs.astype(jnp.bfloat16)
        prob_ref[:, start:stop] = probs
        out_t = dot(value, probs, ((0,), (0,)))
        out_t_ref[:, start:stop] = out_t.astype(jnp.bfloat16).astype(jnp.float32)
    out = jnp.transpose(out_t_ref[...])
    for m, distance in enumerate(DISTANCES):
        out_refs[7][me_ref[0] ^ distance] = low(pack(out[m * rows : (m + 1) * rows]))


def affine_kernel(me_ref, slab_ref, act_ref, inc_ref, w_ref, up_ref, out_ref, *term_refs):
    rows, width = act_ref.shape
    columns = [unpack(wide(slab_ref[h]), rows) for h in range(HEADS)]
    attended = low(jnp.concatenate(columns, axis=1))
    factor = jnp.exp(-dot(attended, w_ref[:, width:]))
    scaled = inc_ref[...].astype(jnp.float32) * factor
    up_ref[...] = low(scaled)
    shift_part = dot(attended, w_ref[:, :width])
    latent_part = scaled * (act_ref[...].astype(jnp.float32) - shift_part)
    grad_affine = jnp.concatenate([-scaled, 1.0 - latent_part], axis=1).astype(jnp.bfloat16)
    grad = dot(grad_affine, w_ref[...], ((1,), (1,)))
    for h in range(HEADS):
        out_ref[h] = low(pack(grad[:, h * HEAD_DIM : (h + 1) * HEAD_DIM]))
    columns = [unpack(wide(slab_ref[me_ref[0] ^ m]), rows) for m in range(HEADS)]
    for half, order in enumerate(ORDERS):
        right = grad_affine[:, half * width : (half + 1) * width]
        for term_ref, group in zip(term_refs[4 * half : 4 * half + 4], order):
            left = low(jnp.concatenate([columns[m] for m in group], axis=1))
            term_ref[...] = low(dot(left, right, ((0,), (0,))))


ORDERS = (((1, 5, 3, 7), (2, 6), (4,), (0,)), ((2, 6, 3, 7), (1, 5), (4,), (0,)))


def backward_kernel(me_ref, slab_ref, prob_ref, qk_ref, v_ref, out_t_ref, *refs):
    early, late, out_refs = refs[:3], refs[3:6], refs[7:-4]
    gk_ref, gv_ref, gq_ref, held_ref = refs[-4:]
    first, rows = early[0].shape[:2]
    slabs = [wide(slab_ref[me_ref[0] ^ distance]) for distance in DISTANCES]
    grad_f = jnp.concatenate([unpack(slab, rows) for slab in slabs], axis=0)
    grad = grad_f.astype(jnp.bfloat16)
    tokens = grad_f.shape[0]
    grad_t = jnp.transpose(grad_f)
    correction = jnp.sum(grad_t * out_t_ref[...], axis=0, keepdims=True)
    grad_t = grad_t.astype(jnp.bfloat16)
    qk, value = qk_ref[...], v_ref[...]
    query, key = qk[:, :HEAD_DIM], qk[:, HEAD_DIM:]
    gk_ref[...] = jnp.zeros_like(gk_ref)
    gv_ref[...] = jnp.zeros_like(gv_ref)
    for start, stop in tiles(tokens):
        probs = prob_ref[:, start:stop]
        grad_probs = dot(value, grad_t[:, start:stop])
        scores = probs.astype(jnp.float32) * (grad_probs - correction[:, start:stop])
        scores = scores.astype(jnp.bfloat16)
        gv_ref[...] += dot(probs, grad[start:stop])
        gk_ref[...] += dot(scores, query[start:stop])
        gq_ref[:, start:stop] = dot(key, scores, ((0,), (0,)))
    grad_q = jnp.transpose(gq_ref[...])
    qk_sum = v_sum = 0.0
    for m in range(HEADS):
        own = slice(m * rows, (m + 1) * rows)
        normed, unit, scale = [
            early[i][m] if m < first else late[i][m - first] for i in range(3)
        ]
        raw = jnp.concatenate([grad_q[own], gk_ref[own, :]], axis=1) * HEAD_DIM ** (-0.5)
        back = scale * (raw - unit * (half_sums(raw * unit) / HEAD_DIM))
        back, grad_v = back.astype(jnp.bfloat16), gv_ref[own, :]
        mirrored = out_refs[DISTANCES.index(DISTANCES[m] ^ HEADS - 1)]
        mirrored[:PACKED, :] = low(pack(grad_v))
        mirrored[PACKED : PACKED + rows, :] = back
        qk_sum = qk_sum + dot(back, normed, ((0,), (0,)))
        v_sum = v_sum + dot(grad_v.astype(jnp.bfloat16), normed, ((0,), (0,)))
    step = qk_sum.shape[1] // HEADS
    for g in range(HEADS):
        own = slice(g * step, (g + 1) * step)
        held_ref[g] = low(jnp.concatenate([qk_sum[:, own], v_sum[:, own]], axis=0))
    for m, out_ref in enumerate(out_refs):
        out_ref[PACKED + rows :, :] = held_ref[me_ref[0] ^ DISTANCES[m]]


def turn_kernel(me_ref, *refs):
    slabs, out_refs, held_ref = refs[:HEADS], refs[HEADS + 2 : -1], refs[-1]
    start = slabs[0].shape[0] - 3 * HEAD_DIM
    for m, slab in enumerate(slabs):
        held_ref[me_ref[0] ^ DISTANCES[m]] = slab[start:, :]
    for i, out_ref in enumerate(out_refs):
        own = slice(i * HEAD_DIM, (i + 1) * HEAD_DIM)
        heads = [wide(held_ref[h, own, :]) for h in range(HEADS)]
        out_ref[0] = jnp.transpose(jnp.concatenate(heads, axis=0))


def second_sum_kernel(*refs):
    for second, got, out in zip(refs[0:2], refs[2:4], refs[-2:]):
        start = got.shape[0] - second.shape[0]
        out[...] = low(wide(second[...]) + wide(got[start:, :]))


def third_sum_kernel(*refs):
    for i in range(2):
        third, keep, got, more = [ref[...] for ref in refs[i:8:2]]
        size = third.shape[0]
        leaving, staying = refs[9 + i], refs[11 + i]
        leaving[...] = low(wide(third) + wide(got[size : 2 * size]) + wide(more[size:]))
        staying[...] = wide(keep) + wide(got[:size]) + wide(more[:size])


def last_sum_kernel(keep_a, keep_b, got_a, got_b, out_ref):
    for i, (keep, got) in enumerate(((keep_a, got_a), (keep_b, got_b))):
        width = keep.shape[1]
        out_ref[0, :, i * width : (i + 1) * width] = keep[...] + wide(got[...])


def input_kernel(me_ref, *refs):
    slabs, (wq_ref, wk_ref, wv_ref, *acts, up_ref, _, out_ref) = refs[:HEADS], refs[HEADS:-1]
    held_ref = refs[-1]
    rows = up_ref.shape[0]
    for m, slab in enumerate(slabs):
        held_ref[me_ref[0] ^ DISTANCES[m]] = slab[: PACKED + rows, :]
    unit, row_scale = normalize(joined(acts, up_ref.shape[1])[0])
    queries, keys, values = [], [], []
    for pair in range(HEADS // 2):
        even, odd = [wide(held_ref[2 * pair + i]) for i in range(2)]
        lower = low_lanes(even[PACKED:])
        queries.append(jnp.where(lower, even[PACKED:], swap(odd[PACKED:])))
        keys.append(jnp.where(lower, swap(even[PACKED:]), odd[PACKED:]))
        values += [unpack(even[:PACKED], rows), unpack(odd[:PACKED], rows)]
    total = 0.0
    for parts, ref in ((queries, wq_ref), (keys, wk_ref), (values, wv_ref)):
        left = jnp.concatenate(parts, axis=1).astype(jnp.bfloat16)
        total = total + dot(left, ref[...], ((1,), (1,)))
    total = total - unit * jnp.mean(total * unit, axis=-1, keepdims=True)
    out_ref[...] = (wide(up_ref[...]) + row_scale * total).astype(jnp.bfloat16)


def reorder_kernel(order_ref, rows_ref, out_ref):
    rows = rows_ref.shape[0]
    chosen = lax.broadcasted_iota(jnp.int32, (rows, rows), 0) == order_ref[...]
    chosen = low(jnp.where(chosen, 1.0, 0.0))
    out_ref[0] = low(dot(chosen, rows_ref[...], ((0,), (0,))))


def hop(block, distance):
    route = [(i, i ^ distance) for i in range(lax.axis_size("seq"))]
    return lax.ppermute(block, "seq", route)


def exchange(slabs):
    return [hop(slab, m) if m else slab for m, slab in zip(DISTANCES, slabs)]


def switch(slabs):
    return lax.all_to_all(slabs, "seq", split_axis=0, concat_axis=0, tiled=True)


def spread(block, weight):
    middle = block.shape[1] // 2
    pieces = [block[:, :middle], block[:, middle:]]
    far = [hop(piece, 4) for piece in pieces]
    near, side = hop(block, 2), hop(block, 1)
    near, weight = lax.optimization_barrier((near, weight))
    side_far = [hop(piece, 1) for piece in far]
    near_far = [hop(piece, 2) for piece in far]
    side_near = hop(near, 1)
    last = [hop(side_far[0], 2), hop(near_far[1], 1)]
    early = [block, side, near, *far, side_near, *side_far]
    return early, near_far, last, weight


DISTANCES = (0, 1, 2, 4, 3, 5, 6, 7)


def wide(matrix):
    return matrix.astype(jnp.float32)


def low(matrix):
    return matrix.astype(jnp.bfloat16)


EARLY = 6


def head_shards(
    activations, incoming, w_query, w_key, w_value, w_out, block_ids, flip_order
):
    parts = lax.axis_size("seq")
    me = lax.axis_index("seq").astype(jnp.int32).reshape(1)
    field, upstream = activations[0], incoming[0]
    wq, wk, wv, wo = w_query[0], w_key[0], w_value[0], w_out[0]
    rows, width = field.shape
    inner = wq.shape[1]
    tokens = parts * rows
    f32 = jnp.float32

    def out(*dims, dtype=jnp.bfloat16):
        return jax.ShapeDtypeStruct(dims, dtype)

    order = me[0] ^ jnp.array(DISTANCES, jnp.int32)
    ids = jnp.take(block_ids.reshape(parts, rows), order, axis=0).reshape(tokens)
    (weight,) = call(
        select_kernel,
        1.5,
        [("s", me), ("a", wq), ("a", wk), ("a", wv)],
        [out(width, 3 * HEAD_DIM)],
        [pltpu.VMEM((width, 2 * HEAD_DIM), jnp.bfloat16)] * 3 + [pltpu.SemaphoreType.DMA((3,))],
    )
    first_blocks, near_far, mirrored, weight = spread(field, weight)
    pair = 2 * HEAD_DIM
    normed, unit, unit_scale, projected = call(
        project_kernel,
        2,
        [("v", block) for block in first_blocks] + [("v", weight)],
        [
            out(EARLY, rows, width),
            out(EARLY, rows, pair, dtype=f32),
            out(EARLY, rows, pair, dtype=f32),
            out(EARLY, rows, HEAD_DIM, dtype=f32),
        ],
    )
    late = parts - EARLY
    made = call(
        attend_kernel,
        5,
        [("s", me), ("v", unit), ("v", projected), ("v", weight)]
        + [("v", ids[None, :]), ("v", ids[:, None])]
        + [("v", block) for block in (*near_far, *mirrored)],
        [
            out(late, rows, width),
            out(late, rows, pair, dtype=f32),
            out(late, rows, pair, dtype=f32),
            out(tokens, tokens),
            out(tokens, pair),
            out(tokens, HEAD_DIM),
            out(HEAD_DIM, tokens, dtype=f32),
        ]
        + [out(parts, PACKED, 128)],
    )
    late_parts, (probs, qk, value, out_t), packed = made[:3], made[3:7], switch(made[7])
    scaled, grad_slabs, *terms = call(
        affine_kernel,
        3,
        [("s", me)] + [("v", x) for x in (packed, field, upstream, wo)],
        [out(rows, width), out(HEADS, PACKED, 128)]
        + [out(len(group) * HEAD_DIM, width) for order in ORDERS for group in order],
    )
    grad_slabs = switch(grad_slabs)
    scaled = hop(scaled, parts - 1)
    grad_slabs, terms = lax.optimization_barrier((grad_slabs, terms))
    first, second, third, keep = zip(terms[:4], terms[4:])
    got = [partner(part, "seq", bit) for bit, part in enumerate(first)]
    grads = call(
        backward_kernel,
        6,
        [("s", me)]
        + [("v", x) for x in (grad_slabs, probs, qk, value, out_t)]
        + [("v", x) for x in (normed, unit, unit_scale, *late_parts)]
        + [("a", scaled)],
        [out(PACKED + rows + 3 * HEAD_DIM, 128)] * parts,
        [
            pltpu.VMEM((tokens, HEAD_DIM), f32),
            pltpu.VMEM((tokens, HEAD_DIM), f32),
            pltpu.VMEM((HEAD_DIM, tokens), f32),
            pltpu.VMEM((HEADS, 3 * HEAD_DIM, 128), jnp.bfloat16),
        ],
    )
    slabs = exchange(grads)
    leaving = call(
        second_sum_kernel,
        1,
        [("v", x) for x in (*second, *got)] + [("a", x) for x in (slabs[3], slabs[6])],
        [out(*second[0].shape)] * 2,
    )
    more = [partner(part, "seq", 1 - bit) for bit, part in enumerate(leaving)]
    *leaving, keep_a, keep_b = call(
        third_sum_kernel,
        2,
        [("v", x) for x in (*third, *keep, *got, *more)] + [("a", slabs[5])],
        [out(*third[0].shape)] * 2 + [out(*keep[0].shape, dtype=f32)] * 2,
    )
    rest = [partner(part, "seq", 2) for part in leaving]
    (grad_input,) = call(
        input_kernel,
        1.5,
        [("s", me)] + [("v", x) for x in (*slabs, wq, wk, wv, *mirrored, scaled)] + [("a", leaving[0])],
        [out(rows, width)],
        [pltpu.VMEM((HEADS, PACKED + rows, 128), jnp.bfloat16)],
    )
    moved = to_previous(grad_input)
    (grad_out,) = call(
        last_sum_kernel,
        2,
        [("v", x) for x in (keep_a, keep_b, *rest)],
        [out(1, keep_a.shape[0], 2 * width, dtype=f32)],
    )
    grad_q, grad_k, grad_v = call(
        turn_kernel,
        3,
        [("s", me)] + [("v", x) for x in slabs] + [("a", x) for x in rest],
        [out(1, width // parts, inner, dtype=f32)] * 3,
        [pltpu.VMEM((HEADS, 3 * HEAD_DIM, 128), jnp.bfloat16)],
    )
    (carry,) = call(
        reorder_kernel, 1, [("v", flip_order), ("v", moved)], [out(1, rows, width)]
    )
    return (carry, grad_q, grad_k, grad_v, grad_out)


def solution(mesh):
    shards = head_shards if mesh.shape["seq"] == HEADS else general_shards
    in_specs = (
        P("section", "seq", None),
        P("section", "seq", None),
        P("section", None, None),
        P("section", None, None),
        P("section", None, None),
        P("section", None, None),
        P(),
        P("section", None),
    )
    out_specs = (
        P("section", "seq", None),
        P("section", "seq", None),
        P("section", "seq", None),
        P("section", "seq", None),
        P("section", "seq", None),
    )
    return jax.shard_map(shards, mesh=mesh, in_specs=in_specs, out_specs=out_specs, check_vma=False)
```

```python
import jax
import jax.numpy as jnp
from jax import lax
from jax.experimental import pallas as pl
from jax.experimental.pallas import tpu as pltpu
from jax.sharding import PartitionSpec as P

HEADS = 8
HEAD_DIM = 64


EPSILON = 1e-06


def partner(block, axis, stride):
    count = lax.axis_size(axis)
    route = []
    for low in range(count):
        high = low | 1 << stride
        if high != low and high < count:
            route += [(low, high), (high, low)]
    return lax.ppermute(block, axis, route)


def shifted(block, axis, distance):
    devices = range(lax.axis_size(axis))
    route = [(i - distance, i) for i in devices if i - distance in devices]
    return lax.ppermute(block, axis, route)


def split_heads(matrix):
    return matrix.reshape(matrix.shape[0], HEADS, HEAD_DIM)


def head_major(matrix):
    return jnp.transpose(split_heads(matrix), (1, 0, 2))


def unit_heads(projected):
    parts = split_heads(projected)
    factor = lax.rsqrt(jnp.mean(parts * parts, axis=-1, keepdims=True) + EPSILON)
    return (parts * factor, factor)


def unit_back(grad_heads, unit, factor):
    return factor * (grad_heads - unit * jnp.mean(grad_heads * unit, axis=-1, keepdims=True))


def mirror(rows):
    for bit in range(lax.axis_size("seq").bit_length() - 1):
        rows = partner(rows, "seq", bit)
    return rows


def to_previous(rows):
    return shifted(rows, "section", -1)


def general_shards(activations, incoming, w_query, w_key, w_value, w_out, block_ids, flip_order):
    field = activations[0].astype(jnp.float32)
    upstream = incoming[0].astype(jnp.float32)
    weight_query = w_query[0]
    weight_key = w_key[0]
    weight_value = w_value[0]
    weight_out = w_out[0]
    flip_row = flip_order[0]
    rows = field.shape[0]
    width = field.shape[1]
    inner = weight_query.shape[1]
    scale = HEAD_DIM ** (-0.5)
    first = lax.axis_index("seq") * rows
    my_blocks = lax.dynamic_slice_in_dim(block_ids, first, rows)
    row_scale = lax.rsqrt(jnp.mean(field * field, axis=-1, keepdims=True) + EPSILON)
    unit_rows = field * row_scale
    normed = unit_rows.astype(jnp.bfloat16)
    query_raw = jnp.dot(normed, weight_query, preferred_element_type=jnp.float32)
    key_raw = jnp.dot(normed, weight_key, preferred_element_type=jnp.float32)
    values = jnp.dot(normed, weight_value, preferred_element_type=jnp.float32).astype(jnp.bfloat16)
    query_unit, query_scale = unit_heads(query_raw)
    key_unit, key_scale = unit_heads(key_raw)
    queries = query_unit.astype(jnp.bfloat16).reshape(rows, inner)
    keys = key_unit.astype(jnp.bfloat16).reshape(rows, inner)
    keys_all, values_all = (
        lax.all_gather(keys, "seq", axis=0, tiled=True),
        lax.all_gather(values, "seq", axis=0, tiled=True),
    )
    allowed = block_ids[None, :] <= my_blocks[:, None]
    query_heads = head_major(queries)
    key_heads_all = head_major(keys_all)
    value_heads_all = head_major(values_all)

    def probabilities(query_part, key_part):
        scores = jnp.dot(query_part, key_part.T, preferred_element_type=jnp.float32) * scale
        numerator = jnp.where(allowed, jnp.exp(scores), 0.0)
        denominator = jnp.sum(numerator, axis=-1, keepdims=True)
        return (numerator / denominator, denominator)

    def forward_head(operands):
        query_part, key_part, value_part = operands
        probs, denominator = probabilities(query_part, key_part)
        out_part = jnp.dot(
            probs.astype(jnp.bfloat16), value_part, preferred_element_type=jnp.float32
        ).astype(jnp.bfloat16)
        return (out_part, denominator[:, 0])

    heads_out, denominators = lax.map(forward_head, (query_heads, key_heads_all, value_heads_all))
    attended = jnp.transpose(heads_out, (1, 0, 2)).reshape(rows, inner)
    affine = jnp.dot(attended, weight_out, preferred_element_type=jnp.float32)
    shift_part = affine[:, :width]
    log_scale = affine[:, width:]
    factor = jnp.exp(-log_scale)
    latent = (field - shift_part) * factor
    grad_affine = jnp.concatenate([-upstream * factor, 1.0 - upstream * latent], axis=-1).astype(
        jnp.bfloat16
    )
    out_term = jnp.dot(attended.T, grad_affine, preferred_element_type=jnp.float32)
    grad_attn = jnp.dot(grad_affine, weight_out.T, preferred_element_type=jnp.float32).astype(
        jnp.bfloat16
    )
    correction = jnp.sum(
        split_heads(grad_attn.astype(jnp.float32)) * split_heads(attended.astype(jnp.float32)),
        axis=-1,
    )
    grad_heads = head_major(grad_attn)
    correction_heads = jnp.transpose(correction)[:, :, None]

    def backward_head(operands):
        query_part, key_part, value_part, grad_part, corr_part = operands
        probs, denominator = probabilities(query_part, key_part)
        grad_probs = jnp.dot(grad_part, value_part.T, preferred_element_type=jnp.float32)
        grad_scores = (probs * (grad_probs - corr_part)).astype(jnp.bfloat16)
        grad_qpart = jnp.dot(grad_scores, key_part, preferred_element_type=jnp.float32) * scale
        grad_kpart = jnp.dot(grad_scores.T, query_part, preferred_element_type=jnp.float32) * scale
        grad_vpart = jnp.dot(
            probs.astype(jnp.bfloat16).T, grad_part, preferred_element_type=jnp.float32
        )
        return (grad_qpart, grad_kpart, grad_vpart)

    grad_qheads, grad_kall, grad_vall = lax.map(
        backward_head, (query_heads, key_heads_all, value_heads_all, grad_heads, correction_heads)
    )
    key_terms = jnp.transpose(grad_kall, (1, 0, 2)).reshape(-1, inner)
    value_terms = jnp.transpose(grad_vall, (1, 0, 2)).reshape(-1, inner)
    grad_kunit, grad_vsum = (
        lax.psum_scatter(
            key_terms.astype(jnp.bfloat16), "seq", scatter_dimension=0, tiled=True
        ).astype(jnp.float32),
        lax.psum_scatter(
            value_terms.astype(jnp.bfloat16), "seq", scatter_dimension=0, tiled=True
        ).astype(jnp.float32),
    )
    grad_queries = (
        unit_back(jnp.transpose(grad_qheads, (1, 0, 2)), query_unit, query_scale)
        .reshape(rows, inner)
        .astype(jnp.bfloat16)
    )
    grad_keys = (
        unit_back(split_heads(grad_kunit), key_unit, key_scale)
        .reshape(rows, inner)
        .astype(jnp.bfloat16)
    )
    grad_values = grad_vsum.astype(jnp.bfloat16)
    query_term = jnp.dot(normed.T, grad_queries, preferred_element_type=jnp.float32)
    key_term = jnp.dot(normed.T, grad_keys, preferred_element_type=jnp.float32)
    value_term = jnp.dot(normed.T, grad_values, preferred_element_type=jnp.float32)
    sums = (
        lax.psum_scatter(
            query_term.astype(jnp.bfloat16), "seq", scatter_dimension=0, tiled=True
        ).astype(jnp.float32),
        lax.psum_scatter(
            key_term.astype(jnp.bfloat16), "seq", scatter_dimension=0, tiled=True
        ).astype(jnp.float32),
        lax.psum_scatter(
            value_term.astype(jnp.bfloat16), "seq", scatter_dimension=0, tiled=True
        ).astype(jnp.float32),
        lax.psum_scatter(
            out_term.astype(jnp.bfloat16), "seq", scatter_dimension=0, tiled=True
        ).astype(jnp.float32),
    )
    grad_normed = jnp.dot(grad_queries, weight_query.T, preferred_element_type=jnp.float32)
    grad_normed = grad_normed + jnp.dot(grad_keys, weight_key.T, preferred_element_type=jnp.float32)
    grad_normed = grad_normed + jnp.dot(
        grad_values, weight_value.T, preferred_element_type=jnp.float32
    )
    grad_input = upstream * factor + row_scale * (
        grad_normed - unit_rows * jnp.mean(grad_normed * unit_rows, axis=-1, keepdims=True)
    )
    grad_input = grad_input.astype(jnp.bfloat16)
    moved = mirror(to_previous(grad_input))
    carry = jnp.take(moved, flip_row, axis=0)
    return (carry[None], sums[0][None], sums[1][None], sums[2][None], sums[3][None])


PACKED = 80


def call(kernel, microseconds, ins, outs, scratch=()):
    spaces = {"s": pltpu.SMEM, "v": pltpu.VMEM, "a": pl.ANY}
    places, operands = zip(*ins)
    return pl.pallas_call(
        kernel,
        out_shape=tuple(outs),
        in_specs=[pl.BlockSpec(memory_space=spaces[place]) for place in places],
        out_specs=(pl.BlockSpec(memory_space=pltpu.VMEM),) * len(outs),
        scratch_shapes=list(scratch),
        compiler_params=pltpu.CompilerParams(vmem_limit_bytes=14 * 2**20),
        cost_estimate=pl.CostEstimate(
            flops=int(microseconds * 1e9), bytes_accessed=1024, transcendentals=0
        ),
    )(*operands)


def dot(left, right, contract=((1,), (0,))):
    return lax.dot_general(left, right, (contract, ((), ())), preferred_element_type=jnp.float32)


def low_lanes(block):
    return lax.broadcasted_iota(jnp.int32, block.shape, len(block.shape) - 1) < HEAD_DIM


def swap(block):
    return pltpu.roll(block, HEAD_DIM, 1)


def half_sums(block):
    low = low_lanes(block)
    first = jnp.sum(jnp.where(low, block, 0.0), axis=-1, keepdims=True)
    second = jnp.sum(jnp.where(low, 0.0, block), axis=-1, keepdims=True)
    return jnp.where(low, first, second)


def pack(block):
    rows = block.shape[0]
    return jnp.concatenate([block[:PACKED], block[rows - PACKED :]], axis=1)


def unpack(slab, rows):
    right = swap(slab)[2 * PACKED - rows :, :HEAD_DIM]
    return jnp.concatenate([slab[:, :HEAD_DIM], right], axis=0)


def normalize(block):
    field = block.astype(jnp.float32)
    row_scale = lax.rsqrt(jnp.mean(field * field, axis=-1, keepdims=True) + EPSILON)
    return field * row_scale, row_scale


def project(block, weight):
    normed = normalize(block)[0].astype(jnp.bfloat16)
    product = dot(normed, weight)
    raw, value = product[:, : 2 * HEAD_DIM], product[:, 2 * HEAD_DIM :]
    scale = lax.rsqrt(half_sums(raw * raw) / HEAD_DIM + EPSILON)
    return normed, raw * scale, scale, value


def select_kernel(me_ref, wq_ref, wk_ref, wv_ref, out_ref, *scratch):
    held, semaphores = scratch[:3], scratch[3]
    odd = lax.rem(me_ref[0], 2) == 1
    pair = pl.multiple_of(lax.div(me_ref[0], 2) * 2 * HEAD_DIM, 2 * HEAD_DIM)
    copies = [
        pltpu.make_async_copy(ref.at[:, pl.ds(pair, 2 * HEAD_DIM)], kept, semaphores.at[i])
        for i, (ref, kept) in enumerate(zip((wq_ref, wk_ref, wv_ref), held))
    ]
    for copy in copies:
        copy.start()
    for copy in copies:
        copy.wait()
    q, k, v = [wide(kept[...]) for kept in held]
    lower = low_lanes(q)
    qk = jnp.where(lower, jnp.where(odd, swap(q), q), jnp.where(odd, k, swap(k)))
    out_ref[:, : 2 * HEAD_DIM] = low(qk)
    out_ref[:, 2 * HEAD_DIM :] = low(jnp.where(odd, swap(v), v)[:, :HEAD_DIM])


def joined(refs, width):
    pieces, blocks = [], []
    for ref in refs:
        pieces.append(ref[...])
        if sum(piece.shape[1] for piece in pieces) == width:
            blocks.append(jnp.concatenate(pieces, axis=1) if len(pieces) > 1 else pieces[0])
            pieces = []
    return blocks


def project_kernel(*refs):
    blocks, (weight_ref, normed_ref, unit_ref, scale_ref, value_ref) = refs[:-5], refs[-5:]
    for m, block in enumerate(joined(blocks, normed_ref.shape[2])):
        made = project(block, weight_ref[...])
        for ref, part in zip((normed_ref, unit_ref, scale_ref, value_ref), made):
            ref[m] = part.astype(ref.dtype)


TILE = 256


def tiles(tokens):
    starts = range(0, tokens, TILE)
    return [(start, min(tokens, start + TILE)) for start in starts]


def attend_kernel(
    me_ref, unit_ref, value_ref, weight_ref, row_ids, column_ids, *refs
):
    pieces, out_refs = refs[:-8], refs[-8:]
    normed_ref, late_unit, late_scale, prob_ref, qk_ref, v_ref, out_t_ref = out_refs[:7]
    early, rows = unit_ref.shape[:2]
    units = [unit_ref[m] for m in range(early)]
    values = [value_ref[m] for m in range(early)]
    for m, block in enumerate(joined(pieces, normed_ref.shape[2])):
        normed, unit, scale, value = project(block, weight_ref[...])
        normed_ref[m], late_unit[m], late_scale[m] = normed, unit, scale
        units.append(unit)
        values.append(value)
    parts = early + normed_ref.shape[0]
    tokens = parts * rows
    qk = jnp.concatenate(units, axis=0).astype(jnp.bfloat16)
    value = jnp.concatenate(values, axis=0).astype(jnp.bfloat16)
    qk_ref[...] = qk
    v_ref[...] = value
    query, key = qk[:, :HEAD_DIM] * HEAD_DIM ** (-0.5), qk[:, HEAD_DIM:]
    for start, stop in tiles(tokens):
        scores = dot(key, query[start:stop], ((1,), (1,)))
        allowed = column_ids[...] <= row_ids[:, start:stop]
        numerator = jnp.where(allowed, jnp.exp(scores), 0.0)
        probs = numerator * (1.0 / jnp.sum(numerator, axis=0, keepdims=True))
        probs = probs.astype(jnp.bfloat16)
        prob_ref[:, start:stop] = probs
        out_t = dot(value, probs, ((0,), (0,)))
        out_t_ref[:, start:stop] = out_t.astype(jnp.bfloat16).astype(jnp.float32)
    out = jnp.transpose(out_t_ref[...])
    for m, distance in enumerate(DISTANCES):
        out_refs[7][me_ref[0] ^ distance] = low(pack(out[m * rows : (m + 1) * rows]))


def affine_kernel(me_ref, slab_ref, act_ref, inc_ref, w_ref, up_ref, out_ref, *term_refs):
    rows, width = act_ref.shape
    columns = [unpack(wide(slab_ref[h]), rows) for h in range(HEADS)]
    attended = low(jnp.concatenate(columns, axis=1))
    factor = jnp.exp(-dot(attended, w_ref[:, width:]))
    scaled = inc_ref[...].astype(jnp.float32) * factor
    up_ref[...] = low(scaled)
    shift_part = dot(attended, w_ref[:, :width])
    latent_part = scaled * (act_ref[...].astype(jnp.float32) - shift_part)
    grad_affine = jnp.concatenate([-scaled, 1.0 - latent_part], axis=1).astype(jnp.bfloat16)
    grad = dot(grad_affine, w_ref[...], ((1,), (1,)))
    for h in range(HEADS):
        out_ref[h] = low(pack(grad[:, h * HEAD_DIM : (h + 1) * HEAD_DIM]))
    columns = [unpack(wide(slab_ref[me_ref[0] ^ m]), rows) for m in range(HEADS)]
    for half, order in enumerate(ORDERS):
        right = grad_affine[:, half * width : (half + 1) * width]
        for term_ref, group in zip(term_refs[4 * half : 4 * half + 4], order):
            left = low(jnp.concatenate([columns[m] for m in group], axis=1))
            term_ref[...] = low(dot(left, right, ((0,), (0,))))


ORDERS = (((1, 5, 3, 7), (2, 6), (4,), (0,)), ((2, 6, 3, 7), (1, 5), (4,), (0,)))


def backward_kernel(me_ref, slab_ref, prob_ref, qk_ref, v_ref, out_t_ref, *refs):
    early, late, out_refs = refs[:3], refs[3:6], refs[6:-4]
    gk_ref, gv_ref, gq_ref, held_ref = refs[-4:]
    first, rows = early[0].shape[:2]
    slabs = [wide(slab_ref[me_ref[0] ^ distance]) for distance in DISTANCES]
    grad_f = jnp.concatenate([unpack(slab, rows) for slab in slabs], axis=0)
    grad = grad_f.astype(jnp.bfloat16)
    tokens = grad_f.shape[0]
    grad_t = jnp.transpose(grad_f)
    correction = jnp.sum(grad_t * out_t_ref[...], axis=0, keepdims=True)
    grad_t = grad_t.astype(jnp.bfloat16)
    qk, value = qk_ref[...], v_ref[...]
    query, key = qk[:, :HEAD_DIM], qk[:, HEAD_DIM:]
    gk_ref[...] = jnp.zeros_like(gk_ref)
    gv_ref[...] = jnp.zeros_like(gv_ref)
    for start, stop in tiles(tokens):
        probs = prob_ref[:, start:stop]
        grad_probs = dot(value, grad_t[:, start:stop])
        scores = probs.astype(jnp.float32) * (grad_probs - correction[:, start:stop])
        scores = scores.astype(jnp.bfloat16)
        gv_ref[...] += dot(probs, grad[start:stop])
        gk_ref[...] += dot(scores, query[start:stop])
        gq_ref[:, start:stop] = dot(key, scores, ((0,), (0,)))
    grad_q = jnp.transpose(gq_ref[...])
    qk_sum = v_sum = 0.0
    for m in range(HEADS):
        own = slice(m * rows, (m + 1) * rows)
        normed, unit, scale = [
            early[i][m] if m < first else late[i][m - first] for i in range(3)
        ]
        raw = jnp.concatenate([grad_q[own], gk_ref[own, :]], axis=1) * HEAD_DIM ** (-0.5)
        back = scale * (raw - unit * (half_sums(raw * unit) / HEAD_DIM))
        back, grad_v = back.astype(jnp.bfloat16), gv_ref[own, :]
        mirrored = out_refs[DISTANCES.index(DISTANCES[m] ^ HEADS - 1)]
        mirrored[:PACKED, :] = low(pack(grad_v))
        mirrored[PACKED : PACKED + rows, :] = back
        qk_sum = qk_sum + dot(back, normed, ((0,), (0,)))
        v_sum = v_sum + dot(grad_v.astype(jnp.bfloat16), normed, ((0,), (0,)))
    step = qk_sum.shape[1] // HEADS
    for g in range(HEADS):
        own = slice(g * step, (g + 1) * step)
        held_ref[g] = low(jnp.concatenate([qk_sum[:, own], v_sum[:, own]], axis=0))
    for m, out_ref in enumerate(out_refs):
        out_ref[PACKED + rows :, :] = held_ref[me_ref[0] ^ DISTANCES[m]]


def turn_kernel(me_ref, *refs):
    slabs, out_refs, held_ref = refs[:HEADS], refs[HEADS + 2 : -1], refs[-1]
    start = slabs[0].shape[0] - 3 * HEAD_DIM
    for m, slab in enumerate(slabs):
        held_ref[me_ref[0] ^ DISTANCES[m]] = slab[start:, :]
    for i, out_ref in enumerate(out_refs):
        own = slice(i * HEAD_DIM, (i + 1) * HEAD_DIM)
        heads = [wide(held_ref[h, own, :]) for h in range(HEADS)]
        out_ref[0] = jnp.transpose(jnp.concatenate(heads, axis=0))


def second_sum_kernel(*refs):
    for second, got, out in zip(refs[0:2], refs[2:4], refs[-2:]):
        start = got.shape[0] - second.shape[0]
        out[...] = low(wide(second[...]) + wide(got[start:, :]))


def third_sum_kernel(*refs):
    for i in range(2):
        third, keep, got, more = [ref[...] for ref in refs[i:8:2]]
        size = third.shape[0]
        leaving, staying = refs[9 + i], refs[11 + i]
        leaving[...] = low(wide(third) + wide(got[size : 2 * size]) + wide(more[size:]))
        staying[...] = wide(keep) + wide(got[:size]) + wide(more[:size])


def last_sum_kernel(keep_a, keep_b, got_a, got_b, out_ref):
    for i, (keep, got) in enumerate(((keep_a, got_a), (keep_b, got_b))):
        width = keep.shape[1]
        out_ref[0, :, i * width : (i + 1) * width] = keep[...] + wide(got[...])


def input_kernel(me_ref, *refs):
    slabs, (wq_ref, wk_ref, wv_ref, *acts, up_ref, _, out_ref) = refs[:HEADS], refs[HEADS:-1]
    held_ref = refs[-1]
    rows = up_ref.shape[0]
    for m, slab in enumerate(slabs):
        held_ref[me_ref[0] ^ DISTANCES[m]] = slab[: PACKED + rows, :]
    unit, row_scale = normalize(joined(acts, up_ref.shape[1])[0])
    queries, keys, values = [], [], []
    for pair in range(HEADS // 2):
        even, odd = [wide(held_ref[2 * pair + i]) for i in range(2)]
        lower = low_lanes(even[PACKED:])
        queries.append(jnp.where(lower, even[PACKED:], swap(odd[PACKED:])))
        keys.append(jnp.where(lower, swap(even[PACKED:]), odd[PACKED:]))
        values += [unpack(even[:PACKED], rows), unpack(odd[:PACKED], rows)]
    total = 0.0
    for parts, ref in ((queries, wq_ref), (keys, wk_ref), (values, wv_ref)):
        left = jnp.concatenate(parts, axis=1).astype(jnp.bfloat16)
        total = total + dot(left, ref[...], ((1,), (1,)))
    total = total - unit * jnp.mean(total * unit, axis=-1, keepdims=True)
    out_ref[...] = (wide(up_ref[...]) + row_scale * total).astype(jnp.bfloat16)


def reorder_kernel(order_ref, rows_ref, out_ref):
    rows = rows_ref.shape[0]
    chosen = lax.broadcasted_iota(jnp.int32, (rows, rows), 0) == order_ref[...]
    chosen = low(jnp.where(chosen, 1.0, 0.0))
    out_ref[0] = low(dot(chosen, rows_ref[...], ((0,), (0,))))


def hop(block, distance):
    route = [(i, i ^ distance) for i in range(lax.axis_size("seq"))]
    return lax.ppermute(block, "seq", route)


def exchange(slabs):
    return [hop(slab, m) if m else slab for m, slab in zip(DISTANCES, slabs)]


def switch(slabs):
    return lax.all_to_all(slabs, "seq", split_axis=0, concat_axis=0, tiled=True)


def spread(block, weight):
    middle = block.shape[1] // 2
    pieces = [block[:, :middle], block[:, middle:]]
    far = [hop(piece, 4) for piece in pieces]
    near, side = hop(block, 2), hop(block, 1)
    near, weight = lax.optimization_barrier((near, weight))
    side_far = [hop(piece, 1) for piece in far]
    near_far = [hop(piece, 2) for piece in far]
    side_near = hop(near, 1)
    last = [hop(side_far[0], 2), hop(near_far[1], 1)]
    early = [block, side, near, *far, side_near, *side_far]
    return early, near_far, last, weight


DISTANCES = (0, 1, 2, 4, 3, 5, 6, 7)


def wide(matrix):
    return matrix.astype(jnp.float32)


def low(matrix):
    return matrix.astype(jnp.bfloat16)


EARLY = 6


def head_shards(
    activations, incoming, w_query, w_key, w_value, w_out, block_ids, flip_order
):
    parts = lax.axis_size("seq")
    me = lax.axis_index("seq").astype(jnp.int32).reshape(1)
    field, upstream = activations[0], incoming[0]
    wq, wk, wv, wo = w_query[0], w_key[0], w_value[0], w_out[0]
    rows, width = field.shape
    inner = wq.shape[1]
    tokens = parts * rows
    f32 = jnp.float32

    def out(*dims, dtype=jnp.bfloat16):
        return jax.ShapeDtypeStruct(dims, dtype)

    order = me[0] ^ jnp.array(DISTANCES, jnp.int32)
    ids = jnp.take(block_ids.reshape(parts, rows), order, axis=0).reshape(tokens)
    (weight,) = call(
        select_kernel,
        1.5,
        [("s", me), ("a", wq), ("a", wk), ("a", wv)],
        [out(width, 3 * HEAD_DIM)],
        [pltpu.VMEM((width, 2 * HEAD_DIM), jnp.bfloat16)] * 3 + [pltpu.SemaphoreType.DMA((3,))],
    )
    first_blocks, near_far, mirrored, weight = spread(field, weight)
    pair = 2 * HEAD_DIM
    normed, unit, unit_scale, projected = call(
        project_kernel,
        2,
        [("v", block) for block in first_blocks] + [("v", weight)],
        [
            out(EARLY, rows, width),
            out(EARLY, rows, pair, dtype=f32),
            out(EARLY, rows, pair, dtype=f32),
            out(EARLY, rows, HEAD_DIM, dtype=f32),
        ],
    )
    late = parts - EARLY
    made = call(
        attend_kernel,
        5,
        [("s", me), ("v", unit), ("v", projected), ("v", weight)]
        + [("v", ids[None, :]), ("v", ids[:, None])]
        + [("v", block) for block in (*near_far, *mirrored)],
        [
            out(late, rows, width),
            out(late, rows, pair, dtype=f32),
            out(late, rows, pair, dtype=f32),
            out(tokens, tokens),
            out(tokens, pair),
            out(tokens, HEAD_DIM),
            out(HEAD_DIM, tokens, dtype=f32),
        ]
        + [out(parts, PACKED, 128)],
    )
    late_parts, (probs, qk, value, out_t), packed = made[:3], made[3:7], switch(made[7])
    scaled, grad_slabs, *terms = call(
        affine_kernel,
        3,
        [("s", me)] + [("v", x) for x in (packed, field, upstream, wo)],
        [out(rows, width), out(HEADS, PACKED, 128)]
        + [out(len(group) * HEAD_DIM, width) for order in ORDERS for group in order],
    )
    grad_slabs = switch(grad_slabs)
    grad_slabs, terms, scaled = lax.optimization_barrier((grad_slabs, terms, scaled))
    scaled = hop(scaled, parts - 1)
    first, second, third, keep = zip(terms[:4], terms[4:])
    got = [partner(part, "seq", bit) for bit, part in enumerate(first)]
    grads = call(
        backward_kernel,
        6,
        [("s", me)]
        + [("v", x) for x in (grad_slabs, probs, qk, value, out_t)]
        + [("v", x) for x in (normed, unit, unit_scale, *late_parts)],
        [out(PACKED + rows + 3 * HEAD_DIM, 128)] * parts,
        [
            pltpu.VMEM((tokens, HEAD_DIM), f32),
            pltpu.VMEM((tokens, HEAD_DIM), f32),
            pltpu.VMEM((HEAD_DIM, tokens), f32),
            pltpu.VMEM((HEADS, 3 * HEAD_DIM, 128), jnp.bfloat16),
        ],
    )
    slabs = exchange(grads)
    leaving = call(
        second_sum_kernel,
        1,
        [("v", x) for x in (*second, *got)] + [("a", slabs[i]) for i in (3, 6, 7)],
        [out(*second[0].shape)] * 2,
    )
    more = [partner(part, "seq", 1 - bit) for bit, part in enumerate(leaving)]
    *leaving, keep_a, keep_b = call(
        third_sum_kernel,
        2,
        [("v", x) for x in (*third, *keep, *got, *more)] + [("a", slabs[2])],
        [out(*third[0].shape)] * 2 + [out(*keep[0].shape, dtype=f32)] * 2,
    )
    rest = [partner(part, "seq", 2) for part in leaving]
    (grad_input,) = call(
        input_kernel,
        1.5,
        [("s", me)] + [("v", x) for x in (*slabs, wq, wk, wv, *mirrored, scaled)] + [("a", leaving[0])],
        [out(rows, width)],
        [pltpu.VMEM((HEADS, PACKED + rows, 128), jnp.bfloat16)],
    )
    moved = to_previous(grad_input)
    (grad_out,) = call(
        last_sum_kernel,
        2,
        [("v", x) for x in (keep_a, keep_b, *rest)],
        [out(1, keep_a.shape[0], 2 * width, dtype=f32)],
    )
    grad_q, grad_k, grad_v = call(
        turn_kernel,
        3,
        [("s", me)] + [("v", x) for x in slabs] + [("a", x) for x in rest],
        [out(1, width // parts, inner, dtype=f32)] * 3,
        [pltpu.VMEM((HEADS, 3 * HEAD_DIM, 128), jnp.bfloat16)],
    )
    (carry,) = call(
        reorder_kernel, 1, [("v", flip_order), ("v", moved)], [out(1, rows, width)]
    )
    return (carry, grad_q, grad_k, grad_v, grad_out)


def solution(mesh):
    shards = head_shards if mesh.shape["seq"] == HEADS else general_shards
    in_specs = (
        P("section", "seq", None),
        P("section", "seq", None),
        P("section", None, None),
        P("section", None, None),
        P("section", None, None),
        P("section", None, None),
        P(),
        P("section", None),
    )
    out_specs = (
        P("section", "seq", None),
        P("section", "seq", None),
        P("section", "seq", None),
        P("section", "seq", None),
        P("section", "seq", None),
    )
    return jax.shard_map(shards, mesh=mesh, in_specs=in_specs, out_specs=out_specs, check_vma=False)
```

```python
import jax
import jax.numpy as jnp
from jax import lax
from jax.experimental import pallas as pl
from jax.experimental.pallas import tpu as pltpu
from jax.sharding import PartitionSpec as P

HEADS = 8
HEAD_DIM = 64


EPSILON = 1e-06


def partner(block, axis, stride):
    count = lax.axis_size(axis)
    route = []
    for low in range(count):
        high = low | 1 << stride
        if high != low and high < count:
            route += [(low, high), (high, low)]
    return lax.ppermute(block, axis, route)


def shifted(block, axis, distance):
    devices = range(lax.axis_size(axis))
    route = [(i - distance, i) for i in devices if i - distance in devices]
    return lax.ppermute(block, axis, route)


def split_heads(matrix):
    return matrix.reshape(matrix.shape[0], HEADS, HEAD_DIM)


def head_major(matrix):
    return jnp.transpose(split_heads(matrix), (1, 0, 2))


def unit_heads(projected):
    parts = split_heads(projected)
    factor = lax.rsqrt(jnp.mean(parts * parts, axis=-1, keepdims=True) + EPSILON)
    return (parts * factor, factor)


def unit_back(grad_heads, unit, factor):
    return factor * (grad_heads - unit * jnp.mean(grad_heads * unit, axis=-1, keepdims=True))


def mirror(rows):
    for bit in range(lax.axis_size("seq").bit_length() - 1):
        rows = partner(rows, "seq", bit)
    return rows


def to_previous(rows):
    return shifted(rows, "section", -1)


def general_shards(activations, incoming, w_query, w_key, w_value, w_out, block_ids, flip_order):
    field = activations[0].astype(jnp.float32)
    upstream = incoming[0].astype(jnp.float32)
    weight_query = w_query[0]
    weight_key = w_key[0]
    weight_value = w_value[0]
    weight_out = w_out[0]
    flip_row = flip_order[0]
    rows = field.shape[0]
    width = field.shape[1]
    inner = weight_query.shape[1]
    scale = HEAD_DIM ** (-0.5)
    first = lax.axis_index("seq") * rows
    my_blocks = lax.dynamic_slice_in_dim(block_ids, first, rows)
    row_scale = lax.rsqrt(jnp.mean(field * field, axis=-1, keepdims=True) + EPSILON)
    unit_rows = field * row_scale
    normed = unit_rows.astype(jnp.bfloat16)
    query_raw = jnp.dot(normed, weight_query, preferred_element_type=jnp.float32)
    key_raw = jnp.dot(normed, weight_key, preferred_element_type=jnp.float32)
    values = jnp.dot(normed, weight_value, preferred_element_type=jnp.float32).astype(jnp.bfloat16)
    query_unit, query_scale = unit_heads(query_raw)
    key_unit, key_scale = unit_heads(key_raw)
    queries = query_unit.astype(jnp.bfloat16).reshape(rows, inner)
    keys = key_unit.astype(jnp.bfloat16).reshape(rows, inner)
    keys_all, values_all = (
        lax.all_gather(keys, "seq", axis=0, tiled=True),
        lax.all_gather(values, "seq", axis=0, tiled=True),
    )
    allowed = block_ids[None, :] <= my_blocks[:, None]
    query_heads = head_major(queries)
    key_heads_all = head_major(keys_all)
    value_heads_all = head_major(values_all)

    def probabilities(query_part, key_part):
        scores = jnp.dot(query_part, key_part.T, preferred_element_type=jnp.float32) * scale
        numerator = jnp.where(allowed, jnp.exp(scores), 0.0)
        denominator = jnp.sum(numerator, axis=-1, keepdims=True)
        return (numerator / denominator, denominator)

    def forward_head(operands):
        query_part, key_part, value_part = operands
        probs, denominator = probabilities(query_part, key_part)
        out_part = jnp.dot(
            probs.astype(jnp.bfloat16), value_part, preferred_element_type=jnp.float32
        ).astype(jnp.bfloat16)
        return (out_part, denominator[:, 0])

    heads_out, denominators = lax.map(forward_head, (query_heads, key_heads_all, value_heads_all))
    attended = jnp.transpose(heads_out, (1, 0, 2)).reshape(rows, inner)
    affine = jnp.dot(attended, weight_out, preferred_element_type=jnp.float32)
    shift_part = affine[:, :width]
    log_scale = affine[:, width:]
    factor = jnp.exp(-log_scale)
    latent = (field - shift_part) * factor
    grad_affine = jnp.concatenate([-upstream * factor, 1.0 - upstream * latent], axis=-1).astype(
        jnp.bfloat16
    )
    out_term = jnp.dot(attended.T, grad_affine, preferred_element_type=jnp.float32)
    grad_attn = jnp.dot(grad_affine, weight_out.T, preferred_element_type=jnp.float32).astype(
        jnp.bfloat16
    )
    correction = jnp.sum(
        split_heads(grad_attn.astype(jnp.float32)) * split_heads(attended.astype(jnp.float32)),
        axis=-1,
    )
    grad_heads = head_major(grad_attn)
    correction_heads = jnp.transpose(correction)[:, :, None]

    def backward_head(operands):
        query_part, key_part, value_part, grad_part, corr_part = operands
        probs, denominator = probabilities(query_part, key_part)
        grad_probs = jnp.dot(grad_part, value_part.T, preferred_element_type=jnp.float32)
        grad_scores = (probs * (grad_probs - corr_part)).astype(jnp.bfloat16)
        grad_qpart = jnp.dot(grad_scores, key_part, preferred_element_type=jnp.float32) * scale
        grad_kpart = jnp.dot(grad_scores.T, query_part, preferred_element_type=jnp.float32) * scale
        grad_vpart = jnp.dot(
            probs.astype(jnp.bfloat16).T, grad_part, preferred_element_type=jnp.float32
        )
        return (grad_qpart, grad_kpart, grad_vpart)

    grad_qheads, grad_kall, grad_vall = lax.map(
        backward_head, (query_heads, key_heads_all, value_heads_all, grad_heads, correction_heads)
    )
    key_terms = jnp.transpose(grad_kall, (1, 0, 2)).reshape(-1, inner)
    value_terms = jnp.transpose(grad_vall, (1, 0, 2)).reshape(-1, inner)
    grad_kunit, grad_vsum = (
        lax.psum_scatter(
            key_terms.astype(jnp.bfloat16), "seq", scatter_dimension=0, tiled=True
        ).astype(jnp.float32),
        lax.psum_scatter(
            value_terms.astype(jnp.bfloat16), "seq", scatter_dimension=0, tiled=True
        ).astype(jnp.float32),
    )
    grad_queries = (
        unit_back(jnp.transpose(grad_qheads, (1, 0, 2)), query_unit, query_scale)
        .reshape(rows, inner)
        .astype(jnp.bfloat16)
    )
    grad_keys = (
        unit_back(split_heads(grad_kunit), key_unit, key_scale)
        .reshape(rows, inner)
        .astype(jnp.bfloat16)
    )
    grad_values = grad_vsum.astype(jnp.bfloat16)
    query_term = jnp.dot(normed.T, grad_queries, preferred_element_type=jnp.float32)
    key_term = jnp.dot(normed.T, grad_keys, preferred_element_type=jnp.float32)
    value_term = jnp.dot(normed.T, grad_values, preferred_element_type=jnp.float32)
    sums = (
        lax.psum_scatter(
            query_term.astype(jnp.bfloat16), "seq", scatter_dimension=0, tiled=True
        ).astype(jnp.float32),
        lax.psum_scatter(
            key_term.astype(jnp.bfloat16), "seq", scatter_dimension=0, tiled=True
        ).astype(jnp.float32),
        lax.psum_scatter(
            value_term.astype(jnp.bfloat16), "seq", scatter_dimension=0, tiled=True
        ).astype(jnp.float32),
        lax.psum_scatter(
            out_term.astype(jnp.bfloat16), "seq", scatter_dimension=0, tiled=True
        ).astype(jnp.float32),
    )
    grad_normed = jnp.dot(grad_queries, weight_query.T, preferred_element_type=jnp.float32)
    grad_normed = grad_normed + jnp.dot(grad_keys, weight_key.T, preferred_element_type=jnp.float32)
    grad_normed = grad_normed + jnp.dot(
        grad_values, weight_value.T, preferred_element_type=jnp.float32
    )
    grad_input = upstream * factor + row_scale * (
        grad_normed - unit_rows * jnp.mean(grad_normed * unit_rows, axis=-1, keepdims=True)
    )
    grad_input = grad_input.astype(jnp.bfloat16)
    moved = mirror(to_previous(grad_input))
    carry = jnp.take(moved, flip_row, axis=0)
    return (carry[None], sums[0][None], sums[1][None], sums[2][None], sums[3][None])


PACKED = 80


def call(kernel, microseconds, ins, outs, scratch=()):
    spaces = {"s": pltpu.SMEM, "v": pltpu.VMEM, "a": pl.ANY}
    places, operands = zip(*ins)
    return pl.pallas_call(
        kernel,
        out_shape=tuple(outs),
        in_specs=[pl.BlockSpec(memory_space=spaces[place]) for place in places],
        out_specs=(pl.BlockSpec(memory_space=pltpu.VMEM),) * len(outs),
        scratch_shapes=list(scratch),
        compiler_params=pltpu.CompilerParams(vmem_limit_bytes=14 * 2**20),
        cost_estimate=pl.CostEstimate(
            flops=int(microseconds * 1e9), bytes_accessed=1024, transcendentals=0
        ),
    )(*operands)


def dot(left, right, contract=((1,), (0,))):
    return lax.dot_general(left, right, (contract, ((), ())), preferred_element_type=jnp.float32)


def low_lanes(block):
    return lax.broadcasted_iota(jnp.int32, block.shape, len(block.shape) - 1) < HEAD_DIM


def swap(block):
    return pltpu.roll(block, HEAD_DIM, 1)


def half_sums(block):
    low = low_lanes(block)
    first = jnp.sum(jnp.where(low, block, 0.0), axis=-1, keepdims=True)
    second = jnp.sum(jnp.where(low, 0.0, block), axis=-1, keepdims=True)
    return jnp.where(low, first, second)


def pack(block):
    rows = block.shape[0]
    return jnp.concatenate([block[:PACKED], block[rows - PACKED :]], axis=1)


def unpack(slab, rows):
    right = swap(slab)[2 * PACKED - rows :, :HEAD_DIM]
    return jnp.concatenate([slab[:, :HEAD_DIM], right], axis=0)


def normalize(block):
    field = block.astype(jnp.float32)
    row_scale = lax.rsqrt(jnp.mean(field * field, axis=-1, keepdims=True) + EPSILON)
    return field * row_scale, row_scale


def project(block, weight):
    normed = normalize(block)[0].astype(jnp.bfloat16)
    product = dot(normed, weight)
    raw, value = product[:, : 2 * HEAD_DIM], product[:, 2 * HEAD_DIM :]
    scale = lax.rsqrt(half_sums(raw * raw) / HEAD_DIM + EPSILON)
    return normed, raw * scale, scale, value


def select_kernel(me_ref, wq_ref, wk_ref, wv_ref, out_ref, *scratch):
    held, semaphores = scratch[:3], scratch[3]
    odd = lax.rem(me_ref[0], 2) == 1
    pair = pl.multiple_of(lax.div(me_ref[0], 2) * 2 * HEAD_DIM, 2 * HEAD_DIM)
    copies = [
        pltpu.make_async_copy(ref.at[:, pl.ds(pair, 2 * HEAD_DIM)], kept, semaphores.at[i])
        for i, (ref, kept) in enumerate(zip((wq_ref, wk_ref, wv_ref), held))
    ]
    for copy in copies:
        copy.start()
    for copy in copies:
        copy.wait()
    q, k, v = [wide(kept[...]) for kept in held]
    lower = low_lanes(q)
    qk = jnp.where(lower, jnp.where(odd, swap(q), q), jnp.where(odd, k, swap(k)))
    out_ref[:, : 2 * HEAD_DIM] = low(qk)
    out_ref[:, 2 * HEAD_DIM :] = low(jnp.where(odd, swap(v), v)[:, :HEAD_DIM])


def joined(refs, width):
    pieces, blocks = [], []
    for ref in refs:
        pieces.append(ref[...])
        if sum(piece.shape[1] for piece in pieces) == width:
            blocks.append(jnp.concatenate(pieces, axis=1) if len(pieces) > 1 else pieces[0])
            pieces = []
    return blocks


def project_kernel(*refs):
    blocks, (weight_ref, normed_ref, unit_ref, scale_ref, value_ref) = refs[:-5], refs[-5:]
    for m, block in enumerate(joined(blocks, normed_ref.shape[2])):
        made = project(block, weight_ref[...])
        for ref, part in zip((normed_ref, unit_ref, scale_ref, value_ref), made):
            ref[m] = part.astype(ref.dtype)


TILE = 256


def tiles(tokens):
    starts = range(0, tokens, TILE)
    return [(start, min(tokens, start + TILE)) for start in starts]


def attend_kernel(
    me_ref, unit_ref, value_ref, weight_ref, row_ids, column_ids, *refs
):
    pieces, out_refs = refs[:-8], refs[-8:]
    normed_ref, late_unit, late_scale, prob_ref, qk_ref, v_ref, out_t_ref = out_refs[:7]
    early, rows = unit_ref.shape[:2]
    units = [unit_ref[m] for m in range(early)]
    values = [value_ref[m] for m in range(early)]
    for m, block in enumerate(joined(pieces, normed_ref.shape[2])):
        normed, unit, scale, value = project(block, weight_ref[...])
        normed_ref[m], late_unit[m], late_scale[m] = normed, unit, scale
        units.append(unit)
        values.append(value)
    parts = early + normed_ref.shape[0]
    tokens = parts * rows
    qk = jnp.concatenate(units, axis=0).astype(jnp.bfloat16)
    value = jnp.concatenate(values, axis=0).astype(jnp.bfloat16)
    qk_ref[...] = qk
    v_ref[...] = value
    query, key = qk[:, :HEAD_DIM] * HEAD_DIM ** (-0.5), qk[:, HEAD_DIM:]
    for start, stop in tiles(tokens):
        scores = dot(key, query[start:stop], ((1,), (1,)))
        allowed = column_ids[...] <= row_ids[:, start:stop]
        numerator = jnp.where(allowed, jnp.exp(scores), 0.0)
        probs = numerator * (1.0 / jnp.sum(numerator, axis=0, keepdims=True))
        probs = probs.astype(jnp.bfloat16)
        prob_ref[:, start:stop] = probs
        out_t = dot(value, probs, ((0,), (0,)))
        out_t_ref[:, start:stop] = out_t.astype(jnp.bfloat16).astype(jnp.float32)
    out = jnp.transpose(out_t_ref[...])
    for m, distance in enumerate(DISTANCES):
        out_refs[7][me_ref[0] ^ distance] = low(pack(out[m * rows : (m + 1) * rows]))


def affine_kernel(me_ref, slab_ref, act_ref, inc_ref, w_ref, up_ref, out_ref, *term_refs):
    rows, width = act_ref.shape
    columns = [unpack(wide(slab_ref[h]), rows) for h in range(HEADS)]
    attended = low(jnp.concatenate(columns, axis=1))
    factor = jnp.exp(-dot(attended, w_ref[:, width:]))
    scaled = inc_ref[...].astype(jnp.float32) * factor
    up_ref[...] = low(scaled)
    shift_part = dot(attended, w_ref[:, :width])
    latent_part = scaled * (act_ref[...].astype(jnp.float32) - shift_part)
    grad_affine = jnp.concatenate([-scaled, 1.0 - latent_part], axis=1).astype(jnp.bfloat16)
    grad = dot(grad_affine, w_ref[...], ((1,), (1,)))
    for h in range(HEADS):
        out_ref[h] = low(pack(grad[:, h * HEAD_DIM : (h + 1) * HEAD_DIM]))
    columns = [unpack(wide(slab_ref[me_ref[0] ^ m]), rows) for m in range(HEADS)]
    for half, order in enumerate(ORDERS):
        right = grad_affine[:, half * width : (half + 1) * width]
        for term_ref, group in zip(term_refs[4 * half : 4 * half + 4], order):
            left = low(jnp.concatenate([columns[m] for m in group], axis=1))
            term_ref[...] = low(dot(left, right, ((0,), (0,))))


ORDERS = (((1, 5, 3, 7), (2, 6), (4,), (0,)), ((2, 6, 3, 7), (1, 5), (4,), (0,)))


def backward_kernel(me_ref, slab_ref, prob_ref, qk_ref, v_ref, out_t_ref, *refs):
    early, late, out_refs = refs[:3], refs[3:6], refs[6:-4]
    gk_ref, gv_ref, gq_ref, held_ref = refs[-4:]
    first, rows = early[0].shape[:2]
    slabs = [wide(slab_ref[me_ref[0] ^ distance]) for distance in DISTANCES]
    grad_f = jnp.concatenate([unpack(slab, rows) for slab in slabs], axis=0)
    grad = grad_f.astype(jnp.bfloat16)
    tokens = grad_f.shape[0]
    grad_t = jnp.transpose(grad_f)
    correction = jnp.sum(grad_t * out_t_ref[...], axis=0, keepdims=True)
    grad_t = grad_t.astype(jnp.bfloat16)
    qk, value = qk_ref[...], v_ref[...]
    query, key = qk[:, :HEAD_DIM], qk[:, HEAD_DIM:]
    gk_ref[...] = jnp.zeros_like(gk_ref)
    gv_ref[...] = jnp.zeros_like(gv_ref)
    for start, stop in tiles(tokens):
        probs = prob_ref[:, start:stop]
        grad_probs = dot(value, grad_t[:, start:stop])
        scores = probs.astype(jnp.float32) * (grad_probs - correction[:, start:stop])
        scores = scores.astype(jnp.bfloat16)
        gv_ref[...] += dot(probs, grad[start:stop])
        gk_ref[...] += dot(scores, query[start:stop])
        gq_ref[:, start:stop] = dot(key, scores, ((0,), (0,)))
    grad_q = jnp.transpose(gq_ref[...])
    qk_sum = v_sum = 0.0
    for m in range(HEADS):
        own = slice(m * rows, (m + 1) * rows)
        normed, unit, scale = [
            early[i][m] if m < first else late[i][m - first] for i in range(3)
        ]
        raw = jnp.concatenate([grad_q[own], gk_ref[own, :]], axis=1) * HEAD_DIM ** (-0.5)
        back = scale * (raw - unit * (half_sums(raw * unit) / HEAD_DIM))
        back, grad_v = back.astype(jnp.bfloat16), gv_ref[own, :]
        mirrored = out_refs[DISTANCES.index(DISTANCES[m] ^ HEADS - 1)]
        mirrored[:PACKED, :] = low(pack(grad_v))
        mirrored[PACKED : PACKED + rows, :] = back
        qk_sum = qk_sum + dot(back, normed, ((0,), (0,)))
        v_sum = v_sum + dot(grad_v.astype(jnp.bfloat16), normed, ((0,), (0,)))
    step = qk_sum.shape[1] // HEADS
    for g in range(HEADS):
        own = slice(g * step, (g + 1) * step)
        held_ref[g] = low(jnp.concatenate([qk_sum[:, own], v_sum[:, own]], axis=0))
    for m, out_ref in enumerate(out_refs):
        out_ref[PACKED + rows :, :] = held_ref[me_ref[0] ^ DISTANCES[m]]


def turn_kernel(me_ref, *refs):
    slabs, out_refs, held_ref = refs[:HEADS], refs[HEADS + 2 : -1], refs[-1]
    start = slabs[0].shape[0] - 3 * HEAD_DIM
    for m, slab in enumerate(slabs):
        held_ref[me_ref[0] ^ DISTANCES[m]] = slab[start:, :]
    for i, out_ref in enumerate(out_refs):
        own = slice(i * HEAD_DIM, (i + 1) * HEAD_DIM)
        heads = [wide(held_ref[h, own, :]) for h in range(HEADS)]
        out_ref[0] = jnp.transpose(jnp.concatenate(heads, axis=0))


def second_sum_kernel(*refs):
    for second, got, out in zip(refs[0:2], refs[2:4], refs[-2:]):
        start = got.shape[0] - second.shape[0]
        out[...] = low(wide(second[...]) + wide(got[start:, :]))


def third_sum_kernel(*refs):
    for i in range(2):
        third, keep, got, more = [ref[...] for ref in refs[i:8:2]]
        size = third.shape[0]
        leaving, staying = refs[9 + i], refs[11 + i]
        leaving[...] = low(wide(third) + wide(got[size : 2 * size]) + wide(more[size:]))
        staying[...] = wide(keep) + wide(got[:size]) + wide(more[:size])


def last_sum_kernel(keep_a, keep_b, got_a, got_b, out_ref):
    for i, (keep, got) in enumerate(((keep_a, got_a), (keep_b, got_b))):
        width = keep.shape[1]
        out_ref[0, :, i * width : (i + 1) * width] = keep[...] + wide(got[...])


def input_kernel(me_ref, *refs):
    slabs, (wq_ref, wk_ref, wv_ref, *acts, up_ref, _, out_ref) = refs[:HEADS], refs[HEADS:-1]
    held_ref = refs[-1]
    rows = up_ref.shape[0]
    for m, slab in enumerate(slabs):
        held_ref[me_ref[0] ^ DISTANCES[m]] = slab[: PACKED + rows, :]
    unit, row_scale = normalize(joined(acts, up_ref.shape[1])[0])
    queries, keys, values = [], [], []
    for pair in range(HEADS // 2):
        even, odd = [wide(held_ref[2 * pair + i]) for i in range(2)]
        lower = low_lanes(even[PACKED:])
        queries.append(jnp.where(lower, even[PACKED:], swap(odd[PACKED:])))
        keys.append(jnp.where(lower, swap(even[PACKED:]), odd[PACKED:]))
        values += [unpack(even[:PACKED], rows), unpack(odd[:PACKED], rows)]
    total = 0.0
    for parts, ref in ((queries, wq_ref), (keys, wk_ref), (values, wv_ref)):
        left = jnp.concatenate(parts, axis=1).astype(jnp.bfloat16)
        total = total + dot(left, ref[...], ((1,), (1,)))
    total = total - unit * jnp.mean(total * unit, axis=-1, keepdims=True)
    out_ref[...] = (wide(up_ref[...]) + row_scale * total).astype(jnp.bfloat16)


def reorder_kernel(order_ref, rows_ref, out_ref):
    rows = rows_ref.shape[0]
    chosen = lax.broadcasted_iota(jnp.int32, (rows, rows), 0) == order_ref[...]
    chosen = low(jnp.where(chosen, 1.0, 0.0))
    out_ref[0] = low(dot(chosen, rows_ref[...], ((0,), (0,))))


def hop(block, distance):
    route = [(i, i ^ distance) for i in range(lax.axis_size("seq"))]
    return lax.ppermute(block, "seq", route)


def exchange(slabs):
    return [hop(slab, m) if m else slab for m, slab in zip(DISTANCES, slabs)]


def switch(slabs):
    return lax.all_to_all(slabs, "seq", split_axis=0, concat_axis=0, tiled=True)


def spread(block, weight):
    middle = block.shape[1] // 2
    pieces = [block[:, :middle], block[:, middle:]]
    far = [hop(piece, 4) for piece in pieces]
    near, side = hop(block, 2), hop(block, 1)
    near, weight = lax.optimization_barrier((near, weight))
    side_far = [hop(piece, 1) for piece in far]
    near_far = [hop(piece, 2) for piece in far]
    side_near = hop(near, 1)
    last = [hop(side_far[0], 2), hop(near_far[1], 1)]
    early = [block, side, near, *far, side_near, *side_far]
    return early, near_far, last, weight


DISTANCES = (0, 1, 2, 4, 3, 5, 6, 7)


def wide(matrix):
    return matrix.astype(jnp.float32)


def low(matrix):
    return matrix.astype(jnp.bfloat16)


EARLY = 6


def head_shards(
    activations, incoming, w_query, w_key, w_value, w_out, block_ids, flip_order
):
    parts = lax.axis_size("seq")
    me = lax.axis_index("seq").astype(jnp.int32).reshape(1)
    field, upstream = activations[0], incoming[0]
    wq, wk, wv, wo = w_query[0], w_key[0], w_value[0], w_out[0]
    rows, width = field.shape
    inner = wq.shape[1]
    tokens = parts * rows
    f32 = jnp.float32

    def out(*dims, dtype=jnp.bfloat16):
        return jax.ShapeDtypeStruct(dims, dtype)

    order = me[0] ^ jnp.array(DISTANCES, jnp.int32)
    ids = jnp.take(block_ids.reshape(parts, rows), order, axis=0).reshape(tokens)
    (weight,) = call(
        select_kernel,
        1.5,
        [("s", me), ("a", wq), ("a", wk), ("a", wv)],
        [out(width, 3 * HEAD_DIM)],
        [pltpu.VMEM((width, 2 * HEAD_DIM), jnp.bfloat16)] * 3 + [pltpu.SemaphoreType.DMA((3,))],
    )
    first_blocks, near_far, mirrored, weight = spread(field, weight)
    pair = 2 * HEAD_DIM
    normed, unit, unit_scale, projected = call(
        project_kernel,
        2,
        [("v", block) for block in first_blocks] + [("v", weight)],
        [
            out(EARLY, rows, width),
            out(EARLY, rows, pair, dtype=f32),
            out(EARLY, rows, pair, dtype=f32),
            out(EARLY, rows, HEAD_DIM, dtype=f32),
        ],
    )
    late = parts - EARLY
    made = call(
        attend_kernel,
        5,
        [("s", me), ("v", unit), ("v", projected), ("v", weight)]
        + [("v", ids[None, :]), ("v", ids[:, None])]
        + [("v", block) for block in (*near_far, *mirrored)],
        [
            out(late, rows, width),
            out(late, rows, pair, dtype=f32),
            out(late, rows, pair, dtype=f32),
            out(tokens, tokens),
            out(tokens, pair),
            out(tokens, HEAD_DIM),
            out(HEAD_DIM, tokens, dtype=f32),
        ]
        + [out(parts, PACKED, 128)],
    )
    late_parts, (probs, qk, value, out_t), packed = made[:3], made[3:7], switch(made[7])
    scaled, grad_slabs, *terms = call(
        affine_kernel,
        3,
        [("s", me)] + [("v", x) for x in (packed, field, upstream, wo)],
        [out(rows, width), out(HEADS, PACKED, 128)]
        + [out(len(group) * HEAD_DIM, width) for order in ORDERS for group in order],
    )
    grad_slabs = switch(grad_slabs)
    grad_slabs, terms, scaled = lax.optimization_barrier((grad_slabs, terms, scaled))
    scaled = hop(scaled, parts - 1)
    first, second, third, keep = zip(terms[:4], terms[4:])
    got = [partner(part, "seq", bit) for bit, part in enumerate(first)]
    grads = call(
        backward_kernel,
        6,
        [("s", me)]
        + [("v", x) for x in (grad_slabs, probs, qk, value, out_t)]
        + [("v", x) for x in (normed, unit, unit_scale, *late_parts)],
        [out(PACKED + rows + 3 * HEAD_DIM, 128)] * parts,
        [
            pltpu.VMEM((tokens, HEAD_DIM), f32),
            pltpu.VMEM((tokens, HEAD_DIM), f32),
            pltpu.VMEM((HEAD_DIM, tokens), f32),
            pltpu.VMEM((HEADS, 3 * HEAD_DIM, 128), jnp.bfloat16),
        ],
    )
    slabs = exchange(grads)
    leaving = call(
        second_sum_kernel,
        1,
        [("v", x) for x in (*second, *got)] + [("a", slabs[i]) for i in (3, 6, 7)],
        [out(*second[0].shape)] * 2,
    )
    more = [partner(part, "seq", 1 - bit) for bit, part in enumerate(leaving)]
    *leaving, keep_a, keep_b = call(
        third_sum_kernel,
        2,
        [("v", x) for x in (*third, *keep, *got, *more)] + [("a", slabs[5])],
        [out(*third[0].shape)] * 2 + [out(*keep[0].shape, dtype=f32)] * 2,
    )
    rest = [partner(part, "seq", 2) for part in leaving]
    (grad_input,) = call(
        input_kernel,
        1.5,
        [("s", me)] + [("v", x) for x in (*slabs, wq, wk, wv, *mirrored, scaled)] + [("a", leaving[0])],
        [out(rows, width)],
        [pltpu.VMEM((HEADS, PACKED + rows, 128), jnp.bfloat16)],
    )
    moved = to_previous(grad_input)
    (grad_out,) = call(
        last_sum_kernel,
        2,
        [("v", x) for x in (keep_a, keep_b, *rest)],
        [out(1, keep_a.shape[0], 2 * width, dtype=f32)],
    )
    grad_q, grad_k, grad_v = call(
        turn_kernel,
        3,
        [("s", me)] + [("v", x) for x in slabs] + [("a", x) for x in rest],
        [out(1, width // parts, inner, dtype=f32)] * 3,
        [pltpu.VMEM((HEADS, 3 * HEAD_DIM, 128), jnp.bfloat16)],
    )
    (carry,) = call(
        reorder_kernel, 1, [("v", flip_order), ("v", moved)], [out(1, rows, width)]
    )
    return (carry, grad_q, grad_k, grad_v, grad_out)


def solution(mesh):
    shards = head_shards if mesh.shape["seq"] == HEADS else general_shards
    in_specs = (
        P("section", "seq", None),
        P("section", "seq", None),
        P("section", None, None),
        P("section", None, None),
        P("section", None, None),
        P("section", None, None),
        P(),
        P("section", None),
    )
    out_specs = (
        P("section", "seq", None),
        P("section", "seq", None),
        P("section", "seq", None),
        P("section", "seq", None),
        P("section", "seq", None),
    )
    return jax.shard_map(shards, mesh=mesh, in_specs=in_specs, out_specs=out_specs, check_vma=False)
```

```python
import jax
import jax.numpy as jnp
from jax import lax
from jax.experimental import pallas as pl
from jax.experimental.pallas import tpu as pltpu
from jax.sharding import PartitionSpec as P

HEADS = 8
HEAD_DIM = 64


EPSILON = 1e-06


def partner(block, axis, stride):
    count = lax.axis_size(axis)
    route = []
    for low in range(count):
        high = low | 1 << stride
        if high != low and high < count:
            route += [(low, high), (high, low)]
    return lax.ppermute(block, axis, route)


def shifted(block, axis, distance):
    devices = range(lax.axis_size(axis))
    route = [(i - distance, i) for i in devices if i - distance in devices]
    return lax.ppermute(block, axis, route)


def split_heads(matrix):
    return matrix.reshape(matrix.shape[0], HEADS, HEAD_DIM)


def head_major(matrix):
    return jnp.transpose(split_heads(matrix), (1, 0, 2))


def unit_heads(projected):
    parts = split_heads(projected)
    factor = lax.rsqrt(jnp.mean(parts * parts, axis=-1, keepdims=True) + EPSILON)
    return (parts * factor, factor)


def unit_back(grad_heads, unit, factor):
    return factor * (grad_heads - unit * jnp.mean(grad_heads * unit, axis=-1, keepdims=True))


def mirror(rows):
    for bit in range(lax.axis_size("seq").bit_length() - 1):
        rows = partner(rows, "seq", bit)
    return rows


def to_previous(rows):
    return shifted(rows, "section", -1)


def general_shards(activations, incoming, w_query, w_key, w_value, w_out, block_ids, flip_order):
    field = activations[0].astype(jnp.float32)
    upstream = incoming[0].astype(jnp.float32)
    weight_query = w_query[0]
    weight_key = w_key[0]
    weight_value = w_value[0]
    weight_out = w_out[0]
    flip_row = flip_order[0]
    rows = field.shape[0]
    width = field.shape[1]
    inner = weight_query.shape[1]
    scale = HEAD_DIM ** (-0.5)
    first = lax.axis_index("seq") * rows
    my_blocks = lax.dynamic_slice_in_dim(block_ids, first, rows)
    row_scale = lax.rsqrt(jnp.mean(field * field, axis=-1, keepdims=True) + EPSILON)
    unit_rows = field * row_scale
    normed = unit_rows.astype(jnp.bfloat16)
    query_raw = jnp.dot(normed, weight_query, preferred_element_type=jnp.float32)
    key_raw = jnp.dot(normed, weight_key, preferred_element_type=jnp.float32)
    values = jnp.dot(normed, weight_value, preferred_element_type=jnp.float32).astype(jnp.bfloat16)
    query_unit, query_scale = unit_heads(query_raw)
    key_unit, key_scale = unit_heads(key_raw)
    queries = query_unit.astype(jnp.bfloat16).reshape(rows, inner)
    keys = key_unit.astype(jnp.bfloat16).reshape(rows, inner)
    keys_all, values_all = (
        lax.all_gather(keys, "seq", axis=0, tiled=True),
        lax.all_gather(values, "seq", axis=0, tiled=True),
    )
    allowed = block_ids[None, :] <= my_blocks[:, None]
    query_heads = head_major(queries)
    key_heads_all = head_major(keys_all)
    value_heads_all = head_major(values_all)

    def probabilities(query_part, key_part):
        scores = jnp.dot(query_part, key_part.T, preferred_element_type=jnp.float32) * scale
        numerator = jnp.where(allowed, jnp.exp(scores), 0.0)
        denominator = jnp.sum(numerator, axis=-1, keepdims=True)
        return (numerator / denominator, denominator)

    def forward_head(operands):
        query_part, key_part, value_part = operands
        probs, denominator = probabilities(query_part, key_part)
        out_part = jnp.dot(
            probs.astype(jnp.bfloat16), value_part, preferred_element_type=jnp.float32
        ).astype(jnp.bfloat16)
        return (out_part, denominator[:, 0])

    heads_out, denominators = lax.map(forward_head, (query_heads, key_heads_all, value_heads_all))
    attended = jnp.transpose(heads_out, (1, 0, 2)).reshape(rows, inner)
    affine = jnp.dot(attended, weight_out, preferred_element_type=jnp.float32)
    shift_part = affine[:, :width]
    log_scale = affine[:, width:]
    factor = jnp.exp(-log_scale)
    latent = (field - shift_part) * factor
    grad_affine = jnp.concatenate([-upstream * factor, 1.0 - upstream * latent], axis=-1).astype(
        jnp.bfloat16
    )
    out_term = jnp.dot(attended.T, grad_affine, preferred_element_type=jnp.float32)
    grad_attn = jnp.dot(grad_affine, weight_out.T, preferred_element_type=jnp.float32).astype(
        jnp.bfloat16
    )
    correction = jnp.sum(
        split_heads(grad_attn.astype(jnp.float32)) * split_heads(attended.astype(jnp.float32)),
        axis=-1,
    )
    grad_heads = head_major(grad_attn)
    correction_heads = jnp.transpose(correction)[:, :, None]

    def backward_head(operands):
        query_part, key_part, value_part, grad_part, corr_part = operands
        probs, denominator = probabilities(query_part, key_part)
        grad_probs = jnp.dot(grad_part, value_part.T, preferred_element_type=jnp.float32)
        grad_scores = (probs * (grad_probs - corr_part)).astype(jnp.bfloat16)
        grad_qpart = jnp.dot(grad_scores, key_part, preferred_element_type=jnp.float32) * scale
        grad_kpart = jnp.dot(grad_scores.T, query_part, preferred_element_type=jnp.float32) * scale
        grad_vpart = jnp.dot(
            probs.astype(jnp.bfloat16).T, grad_part, preferred_element_type=jnp.float32
        )
        return (grad_qpart, grad_kpart, grad_vpart)

    grad_qheads, grad_kall, grad_vall = lax.map(
        backward_head, (query_heads, key_heads_all, value_heads_all, grad_heads, correction_heads)
    )
    key_terms = jnp.transpose(grad_kall, (1, 0, 2)).reshape(-1, inner)
    value_terms = jnp.transpose(grad_vall, (1, 0, 2)).reshape(-1, inner)
    grad_kunit, grad_vsum = (
        lax.psum_scatter(
            key_terms.astype(jnp.bfloat16), "seq", scatter_dimension=0, tiled=True
        ).astype(jnp.float32),
        lax.psum_scatter(
            value_terms.astype(jnp.bfloat16), "seq", scatter_dimension=0, tiled=True
        ).astype(jnp.float32),
    )
    grad_queries = (
        unit_back(jnp.transpose(grad_qheads, (1, 0, 2)), query_unit, query_scale)
        .reshape(rows, inner)
        .astype(jnp.bfloat16)
    )
    grad_keys = (
        unit_back(split_heads(grad_kunit), key_unit, key_scale)
        .reshape(rows, inner)
        .astype(jnp.bfloat16)
    )
    grad_values = grad_vsum.astype(jnp.bfloat16)
    query_term = jnp.dot(normed.T, grad_queries, preferred_element_type=jnp.float32)
    key_term = jnp.dot(normed.T, grad_keys, preferred_element_type=jnp.float32)
    value_term = jnp.dot(normed.T, grad_values, preferred_element_type=jnp.float32)
    sums = (
        lax.psum_scatter(
            query_term.astype(jnp.bfloat16), "seq", scatter_dimension=0, tiled=True
        ).astype(jnp.float32),
        lax.psum_scatter(
            key_term.astype(jnp.bfloat16), "seq", scatter_dimension=0, tiled=True
        ).astype(jnp.float32),
        lax.psum_scatter(
            value_term.astype(jnp.bfloat16), "seq", scatter_dimension=0, tiled=True
        ).astype(jnp.float32),
        lax.psum_scatter(
            out_term.astype(jnp.bfloat16), "seq", scatter_dimension=0, tiled=True
        ).astype(jnp.float32),
    )
    grad_normed = jnp.dot(grad_queries, weight_query.T, preferred_element_type=jnp.float32)
    grad_normed = grad_normed + jnp.dot(grad_keys, weight_key.T, preferred_element_type=jnp.float32)
    grad_normed = grad_normed + jnp.dot(
        grad_values, weight_value.T, preferred_element_type=jnp.float32
    )
    grad_input = upstream * factor + row_scale * (
        grad_normed - unit_rows * jnp.mean(grad_normed * unit_rows, axis=-1, keepdims=True)
    )
    grad_input = grad_input.astype(jnp.bfloat16)
    moved = mirror(to_previous(grad_input))
    carry = jnp.take(moved, flip_row, axis=0)
    return (carry[None], sums[0][None], sums[1][None], sums[2][None], sums[3][None])


PACKED = 80


def call(kernel, microseconds, ins, outs, scratch=()):
    spaces = {"s": pltpu.SMEM, "v": pltpu.VMEM, "a": pl.ANY}
    places, operands = zip(*ins)
    return pl.pallas_call(
        kernel,
        out_shape=tuple(outs),
        in_specs=[pl.BlockSpec(memory_space=spaces[place]) for place in places],
        out_specs=(pl.BlockSpec(memory_space=pltpu.VMEM),) * len(outs),
        scratch_shapes=list(scratch),
        compiler_params=pltpu.CompilerParams(vmem_limit_bytes=14 * 2**20),
        cost_estimate=pl.CostEstimate(
            flops=int(microseconds * 1e9), bytes_accessed=1024, transcendentals=0
        ),
    )(*operands)


def dot(left, right, contract=((1,), (0,))):
    return lax.dot_general(left, right, (contract, ((), ())), preferred_element_type=jnp.float32)


def low_lanes(block):
    return lax.broadcasted_iota(jnp.int32, block.shape, len(block.shape) - 1) < HEAD_DIM


def swap(block):
    return pltpu.roll(block, HEAD_DIM, 1)


def half_sums(block):
    low = low_lanes(block)
    first = jnp.sum(jnp.where(low, block, 0.0), axis=-1, keepdims=True)
    second = jnp.sum(jnp.where(low, 0.0, block), axis=-1, keepdims=True)
    return jnp.where(low, first, second)


def pack(block):
    rows = block.shape[0]
    return jnp.concatenate([block[:PACKED], block[rows - PACKED :]], axis=1)


def unpack(slab, rows):
    right = swap(slab)[2 * PACKED - rows :, :HEAD_DIM]
    return jnp.concatenate([slab[:, :HEAD_DIM], right], axis=0)


def normalize(block):
    field = block.astype(jnp.float32)
    row_scale = lax.rsqrt(jnp.mean(field * field, axis=-1, keepdims=True) + EPSILON)
    return field * row_scale, row_scale


def project(block, weight):
    normed = normalize(block)[0].astype(jnp.bfloat16)
    product = dot(normed, weight)
    raw, value = product[:, : 2 * HEAD_DIM], product[:, 2 * HEAD_DIM :]
    scale = lax.rsqrt(half_sums(raw * raw) / HEAD_DIM + EPSILON)
    return normed, raw * scale, scale, value


def select_kernel(me_ref, wq_ref, wk_ref, wv_ref, out_ref, *scratch):
    held, semaphores = scratch[:3], scratch[3]
    odd = lax.rem(me_ref[0], 2) == 1
    pair = pl.multiple_of(lax.div(me_ref[0], 2) * 2 * HEAD_DIM, 2 * HEAD_DIM)
    copies = [
        pltpu.make_async_copy(ref.at[:, pl.ds(pair, 2 * HEAD_DIM)], kept, semaphores.at[i])
        for i, (ref, kept) in enumerate(zip((wq_ref, wk_ref, wv_ref), held))
    ]
    for copy in copies:
        copy.start()
    for copy in copies:
        copy.wait()
    q, k, v = [wide(kept[...]) for kept in held]
    lower = low_lanes(q)
    qk = jnp.where(lower, jnp.where(odd, swap(q), q), jnp.where(odd, k, swap(k)))
    out_ref[:, : 2 * HEAD_DIM] = low(qk)
    out_ref[:, 2 * HEAD_DIM :] = low(jnp.where(odd, swap(v), v)[:, :HEAD_DIM])


def joined(refs, width):
    pieces, blocks = [], []
    for ref in refs:
        pieces.append(ref[...])
        if sum(piece.shape[1] for piece in pieces) == width:
            blocks.append(jnp.concatenate(pieces, axis=1) if len(pieces) > 1 else pieces[0])
            pieces = []
    return blocks


def project_kernel(*refs):
    blocks, (weight_ref, normed_ref, unit_ref, scale_ref, value_ref) = refs[:-5], refs[-5:]
    for m, block in enumerate(joined(blocks, normed_ref.shape[2])):
        made = project(block, weight_ref[...])
        for ref, part in zip((normed_ref, unit_ref, scale_ref, value_ref), made):
            ref[m] = part.astype(ref.dtype)


TILE = 256


def tiles(tokens):
    starts = range(0, tokens, TILE)
    return [(start, min(tokens, start + TILE)) for start in starts]


def attend_kernel(
    me_ref, unit_ref, value_ref, weight_ref, row_ids, column_ids, *refs
):
    pieces, out_refs = refs[:-8], refs[-8:]
    normed_ref, late_unit, late_scale, prob_ref, qk_ref, v_ref, out_t_ref = out_refs[:7]
    early, rows = unit_ref.shape[:2]
    units = [unit_ref[m] for m in range(early)]
    values = [value_ref[m] for m in range(early)]
    for m, block in enumerate(joined(pieces, normed_ref.shape[2])):
        normed, unit, scale, value = project(block, weight_ref[...])
        normed_ref[m], late_unit[m], late_scale[m] = normed, unit, scale
        units.append(unit)
        values.append(value)
    parts = early + normed_ref.shape[0]
    tokens = parts * rows
    qk = jnp.concatenate(units, axis=0).astype(jnp.bfloat16)
    value = jnp.concatenate(values, axis=0).astype(jnp.bfloat16)
    qk_ref[...] = qk
    v_ref[...] = value
    query, key = qk[:, :HEAD_DIM] * HEAD_DIM ** (-0.5), qk[:, HEAD_DIM:]
    for start, stop in tiles(tokens):
        scores = dot(key, query[start:stop], ((1,), (1,)))
        allowed = column_ids[...] <= row_ids[:, start:stop]
        numerator = jnp.where(allowed, jnp.exp(scores), 0.0)
        probs = numerator * (1.0 / jnp.sum(numerator, axis=0, keepdims=True))
        probs = probs.astype(jnp.bfloat16)
        prob_ref[:, start:stop] = probs
        out_t = dot(value, probs, ((0,), (0,)))
        out_t_ref[:, start:stop] = out_t.astype(jnp.bfloat16).astype(jnp.float32)
    out = jnp.transpose(out_t_ref[...])
    for m, distance in enumerate(DISTANCES):
        out_refs[7][me_ref[0] ^ distance] = low(pack(out[m * rows : (m + 1) * rows]))


def affine_kernel(me_ref, slab_ref, act_ref, inc_ref, w_ref, up_ref, out_ref, *term_refs):
    rows, width = act_ref.shape
    columns = [unpack(wide(slab_ref[h]), rows) for h in range(HEADS)]
    attended = low(jnp.concatenate(columns, axis=1))
    factor = jnp.exp(-dot(attended, w_ref[:, width:]))
    scaled = inc_ref[...].astype(jnp.float32) * factor
    up_ref[...] = low(scaled)
    shift_part = dot(attended, w_ref[:, :width])
    latent_part = scaled * (act_ref[...].astype(jnp.float32) - shift_part)
    grad_affine = jnp.concatenate([-scaled, 1.0 - latent_part], axis=1).astype(jnp.bfloat16)
    grad = dot(grad_affine, w_ref[...], ((1,), (1,)))
    for h in range(HEADS):
        out_ref[h] = low(pack(grad[:, h * HEAD_DIM : (h + 1) * HEAD_DIM]))
    columns = [unpack(wide(slab_ref[me_ref[0] ^ m]), rows) for m in range(HEADS)]
    for half, order in enumerate(ORDERS):
        right = grad_affine[:, half * width : (half + 1) * width]
        for term_ref, group in zip(term_refs[4 * half : 4 * half + 4], order):
            left = low(jnp.concatenate([columns[m] for m in group], axis=1))
            term_ref[...] = low(dot(left, right, ((0,), (0,))))


ORDERS = (((1, 5, 3, 7), (2, 6), (4,), (0,)), ((2, 6, 3, 7), (1, 5), (4,), (0,)))


def backward_kernel(me_ref, slab_ref, prob_ref, qk_ref, v_ref, out_t_ref, *refs):
    early, late, up_ref, out_refs = refs[:3], refs[3:6], refs[6], refs[7:-4]
    gk_ref, gv_ref, gq_ref, held_ref = refs[-4:]
    first, rows = early[0].shape[:2]
    slabs = [wide(slab_ref[me_ref[0] ^ distance]) for distance in DISTANCES]
    grad_f = jnp.concatenate([unpack(slab, rows) for slab in slabs], axis=0)
    grad = grad_f.astype(jnp.bfloat16)
    tokens = grad_f.shape[0]
    grad_t = jnp.transpose(grad_f)
    correction = jnp.sum(grad_t * out_t_ref[...], axis=0, keepdims=True)
    grad_t = grad_t.astype(jnp.bfloat16)
    qk, value = qk_ref[...], v_ref[...]
    query, key = qk[:, :HEAD_DIM], qk[:, HEAD_DIM:]
    gk_ref[...] = jnp.zeros_like(gk_ref)
    gv_ref[...] = jnp.zeros_like(gv_ref)
    for start, stop in tiles(tokens):
        probs = prob_ref[:, start:stop]
        grad_probs = dot(value, grad_t[:, start:stop])
        scores = probs.astype(jnp.float32) * (grad_probs - correction[:, start:stop])
        scores = scores.astype(jnp.bfloat16)
        gv_ref[...] += dot(probs, grad[start:stop])
        gk_ref[...] += dot(scores, query[start:stop])
        gq_ref[:, start:stop] = dot(key, scores, ((0,), (0,)))
    grad_q = jnp.transpose(gq_ref[...])
    qk_sum = v_sum = 0.0
    for m in range(HEADS):
        own = slice(m * rows, (m + 1) * rows)
        normed, unit, scale = [
            early[i][m] if m < first else late[i][m - first] for i in range(3)
        ]
        raw = jnp.concatenate([grad_q[own], gk_ref[own, :]], axis=1) * HEAD_DIM ** (-0.5)
        back = scale * (raw - unit * (half_sums(raw * unit) / HEAD_DIM))
        back, grad_v = back.astype(jnp.bfloat16), gv_ref[own, :]
        mirrored = out_refs[DISTANCES.index(DISTANCES[m] ^ HEADS - 1)]
        mirrored[:PACKED, :] = low(pack(grad_v))
        mirrored[PACKED : PACKED + rows, :] = back
        qk_sum = qk_sum + dot(back, normed, ((0,), (0,)))
        v_sum = v_sum + dot(grad_v.astype(jnp.bfloat16), normed, ((0,), (0,)))
    step = qk_sum.shape[1] // HEADS
    middle = PACKED + rows + 2 * HEAD_DIM
    for g in range(HEADS):
        own = slice(g * step, (g + 1) * step)
        held_ref[g] = low(jnp.concatenate([qk_sum[:, own], v_sum[:, own]], axis=0))
    for m, out_ref in enumerate(out_refs):
        out_ref[PACKED + rows : middle + HEAD_DIM, :] = held_ref[me_ref[0] ^ DISTANCES[m]]
    for i in range(up_ref.shape[1] // 128):
        start = middle + HEAD_DIM + i * rows
        out_refs[-1][start : start + rows, :] = up_ref[:, i * 128 : (i + 1) * 128]


def turn_kernel(me_ref, *refs):
    slabs, out_refs, held_ref = refs[:HEADS], refs[HEADS + 2 : -1], refs[-1]
    start = slabs[0].shape[0] - 3 * HEAD_DIM
    for m, slab in enumerate(slabs):
        held_ref[me_ref[0] ^ DISTANCES[m]] = slab[start : start + 3 * HEAD_DIM, :]
    for i, out_ref in enumerate(out_refs):
        own = slice(i * HEAD_DIM, (i + 1) * HEAD_DIM)
        heads = [wide(held_ref[h, own, :]) for h in range(HEADS)]
        out_ref[0] = jnp.transpose(jnp.concatenate(heads, axis=0))


def second_sum_kernel(*refs):
    for second, got, out in zip(refs[0:2], refs[2:4], refs[-2:]):
        start = got.shape[0] - second.shape[0]
        out[...] = low(wide(second[...]) + wide(got[start:, :]))


def third_sum_kernel(*refs):
    for i in range(2):
        third, keep, got, more = [ref[...] for ref in refs[i:8:2]]
        size = third.shape[0]
        leaving, staying = refs[9 + i], refs[11 + i]
        leaving[...] = low(wide(third) + wide(got[size : 2 * size]) + wide(more[size:]))
        staying[...] = wide(keep) + wide(got[:size]) + wide(more[:size])


def last_sum_kernel(keep_a, keep_b, got_a, got_b, out_ref):
    for i, (keep, got) in enumerate(((keep_a, got_a), (keep_b, got_b))):
        width = keep.shape[1]
        out_ref[0, :, i * width : (i + 1) * width] = keep[...] + wide(got[...])


def input_kernel(me_ref, *refs):
    slabs, (wq_ref, wk_ref, wv_ref, *acts, _, out_ref) = refs[:HEADS], refs[HEADS:-1]
    held_ref = refs[-1]
    rows, width = out_ref.shape
    start = slabs[0].shape[0]
    starts = range(start, start + rows * width // 128, rows)
    scaled = jnp.concatenate([wide(slabs[-1][i : i + rows, :]) for i in starts], axis=1)
    for m, slab in enumerate(slabs):
        held_ref[me_ref[0] ^ DISTANCES[m]] = slab[: PACKED + rows, :]
    unit, row_scale = normalize(joined(acts, width)[0])
    queries, keys, values = [], [], []
    for pair in range(HEADS // 2):
        even, odd = [wide(held_ref[2 * pair + i]) for i in range(2)]
        lower = low_lanes(even[PACKED:])
        queries.append(jnp.where(lower, even[PACKED:], swap(odd[PACKED:])))
        keys.append(jnp.where(lower, swap(even[PACKED:]), odd[PACKED:]))
        values += [unpack(even[:PACKED], rows), unpack(odd[:PACKED], rows)]
    total = 0.0
    for parts, ref in ((queries, wq_ref), (keys, wk_ref), (values, wv_ref)):
        left = jnp.concatenate(parts, axis=1).astype(jnp.bfloat16)
        total = total + dot(left, ref[...], ((1,), (1,)))
    total = total - unit * jnp.mean(total * unit, axis=-1, keepdims=True)
    out_ref[...] = (scaled + row_scale * total).astype(jnp.bfloat16)


def reorder_kernel(order_ref, rows_ref, out_ref):
    rows = rows_ref.shape[0]
    chosen = lax.broadcasted_iota(jnp.int32, (rows, rows), 0) == order_ref[...]
    chosen = low(jnp.where(chosen, 1.0, 0.0))
    out_ref[0] = low(dot(chosen, rows_ref[...], ((0,), (0,))))


def hop(block, distance):
    route = [(i, i ^ distance) for i in range(lax.axis_size("seq"))]
    return lax.ppermute(block, "seq", route)


def exchange(slabs):
    return [hop(slab, m) if m else slab for m, slab in zip(DISTANCES, slabs)]


def switch(slabs):
    return lax.all_to_all(slabs, "seq", split_axis=0, concat_axis=0, tiled=True)


def spread(block, weight):
    middle = block.shape[1] // 2
    pieces = [block[:, :middle], block[:, middle:]]
    far = [hop(piece, 4) for piece in pieces]
    near, side = hop(block, 2), hop(block, 1)
    near, weight = lax.optimization_barrier((near, weight))
    side_far = [hop(piece, 1) for piece in far]
    near_far = [hop(piece, 2) for piece in far]
    side_near = hop(near, 1)
    last = [hop(side_far[0], 2), hop(near_far[1], 1)]
    early = [block, side, near, *far, side_near, *side_far]
    return early, near_far, last, weight


DISTANCES = (0, 1, 2, 4, 3, 5, 6, 7)


def wide(matrix):
    return matrix.astype(jnp.float32)


def low(matrix):
    return matrix.astype(jnp.bfloat16)


EARLY = 6


def head_shards(
    activations, incoming, w_query, w_key, w_value, w_out, block_ids, flip_order
):
    parts = lax.axis_size("seq")
    me = lax.axis_index("seq").astype(jnp.int32).reshape(1)
    field, upstream = activations[0], incoming[0]
    wq, wk, wv, wo = w_query[0], w_key[0], w_value[0], w_out[0]
    rows, width = field.shape
    inner = wq.shape[1]
    tokens = parts * rows
    f32 = jnp.float32

    def out(*dims, dtype=jnp.bfloat16):
        return jax.ShapeDtypeStruct(dims, dtype)

    order = me[0] ^ jnp.array(DISTANCES, jnp.int32)
    ids = jnp.take(block_ids.reshape(parts, rows), order, axis=0).reshape(tokens)
    (weight,) = call(
        select_kernel,
        1.5,
        [("s", me), ("a", wq), ("a", wk), ("a", wv)],
        [out(width, 3 * HEAD_DIM)],
        [pltpu.VMEM((width, 2 * HEAD_DIM), jnp.bfloat16)] * 3 + [pltpu.SemaphoreType.DMA((3,))],
    )
    first_blocks, near_far, mirrored, weight = spread(field, weight)
    pair = 2 * HEAD_DIM
    normed, unit, unit_scale, projected = call(
        project_kernel,
        2,
        [("v", block) for block in first_blocks] + [("v", weight)],
        [
            out(EARLY, rows, width),
            out(EARLY, rows, pair, dtype=f32),
            out(EARLY, rows, pair, dtype=f32),
            out(EARLY, rows, HEAD_DIM, dtype=f32),
        ],
    )
    late = parts - EARLY
    made = call(
        attend_kernel,
        5,
        [("s", me), ("v", unit), ("v", projected), ("v", weight)]
        + [("v", ids[None, :]), ("v", ids[:, None])]
        + [("v", block) for block in (*near_far, *mirrored)],
        [
            out(late, rows, width),
            out(late, rows, pair, dtype=f32),
            out(late, rows, pair, dtype=f32),
            out(tokens, tokens),
            out(tokens, pair),
            out(tokens, HEAD_DIM),
            out(HEAD_DIM, tokens, dtype=f32),
        ]
        + [out(parts, PACKED, 128)],
    )
    late_parts, (probs, qk, value, out_t), packed = made[:3], made[3:7], switch(made[7])
    scaled, grad_slabs, *terms = call(
        affine_kernel,
        3,
        [("s", me)] + [("v", x) for x in (packed, field, upstream, wo)],
        [out(rows, width), out(HEADS, PACKED, 128)]
        + [out(len(group) * HEAD_DIM, width) for order in ORDERS for group in order],
    )
    grad_slabs = switch(grad_slabs)
    grad_slabs, terms = lax.optimization_barrier((grad_slabs, terms))
    first, second, third, keep = zip(terms[:4], terms[4:])
    got = [partner(part, "seq", bit) for bit, part in enumerate(first)]
    grads = call(
        backward_kernel,
        6,
        [("s", me)]
        + [("v", x) for x in (grad_slabs, probs, qk, value, out_t)]
        + [("v", x) for x in (normed, unit, unit_scale, *late_parts, scaled)],
        [out(PACKED + rows + 3 * HEAD_DIM, 128)] * (parts - 1)
        + [out(PACKED + rows + 3 * HEAD_DIM + rows * width // 128, 128)],
        [
            pltpu.VMEM((tokens, HEAD_DIM), f32),
            pltpu.VMEM((tokens, HEAD_DIM), f32),
            pltpu.VMEM((HEAD_DIM, tokens), f32),
            pltpu.VMEM((HEADS, 3 * HEAD_DIM, 128), jnp.bfloat16),
        ],
    )
    slabs = exchange(grads)
    leaving = call(
        second_sum_kernel,
        1,
        [("v", x) for x in (*second, *got)] + [("a", slabs[i]) for i in (3, 6, 7)],
        [out(*second[0].shape)] * 2,
    )
    more = [partner(part, "seq", 1 - bit) for bit, part in enumerate(leaving)]
    *leaving, keep_a, keep_b = call(
        third_sum_kernel,
        2,
        [("v", x) for x in (*third, *keep, *got, *more)] + [("a", slabs[2])],
        [out(*third[0].shape)] * 2 + [out(*keep[0].shape, dtype=f32)] * 2,
    )
    rest = [partner(part, "seq", 2) for part in leaving]
    (grad_input,) = call(
        input_kernel,
        1.5,
        [("s", me)] + [("v", x) for x in (*slabs, wq, wk, wv, *mirrored)] + [("a", leaving[0])],
        [out(rows, width)],
        [pltpu.VMEM((HEADS, PACKED + rows, 128), jnp.bfloat16)],
    )
    moved = to_previous(grad_input)
    (grad_out,) = call(
        last_sum_kernel,
        2,
        [("v", x) for x in (keep_a, keep_b, *rest)],
        [out(1, keep_a.shape[0], 2 * width, dtype=f32)],
    )
    grad_q, grad_k, grad_v = call(
        turn_kernel,
        3,
        [("s", me)] + [("v", x) for x in slabs] + [("a", x) for x in rest],
        [out(1, width // parts, inner, dtype=f32)] * 3,
        [pltpu.VMEM((HEADS, 3 * HEAD_DIM, 128), jnp.bfloat16)],
    )
    (carry,) = call(
        reorder_kernel, 1, [("v", flip_order), ("v", moved)], [out(1, rows, width)]
    )
    return (carry, grad_q, grad_k, grad_v, grad_out)


def solution(mesh):
    shards = head_shards if mesh.shape["seq"] == HEADS else general_shards
    in_specs = (
        P("section", "seq", None),
        P("section", "seq", None),
        P("section", None, None),
        P("section", None, None),
        P("section", None, None),
        P("section", None, None),
        P(),
        P("section", None),
    )
    out_specs = (
        P("section", "seq", None),
        P("section", "seq", None),
        P("section", "seq", None),
        P("section", "seq", None),
        P("section", "seq", None),
    )
    return jax.shard_map(shards, mesh=mesh, in_specs=in_specs, out_specs=out_specs, check_vma=False)
```
